32 devices in a mesh: groups: 2 (over x), blk: 16 (over z, y, core).
Axes of the slice: x: 2, y: 2, z: 4, core: 2. Of those that a mesh axis runs over, the one named last changes fastest.
Arguments:
- records: bfloat16 [8192, 2048], P(('groups', 'blk')), parts along dimension 0, may hold values from -6 to 6
- dest: int32 [8192, 1], P(('groups', 'blk')), parts along dimension 0, may hold values from 0 to 15; in each aligned block of 256 rows (0 to 255, 256 to 511, ...) at most 32 rows name the same one
- slot: int32 [8192, 1], P(('groups', 'blk')), parts along dimension 0, may hold values from 0 to 255
- valid: int32 [8192, 1], P(('groups', 'blk')), parts along dimension 0, may hold values from 256 to 2048
- masks: int32 [2], replicated, may hold values from 1 to 15, as said below
Outputs:
- correlations: bfloat16 [2, 4096, 128, 128], P(None, ('groups', 'blk')), parts along dimension 1
The draws below stay inside these ranges and needn't reach their ends.
There are 2 independent parts, one for each index of `groups`. The reference program is written for one: setup_inputs(seed, part) draws one part's arguments, and reference() takes and returns one part's arrays. A program takes and returns all parts, laid end to end along the dimension named above; an argument that names none is the same for every part. Nothing has to cross between parts.
Inputs may be any that keep to these rules, and one draw needn't show every extreme that they name: `dest`: in the rows of one device no block is named more than 32 times. `masks`: 2 distinct numbers; one of them is 15.
All inputs are finite; a program needn't handle non-finite values.
Results may differ from the reference program's by a relative error of at most 0.0085.
Values may be sent and summed in bfloat16 or wider, within the bound.
No kernel may reach another device: no remote copies, remote signals or barrier semaphores. Data moves between devices by JAX's collectives and lax.ppermute only.
A program may use at most 128 MiB of HBM per device.

```python
import math
import jax
import jax.numpy as jnp
import numpy as np
from jax import lax

CH = 128
NFFT = 2048
F = 256
LAGS = 128
W = 2
ROUNDS = 2
SEG_DEV = 256
CAP = 32
BLOCKS = 16
SEGMENTS = 4096
N_BLK = 16


def draw_masks(key, part):
    third = jax.random.fold_in(jax.random.fold_in(key, 11), 2)
    fourth = jax.random.fold_in(jax.random.fold_in(key, 11), 3)
    count = N_BLK - 1
    score = jax.random.randint(third, (count,), 0, 1 << 20, dtype=jnp.int32)
    score = score * N_BLK + jnp.arange(count, dtype=jnp.int32)
    score = score.at[count - 1].set(-1)
    picked = jnp.argsort(score, stable=True)[:ROUNDS].astype(jnp.int32) + 1
    order = jax.random.permutation(fourth, ROUNDS)
    return picked[order].astype(jnp.int32)


def touch_ends(drawn, key, smallest, top_value):
    longest = drawn.shape.index(max(drawn.shape))
    spots = []
    for shift in (0, 1):
        where = [jax.random.randint(jax.random.fold_in(key, axis), (), 0, length) for axis, length in enumerate(drawn.shape)]
        where[longest] = (where[longest] + shift) % drawn.shape[longest]
        spots.append(tuple(where))
    return drawn.at[spots[0]].set(smallest).at[spots[1]].set(top_value)


def levels(own_key, shape, cuts, low, largest):
    def one(axis_at, shards_of):
        heights = jax.random.uniform(jax.random.fold_in(jax.random.fold_in(own_key, 6), axis_at), (shards_of,), jnp.float32, low / len(cuts), largest / len(cuts))
        return jnp.repeat(jnp.exp(heights), shape[axis_at] // shards_of).reshape((-1,) + (1,) * (len(shape) - axis_at - 1))

    gain = one(*cuts[0])
    for cut in cuts[1:]:
        gain = gain * one(*cut)
    return gain


def assign_block(stream_key, own, number, rows, amount, top, reach, skew):
    sequence = jax.random.permutation(stream_key, amount)
    crowded, common = portions_of(amount, rows * top, reach, skew, True), portions_of(amount, rows * top, reach, skew, False)
    places = jnp.arange(amount)

    def named(lengths, offset_by):
        used = int((lengths > 0).sum())
        fixed = max(1, used // 4)
        passed = fixed + (places - fixed + offset_by * (used - fixed)) % max(1, amount - fixed)
        return jnp.zeros((amount,), jnp.int32).at[sequence[jnp.where(places < fixed, places, passed)]].set(jnp.asarray(lengths, jnp.int32))

    lengths = jnp.where(number % 4 == 0, named(crowded, number // 4), named(common, number - number // 4 - 1))
    mixed = jax.random.permutation(jax.random.fold_in(own, 3), amount)
    source_of, receiver = mixed[0:amount // 2 * 2:2], mixed[1:amount // 2 * 2:2]
    room = jnp.minimum(lengths[source_of] - 1, reach - lengths[receiver]) // 2
    room = jnp.where((source_of == sequence[0]) | (receiver == sequence[0]) | (lengths[receiver] == 0), 0, jnp.maximum(room, 0))
    passed = jax.random.randint(jax.random.fold_in(own, 4), (amount // 2,), 0, 1 << 20) % (room + 1)
    lengths = lengths.at[source_of].add(-passed).at[receiver].add(passed)
    items = jnp.searchsorted(jnp.cumsum(lengths), jnp.arange(rows * top), side="right").astype(jnp.int32)
    table = items.reshape(top, rows).T
    table = table[jax.random.permutation(jax.random.fold_in(own, 1), rows)]
    offset_by = jax.random.randint(jax.random.fold_in(own, 2), (rows, 1), 0, top)
    return jnp.take_along_axis(table, (jnp.arange(top)[None, :] + offset_by) % top, axis=1)


def portions_of(number_of, total, bound, skew, full):
    loads = [(1 << 20) // math.isqrt(grade ** skew) + 1 for grade in range(1, number_of + 1)]
    largest = bound if full else min(bound, max(-(-total // number_of), total * loads[0] // sum(loads)))
    least = 1 if total - largest >= number_of - 1 else 0
    holding, rest = [largest] + [least] * (number_of - 1), total - largest - least * (number_of - 1)
    while rest > 0:
        free = [i for i in range(1, number_of) if holding[i] < largest] or [i for i in range(1, number_of) if holding[i] < bound]
        mass, budget = sum([loads[i] for i in free]), rest
        for i in free:
            addition = min(bound - holding[i], max(1, budget * loads[i] // mass), rest)
            holding[i] = holding[i] + addition
            rest = rest - addition
    return np.array(holding)


def scatter_about(rng, shape, width, limit, cuts=(), kind=jnp.bfloat16):
    drawn = jax.random.normal(rng, shape, jnp.float32) * width
    if len(cuts) > 0:
        drawn = levels(rng, shape, cuts, -0.22, 0.18) * drawn
    return jnp.clip(drawn, min=-limit, max=limit).astype(kind)


def setup_inputs(seed: int = 0, part: int = 0) -> dict:
    arg_keys = jax.random.split(jax.random.key(seed), 6)
    part_keys = jax.random.split(jax.random.fold_in(arg_keys[5], part), 6)
    records = scatter_about(part_keys[0], (SEGMENTS, NFFT), 1.0, 6.0, ((0, 16),))
    dest_keys = jax.random.split(jax.random.fold_in(part_keys[1], 1), SEGMENTS // SEG_DEV)
    dest_turns = jax.random.permutation(jax.random.fold_in(part_keys[1], 3), SEGMENTS // SEG_DEV)
    dest = jax.vmap(lambda own, number: assign_block(jax.random.fold_in(part_keys[1], 2), own, number, SEG_DEV, BLOCKS, 1, CAP, 2))(dest_keys, dest_turns).reshape((SEGMENTS, 1))
    slot = touch_ends(jax.random.randint(part_keys[2], (SEGMENTS, 1), 0, CH * W), jax.random.fold_in(part_keys[2], 1), 0, (CH * W) - 1).astype(jnp.int32)
    valid = touch_ends(jax.random.randint(part_keys[3], (SEGMENTS, 1), NFFT // 8, NFFT + 1), jax.random.fold_in(part_keys[3], 1), NFFT // 8, NFFT).astype(jnp.int32)
    masks = draw_masks(jax.random.fold_in(arg_keys[5], 71), part)
    return dict(records=records, dest=dest, slot=slot, valid=valid, masks=masks)


def forward_table(nfft, bins):
    sample = jnp.arange(nfft, dtype=jnp.int32)[:, None]
    freq = jnp.arange(1, bins + 1, dtype=jnp.int32)[None, :]
    angle = (sample * freq % nfft).astype(jnp.float32) * (2.0 * math.pi / nfft)
    return jnp.concatenate([jnp.cos(angle), -jnp.sin(angle)], axis=1).astype(jnp.bfloat16)

def inverse_table(nfft, bins, lags):
    shift = (jnp.arange(lags, dtype=jnp.int32) - lags // 2) % nfft
    freq = jnp.arange(1, bins + 1, dtype=jnp.int32)[:, None]
    angle = (freq * shift[None, :] % nfft).astype(jnp.float32) * (2.0 * math.pi / nfft)
    return jnp.concatenate([jnp.cos(angle), -jnp.sin(angle)], axis=0).astype(jnp.bfloat16)

def correlate_pair(own, other, itable):
    bins = own.shape[2] // 2
    left = own.astype(jnp.float32)
    right = other.astype(jnp.float32)
    first = jnp.concatenate([left[..., :bins], left[..., bins:]], axis=1)
    second = jnp.concatenate([left[..., bins:], -left[..., :bins]], axis=1)
    both = jnp.concatenate([right[..., :bins], right[..., bins:]], axis=1)
    real_part = jnp.einsum('iwf,jwf->ijf', first, both)
    imag_part = jnp.einsum('iwf,jwf->ijf', second, both)
    cross = jnp.concatenate([real_part, imag_part], axis=-1).astype(jnp.bfloat16)
    chans = own.shape[0]
    scale = 1.0 / math.sqrt(own.shape[1] * bins)
    lagged = jnp.dot(cross.reshape(chans * chans, 2 * bins), itable, preferred_element_type=jnp.float32)
    return (lagged * scale).astype(jnp.bfloat16).reshape(chans, chans, -1)

def reference(records, dest, slot, valid, masks):
    window = jnp.arange(NFFT, dtype=jnp.int32)[None, :] < valid[:, 0:1]
    masked = records * window.astype(jnp.bfloat16)
    target = dest[:, 0] * (CH * W) + slot[:, 0]
    summed = jnp.zeros((BLOCKS * CH * W, NFFT), jnp.float32).at[target].add(masked.astype(jnp.float32))
    coverage = jnp.zeros((BLOCKS * CH * W, NFFT), jnp.float32).at[target].add(window.astype(jnp.float32))
    trace = summed / jnp.maximum(coverage, 1.0)
    meansq = lax.optimization_barrier(jnp.mean(trace * trace, axis=1, keepdims=True))
    normed = (trace * lax.rsqrt(meansq + 1e-06)).astype(jnp.bfloat16)
    spectrum = jnp.dot(normed, forward_table(NFFT, F), preferred_element_type=jnp.float32)
    real_part = spectrum[:, :F]
    imag_part = spectrum[:, F:]
    amplitude = lax.rsqrt(jnp.maximum(real_part * real_part + imag_part * imag_part, NFFT / 4.0))
    white = jnp.concatenate([real_part * amplitude, imag_part * amplitude], axis=1).astype(jnp.bfloat16)
    tiles = white.reshape(BLOCKS, CH, W, 2 * F)
    itable = inverse_table(NFFT, F, LAGS)
    results = []
    for step in range(ROUNDS):
        partner = jnp.arange(BLOCKS, dtype=jnp.int32) ^ masks[step]
        others = tiles[partner]
        out = lax.map(lambda pair: correlate_pair(pair[0], pair[1], itable), (tiles, others))
        results.append(out.reshape(BLOCKS * CH, CH, LAGS))
    return jnp.stack(results)
```

```python
import functools
import math

import jax
import jax.numpy as jnp
import numpy as np
from jax import lax
from jax.experimental import pallas as pl
from jax.experimental.pallas import tpu as pltpu
from jax.sharding import PartitionSpec as P

CH = 128
F = 256
LAGS = 128
W = 2
VALID_BITS = 12
LOW_BITS = 4


def forward_table(nfft, bins):
    sample = np.arange(nfft, dtype=np.int64)[:, None]
    freq = np.arange(1, bins + 1, dtype=np.int64)[None, :]
    angle = (sample * freq % nfft).astype(np.float64) * (2.0 * math.pi / nfft)
    return np.concatenate([np.cos(angle), -np.sin(angle)], axis=1).astype(np.float32).astype(jnp.bfloat16)


def lag_table(nfft, bins, lags):
    shift = (np.arange(lags, dtype=np.int64) - lags // 2) % nfft
    freq = np.arange(1, bins + 1, dtype=np.int64)[None, :]
    angle = (freq * shift[:, None] % nfft).astype(np.float64) * (2.0 * math.pi / nfft)
    return np.concatenate([np.cos(angle), -np.sin(angle)], axis=1).astype(np.float32).astype(jnp.bfloat16)


def iota(shape, dim):
    return lax.broadcasted_iota(jnp.int32, shape, dim)


def pack_kernel(owners, capacity, dest_ref, slot_ref, valid_ref, records_ref, out_ref, label_ref, order_ref):
    held = dest_ref.shape[1]
    rows = owners * capacity

    @pl.when(pl.program_id(0) == 0)
    def _():
        dest = dest_ref[...]
        match = (iota((owners, held), 0) == dest).astype(jnp.float32)
        before = (iota((held, held), 0) < iota((held, held), 1)).astype(jnp.bfloat16)
        earlier = jnp.dot(match.astype(jnp.bfloat16), before, preferred_element_type=jnp.float32)
        rank = jnp.sum(earlier * match, axis=0, keepdims=True).astype(jnp.int32)
        position = dest * capacity + rank
        order = (iota((rows, held), 0) == position).astype(jnp.float32).astype(jnp.bfloat16)
        order_ref[...] = order
        valid = valid_ref[...]
        row = iota((16, held), 0)
        parts = jnp.where(
            row == 0,
            slot_ref[...],
            jnp.where(row == 1, valid >> LOW_BITS, valid & ((1 << LOW_BITS) - 1)),
        )
        moved = lax.dot_general(
            parts.astype(jnp.float32).astype(jnp.bfloat16),
            order,
            (((1,), (1,)), ((), ())),
            preferred_element_type=jnp.float32,
        ).astype(jnp.int32)
        label_ref[...] = (
            (moved[0:1] << VALID_BITS) + (moved[1:2] << LOW_BITS) + moved[2:3]
        )

    out_ref[...] = jnp.dot(
        order_ref[...], records_ref[...], preferred_element_type=jnp.float32
    ).astype(jnp.bfloat16)


def pack(records, dest, slot, valid, owners, capacity):
    held, nfft = records.shape
    rows = owners * capacity
    step = min(nfft, 512)
    whole = pl.BlockSpec((1, held), lambda n: (0, 0))
    return pl.pallas_call(
        functools.partial(pack_kernel, owners, capacity),
        grid=(nfft // step,),
        in_specs=[whole, whole, whole, pl.BlockSpec((held, step), lambda n: (0, n))],
        out_specs=[
            pl.BlockSpec((rows, step), lambda n: (0, n)),
            pl.BlockSpec((1, rows), lambda n: (0, 0)),
        ],
        out_shape=[
            jax.ShapeDtypeStruct((rows, nfft), jnp.bfloat16),
            jax.ShapeDtypeStruct((1, rows), jnp.int32),
        ],
        scratch_shapes=[pltpu.VMEM((rows, held), jnp.bfloat16)],
        compiler_params=pltpu.CompilerParams(vmem_limit_bytes=32 * 1024 * 1024),
        name="pack",
    )(dest.reshape(1, held), slot.reshape(1, held), valid.reshape(1, held), records)


def whiten_kernel(
    owners, capacity, me_ref, labels_ref, arrived_ref, table_ref, out_ref, trace_ref, spectrum_ref
):
    rows, nfft = arrived_ref.shape
    slots = CH * W
    bins = table_ref.shape[1] // 2
    shift = capacity.bit_length() - 1
    labels = labels_ref[...]
    slot = labels >> VALID_BITS
    valid = labels & ((1 << VALID_BITS) - 1)
    parts = jnp.concatenate(
        [
            (slot % W) * CH + slot // W,
            valid >> LOW_BITS,
            valid & ((1 << LOW_BITS) - 1),
        ],
        axis=0,
    )
    mine = me_ref[0] * capacity
    pick = (iota((rows, rows), 0) == mine + (iota((rows, rows), 1) & (capacity - 1)))
    picked = jnp.dot(
        parts.astype(jnp.float32).astype(jnp.bfloat16),
        pick.astype(jnp.float32).astype(jnp.bfloat16),
        preferred_element_type=jnp.float32,
    )
    source = iota((owners, rows), 0) == iota((owners, rows), 1) >> shift
    rowed = [
        jnp.sum(
            jnp.where(source, picked[k * owners : (k + 1) * owners], 0.0), axis=0, keepdims=True
        )
        for k in range(3)
    ]
    slot_row = rowed[0].astype(jnp.int32)
    valid_row = rowed[1] * float(1 << LOW_BITS) + rowed[2]
    scatter = (iota((slots, rows), 0) == slot_row).astype(jnp.float32).astype(jnp.bfloat16)
    valid_col = jnp.transpose(jnp.broadcast_to(valid_row, (128, rows))).astype(jnp.int32)
    width = 256
    power = jnp.zeros((slots, 128), jnp.float32)
    for begin in range(0, nfft, width):
        inside = jnp.concatenate(
            [
                (iota((rows, 128), 1) + (begin + lane) < valid_col)
                .astype(jnp.float32)
                .astype(jnp.bfloat16)
                for lane in range(0, width, 128)
            ],
            axis=1,
        )
        masked = arrived_ref[:, begin : begin + width] * inside
        summed = jnp.dot(scatter, masked, preferred_element_type=jnp.float32)
        coverage = jnp.dot(scatter, inside, preferred_element_type=jnp.float32)
        trace = summed / jnp.maximum(coverage, 1.0)
        trace_ref[:, begin : begin + width] = trace
        square = trace * trace
        for lane in range(0, width, 128):
            power = power + square[:, lane : lane + 128]
    meansq = jnp.sum(power, axis=1, keepdims=True) * (1.0 / nfft)
    gain = lax.rsqrt(meansq + 1e-06)
    width = 512
    for begin in range(0, nfft, width):
        normed = (trace_ref[:, begin : begin + width] * gain).astype(jnp.bfloat16)
        part = jnp.dot(
            normed, table_ref[begin : begin + width, :], preferred_element_type=jnp.float32
        )
        if begin == 0:
            spectrum_ref[...] = part
        else:
            spectrum_ref[...] += part
    real_part = spectrum_ref[:, :bins]
    imag_part = spectrum_ref[:, bins:]
    amplitude = lax.rsqrt(jnp.maximum(real_part * real_part + imag_part * imag_part, nfft / 4.0))
    real_part = (real_part * amplitude).astype(jnp.bfloat16)
    imag_part = (imag_part * amplitude).astype(jnp.bfloat16)
    for w in range(W):
        at = w * 2 * bins
        out_ref[:, at : at + bins] = real_part[w * CH : (w + 1) * CH]
        out_ref[:, at + bins : at + 2 * bins] = imag_part[w * CH : (w + 1) * CH]


def whiten(me, labels, arrived, table, owners, capacity):
    rows, nfft = arrived.shape
    bins = table.shape[1] // 2
    vmem = pl.BlockSpec(memory_space=pltpu.VMEM)
    return pl.pallas_call(
        functools.partial(whiten_kernel, owners, capacity),
        in_specs=[pl.BlockSpec(memory_space=pltpu.SMEM), vmem, vmem, vmem],
        out_specs=vmem,
        out_shape=jax.ShapeDtypeStruct((CH, W * 2 * bins), jnp.bfloat16),
        scratch_shapes=[
            pltpu.VMEM((CH * W, nfft), jnp.float32),
            pltpu.VMEM((CH * W, 2 * bins), jnp.float32),
        ],
        compiler_params=pltpu.CompilerParams(vmem_limit_bytes=40 * 1024 * 1024),
        name="whiten",
    )(me, labels, arrived, table)


GROUP = 16


def correlate_kernel(
    scale, order_ref, own_ref, first_ref, second_ref, table_ref, out_ref, both_ref, wide_ref, turned_a, turned_b
):
    step = pl.program_id(0)
    lags = table_ref.shape[0]
    bins = table_ref.shape[1] // 2

    @pl.when(step == 0)
    def _():
        wide_ref[...] = own_ref[...].astype(jnp.float32)
        at = pl.multiple_of(order_ref[0] * CH, CH)
        both_ref[pl.ds(at, CH), :] = first_ref[...]
        both_ref[pl.ds(CH - at, CH), :] = second_ref[...]

    turned = (turned_a, turned_b)
    for pair in range(GROUP // 2):
        a_ref = turned[pair % 2]
        for half in range(2):
            row = step * GROUP + pair * 2 + half
            u = wide_ref[pl.ds(row, 1), :]
            cos = table_ref[:, :bins]
            msin = table_ref[:, bins:]
            for w in range(W):
                at = w * 2 * bins
                ur = jnp.broadcast_to(u[:, at : at + bins], (lags, bins)).astype(jnp.bfloat16)
                ui = jnp.broadcast_to(u[:, at + bins : at + 2 * bins], (lags, bins)).astype(
                    jnp.bfloat16
                )
                rows = slice(half * lags, (half + 1) * lags)
                a_ref[rows, at : at + bins] = ur * cos + ui * msin
                a_ref[rows, at + bins : at + 2 * bins] = ui * cos - ur * msin
        lagged = lax.dot_general(
            both_ref[...],
            a_ref[...],
            (((1,), (1,)), ((), ())),
            preferred_element_type=jnp.float32,
        )
        lagged = (lagged * scale).astype(jnp.bfloat16)
        for half in range(2):
            for r in range(2):
                out_ref[r, pair * 2 + half] = lagged[
                    r * CH : (r + 1) * CH, half * lags : (half + 1) * lags
                ]


def correlate(order, own, first, second, table):
    lags, width = table.shape
    depth = own.shape[1]
    scale = 1.0 / math.sqrt(W * (width // 2))
    block = pl.BlockSpec((CH, depth), lambda n: (0, 0))
    return pl.pallas_call(
        functools.partial(correlate_kernel, scale),
        grid=(CH // GROUP,),
        in_specs=[
            pl.BlockSpec(memory_space=pltpu.SMEM),
            block,
            block,
            block,
            pl.BlockSpec((lags, width), lambda n: (0, 0)),
        ],
        out_specs=pl.BlockSpec((2, GROUP, CH, lags), lambda n: (0, n, 0, 0)),
        out_shape=jax.ShapeDtypeStruct((2, CH, CH, lags), jnp.bfloat16),
        scratch_shapes=[
            pltpu.VMEM((2 * CH, depth), jnp.bfloat16),
            pltpu.VMEM((CH, depth), jnp.float32),
            pltpu.VMEM((2 * lags, depth), jnp.bfloat16),
            pltpu.VMEM((2 * lags, depth), jnp.bfloat16),
        ],
        compiler_params=pltpu.CompilerParams(vmem_limit_bytes=32 * 1024 * 1024),
        name="correlate",
    )(order, own, first, second, table)


def swap(tile, mask):
    count = lax.axis_size("blk")
    return lax.ppermute(tile, "blk", [(low, low ^ mask) for low in range(count)])


def exchange(tile, mask):
    count = lax.axis_size("blk")
    if count <= 16:
        branches = [
            lambda moving, m=m: (swap(moving, count - 1), swap(moving, m)) for m in range(1, count)
        ]
        return lax.switch(mask - 1, branches, tile)
    moving = tile
    for bit in range(count.bit_length() - 1):
        moving = jnp.where(mask >> bit & 1 == 1, swap(moving, 1 << bit), moving)
    return swap(tile, count - 1), moving


def local(records, dest, slot, valid, masks):
    owners = lax.axis_size("blk")
    held, nfft = records.shape
    capacity = max(2, 2 * held // owners)
    rows = owners * capacity
    outgoing, labels = pack(records, dest, slot, valid, owners, capacity)
    labels = lax.all_gather(labels, "blk", axis=0, tiled=True)
    arrived = lax.all_to_all(
        outgoing.reshape(owners, capacity, nfft), "blk", split_axis=0, concat_axis=0, tiled=True
    ).reshape(rows, nfft)
    me = lax.axis_index("blk").astype(jnp.int32).reshape(1)
    tile = whiten(me, labels, arrived, jnp.asarray(forward_table(nfft, F)), owners, capacity)
    full = owners - 1
    first, second = exchange(tile, masks[0] + masks[1] - full)
    order = (masks[:1] != full).astype(jnp.int32)
    return correlate(order, tile, first, second, jnp.asarray(lag_table(nfft, F, LAGS)))


def solution(mesh):
    return jax.shard_map(
        local,
        mesh=mesh,
        in_specs=(
            P(("groups", "blk"), None),
            P(("groups", "blk"), None),
            P(("groups", "blk"), None),
            P(("groups", "blk"), None),
            P(),
        ),
        out_specs=P(None, ("groups", "blk"), None, None),
        check_vma=False,
    )
```

```python
import functools
import math

import jax
import jax.numpy as jnp
import numpy as np
from jax import lax
from jax.experimental import pallas as pl
from jax.experimental.pallas import tpu as pltpu
from jax.sharding import PartitionSpec as P

CH = 128
F = 256
LAGS = 128
W = 2
LOW_BITS = 4


def forward_table(nfft, bins):
    sample = np.arange(nfft, dtype=np.int64)[:, None]
    freq = np.arange(1, bins + 1, dtype=np.int64)[None, :]
    angle = (sample * freq % nfft).astype(np.float64) * (2.0 * math.pi / nfft)
    return np.concatenate([np.cos(angle), -np.sin(angle)], axis=1).astype(np.float32).astype(jnp.bfloat16)


def lag_table(nfft, bins, lags):
    shift = (np.arange(lags, dtype=np.int64) - lags // 2) % nfft
    freq = np.arange(1, bins + 1, dtype=np.int64)[None, :]
    angle = (freq * shift[:, None] % nfft).astype(np.float64) * (2.0 * math.pi / nfft)
    return np.concatenate([np.cos(angle), -np.sin(angle)], axis=1).astype(np.float32).astype(jnp.bfloat16)


def iota(shape, dim):
    return lax.broadcasted_iota(jnp.int32, shape, dim)


def pack_kernel(
    owners, capacity, dest_hbm, slot_hbm, valid_hbm, records_hbm, out_hbm,
    dest_ref, slot_ref, valid_ref, records_ref, out_ref, in_sems, out_sems,
):
    held, nfft = records_ref.shape
    rows = owners * capacity
    width = 512
    steps = nfft // width
    small = [
        pltpu.make_async_copy(src, dst, in_sems.at[k])
        for k, (src, dst) in enumerate(
            [(dest_hbm, dest_ref), (slot_hbm, slot_ref), (valid_hbm, valid_ref)]
        )
    ]
    large = [
        pltpu.make_async_copy(
            records_hbm.at[:, pl.ds(g * width, width)],
            records_ref.at[:, pl.ds(g * width, width)],
            in_sems.at[3 + g],
        )
        for g in range(steps)
    ]
    for copy in small + large:
        copy.start()
    for copy in small:
        copy.wait()
    dest = dest_ref[...]
    match = (iota((owners, held), 0) == dest).astype(jnp.float32)
    before = (iota((held, held), 0) < iota((held, held), 1)).astype(jnp.float32)
    earlier = jnp.dot(
        match.astype(jnp.bfloat16), before.astype(jnp.bfloat16), preferred_element_type=jnp.float32
    )
    rank = jnp.sum(earlier * match, axis=0, keepdims=True).astype(jnp.int32)
    position = dest * capacity + rank
    order = (iota((rows, held), 0) == position).astype(jnp.float32).astype(jnp.bfloat16)
    valid = valid_ref[...]
    row = iota((16, held), 0)
    parts = jnp.where(
        row == 0,
        slot_ref[...],
        jnp.where(
            row == 1, valid >> LOW_BITS, jnp.where(row == 2, valid & ((1 << LOW_BITS) - 1), 0)
        ),
    )
    moved = lax.dot_general(
        parts.astype(jnp.float32).astype(jnp.bfloat16),
        order,
        (((1,), (1,)), ((), ())),
        preferred_element_type=jnp.float32,
    ).astype(jnp.bfloat16)
    head = nfft // 128 * capacity
    for d in range(owners):
        at = d * capacity // 128 * 128
        out_ref[d, head : head + 16, :] = moved[:, at : at + 128]
    outs = [
        pltpu.make_async_copy(
            out_ref.at[:, pl.ds(head, 16)], out_hbm.at[:, pl.ds(head, 16)], out_sems.at[steps]
        )
    ]
    outs[0].start()
    for g in range(steps):
        large[g].wait()
        ordered = jnp.dot(
            order, records_ref[:, g * width : (g + 1) * width], preferred_element_type=jnp.float32
        ).astype(jnp.bfloat16)
        for lane in range(0, width, 128):
            at = (g * width + lane) // 128 * capacity
            out_ref[:, at : at + capacity, :] = ordered[:, lane : lane + 128].reshape(
                owners, capacity, 128
            )
        at, count = g * width // 128 * capacity, width // 128 * capacity
        outs.append(
            pltpu.make_async_copy(
                out_ref.at[:, pl.ds(at, count)], out_hbm.at[:, pl.ds(at, count)], out_sems.at[g]
            )
        )
        outs[-1].start()
    for copy in outs:
        copy.wait()


def pack(records, dest, slot, valid, owners, capacity):
    held, nfft = records.shape
    hbm = pl.BlockSpec(memory_space=pltpu.HBM)
    shape = (owners, nfft // 128 * capacity + 16, 128)
    return pl.pallas_call(
        functools.partial(pack_kernel, owners, capacity),
        in_specs=[hbm] * 4,
        out_specs=hbm,
        out_shape=jax.ShapeDtypeStruct(shape, jnp.bfloat16),
        scratch_shapes=[pltpu.VMEM((1, held), jnp.int32)] * 3
        + [
            pltpu.VMEM((held, nfft), jnp.bfloat16),
            pltpu.VMEM(shape, jnp.bfloat16),
            pltpu.SemaphoreType.DMA((3 + nfft // 512,)),
            pltpu.SemaphoreType.DMA((1 + nfft // 512,)),
        ],
        compiler_params=pltpu.CompilerParams(vmem_limit_bytes=40 * 1024 * 1024),
        name="pack",
    )(dest.reshape(1, held), slot.reshape(1, held), valid.reshape(1, held), records)


def whiten_kernel(
    capacity, me_ref, arrived_ref, table_hbm, out_ref, table_ref, trace_ref, spectrum_ref, sem
):
    owners = arrived_ref.shape[0]
    nfft = trace_ref.shape[1]
    rows = owners * capacity
    slots = CH * W
    bins = table_ref.shape[1] // 2
    shift = capacity.bit_length() - 1
    load = pltpu.make_async_copy(table_hbm, table_ref, sem)
    load.start()
    head = nfft // 128 * capacity
    labels = arrived_ref[:, head : head + 16, :].astype(jnp.float32)
    which = iota((owners, 16, 128), 1)
    parts = jnp.concatenate(
        [jnp.sum(jnp.where(which == k, labels, 0.0), axis=1) for k in range(3)], axis=0
    )
    base = (me_ref[0] * capacity) & 127
    pick = iota((128, rows), 0) == base + (iota((128, rows), 1) & (capacity - 1))
    picked = jnp.dot(
        parts.astype(jnp.bfloat16),
        pick.astype(jnp.float32).astype(jnp.bfloat16),
        preferred_element_type=jnp.float32,
    )
    source = iota((owners, rows), 0) == iota((owners, rows), 1) >> shift
    rowed = [
        jnp.sum(
            jnp.where(source, picked[k * owners : (k + 1) * owners], 0.0), axis=0, keepdims=True
        )
        for k in range(3)
    ]
    slot_row = rowed[0].astype(jnp.int32)
    place = (slot_row & (W - 1)) * CH + (slot_row >> (W.bit_length() - 1))
    valid_row = rowed[1] * float(1 << LOW_BITS) + rowed[2]
    scatter = (iota((slots, rows), 0) == place).astype(jnp.float32).astype(jnp.bfloat16)
    valid_col = jnp.transpose(jnp.broadcast_to(valid_row, (128, rows))).astype(jnp.int32)
    width = 256
    power = jnp.zeros((slots, 128), jnp.float32)
    for begin in range(0, nfft, width):
        lanes = range(begin, begin + width, 128)
        inside = jnp.concatenate(
            [
                (iota((rows, 128), 1) + lane < valid_col).astype(jnp.float32).astype(jnp.bfloat16)
                for lane in lanes
            ],
            axis=1,
        )
        arrived = jnp.concatenate(
            [
                arrived_ref[:, lane // 128 * capacity : (lane // 128 + 1) * capacity, :].reshape(
                    rows, 128
                )
                for lane in lanes
            ],
            axis=1,
        )
        summed = jnp.dot(scatter, arrived * inside, preferred_element_type=jnp.float32)
        coverage = jnp.dot(scatter, inside, preferred_element_type=jnp.float32)
        trace = summed / jnp.maximum(coverage, 1.0)
        trace_ref[:, begin : begin + width] = trace
        square = trace * trace
        for lane in range(0, width, 128):
            power = power + square[:, lane : lane + 128]
    meansq = jnp.sum(power, axis=1, keepdims=True) * (1.0 / nfft)
    gain = lax.rsqrt(meansq + 1e-06)
    load.wait()
    width = 512
    for begin in range(0, nfft, width):
        normed = (trace_ref[:, begin : begin + width] * gain).astype(jnp.bfloat16)
        part = jnp.dot(
            normed, table_ref[begin : begin + width, :], preferred_element_type=jnp.float32
        )
        if begin == 0:
            spectrum_ref[...] = part
        else:
            spectrum_ref[...] += part
    real_part = spectrum_ref[:, :bins]
    imag_part = spectrum_ref[:, bins:]
    amplitude = lax.rsqrt(jnp.maximum(real_part * real_part + imag_part * imag_part, nfft / 4.0))
    real_part = (real_part * amplitude).astype(jnp.bfloat16)
    imag_part = (imag_part * amplitude).astype(jnp.bfloat16)
    for w in range(W):
        at = w * 2 * bins
        out_ref[:, at : at + bins] = real_part[w * CH : (w + 1) * CH]
        out_ref[:, at + bins : at + 2 * bins] = imag_part[w * CH : (w + 1) * CH]


def whiten(me, arrived, table, capacity):
    nfft, width = table.shape
    vmem = pl.BlockSpec(memory_space=pltpu.VMEM)
    return pl.pallas_call(
        functools.partial(whiten_kernel, capacity),
        in_specs=[
            pl.BlockSpec(memory_space=pltpu.SMEM),
            vmem,
            pl.BlockSpec(memory_space=pltpu.HBM),
        ],
        out_specs=vmem,
        out_shape=jax.ShapeDtypeStruct((CH, W * width), jnp.bfloat16),
        scratch_shapes=[
            pltpu.VMEM(table.shape, jnp.bfloat16),
            pltpu.VMEM((CH * W, nfft), jnp.float32),
            pltpu.VMEM((CH * W, width), jnp.float32),
            pltpu.SemaphoreType.DMA(()),
        ],
        compiler_params=pltpu.CompilerParams(vmem_limit_bytes=40 * 1024 * 1024),
        name="whiten",
    )(me, arrived, table)


GROUP = 16


def correlate_kernel(
    scale, order_ref, own_ref, first_ref, second_ref, table_ref, out_ref, both_ref, wide_ref, turned_a, turned_b
):
    step = pl.program_id(0)
    lags = table_ref.shape[0]
    bins = table_ref.shape[1] // 2

    @pl.when(step == 0)
    def _():
        wide_ref[...] = own_ref[...].astype(jnp.float32)
        at = pl.multiple_of(order_ref[0] * CH, CH)
        both_ref[pl.ds(at, CH), :] = first_ref[...]
        both_ref[pl.ds(CH - at, CH), :] = second_ref[...]

    turned = (turned_a, turned_b)

    def turn(pair):
        a_ref = turned[pair % 2]
        for half in range(2):
            u = wide_ref[pl.ds(step * GROUP + pair * 2 + half, 1), :]
            cos = table_ref[:, :bins]
            msin = table_ref[:, bins:]
            rows = slice(half * lags, (half + 1) * lags)
            for w in range(W):
                at = w * 2 * bins
                ur = jnp.broadcast_to(u[:, at : at + bins], (lags, bins)).astype(jnp.bfloat16)
                ui = jnp.broadcast_to(u[:, at + bins : at + 2 * bins], (lags, bins)).astype(
                    jnp.bfloat16
                )
                a_ref[rows, at : at + bins] = ur * cos + ui * msin
                a_ref[rows, at + bins : at + 2 * bins] = ui * cos - ur * msin

    turn(0)
    for pair in range(GROUP // 2):
        if pair + 1 < GROUP // 2:
            turn(pair + 1)
        lagged = lax.dot_general(
            both_ref[...],
            turned[pair % 2][...],
            (((1,), (1,)), ((), ())),
            preferred_element_type=jnp.float32,
        )
        lagged = (lagged * scale).astype(jnp.bfloat16)
        for half in range(2):
            for r in range(2):
                out_ref[r, pair * 2 + half] = lagged[
                    r * CH : (r + 1) * CH, half * lags : (half + 1) * lags
                ]


def correlate(order, own, first, second, table):
    lags, width = table.shape
    depth = own.shape[1]
    scale = 1.0 / math.sqrt(W * (width // 2))
    block = pl.BlockSpec((CH, depth), lambda n: (0, 0))
    return pl.pallas_call(
        functools.partial(correlate_kernel, scale),
        grid=(CH // GROUP,),
        in_specs=[
            pl.BlockSpec(memory_space=pltpu.SMEM),
            block,
            block,
            block,
            pl.BlockSpec((lags, width), lambda n: (0, 0)),
        ],
        out_specs=pl.BlockSpec((2, GROUP, CH, lags), lambda n: (0, n, 0, 0)),
        out_shape=jax.ShapeDtypeStruct((2, CH, CH, lags), jnp.bfloat16),
        scratch_shapes=[
            pltpu.VMEM((2 * CH, depth), jnp.bfloat16),
            pltpu.VMEM((CH, depth), jnp.float32),
            pltpu.VMEM((2 * lags, depth), jnp.bfloat16),
            pltpu.VMEM((2 * lags, depth), jnp.bfloat16),
        ],
        compiler_params=pltpu.CompilerParams(vmem_limit_bytes=32 * 1024 * 1024),
        name="correlate",
    )(order, own, first, second, table)


def swap(tile, mask):
    count = lax.axis_size("blk")
    return lax.ppermute(tile, "blk", [(low, low ^ mask) for low in range(count)])


def exchange(tile, mask):
    count = lax.axis_size("blk")
    full = count - 1
    if count <= 16:

        def branch(m, moving):
            first = swap(moving, full)
            return first, swap(first, m ^ full) if 2 * m >= count else swap(moving, m)

        branches = [functools.partial(branch, m) for m in range(1, full)]
        return lax.switch(mask - 1, branches, tile)
    moving = tile
    for bit in range(count.bit_length() - 1):
        moving = jnp.where(mask >> bit & 1 == 1, swap(moving, 1 << bit), moving)
    return swap(tile, full), moving


def local(records, dest, slot, valid, masks):
    owners = lax.axis_size("blk")
    held, nfft = records.shape
    capacity = max(16, 2 * held // owners)
    outgoing = pack(records, dest, slot, valid, owners, capacity)
    arrived = lax.all_to_all(outgoing, "blk", split_axis=0, concat_axis=0, tiled=True)
    me = lax.axis_index("blk").astype(jnp.int32).reshape(1)
    tile = whiten(me, arrived, jnp.asarray(forward_table(nfft, F)), capacity)
    full = owners - 1
    first, second = exchange(tile, masks[0] + masks[1] - full)
    order = (masks[:1] != full).astype(jnp.int32)
    return correlate(order, tile, first, second, jnp.asarray(lag_table(nfft, F, LAGS)))


def solution(mesh):
    return jax.shard_map(
        local,
        mesh=mesh,
        in_specs=(
            P(("groups", "blk"), None),
            P(("groups", "blk"), None),
            P(("groups", "blk"), None),
            P(("groups", "blk"), None),
            P(),
        ),
        out_specs=P(None, ("groups", "blk"), None, None),
        check_vma=False,
    )
```

```python
import functools
import math

import jax
import jax.numpy as jnp
import numpy as np
from jax import lax
from jax.experimental import pallas as pl
from jax.experimental.pallas import tpu as pltpu
from jax.sharding import PartitionSpec as P

CH = 128
F = 256
LAGS = 128
W = 2
LOW_BITS = 4


def forward_table(nfft, bins):
    sample = np.arange(nfft, dtype=np.int64)[:, None]
    freq = np.arange(1, bins + 1, dtype=np.int64)[None, :]
    angle = (sample * freq % nfft).astype(np.float64) * (2.0 * math.pi / nfft)
    return np.concatenate([np.cos(angle), -np.sin(angle)], axis=1).astype(np.float32).astype(jnp.bfloat16)


def lag_table(nfft, bins, lags):
    shift = (np.arange(lags, dtype=np.int64) - lags // 2) % nfft
    freq = np.arange(1, bins + 1, dtype=np.int64)[None, :]
    angle = (freq * shift[:, None] % nfft).astype(np.float64) * (2.0 * math.pi / nfft)
    return np.concatenate([np.cos(angle), -np.sin(angle)], axis=1).astype(np.float32).astype(jnp.bfloat16)


def iota(shape, dim):
    return lax.broadcasted_iota(jnp.int32, shape, dim)


def pack_kernel(
    owners, capacity, dest_hbm, slot_hbm, valid_hbm, records_hbm, out_hbm,
    dest_ref, slot_ref, valid_ref, records_ref, out_ref, in_sems, out_sems,
):
    held, nfft = records_ref.shape
    rows = owners * capacity
    width = 512
    steps = nfft // width
    small = [
        pltpu.make_async_copy(src, dst, in_sems.at[k])
        for k, (src, dst) in enumerate(
            [(dest_hbm, dest_ref), (slot_hbm, slot_ref), (valid_hbm, valid_ref)]
        )
    ]
    large = [
        pltpu.make_async_copy(
            records_hbm.at[:, pl.ds(g * width, width)],
            records_ref.at[:, pl.ds(g * width, width)],
            in_sems.at[3 + g],
        )
        for g in range(steps)
    ]
    for copy in small + large:
        copy.start()
    for copy in small:
        copy.wait()
    dest = dest_ref[...]
    match = (iota((owners, held), 0) == dest).astype(jnp.float32)
    before = (iota((held, held), 0) < iota((held, held), 1)).astype(jnp.float32)
    earlier = jnp.dot(
        match.astype(jnp.bfloat16), before.astype(jnp.bfloat16), preferred_element_type=jnp.float32
    )
    rank = jnp.sum(earlier * match, axis=0, keepdims=True).astype(jnp.int32)
    position = dest * capacity + rank
    order = (iota((rows, held), 0) == position).astype(jnp.float32).astype(jnp.bfloat16)
    valid = valid_ref[...]
    row = iota((16, held), 0)
    parts = jnp.where(
        row == 0,
        slot_ref[...],
        jnp.where(
            row == 1, valid >> LOW_BITS, jnp.where(row == 2, valid & ((1 << LOW_BITS) - 1), 0)
        ),
    )
    moved = lax.dot_general(
        parts.astype(jnp.float32).astype(jnp.bfloat16),
        order,
        (((1,), (1,)), ((), ())),
        preferred_element_type=jnp.float32,
    ).astype(jnp.bfloat16)
    head = nfft // 128 * capacity
    for d in range(owners):
        at = d * capacity // 128 * 128
        out_ref[d, head : head + 16, :] = moved[:, at : at + 128]
    outs = [
        pltpu.make_async_copy(
            out_ref.at[:, pl.ds(head, 16)], out_hbm.at[:, pl.ds(head, 16)], out_sems.at[steps]
        )
    ]
    outs[0].start()
    for g in range(steps):
        large[g].wait()
        ordered = jnp.dot(
            order, records_ref[:, g * width : (g + 1) * width], preferred_element_type=jnp.float32
        ).astype(jnp.bfloat16)
        for lane in range(0, width, 128):
            at = (g * width + lane) // 128 * capacity
            out_ref[:, at : at + capacity, :] = ordered[:, lane : lane + 128].reshape(
                owners, capacity, 128
            )
        at, count = g * width // 128 * capacity, width // 128 * capacity
        outs.append(
            pltpu.make_async_copy(
                out_ref.at[:, pl.ds(at, count)], out_hbm.at[:, pl.ds(at, count)], out_sems.at[g]
            )
        )
        outs[-1].start()
    for copy in outs:
        copy.wait()


def pack(records, dest, slot, valid, owners, capacity):
    held, nfft = records.shape
    hbm = pl.BlockSpec(memory_space=pltpu.HBM)
    shape = (owners, nfft // 128 * capacity + 16, 128)
    return pl.pallas_call(
        functools.partial(pack_kernel, owners, capacity),
        in_specs=[hbm] * 4,
        out_specs=hbm,
        out_shape=jax.ShapeDtypeStruct(shape, jnp.bfloat16),
        scratch_shapes=[pltpu.VMEM((1, held), jnp.int32)] * 3
        + [
            pltpu.VMEM((held, nfft), jnp.bfloat16),
            pltpu.VMEM(shape, jnp.bfloat16),
            pltpu.SemaphoreType.DMA((3 + nfft // 512,)),
            pltpu.SemaphoreType.DMA((1 + nfft // 512,)),
        ],
        compiler_params=pltpu.CompilerParams(vmem_limit_bytes=62 * 1024 * 1024),
        name="pack",
    )(dest.reshape(1, held), slot.reshape(1, held), valid.reshape(1, held), records)


def whiten_kernel(
    capacity, me_ref, arrived_hbm, table_hbm, out_ref,
    arrived_ref, table_ref, trace_ref, spectrum_ref, sems,
):
    owners = arrived_ref.shape[0]
    nfft = trace_ref.shape[1]
    rows = owners * capacity
    slots = CH * W
    bins = table_ref.shape[1] // 2
    shift = capacity.bit_length() - 1
    head = nfft // 128 * capacity
    width = 256
    steps = nfft // width
    stride = width // 128 * capacity
    spans = [(head, 16)] + [(g * stride, stride) for g in range(steps)]
    loads = [
        pltpu.make_async_copy(
            arrived_hbm.at[:, pl.ds(at, count)], arrived_ref.at[:, pl.ds(at, count)], sems.at[k]
        )
        for k, (at, count) in enumerate(spans)
    ]
    loads.append(pltpu.make_async_copy(table_hbm, table_ref, sems.at[1 + steps]))
    for copy in loads:
        copy.start()
    loads[0].wait()
    labels = arrived_ref[:, head : head + 16, :].astype(jnp.float32)
    which = iota((owners, 16, 128), 1)
    parts = jnp.concatenate(
        [jnp.sum(jnp.where(which == k, labels, 0.0), axis=1) for k in range(3)], axis=0
    )
    base = (me_ref[0] * capacity) & 127
    pick = iota((128, rows), 0) == base + (iota((128, rows), 1) & (capacity - 1))
    picked = jnp.dot(
        parts.astype(jnp.bfloat16),
        pick.astype(jnp.float32).astype(jnp.bfloat16),
        preferred_element_type=jnp.float32,
    )
    source = iota((owners, rows), 0) == iota((owners, rows), 1) >> shift
    rowed = [
        jnp.sum(
            jnp.where(source, picked[k * owners : (k + 1) * owners], 0.0), axis=0, keepdims=True
        )
        for k in range(3)
    ]
    slot_row = rowed[0].astype(jnp.int32)
    place = (slot_row & (W - 1)) * CH + (slot_row >> (W.bit_length() - 1))
    valid_row = rowed[1] * float(1 << LOW_BITS) + rowed[2]
    scatter = (iota((slots, rows), 0) == place).astype(jnp.float32).astype(jnp.bfloat16)
    valid_col = jnp.transpose(jnp.broadcast_to(valid_row, (128, rows))).astype(jnp.int32)
    power = jnp.zeros((slots, 128), jnp.float32)
    for begin in range(0, nfft, width):
        loads[1 + begin // width].wait()
        lanes = range(begin, begin + width, 128)
        inside = jnp.concatenate(
            [
                (iota((rows, 128), 1) + lane < valid_col).astype(jnp.float32).astype(jnp.bfloat16)
                for lane in lanes
            ],
            axis=1,
        )
        arrived = jnp.concatenate(
            [
                arrived_ref[:, lane // 128 * capacity : (lane // 128 + 1) * capacity, :].reshape(
                    rows, 128
                )
                for lane in lanes
            ],
            axis=1,
        )
        summed = jnp.dot(scatter, arrived * inside, preferred_element_type=jnp.float32)
        coverage = jnp.dot(scatter, inside, preferred_element_type=jnp.float32)
        trace = summed / jnp.maximum(coverage, 1.0)
        trace_ref[:, begin : begin + width] = trace
        square = trace * trace
        for lane in range(0, width, 128):
            power = power + square[:, lane : lane + 128]
    meansq = jnp.sum(power, axis=1, keepdims=True) * (1.0 / nfft)
    gain = lax.rsqrt(meansq + 1e-06)
    loads[1 + steps].wait()
    width = 512
    for begin in range(0, nfft, width):
        normed = (trace_ref[:, begin : begin + width] * gain).astype(jnp.bfloat16)
        part = jnp.dot(
            normed, table_ref[begin : begin + width, :], preferred_element_type=jnp.float32
        )
        if begin == 0:
            spectrum_ref[...] = part
        else:
            spectrum_ref[...] += part
    real_part = spectrum_ref[:, :bins]
    imag_part = spectrum_ref[:, bins:]
    amplitude = lax.rsqrt(jnp.maximum(real_part * real_part + imag_part * imag_part, nfft / 4.0))
    real_part = (real_part * amplitude).astype(jnp.bfloat16)
    imag_part = (imag_part * amplitude).astype(jnp.bfloat16)
    for w in range(W):
        at = w * 2 * bins
        out_ref[:, at : at + bins] = real_part[w * CH : (w + 1) * CH]
        out_ref[:, at + bins : at + 2 * bins] = imag_part[w * CH : (w + 1) * CH]


def whiten(me, arrived, table, capacity):
    nfft, width = table.shape
    hbm = pl.BlockSpec(memory_space=pltpu.HBM)
    return pl.pallas_call(
        functools.partial(whiten_kernel, capacity),
        in_specs=[pl.BlockSpec(memory_space=pltpu.SMEM), hbm, hbm],
        out_specs=pl.BlockSpec(memory_space=pltpu.VMEM),
        out_shape=jax.ShapeDtypeStruct((CH, W * width), jnp.bfloat16),
        scratch_shapes=[
            pltpu.VMEM(arrived.shape, jnp.bfloat16),
            pltpu.VMEM(table.shape, jnp.bfloat16),
            pltpu.VMEM((CH * W, nfft), jnp.float32),
            pltpu.VMEM((CH * W, width), jnp.float32),
            pltpu.SemaphoreType.DMA((2 + nfft // 256,)),
        ],
        compiler_params=pltpu.CompilerParams(vmem_limit_bytes=62 * 1024 * 1024),
        name="whiten",
    )(me, arrived, table)


GROUP = 16
BLOCK = 4


def correlate_kernel(
    scale, order_ref, own_ref, first_ref, second_ref, table_ref, out_ref, both_ref, wide_ref, turned_a, turned_b
):
    step = pl.program_id(0)
    lags = table_ref.shape[0]
    bins = table_ref.shape[1] // 2
    blocks = GROUP // BLOCK
    turned = (turned_a, turned_b)

    def turn(block):
        a_ref = turned[block % 2]
        for k in range(BLOCK):
            row = jnp.minimum(step * GROUP + block * BLOCK + k, CH - 1)
            u = wide_ref[pl.ds(row, 1), :]
            cos = table_ref[:, :bins]
            msin = table_ref[:, bins:]
            rows = slice(k * lags, (k + 1) * lags)
            for w in range(W):
                at = w * 2 * bins
                ur = jnp.broadcast_to(u[:, at : at + bins], (lags, bins)).astype(jnp.bfloat16)
                ui = jnp.broadcast_to(u[:, at + bins : at + 2 * bins], (lags, bins)).astype(
                    jnp.bfloat16
                )
                a_ref[rows, at : at + bins] = ur * cos + ui * msin
                a_ref[rows, at + bins : at + 2 * bins] = ui * cos - ur * msin

    @pl.when(step == 0)
    def _():
        wide_ref[...] = own_ref[...].astype(jnp.float32)
        at = pl.multiple_of(order_ref[0] * CH, CH)
        both_ref[:, pl.ds(at, CH)] = jnp.transpose(first_ref[...].astype(jnp.float32)).astype(
            jnp.bfloat16
        )
        both_ref[:, pl.ds(CH - at, CH)] = jnp.transpose(
            second_ref[...].astype(jnp.float32)
        ).astype(jnp.bfloat16)
        turn(0)

    for block in range(blocks):
        turn(block + 1)
        lagged = jnp.dot(
            turned[block % 2][...], both_ref[...], preferred_element_type=jnp.float32
        )
        lagged = (lagged * scale).astype(jnp.bfloat16)
        for k in range(BLOCK):
            for r in range(2):
                out_ref[r, block * BLOCK + k] = jnp.transpose(
                    lagged[k * lags : (k + 1) * lags, r * CH : (r + 1) * CH]
                )


def correlate(order, own, first, second, table):
    lags, width = table.shape
    depth = own.shape[1]
    scale = 1.0 / math.sqrt(W * (width // 2))
    block = pl.BlockSpec((CH, depth), lambda n: (0, 0))
    return pl.pallas_call(
        functools.partial(correlate_kernel, scale),
        grid=(CH // GROUP,),
        in_specs=[
            pl.BlockSpec(memory_space=pltpu.SMEM),
            block,
            block,
            block,
            pl.BlockSpec((lags, width), lambda n: (0, 0)),
        ],
        out_specs=pl.BlockSpec((2, GROUP, CH, lags), lambda n: (0, n, 0, 0)),
        out_shape=jax.ShapeDtypeStruct((2, CH, CH, lags), jnp.bfloat16),
        scratch_shapes=[
            pltpu.VMEM((depth, 2 * CH), jnp.bfloat16),
            pltpu.VMEM((CH, depth), jnp.float32),
            pltpu.VMEM((BLOCK * lags, depth), jnp.bfloat16),
            pltpu.VMEM((BLOCK * lags, depth), jnp.bfloat16),
        ],
        compiler_params=pltpu.CompilerParams(vmem_limit_bytes=32 * 1024 * 1024),
        name="correlate",
    )(order, own, first, second, table)


def swap(tile, mask):
    count = lax.axis_size("blk")
    return lax.ppermute(tile, "blk", [(low, low ^ mask) for low in range(count)])


def exchange(tile, mask):
    count = lax.axis_size("blk")
    full = count - 1
    if count <= 16:

        def branch(m, moving):
            first = swap(moving, full)
            return first, swap(first, m ^ full) if 2 * m >= count else swap(moving, m)

        branches = [functools.partial(branch, m) for m in range(1, full)]
        return lax.switch(mask - 1, branches, tile)
    moving = tile
    for bit in range(count.bit_length() - 1):
        moving = jnp.where(mask >> bit & 1 == 1, swap(moving, 1 << bit), moving)
    return swap(tile, full), moving


def local(records, dest, slot, valid, masks):
    owners = lax.axis_size("blk")
    held, nfft = records.shape
    capacity = max(16, 2 * held // owners)
    outgoing = pack(records, dest, slot, valid, owners, capacity)
    arrived = lax.all_to_all(outgoing, "blk", split_axis=0, concat_axis=0, tiled=True)
    me = lax.axis_index("blk").astype(jnp.int32).reshape(1)
    tile = whiten(me, arrived, jnp.asarray(forward_table(nfft, F)), capacity)
    full = owners - 1
    first, second = exchange(tile, masks[0] + masks[1] - full)
    order = (masks[:1] != full).astype(jnp.int32)
    return correlate(order, tile, first, second, jnp.asarray(lag_table(nfft, F, LAGS)))


def solution(mesh):
    return jax.shard_map(
        local,
        mesh=mesh,
        in_specs=(
            P(("groups", "blk"), None),
            P(("groups", "blk"), None),
            P(("groups", "blk"), None),
            P(("groups", "blk"), None),
            P(),
        ),
        out_specs=P(None, ("groups", "blk"), None, None),
        check_vma=False,
    )
```

```python
import functools
import math

import jax
import jax.numpy as jnp
import numpy as np
from jax import lax
from jax.experimental import pallas as pl
from jax.experimental.pallas import tpu as pltpu
from jax.sharding import PartitionSpec as P

CH = 128
F = 256
LAGS = 128
W = 2
LOW_BITS = 4


def forward_table(nfft, bins):
    sample = np.arange(nfft, dtype=np.int64)[:, None]
    freq = np.arange(1, bins + 1, dtype=np.int64)[None, :]
    angle = (sample * freq % nfft).astype(np.float64) * (2.0 * math.pi / nfft)
    return np.concatenate([np.cos(angle), -np.sin(angle)], axis=1).astype(np.float32).astype(jnp.bfloat16)


def turn_tables(nfft, bins, lags, fine, scale):
    freq = np.arange(1, bins + 1, dtype=np.int64)

    def both(shift):
        angle = (freq * shift % nfft).astype(np.float64) * (2.0 * math.pi / nfft)
        return np.cos(angle), np.sin(angle)

    own = np.stack([np.concatenate(both(at)) * scale for at in range(fine)])
    start = both(lags // 2) + both(-fine)
    other = np.stack([np.broadcast_to(part[:, None], (bins, 128)) for part in start])
    return own.astype(np.float32), other.astype(np.float32)


def iota(shape, dim):
    return lax.broadcasted_iota(jnp.int32, shape, dim)


def pack_kernel(
    owners, capacity, dest_hbm, slot_hbm, valid_hbm, records_hbm, out_hbm,
    dest_ref, slot_ref, valid_ref, records_ref, out_ref, in_sems, out_sems,
):
    held, nfft = records_ref.shape
    rows = owners * capacity
    width = 512
    steps = nfft // width
    small = [
        pltpu.make_async_copy(src, dst, in_sems.at[k])
        for k, (src, dst) in enumerate(
            [(dest_hbm, dest_ref), (slot_hbm, slot_ref), (valid_hbm, valid_ref)]
        )
    ]
    large = [
        pltpu.make_async_copy(
            records_hbm.at[:, pl.ds(g * width, width)],
            records_ref.at[:, pl.ds(g * width, width)],
            in_sems.at[3 + g],
        )
        for g in range(steps)
    ]
    for copy in small + large:
        copy.start()
    for copy in small:
        copy.wait()
    dest = dest_ref[...]
    match = (iota((owners, held), 0) == dest).astype(jnp.float32)
    before = (iota((held, held), 0) < iota((held, held), 1)).astype(jnp.float32)
    earlier = jnp.dot(
        match.astype(jnp.bfloat16), before.astype(jnp.bfloat16), preferred_element_type=jnp.float32
    )
    rank = jnp.sum(earlier * match, axis=0, keepdims=True).astype(jnp.int32)
    position = dest * capacity + rank
    order = (iota((rows, held), 0) == position).astype(jnp.float32).astype(jnp.bfloat16)
    valid = valid_ref[...]
    row = iota((16, held), 0)
    parts = jnp.where(
        row == 0,
        slot_ref[...],
        jnp.where(
            row == 1, valid >> LOW_BITS, jnp.where(row == 2, valid & ((1 << LOW_BITS) - 1), 0)
        ),
    )
    moved = lax.dot_general(
        parts.astype(jnp.float32).astype(jnp.bfloat16),
        order,
        (((1,), (1,)), ((), ())),
        preferred_element_type=jnp.float32,
    ).astype(jnp.bfloat16)
    head = nfft // 128 * capacity
    for d in range(owners):
        at = d * capacity // 128 * 128
        out_ref[d, head : head + 16, :] = moved[:, at : at + 128]
    outs = [
        pltpu.make_async_copy(
            out_ref.at[:, pl.ds(head, 16)], out_hbm.at[:, pl.ds(head, 16)], out_sems.at[steps]
        )
    ]
    outs[0].start()
    for g in range(steps):
        large[g].wait()
        ordered = jnp.dot(
            order, records_ref[:, g * width : (g + 1) * width], preferred_element_type=jnp.float32
        ).astype(jnp.bfloat16)
        for lane in range(0, width, 128):
            at = (g * width + lane) // 128 * capacity
            out_ref[:, at : at + capacity, :] = ordered[:, lane : lane + 128].reshape(
                owners, capacity, 128
            )
        at, count = g * width // 128 * capacity, width // 128 * capacity
        outs.append(
            pltpu.make_async_copy(
                out_ref.at[:, pl.ds(at, count)], out_hbm.at[:, pl.ds(at, count)], out_sems.at[g]
            )
        )
        outs[-1].start()
    for copy in outs:
        copy.wait()


def pack(records, dest, slot, valid, owners, capacity):
    held, nfft = records.shape
    hbm = pl.BlockSpec(memory_space=pltpu.HBM)
    shape = (owners, nfft // 128 * capacity + 16, 128)
    return pl.pallas_call(
        functools.partial(pack_kernel, owners, capacity),
        in_specs=[hbm] * 4,
        out_specs=hbm,
        out_shape=jax.ShapeDtypeStruct(shape, jnp.bfloat16),
        scratch_shapes=[pltpu.VMEM((1, held), jnp.int32)] * 3
        + [
            pltpu.VMEM((held, nfft), jnp.bfloat16),
            pltpu.VMEM(shape, jnp.bfloat16),
            pltpu.SemaphoreType.DMA((3 + nfft // 512,)),
            pltpu.SemaphoreType.DMA((1 + nfft // 512,)),
        ],
        compiler_params=pltpu.CompilerParams(vmem_limit_bytes=62 * 1024 * 1024),
        name="pack",
    )(dest.reshape(1, held), slot.reshape(1, held), valid.reshape(1, held), records)


def whiten_kernel(
    capacity, me_ref, arrived_ref, table_hbm, out_ref, table_ref, trace_ref, spectrum_ref, sem
):
    owners = arrived_ref.shape[0]
    nfft = trace_ref.shape[1]
    rows = owners * capacity
    slots = CH * W
    bins = table_ref.shape[1] // 2
    shift = capacity.bit_length() - 1
    head = nfft // 128 * capacity
    width = 256
    load = pltpu.make_async_copy(table_hbm, table_ref, sem)
    load.start()
    labels = arrived_ref[:, head : head + 16, :].astype(jnp.float32)
    which = iota((owners, 16, 128), 1)
    parts = jnp.concatenate(
        [jnp.sum(jnp.where(which == k, labels, 0.0), axis=1) for k in range(3)], axis=0
    )
    base = (me_ref[0] * capacity) & 127
    pick = iota((128, rows), 0) == base + (iota((128, rows), 1) & (capacity - 1))
    picked = jnp.dot(
        parts.astype(jnp.bfloat16),
        pick.astype(jnp.float32).astype(jnp.bfloat16),
        preferred_element_type=jnp.float32,
    )
    source = iota((owners, rows), 0) == iota((owners, rows), 1) >> shift
    rowed = [
        jnp.sum(
            jnp.where(source, picked[k * owners : (k + 1) * owners], 0.0), axis=0, keepdims=True
        )
        for k in range(3)
    ]
    slot_row = rowed[0].astype(jnp.int32)
    place = (slot_row & (W - 1)) * CH + (slot_row >> (W.bit_length() - 1))
    valid_row = rowed[1] * float(1 << LOW_BITS) + rowed[2]
    scatter = (iota((slots, rows), 0) == place).astype(jnp.float32).astype(jnp.bfloat16)
    valid_col = jnp.transpose(jnp.broadcast_to(valid_row, (128, rows))).astype(jnp.int32)
    power = jnp.zeros((slots, 128), jnp.float32)
    for begin in range(0, nfft, width):
        lanes = range(begin, begin + width, 128)
        inside = jnp.concatenate(
            [
                (iota((rows, 128), 1) + lane < valid_col).astype(jnp.float32).astype(jnp.bfloat16)
                for lane in lanes
            ],
            axis=1,
        )
        arrived = jnp.concatenate(
            [
                arrived_ref[:, lane // 128 * capacity : (lane // 128 + 1) * capacity, :].reshape(
                    rows, 128
                )
                for lane in lanes
            ],
            axis=1,
        )
        summed = jnp.dot(scatter, arrived * inside, preferred_element_type=jnp.float32)
        coverage = jnp.dot(scatter, inside, preferred_element_type=jnp.float32)
        trace = summed / jnp.maximum(coverage, 1.0)
        trace_ref[:, begin : begin + width] = trace
        square = trace * trace
        for lane in range(0, width, 128):
            power = power + square[:, lane : lane + 128]
    meansq = jnp.sum(power, axis=1, keepdims=True) * (1.0 / nfft)
    gain = lax.rsqrt(meansq + 1e-06)
    load.wait()
    width = 512
    for begin in range(0, nfft, width):
        normed = (trace_ref[:, begin : begin + width] * gain).astype(jnp.bfloat16)
        part = jnp.dot(
            normed, table_ref[begin : begin + width, :], preferred_element_type=jnp.float32
        )
        if begin == 0:
            spectrum_ref[...] = part
        else:
            spectrum_ref[...] += part
    real_part = spectrum_ref[:, :bins]
    imag_part = spectrum_ref[:, bins:]
    amplitude = lax.rsqrt(jnp.maximum(real_part * real_part + imag_part * imag_part, nfft / 4.0))
    real_part = (real_part * amplitude).astype(jnp.bfloat16)
    imag_part = (imag_part * amplitude).astype(jnp.bfloat16)
    for w in range(W):
        at = w * 2 * bins
        out_ref[:, at : at + bins] = real_part[w * CH : (w + 1) * CH]
        out_ref[:, at + bins : at + 2 * bins] = imag_part[w * CH : (w + 1) * CH]


def whiten(me, arrived, table, capacity):
    nfft, width = table.shape
    vmem = pl.BlockSpec(memory_space=pltpu.VMEM)
    return pl.pallas_call(
        functools.partial(whiten_kernel, capacity),
        in_specs=[
            pl.BlockSpec(memory_space=pltpu.SMEM),
            vmem,
            pl.BlockSpec(memory_space=pltpu.HBM),
        ],
        out_specs=vmem,
        out_shape=jax.ShapeDtypeStruct((CH, W * width), jnp.bfloat16),
        scratch_shapes=[
            pltpu.VMEM(table.shape, jnp.bfloat16),
            pltpu.VMEM((CH * W, nfft), jnp.float32),
            pltpu.VMEM((CH * W, width), jnp.float32),
            pltpu.SemaphoreType.DMA(()),
        ],
        compiler_params=pltpu.CompilerParams(vmem_limit_bytes=48 * 1024 * 1024),
        name="whiten",
    )(me, arrived, table)


GROUP = 32
FINE = 16


def correlate_kernel(
    order_ref, own_ref, first_ref, second_ref, fine_ref, coarse_ref, out_ref,
    wide_ref, flat_ref, back_ref, turned_ref, rows_ref,
):
    step = pl.program_id(0)
    bins = coarse_ref.shape[1]
    lags = out_ref.shape[3]
    coarse = lags // FINE

    @pl.when(step == 0)
    def _():
        wide_ref[...] = own_ref[...].astype(jnp.float32)
        at = pl.multiple_of(order_ref[0] * CH, CH)
        flat_ref[:, pl.ds(at, CH)] = jnp.transpose(first_ref[...].astype(jnp.float32))
        flat_ref[:, pl.ds(CH - at, CH)] = jnp.transpose(second_ref[...].astype(jnp.float32))
        size = 32
        for k in range(0, bins, size):
            tables = [
                jnp.concatenate([coarse_ref[n, k : k + size, :]] * 2, axis=1) for n in range(4)
            ]
            for w in range(W):
                top = w * 2 * bins + k
                vr = flat_ref[top : top + size, :]
                vi = flat_ref[top + bins : top + bins + size, :]
                for b in range(coarse):
                    cos, sin = tables[:2] if b == 0 else tables[2:]
                    vr, vi = vr * cos - vi * sin, vi * cos + vr * sin
                    for r in range(2):
                        lanes = slice((r * coarse + b) * CH, (r * coarse + b + 1) * CH)
                        half = slice(r * CH, (r + 1) * CH)
                        back_ref[top : top + size, lanes] = vr[:, half].astype(jnp.bfloat16)
                        back_ref[top + bins : top + bins + size, lanes] = vi[:, half].astype(
                            jnp.bfloat16
                        )

    cos = fine_ref[:, :bins]
    sin = fine_ref[:, bins:]
    for k in range(GROUP):
        u = wide_ref[pl.ds(step * GROUP + k, 1), :]
        rows = slice(k * FINE, (k + 1) * FINE)
        for w in range(W):
            at = w * 2 * bins
            ur = jnp.broadcast_to(u[:, at : at + bins], (FINE, bins))
            ui = jnp.broadcast_to(u[:, at + bins : at + 2 * bins], (FINE, bins))
            turned_ref[rows, at : at + bins] = (ur * cos - ui * sin).astype(jnp.bfloat16)
            turned_ref[rows, at + bins : at + 2 * bins] = (ur * sin + ui * cos).astype(
                jnp.bfloat16
            )
    for r in range(2):
        for b in range(0, coarse, 2):
            lanes = slice((r * coarse + b) * CH, (r * coarse + b + 2) * CH)
            lagged = jnp.dot(
                turned_ref[...], back_ref[:, lanes], preferred_element_type=jnp.float32
            ).astype(jnp.bfloat16)
            for k in range(GROUP):
                for h in range(2):
                    rows_ref[r, k, (b + h) * FINE : (b + h + 1) * FINE, :] = lagged[
                        k * FINE : (k + 1) * FINE, h * CH : (h + 1) * CH
                    ]
        for k in range(GROUP):
            out_ref[r, k] = jnp.transpose(rows_ref[r, k])


def correlate(order, own, first, second, nfft, lags):
    depth = own.shape[1]
    bins = depth // (2 * W)
    fine, coarse = turn_tables(nfft, bins, lags, FINE, 1.0 / math.sqrt(W * bins))
    whole = lambda *shape: pl.BlockSpec(shape, lambda n: (0,) * len(shape))
    return pl.pallas_call(
        correlate_kernel,
        grid=(CH // GROUP,),
        in_specs=[
            pl.BlockSpec(memory_space=pltpu.SMEM),
            whole(CH, depth),
            whole(CH, depth),
            whole(CH, depth),
            whole(*fine.shape),
            whole(*coarse.shape),
        ],
        out_specs=pl.BlockSpec((2, GROUP, CH, lags), lambda n: (0, n, 0, 0)),
        out_shape=jax.ShapeDtypeStruct((2, CH, CH, lags), jnp.bfloat16),
        scratch_shapes=[
            pltpu.VMEM((CH, depth), jnp.float32),
            pltpu.VMEM((depth, 2 * CH), jnp.float32),
            pltpu.VMEM((depth, 2 * lags // FINE * CH), jnp.bfloat16),
            pltpu.VMEM((GROUP * FINE, depth), jnp.bfloat16),
            pltpu.VMEM((2, GROUP, lags, CH), jnp.bfloat16),
        ],
        compiler_params=pltpu.CompilerParams(vmem_limit_bytes=40 * 1024 * 1024),
        name="correlate",
    )(order, own, first, second, jnp.asarray(fine), jnp.asarray(coarse))


def swap(tile, mask):
    count = lax.axis_size("blk")
    return lax.ppermute(tile, "blk", [(low, low ^ mask) for low in range(count)])


def exchange(tile, mask):
    count = lax.axis_size("blk")
    full = count - 1
    if count <= 16:

        def branch(m, moving):
            first = swap(moving, full)
            return first, swap(first, m ^ full) if 2 * m >= count else swap(moving, m)

        branches = [functools.partial(branch, m) for m in range(1, full)]
        return lax.switch(mask - 1, branches, tile)
    moving = tile
    for bit in range(count.bit_length() - 1):
        moving = jnp.where(mask >> bit & 1 == 1, swap(moving, 1 << bit), moving)
    return swap(tile, full), moving


def local(records, dest, slot, valid, masks):
    owners = lax.axis_size("blk")
    held, nfft = records.shape
    capacity = max(16, 2 * held // owners)
    outgoing = pack(records, dest, slot, valid, owners, capacity)
    arrived = lax.all_to_all(outgoing, "blk", split_axis=0, concat_axis=0, tiled=True)
    me = lax.axis_index("blk").astype(jnp.int32).reshape(1)
    tile = whiten(me, arrived, jnp.asarray(forward_table(nfft, F)), capacity)
    full = owners - 1
    first, second = exchange(tile, masks[0] + masks[1] - full)
    order = (masks[:1] != full).astype(jnp.int32)
    return correlate(order, tile, first, second, nfft, LAGS)


def solution(mesh):
    return jax.shard_map(
        local,
        mesh=mesh,
        in_specs=(
            P(("groups", "blk"), None),
            P(("groups", "blk"), None),
            P(("groups", "blk"), None),
            P(("groups", "blk"), None),
            P(),
        ),
        out_specs=P(None, ("groups", "blk"), None, None),
        check_vma=False,
    )
```

```python
import functools
import math

import jax
import jax.numpy as jnp
import numpy as np
from jax import lax
from jax.experimental import pallas as pl
from jax.experimental.pallas import tpu as pltpu
from jax.sharding import PartitionSpec as P

CH = 128
F = 256
LAGS = 128
W = 2
SLOT_BITS = 8
VALID_BITS = 12
LOW_BITS = 4


def forward_table(nfft, bins):
    sample = np.arange(nfft, dtype=np.int64)[:, None]
    freq = np.arange(1, bins + 1, dtype=np.int64)[None, :]
    angle = (sample * freq % nfft).astype(np.float64) * (2.0 * math.pi / nfft)
    return np.concatenate([np.cos(angle), -np.sin(angle)], axis=1).astype(np.float32).astype(jnp.bfloat16)


def turn_tables(nfft, bins, lags, fine, scale):
    freq = np.arange(1, bins + 1, dtype=np.int64)

    def both(shift):
        angle = (freq * shift % nfft).astype(np.float64) * (2.0 * math.pi / nfft)
        return np.cos(angle), np.sin(angle)

    own = np.stack([np.concatenate(both(at)) * scale for at in range(fine)])
    start = both(lags // 2) + both(-fine)
    other = np.stack([np.broadcast_to(part[:, None], (bins, 128)) for part in start])
    return own.astype(np.float32), other.astype(np.float32)


def iota(shape, dim):
    return lax.broadcasted_iota(jnp.int32, shape, dim)


def pack_kernel(owners, capacity, me_ref, key_ref, records_ref, *out_refs):
    held, nfft = records_ref.shape
    rows = owners * capacity
    width = 512
    key = key_ref[...]
    part = key >> (SLOT_BITS + VALID_BITS)
    if len(out_refs) > 1:
        part = part ^ me_ref[0]
    match = (iota((owners, held), 0) == part).astype(jnp.float32)
    before = (iota((held, held), 0) < iota((held, held), 1)).astype(jnp.float32)
    earlier = jnp.dot(
        match.astype(jnp.bfloat16), before.astype(jnp.bfloat16), preferred_element_type=jnp.float32
    )
    rank = jnp.sum(earlier * match, axis=0, keepdims=True).astype(jnp.int32)
    position = part * capacity + rank
    order = (iota((rows, held), 0) == position).astype(jnp.float32).astype(jnp.bfloat16)
    slot = (key >> VALID_BITS) & ((1 << SLOT_BITS) - 1)
    high = (key & ((1 << VALID_BITS) - 1)) >> LOW_BITS
    low = key & ((1 << LOW_BITS) - 1)
    row = iota((16, held), 0)
    labels = jnp.where(row == 0, slot, jnp.where(row == 1, high, jnp.where(row == 2, low, 0)))
    moved = lax.dot_general(
        labels.astype(jnp.float32).astype(jnp.bfloat16),
        order,
        (((1,), (1,)), ((), ())),
        preferred_element_type=jnp.float32,
    ).astype(jnp.bfloat16)

    def put(d, at, value):
        if len(out_refs) > 1:
            out_refs[d][at : at + value.shape[0], :] = value
        else:
            out_refs[0][d, at : at + value.shape[0], :] = value

    for d in range(owners):
        at = d * capacity // 128 * 128
        put(d, nfft // 128 * capacity, moved[:, at : at + 128])
    for begin in range(0, nfft, width):
        ordered = jnp.dot(
            order, records_ref[:, begin : begin + width], preferred_element_type=jnp.float32
        ).astype(jnp.bfloat16)
        for lane in range(0, width, 128):
            at = (begin + lane) // 128 * capacity
            for d in range(owners):
                put(d, at, ordered[d * capacity : (d + 1) * capacity, lane : lane + 128])


def pack(me, key, records, owners, capacity, split):
    held, nfft = records.shape
    vmem = pl.BlockSpec(memory_space=pltpu.VMEM)
    shape = (nfft // 128 * capacity + 16, 128)
    if split:
        outs = [jax.ShapeDtypeStruct(shape, jnp.bfloat16)] * owners
    else:
        outs = [jax.ShapeDtypeStruct((owners,) + shape, jnp.bfloat16)]
    return pl.pallas_call(
        functools.partial(pack_kernel, owners, capacity),
        in_specs=[pl.BlockSpec(memory_space=pltpu.SMEM), vmem, vmem],
        out_specs=[vmem] * len(outs),
        out_shape=outs,
        compiler_params=pltpu.CompilerParams(vmem_limit_bytes=48 * 1024 * 1024),
        name="pack",
    )(me, key, records)


def whiten_kernel(owners, capacity, places, me_ref, *refs):
    *arrived_refs, table_hbm, out_ref, table_ref, trace_ref, spectrum_ref, sem = refs
    split = len(arrived_refs) > 1
    nfft = trace_ref.shape[1]
    rows = owners * capacity
    slots = CH * W
    bins = table_ref.shape[1] // 2
    shift = capacity.bit_length() - 1
    head = nfft // 128 * capacity
    width = 256
    load = pltpu.make_async_copy(table_hbm, table_ref, sem)
    load.start()

    def take(at, count):
        if split:
            return jnp.concatenate([ref[at : at + count, :] for ref in arrived_refs], axis=0)
        return arrived_refs[0][:, at : at + count, :].reshape(owners * count, 128)

    labels = take(head, 16).astype(jnp.float32).reshape(owners, 16, 128)
    which = iota((owners, 16, 128), 1)
    parts = jnp.concatenate(
        [jnp.sum(jnp.where(which == k, labels, 0.0), axis=1) for k in range(3)], axis=0
    )
    if split:
        part = iota((1, rows), 1) >> shift
        place = functools.reduce(
            lambda total, p: total + jnp.where(part == p, places[p], 0),
            range(owners),
            jnp.zeros((1, rows), jnp.int32),
        )
    else:
        place = me_ref[0]
    base = (place * capacity) & 127
    pick = iota((128, rows), 0) == base + (iota((128, rows), 1) & (capacity - 1))
    picked = jnp.dot(
        parts.astype(jnp.bfloat16),
        pick.astype(jnp.float32).astype(jnp.bfloat16),
        preferred_element_type=jnp.float32,
    )
    source = iota((owners, rows), 0) == iota((owners, rows), 1) >> shift
    rowed = [
        jnp.sum(
            jnp.where(source, picked[k * owners : (k + 1) * owners], 0.0), axis=0, keepdims=True
        )
        for k in range(3)
    ]
    slot_row = rowed[0].astype(jnp.int32)
    place = (slot_row & (W - 1)) * CH + (slot_row >> (W.bit_length() - 1))
    valid_row = rowed[1] * float(1 << LOW_BITS) + rowed[2]
    scatter = (iota((slots, rows), 0) == place).astype(jnp.float32).astype(jnp.bfloat16)
    valid_col = jnp.transpose(jnp.broadcast_to(valid_row, (128, rows))).astype(jnp.int32)
    power = jnp.zeros((slots, 128), jnp.float32)
    for begin in range(0, nfft, width):
        lanes = range(begin, begin + width, 128)
        inside = jnp.concatenate(
            [
                (iota((rows, 128), 1) + lane < valid_col).astype(jnp.float32).astype(jnp.bfloat16)
                for lane in lanes
            ],
            axis=1,
        )
        arrived = jnp.concatenate([take(lane // 128 * capacity, capacity) for lane in lanes], axis=1)
        summed = jnp.dot(scatter, arrived * inside, preferred_element_type=jnp.float32)
        coverage = jnp.dot(scatter, inside, preferred_element_type=jnp.float32)
        trace = summed / jnp.maximum(coverage, 1.0)
        trace_ref[:, begin : begin + width] = trace
        square = trace * trace
        for lane in range(0, width, 128):
            power = power + square[:, lane : lane + 128]
    meansq = jnp.sum(power, axis=1, keepdims=True) * (1.0 / nfft)
    gain = lax.rsqrt(meansq + 1e-06)
    load.wait()
    width = 512
    for begin in range(0, nfft, width):
        normed = (trace_ref[:, begin : begin + width] * gain).astype(jnp.bfloat16)
        part = jnp.dot(
            normed, table_ref[begin : begin + width, :], preferred_element_type=jnp.float32
        )
        if begin == 0:
            spectrum_ref[...] = part
        else:
            spectrum_ref[...] += part
    real_part = spectrum_ref[:, :bins]
    imag_part = spectrum_ref[:, bins:]
    amplitude = lax.rsqrt(jnp.maximum(real_part * real_part + imag_part * imag_part, nfft / 4.0))
    real_part = (real_part * amplitude).astype(jnp.bfloat16)
    imag_part = (imag_part * amplitude).astype(jnp.bfloat16)
    for w in range(W):
        at = w * 2 * bins
        out_ref[:, at : at + bins] = real_part[w * CH : (w + 1) * CH]
        out_ref[:, at + bins : at + 2 * bins] = imag_part[w * CH : (w + 1) * CH]


def whiten(me, arrived, table, owners, capacity, places):
    nfft, width = table.shape
    vmem = pl.BlockSpec(memory_space=pltpu.VMEM)
    return pl.pallas_call(
        functools.partial(whiten_kernel, owners, capacity, places),
        in_specs=[pl.BlockSpec(memory_space=pltpu.SMEM)]
        + [vmem] * len(arrived)
        + [pl.BlockSpec(memory_space=pltpu.HBM)],
        out_specs=vmem,
        out_shape=jax.ShapeDtypeStruct((CH, W * width), jnp.bfloat16),
        scratch_shapes=[
            pltpu.VMEM(table.shape, jnp.bfloat16),
            pltpu.VMEM((CH * W, nfft), jnp.float32),
            pltpu.VMEM((CH * W, width), jnp.float32),
            pltpu.SemaphoreType.DMA(()),
        ],
        compiler_params=pltpu.CompilerParams(vmem_limit_bytes=48 * 1024 * 1024),
        name="whiten",
    )(me, *arrived, table)


GROUP = 32
FINE = 16


def correlate_kernel(
    order_ref, own_ref, first_ref, second_ref, fine_ref, coarse_ref, out_ref,
    wide_ref, flat_ref, back_ref, turned_ref, rows_ref,
):
    step = pl.program_id(0)
    bins = coarse_ref.shape[1]
    lags = out_ref.shape[3]
    coarse = lags // FINE

    @pl.when(step == 0)
    def _():
        wide_ref[...] = own_ref[...].astype(jnp.float32)
        at = pl.multiple_of(order_ref[0] * CH, CH)
        flat_ref[:, pl.ds(at, CH)] = jnp.transpose(first_ref[...].astype(jnp.float32))
        flat_ref[:, pl.ds(CH - at, CH)] = jnp.transpose(second_ref[...].astype(jnp.float32))
        size = 32
        for k in range(0, bins, size):
            tables = [
                jnp.concatenate([coarse_ref[n, k : k + size, :]] * 2, axis=1) for n in range(4)
            ]
            for w in range(W):
                top = w * 2 * bins + k
                vr = flat_ref[top : top + size, :]
                vi = flat_ref[top + bins : top + bins + size, :]
                for b in range(coarse):
                    cos, sin = tables[:2] if b == 0 else tables[2:]
                    vr, vi = vr * cos - vi * sin, vi * cos + vr * sin
                    for r in range(2):
                        lanes = slice((r * coarse + b) * CH, (r * coarse + b + 1) * CH)
                        half = slice(r * CH, (r + 1) * CH)
                        back_ref[top : top + size, lanes] = vr[:, half].astype(jnp.bfloat16)
                        back_ref[top + bins : top + bins + size, lanes] = vi[:, half].astype(
                            jnp.bfloat16
                        )

    cos = fine_ref[:, :bins]
    sin = fine_ref[:, bins:]
    for k in range(GROUP):
        u = wide_ref[pl.ds(step * GROUP + k, 1), :]
        rows = slice(k * FINE, (k + 1) * FINE)
        for w in range(W):
            at = w * 2 * bins
            ur = jnp.broadcast_to(u[:, at : at + bins], (FINE, bins))
            ui = jnp.broadcast_to(u[:, at + bins : at + 2 * bins], (FINE, bins))
            turned_ref[rows, at : at + bins] = (ur * cos - ui * sin).astype(jnp.bfloat16)
            turned_ref[rows, at + bins : at + 2 * bins] = (ur * sin + ui * cos).astype(
                jnp.bfloat16
            )
    for r in range(2):
        for b in range(0, coarse, 2):
            lanes = slice((r * coarse + b) * CH, (r * coarse + b + 2) * CH)
            lagged = jnp.dot(
                turned_ref[...], back_ref[:, lanes], preferred_element_type=jnp.float32
            ).astype(jnp.bfloat16)
            for k in range(GROUP):
                for h in range(2):
                    rows_ref[r, k, (b + h) * FINE : (b + h + 1) * FINE, :] = lagged[
                        k * FINE : (k + 1) * FINE, h * CH : (h + 1) * CH
                    ]
        for k in range(GROUP):
            out_ref[r, k] = jnp.transpose(rows_ref[r, k])


def correlate(order, own, first, second, nfft, lags):
    depth = own.shape[1]
    bins = depth // (2 * W)
    fine, coarse = turn_tables(nfft, bins, lags, FINE, 1.0 / math.sqrt(W * bins))
    whole = lambda *shape: pl.BlockSpec(shape, lambda n: (0,) * len(shape))
    return pl.pallas_call(
        correlate_kernel,
        grid=(CH // GROUP,),
        in_specs=[
            pl.BlockSpec(memory_space=pltpu.SMEM),
            whole(CH, depth),
            whole(CH, depth),
            whole(CH, depth),
            whole(*fine.shape),
            whole(*coarse.shape),
        ],
        out_specs=pl.BlockSpec((2, GROUP, CH, lags), lambda n: (0, n, 0, 0)),
        out_shape=jax.ShapeDtypeStruct((2, CH, CH, lags), jnp.bfloat16),
        scratch_shapes=[
            pltpu.VMEM((CH, depth), jnp.float32),
            pltpu.VMEM((depth, 2 * CH), jnp.float32),
            pltpu.VMEM((depth, 2 * lags // FINE * CH), jnp.bfloat16),
            pltpu.VMEM((GROUP * FINE, depth), jnp.bfloat16),
            pltpu.VMEM((2, GROUP, lags, CH), jnp.bfloat16),
        ],
        compiler_params=pltpu.CompilerParams(vmem_limit_bytes=40 * 1024 * 1024),
        name="correlate",
    )(order, own, first, second, jnp.asarray(fine), jnp.asarray(coarse))


def swap(tile, mask):
    count = lax.axis_size("blk")
    return lax.ppermute(tile, "blk", [(low, low ^ mask) for low in range(count)])


def exchange(tile, mask):
    count = lax.axis_size("blk")
    full = count - 1
    if count <= 16:

        def branch(m, moving):
            first = swap(moving, full)
            return first, swap(first, m ^ full) if 2 * m >= count else swap(moving, m)

        branches = [functools.partial(branch, m) for m in range(1, full)]
        return lax.switch(mask - 1, branches, tile)
    moving = tile
    for bit in range(count.bit_length() - 1):
        moving = jnp.where(mask >> bit & 1 == 1, swap(moving, 1 << bit), moving)
    return swap(tile, full), moving


def local(records, dest, slot, valid, masks):
    owners = lax.axis_size("blk")
    held, nfft = records.shape
    capacity = max(16, 2 * held // owners)
    me = lax.axis_index("blk").astype(jnp.int32).reshape(1)
    key = ((dest << SLOT_BITS) + slot << VALID_BITS) + valid
    split = owners <= 16
    outgoing = pack(me, key.reshape(1, held), records, owners, capacity, split)
    if split:
        half = owners // 2
        places = [half]
        for distance in range(1, half):
            places += [distance, half + distance]
        arrived = [swap(outgoing[distance], distance) for distance in places] + [outgoing[0]]
        places.append(0)
    else:
        places = None
        arrived = [lax.all_to_all(outgoing[0], "blk", split_axis=0, concat_axis=0, tiled=True)]
    tile = whiten(me, arrived, jnp.asarray(forward_table(nfft, F)), owners, capacity, places)
    full = owners - 1
    first, second = exchange(tile, masks[0] + masks[1] - full)
    order = (masks[:1] != full).astype(jnp.int32)
    return correlate(order, tile, first, second, nfft, LAGS)


def solution(mesh):
    return jax.shard_map(
        local,
        mesh=mesh,
        in_specs=(
            P(("groups", "blk"), None),
            P(("groups", "blk"), None),
            P(("groups", "blk"), None),
            P(("groups", "blk"), None),
            P(),
        ),
        out_specs=P(None, ("groups", "blk"), None, None),
        check_vma=False,
    )
```

```python
import functools
import math

import jax
import jax.numpy as jnp
import numpy as np
from jax import lax
from jax.experimental import pallas as pl
from jax.experimental.pallas import tpu as pltpu
from jax.sharding import PartitionSpec as P

CH = 128
F = 256
LAGS = 128
W = 2
SLOT_BITS = 8
VALID_BITS = 12
LOW_BITS = 4


def forward_table(nfft, bins):
    sample = np.arange(nfft, dtype=np.int64)[:, None]
    freq = np.arange(1, bins + 1, dtype=np.int64)[None, :]
    angle = (sample * freq % nfft).astype(np.float64) * (2.0 * math.pi / nfft)
    return np.concatenate([np.cos(angle), -np.sin(angle)], axis=1).astype(np.float32).astype(jnp.bfloat16)


def turn_tables(nfft, bins, lags, fine, scale):
    freq = np.arange(1, bins + 1, dtype=np.int64)

    def both(shift):
        angle = (freq * shift % nfft).astype(np.float64) * (2.0 * math.pi / nfft)
        return np.cos(angle), np.sin(angle)

    own = np.stack([np.concatenate(both(at)) * scale for at in range(fine)])
    start = both(lags // 2) + both(-fine)
    other = np.stack([np.broadcast_to(part[:, None], (bins, 128)) for part in start])
    return own.astype(np.float32), other.astype(np.float32)


def iota(shape, dim):
    return lax.broadcasted_iota(jnp.int32, shape, dim)


def pack_kernel(owners, capacity, me_ref, key_ref, records_ref, *out_refs):
    held, nfft = records_ref.shape
    rows = owners * capacity
    width = 512
    key = key_ref[...]
    part = key >> (SLOT_BITS + VALID_BITS)
    if len(out_refs) > 1:
        part = part ^ me_ref[0]
    match = (iota((owners, held), 0) == part).astype(jnp.float32)
    before = (iota((held, held), 0) < iota((held, held), 1)).astype(jnp.float32)
    earlier = jnp.dot(
        match.astype(jnp.bfloat16), before.astype(jnp.bfloat16), preferred_element_type=jnp.float32
    )
    rank = jnp.sum(earlier * match, axis=0, keepdims=True).astype(jnp.int32)
    position = part * capacity + rank
    order = (iota((rows, held), 0) == position).astype(jnp.float32).astype(jnp.bfloat16)
    slot = (key >> VALID_BITS) & ((1 << SLOT_BITS) - 1)
    high = (key & ((1 << VALID_BITS) - 1)) >> LOW_BITS
    low = key & ((1 << LOW_BITS) - 1)
    row = iota((16, held), 0)
    labels = jnp.where(row == 0, slot, jnp.where(row == 1, high, jnp.where(row == 2, low, 0)))
    moved = lax.dot_general(
        labels.astype(jnp.float32).astype(jnp.bfloat16),
        order,
        (((1,), (1,)), ((), ())),
        preferred_element_type=jnp.float32,
    ).astype(jnp.bfloat16)

    def put(d, at, value):
        if len(out_refs) > 1:
            out_refs[d][at : at + value.shape[0], :] = value
        else:
            out_refs[0][d, at : at + value.shape[0], :] = value

    for d in range(owners):
        at = d * capacity // 128 * 128
        put(d, nfft // 128 * capacity, moved[:, at : at + 128])
    for begin in range(0, nfft, width):
        ordered = jnp.dot(
            order, records_ref[:, begin : begin + width], preferred_element_type=jnp.float32
        ).astype(jnp.bfloat16)
        for lane in range(0, width, 128):
            at = (begin + lane) // 128 * capacity
            for d in range(owners):
                put(d, at, ordered[d * capacity : (d + 1) * capacity, lane : lane + 128])


def pack(me, key, records, owners, capacity, split):
    held, nfft = records.shape
    vmem = pl.BlockSpec(memory_space=pltpu.VMEM)
    shape = (nfft // 128 * capacity + 16, 128)
    if split:
        outs = [jax.ShapeDtypeStruct(shape, jnp.bfloat16)] * owners
    else:
        outs = [jax.ShapeDtypeStruct((owners,) + shape, jnp.bfloat16)]
    return pl.pallas_call(
        functools.partial(pack_kernel, owners, capacity),
        in_specs=[pl.BlockSpec(memory_space=pltpu.SMEM), vmem, vmem],
        out_specs=[vmem] * len(outs),
        out_shape=outs,
        compiler_params=pltpu.CompilerParams(vmem_limit_bytes=48 * 1024 * 1024),
        name="pack",
    )(me, key, records)


def whiten_kernel(owners, capacity, places, me_ref, *refs):
    *arrived_refs, table_hbm, out_ref, table_ref, trace_ref, spectrum_ref, sem = refs
    split = len(arrived_refs) > 1
    nfft = trace_ref.shape[1]
    rows = owners * capacity
    slots = CH * W
    bins = table_ref.shape[1] // 2
    shift = capacity.bit_length() - 1
    head = nfft // 128 * capacity
    width = 256
    load = pltpu.make_async_copy(table_hbm, table_ref, sem)
    load.start()

    def take(at, count):
        if split:
            return jnp.concatenate([ref[at : at + count, :] for ref in arrived_refs], axis=0)
        return arrived_refs[0][:, at : at + count, :].reshape(owners * count, 128)

    labels = take(head, 16).astype(jnp.float32).reshape(owners, 16, 128)
    which = iota((owners, 16, 128), 1)
    parts = jnp.concatenate(
        [jnp.sum(jnp.where(which == k, labels, 0.0), axis=1) for k in range(3)], axis=0
    )
    if split:
        part = iota((1, rows), 1) >> shift
        place = functools.reduce(
            lambda total, p: total + jnp.where(part == p, places[p], 0),
            range(owners),
            jnp.zeros((1, rows), jnp.int32),
        )
    else:
        place = me_ref[0]
    base = (place * capacity) & 127
    pick = iota((128, rows), 0) == base + (iota((128, rows), 1) & (capacity - 1))
    picked = jnp.dot(
        parts.astype(jnp.bfloat16),
        pick.astype(jnp.float32).astype(jnp.bfloat16),
        preferred_element_type=jnp.float32,
    )
    source = iota((owners, rows), 0) == iota((owners, rows), 1) >> shift
    rowed = [
        jnp.sum(
            jnp.where(source, picked[k * owners : (k + 1) * owners], 0.0), axis=0, keepdims=True
        )
        for k in range(3)
    ]
    slot_row = rowed[0].astype(jnp.int32)
    place = (slot_row & (W - 1)) * CH + (slot_row >> (W.bit_length() - 1))
    valid_row = rowed[1] * float(1 << LOW_BITS) + rowed[2]
    scatter = (iota((slots, rows), 0) == place).astype(jnp.float32).astype(jnp.bfloat16)
    valid_col = jnp.transpose(jnp.broadcast_to(valid_row, (128, rows))).astype(jnp.int32)
    power = jnp.zeros((slots, 128), jnp.float32)
    for begin in range(0, nfft, width):
        lanes = range(begin, begin + width, 128)
        inside = jnp.concatenate(
            [
                (iota((rows, 128), 1) + lane < valid_col).astype(jnp.float32).astype(jnp.bfloat16)
                for lane in lanes
            ],
            axis=1,
        )
        arrived = jnp.concatenate([take(lane // 128 * capacity, capacity) for lane in lanes], axis=1)
        summed = jnp.dot(scatter, arrived * inside, preferred_element_type=jnp.float32)
        coverage = jnp.dot(scatter, inside, preferred_element_type=jnp.float32)
        trace = summed / jnp.maximum(coverage, 1.0)
        trace_ref[:, begin : begin + width] = trace
        square = trace * trace
        for lane in range(0, width, 128):
            power = power + square[:, lane : lane + 128]
    meansq = jnp.sum(power, axis=1, keepdims=True) * (1.0 / nfft)
    gain = lax.rsqrt(meansq + 1e-06)
    load.wait()
    width = 512
    for begin in range(0, nfft, width):
        normed = (trace_ref[:, begin : begin + width] * gain).astype(jnp.bfloat16)
        part = jnp.dot(
            normed, table_ref[begin : begin + width, :], preferred_element_type=jnp.float32
        )
        if begin == 0:
            spectrum_ref[...] = part
        else:
            spectrum_ref[...] += part
    real_part = spectrum_ref[:, :bins]
    imag_part = spectrum_ref[:, bins:]
    amplitude = lax.rsqrt(jnp.maximum(real_part * real_part + imag_part * imag_part, nfft / 4.0))
    real_part = (real_part * amplitude).astype(jnp.bfloat16)
    imag_part = (imag_part * amplitude).astype(jnp.bfloat16)
    for w in range(W):
        at = w * 2 * bins
        out_ref[:, at : at + bins] = real_part[w * CH : (w + 1) * CH]
        out_ref[:, at + bins : at + 2 * bins] = imag_part[w * CH : (w + 1) * CH]


def whiten(me, arrived, table, owners, capacity, places):
    nfft, width = table.shape
    vmem = pl.BlockSpec(memory_space=pltpu.VMEM)
    return pl.pallas_call(
        functools.partial(whiten_kernel, owners, capacity, places),
        in_specs=[pl.BlockSpec(memory_space=pltpu.SMEM)]
        + [vmem] * len(arrived)
        + [pl.BlockSpec(memory_space=pltpu.HBM)],
        out_specs=vmem,
        out_shape=jax.ShapeDtypeStruct((CH, W * width), jnp.bfloat16),
        scratch_shapes=[
            pltpu.VMEM(table.shape, jnp.bfloat16),
            pltpu.VMEM((CH * W, nfft), jnp.float32),
            pltpu.VMEM((CH * W, width), jnp.float32),
            pltpu.SemaphoreType.DMA(()),
        ],
        compiler_params=pltpu.CompilerParams(vmem_limit_bytes=60 * 1024 * 1024),
        name="whiten",
    )(me, *arrived, table)


GROUP = 32
FINE = 16


def correlate_kernel(
    order_ref, own_ref, first_ref, second_ref, fine_ref, coarse_ref, out_ref,
    wide_ref, flat_ref, back_ref, turned_ref, rows_ref,
):
    step = pl.program_id(0)
    bins = coarse_ref.shape[1]
    lags = out_ref.shape[3]
    coarse = lags // FINE
    half = coarse // 2

    def turn(group, slot, begin, count):
        cos = fine_ref[:, :bins]
        sin = fine_ref[:, bins:]
        for k in range(begin, begin + count):
            u = wide_ref[pl.ds(group * GROUP + k, 1), :]
            rows = slice(k * FINE, (k + 1) * FINE)
            for w in range(W):
                at = w * 2 * bins
                ur = jnp.broadcast_to(u[:, at : at + bins], (FINE, bins))
                ui = jnp.broadcast_to(u[:, at + bins : at + 2 * bins], (FINE, bins))
                turned_ref[slot, rows, at : at + bins] = (ur * cos - ui * sin).astype(jnp.bfloat16)
                turned_ref[slot, rows, at + bins : at + 2 * bins] = (ur * sin + ui * cos).astype(
                    jnp.bfloat16
                )

    def emit(slot, begin, count):
        for k in range(begin, begin + count):
            out_ref[0, k] = jnp.transpose(rows_ref[slot, k])

    @pl.when(step == 0)
    def _():
        wide_ref[...] = own_ref[...].astype(jnp.float32)
        at = pl.multiple_of(order_ref[0] * CH, CH)
        flat_ref[:, pl.ds(at, CH)] = jnp.transpose(first_ref[...].astype(jnp.float32))
        flat_ref[:, pl.ds(CH - at, CH)] = jnp.transpose(second_ref[...].astype(jnp.float32))
        size = 32
        for k in range(0, bins, size):
            tables = [
                jnp.concatenate([coarse_ref[n, k : k + size, :]] * 2, axis=1) for n in range(4)
            ]
            for w in range(W):
                top = w * 2 * bins + k
                vr = flat_ref[top : top + size, :]
                vi = flat_ref[top + bins : top + bins + size, :]
                for b in range(coarse):
                    cos, sin = tables[:2] if b == 0 else tables[2:]
                    vr, vi = vr * cos - vi * sin, vi * cos + vr * sin
                    lanes = slice(b % 2 * CH, (b % 2 + 1) * CH)
                    for r in range(2):
                        side = slice(r * CH, (r + 1) * CH)
                        back_ref[r, b // 2, top : top + size, lanes] = vr[:, side].astype(
                            jnp.bfloat16
                        )
                        back_ref[r, b // 2, top + bins : top + bins + size, lanes] = vi[
                            :, side
                        ].astype(jnp.bfloat16)
        turn(0, 0, 0, GROUP)

    chunks = 2 * (CH // GROUP)
    now, before = step % 2, (step + 1) % 2

    @pl.when(step < chunks)
    def _():
        group = step // 2
        follow = jnp.minimum(group + 1, CH // GROUP - 1)
        share = GROUP // half
        for n in range(half):
            lagged = jnp.dot(
                turned_ref[group % 2], back_ref[now, n], preferred_element_type=jnp.float32
            ).astype(jnp.bfloat16)
            for k in range(GROUP):
                for h in range(2):
                    at = (2 * n + h) * FINE
                    rows_ref[now, k, at : at + FINE, :] = lagged[
                        k * FINE : (k + 1) * FINE, h * CH : (h + 1) * CH
                    ]
            emit(before, n * share, share)
            turn(follow, (group + 1) % 2, n * share, share)

    @pl.when(step == chunks)
    def _():
        emit(before, 0, GROUP)


def correlate(order, own, first, second, nfft, lags):
    depth = own.shape[1]
    bins = depth // (2 * W)
    fine, coarse = turn_tables(nfft, bins, lags, FINE, 1.0 / math.sqrt(W * bins))
    whole = lambda *shape: pl.BlockSpec(shape, lambda n: (0,) * len(shape))

    def place(n):
        chunk = jnp.maximum(n - 1, 0)
        return chunk % 2, chunk // 2, 0, 0

    return pl.pallas_call(
        correlate_kernel,
        grid=(2 * (CH // GROUP) + 1,),
        in_specs=[
            pl.BlockSpec(memory_space=pltpu.SMEM),
            whole(CH, depth),
            whole(CH, depth),
            whole(CH, depth),
            whole(*fine.shape),
            whole(*coarse.shape),
        ],
        out_specs=pl.BlockSpec((1, GROUP, CH, lags), place),
        out_shape=jax.ShapeDtypeStruct((2, CH, CH, lags), jnp.bfloat16),
        scratch_shapes=[
            pltpu.VMEM((CH, depth), jnp.float32),
            pltpu.VMEM((depth, 2 * CH), jnp.float32),
            pltpu.VMEM((2, lags // FINE // 2, depth, 2 * CH), jnp.bfloat16),
            pltpu.VMEM((2, GROUP * FINE, depth), jnp.bfloat16),
            pltpu.VMEM((2, GROUP, lags, CH), jnp.bfloat16),
        ],
        compiler_params=pltpu.CompilerParams(vmem_limit_bytes=60 * 1024 * 1024),
        name="correlate",
    )(order, own, first, second, jnp.asarray(fine), jnp.asarray(coarse))


def swap(tile, mask):
    count = lax.axis_size("blk")
    return lax.ppermute(tile, "blk", [(low, low ^ mask) for low in range(count)])


def exchange(tile, mask):
    count = lax.axis_size("blk")
    full = count - 1
    if count <= 16:

        def branch(m, moving):
            first = swap(moving, full)
            return first, swap(first, m ^ full) if 2 * m >= count else swap(moving, m)

        branches = [functools.partial(branch, m) for m in range(1, full)]
        return lax.switch(mask - 1, branches, tile)
    moving = tile
    for bit in range(count.bit_length() - 1):
        moving = jnp.where(mask >> bit & 1 == 1, swap(moving, 1 << bit), moving)
    return swap(tile, full), moving


def local(records, dest, slot, valid, masks):
    owners = lax.axis_size("blk")
    held, nfft = records.shape
    capacity = max(16, 2 * held // owners)
    me = lax.axis_index("blk").astype(jnp.int32).reshape(1)
    key = ((dest << SLOT_BITS) + slot << VALID_BITS) + valid
    split = owners <= 16
    outgoing = pack(me, key.reshape(1, held), records, owners, capacity, split)
    if split:
        half = owners // 2
        ahead = min(3, half)
        places = list(range(half, half + ahead))
        for distance in range(1, half):
            places += [half + k for k in [distance + ahead - 1] if k < half] + [distance]
        arrived = [swap(outgoing[distance], distance) for distance in places] + [outgoing[0]]
        places.append(0)
    else:
        places = None
        arrived = [lax.all_to_all(outgoing[0], "blk", split_axis=0, concat_axis=0, tiled=True)]
    tile = whiten(me, arrived, jnp.asarray(forward_table(nfft, F)), owners, capacity, places)
    full = owners - 1
    first, second = exchange(tile, masks[0] + masks[1] - full)
    order = (masks[:1] != full).astype(jnp.int32)
    return correlate(order, tile, first, second, nfft, LAGS)


def solution(mesh):
    return jax.shard_map(
        local,
        mesh=mesh,
        in_specs=(
            P(("groups", "blk"), None),
            P(("groups", "blk"), None),
            P(("groups", "blk"), None),
            P(("groups", "blk"), None),
            P(),
        ),
        out_specs=P(None, ("groups", "blk"), None, None),
        check_vma=False,
    )
```

```python
import functools
import math

import jax
import jax.numpy as jnp
import numpy as np
from jax import lax
from jax.experimental import pallas as pl
from jax.experimental.pallas import tpu as pltpu
from jax.sharding import PartitionSpec as P

CH = 128
F = 256
LAGS = 128
W = 2
SLOT_BITS = 8
VALID_BITS = 12
LOW_BITS = 4


def forward_table(nfft, bins):
    sample = np.arange(nfft, dtype=np.int64)[:, None]
    freq = np.arange(1, bins + 1, dtype=np.int64)[None, :]
    angle = (sample * freq % nfft).astype(np.float64) * (2.0 * math.pi / nfft)
    return np.concatenate([np.cos(angle), -np.sin(angle)], axis=1).astype(np.float32).astype(jnp.bfloat16)


def turn_table(nfft, bins, lags, scale):
    freq = np.arange(1, bins + 1, dtype=np.int64)[None, :]
    shift = np.arange(lags // 2 + 16, dtype=np.int64)[:, None]
    angle = (freq * shift % nfft).astype(np.float64) * (2.0 * math.pi / nfft)
    table = np.concatenate([np.cos(angle), np.sin(angle)], axis=1)
    table[: lags // 2] *= scale
    return table.astype(np.float32).astype(jnp.bfloat16)


def iota(shape, dim):
    return lax.broadcasted_iota(jnp.int32, shape, dim)


def pack_kernel(owners, capacity, me_ref, key_ref, records_ref, *out_refs):
    held, nfft = records_ref.shape
    rows = owners * capacity
    width = 512
    key = key_ref[...]
    part = key >> (SLOT_BITS + VALID_BITS)
    if len(out_refs) > 1:
        part = part ^ me_ref[0]
    match = (iota((owners, held), 0) == part).astype(jnp.float32)
    before = (iota((held, held), 0) < iota((held, held), 1)).astype(jnp.float32)
    earlier = jnp.dot(
        match.astype(jnp.bfloat16), before.astype(jnp.bfloat16), preferred_element_type=jnp.float32
    )
    rank = jnp.sum(earlier * match, axis=0, keepdims=True).astype(jnp.int32)
    position = part * capacity + rank
    order = (iota((rows, held), 0) == position).astype(jnp.float32).astype(jnp.bfloat16)
    slot = (key >> VALID_BITS) & ((1 << SLOT_BITS) - 1)
    high = (key & ((1 << VALID_BITS) - 1)) >> LOW_BITS
    low = key & ((1 << LOW_BITS) - 1)
    row = iota((16, held), 0)
    labels = jnp.where(row == 0, slot, jnp.where(row == 1, high, jnp.where(row == 2, low, 0)))
    moved = lax.dot_general(
        labels.astype(jnp.float32).astype(jnp.bfloat16),
        order,
        (((1,), (1,)), ((), ())),
        preferred_element_type=jnp.float32,
    ).astype(jnp.bfloat16)

    def put(d, at, value):
        if len(out_refs) > 1:
            out_refs[d][at : at + value.shape[0], :] = value
        else:
            out_refs[0][d, at : at + value.shape[0], :] = value

    for d in range(owners):
        at = d * capacity // 128 * 128
        put(d, nfft // 128 * capacity, moved[:, at : at + 128])
    for begin in range(0, nfft, width):
        ordered = jnp.dot(
            order, records_ref[:, begin : begin + width], preferred_element_type=jnp.float32
        ).astype(jnp.bfloat16)
        for lane in range(0, width, 128):
            at = (begin + lane) // 128 * capacity
            for d in range(owners):
                put(d, at, ordered[d * capacity : (d + 1) * capacity, lane : lane + 128])


def pack(me, key, records, owners, capacity, split):
    held, nfft = records.shape
    vmem = pl.BlockSpec(memory_space=pltpu.VMEM)
    shape = (nfft // 128 * capacity + 16, 128)
    if split:
        outs = [jax.ShapeDtypeStruct(shape, jnp.bfloat16)] * owners
    else:
        outs = [jax.ShapeDtypeStruct((owners,) + shape, jnp.bfloat16)]
    return pl.pallas_call(
        functools.partial(pack_kernel, owners, capacity),
        in_specs=[pl.BlockSpec(memory_space=pltpu.SMEM), vmem, vmem],
        out_specs=[vmem] * len(outs),
        out_shape=outs,
        compiler_params=pltpu.CompilerParams(vmem_limit_bytes=48 * 1024 * 1024),
        name="pack",
    )(me, key, records)


def whiten_kernel(owners, capacity, places, me_ref, *refs):
    *arrived_refs, table_ref, out_ref, trace_ref, spectrum_ref = refs
    split = len(arrived_refs) > 1
    nfft = trace_ref.shape[1]
    rows = owners * capacity
    slots = CH * W
    bins = table_ref.shape[1] // 2
    shift = capacity.bit_length() - 1
    head = nfft // 128 * capacity
    width = 256

    def take(at, count):
        if split:
            return jnp.concatenate([ref[at : at + count, :] for ref in arrived_refs], axis=0)
        return arrived_refs[0][:, at : at + count, :].reshape(owners * count, 128)

    labels = take(head, 16).astype(jnp.float32).reshape(owners, 16, 128)
    which = iota((owners, 16, 128), 1)
    parts = jnp.concatenate(
        [jnp.sum(jnp.where(which == k, labels, 0.0), axis=1) for k in range(3)], axis=0
    )
    if split:
        part = iota((1, rows), 1) >> shift
        place = functools.reduce(
            lambda total, p: total + jnp.where(part == p, places[p], 0),
            range(owners),
            jnp.zeros((1, rows), jnp.int32),
        )
    else:
        place = me_ref[0]
    base = (place * capacity) & 127
    pick = iota((128, rows), 0) == base + (iota((128, rows), 1) & (capacity - 1))
    picked = jnp.dot(
        parts.astype(jnp.bfloat16),
        pick.astype(jnp.float32).astype(jnp.bfloat16),
        preferred_element_type=jnp.float32,
    )
    source = iota((owners, rows), 0) == iota((owners, rows), 1) >> shift
    rowed = [
        jnp.sum(
            jnp.where(source, picked[k * owners : (k + 1) * owners], 0.0), axis=0, keepdims=True
        )
        for k in range(3)
    ]
    slot_row = rowed[0].astype(jnp.int32)
    place = (slot_row & (W - 1)) * CH + (slot_row >> (W.bit_length() - 1))
    valid_row = rowed[1] * float(1 << LOW_BITS) + rowed[2]
    scatter = (iota((slots, rows), 0) == place).astype(jnp.float32).astype(jnp.bfloat16)
    valid_col = jnp.transpose(jnp.broadcast_to(valid_row, (128, rows))).astype(jnp.int32)
    power = jnp.zeros((slots, 128), jnp.float32)
    for begin in range(0, nfft, width):
        lanes = range(begin, begin + width, 128)
        inside = jnp.concatenate(
            [
                (iota((rows, 128), 1) + lane < valid_col).astype(jnp.float32).astype(jnp.bfloat16)
                for lane in lanes
            ],
            axis=1,
        )
        arrived = jnp.concatenate([take(lane // 128 * capacity, capacity) for lane in lanes], axis=1)
        summed = jnp.dot(scatter, arrived * inside, preferred_element_type=jnp.float32)
        coverage = jnp.dot(scatter, inside, preferred_element_type=jnp.float32)
        trace = summed / jnp.maximum(coverage, 1.0)
        trace_ref[:, begin : begin + width] = trace
        square = trace * trace
        for lane in range(0, width, 128):
            power = power + square[:, lane : lane + 128]
    meansq = jnp.sum(power, axis=1, keepdims=True) * (1.0 / nfft)
    gain = lax.rsqrt(meansq + 1e-06)
    width = 512
    for begin in range(0, nfft, width):
        normed = (trace_ref[:, begin : begin + width] * gain).astype(jnp.bfloat16)
        part = jnp.dot(
            normed, table_ref[begin : begin + width, :], preferred_element_type=jnp.float32
        )
        if begin == 0:
            spectrum_ref[...] = part
        else:
            spectrum_ref[...] += part
    real_part = spectrum_ref[:, :bins]
    imag_part = spectrum_ref[:, bins:]
    amplitude = lax.rsqrt(jnp.maximum(real_part * real_part + imag_part * imag_part, nfft / 4.0))
    real_part = (real_part * amplitude).astype(jnp.bfloat16)
    imag_part = (imag_part * amplitude).astype(jnp.bfloat16)
    for w in range(W):
        at = w * 2 * bins
        out_ref[:, at : at + bins] = real_part[w * CH : (w + 1) * CH]
        out_ref[:, at + bins : at + 2 * bins] = imag_part[w * CH : (w + 1) * CH]


def whiten(me, arrived, table, owners, capacity, places):
    nfft, width = table.shape
    vmem = pl.BlockSpec(memory_space=pltpu.VMEM)
    return pl.pallas_call(
        functools.partial(whiten_kernel, owners, capacity, places),
        in_specs=[pl.BlockSpec(memory_space=pltpu.SMEM)]
        + [vmem] * (len(arrived) + 1),
        out_specs=vmem,
        out_shape=jax.ShapeDtypeStruct((CH, W * width), jnp.bfloat16),
        scratch_shapes=[
            pltpu.VMEM((CH * W, nfft), jnp.float32),
            pltpu.VMEM((CH * W, width), jnp.float32),
        ],
        compiler_params=pltpu.CompilerParams(vmem_limit_bytes=40 * 1024 * 1024),
        name="whiten",
    )(me, *arrived, table)


GROUP = 16
BLOCK = 4


def correlate_kernel(
    order_ref, own_ref, first_ref, second_ref, table_ref, out_ref, back_ref, wide_ref, turned_a, turned_b
):
    step = pl.program_id(0)
    bins = table_ref.shape[1] // 2
    half = out_ref.shape[3] // 2
    blocks = GROUP // BLOCK
    turned = (turned_a, turned_b)

    def turn(block):
        cos = table_ref[:half, :bins]
        sin = table_ref[:half, bins:]
        for k in range(BLOCK):
            row = jnp.minimum(step * GROUP + block * BLOCK + k, CH - 1)
            u = wide_ref[pl.ds(row, 1), :]
            rows = slice(k * half, (k + 1) * half)
            for w in range(W):
                at = w * 2 * bins
                ur = jnp.broadcast_to(u[:, at : at + bins], (half, bins)).astype(jnp.bfloat16)
                ui = jnp.broadcast_to(u[:, at + bins : at + 2 * bins], (half, bins)).astype(
                    jnp.bfloat16
                )
                turned[block % 2][rows, at : at + bins] = ur * cos - ui * sin
                turned[block % 2][rows, at + bins : at + 2 * bins] = ur * sin + ui * cos

    @pl.when(step == 0)
    def _():
        wide_ref[...] = own_ref[...].astype(jnp.float32)
        corner = table_ref[half : half + 16, :].astype(jnp.float32)
        cos, sin = corner[:1, :bins], corner[:1, bins:]
        for place, ref in ((order_ref[0], first_ref), (1 - order_ref[0], second_ref)):
            early = pl.ds(pl.multiple_of(place * 2 * CH, 2 * CH), CH)
            late = pl.ds(pl.multiple_of(place * 2 * CH + CH, CH), CH)
            back_ref[late, :] = ref[...]
            for w in range(W):
                at = w * 2 * bins
                vr = ref[:, at : at + bins].astype(jnp.float32)
                vi = ref[:, at + bins : at + 2 * bins].astype(jnp.float32)
                back_ref[early, at : at + bins] = (vr * cos - vi * sin).astype(jnp.bfloat16)
                back_ref[early, at + bins : at + 2 * bins] = (vr * sin + vi * cos).astype(
                    jnp.bfloat16
                )
        turn(0)

    for block in range(blocks):
        turn(block + 1)
        lagged = lax.dot_general(
            back_ref[...],
            turned[block % 2][...],
            (((1,), (1,)), ((), ())),
            preferred_element_type=jnp.float32,
        ).astype(jnp.bfloat16)
        for k in range(BLOCK):
            lanes = slice(k * half, (k + 1) * half)
            for r in range(2):
                top = r * 2 * CH
                out_ref[r, block * BLOCK + k] = jnp.concatenate(
                    [lagged[top : top + CH, lanes], lagged[top + CH : top + 2 * CH, lanes]], axis=1
                )


def correlate(order, own, first, second, table, lags):
    depth = own.shape[1]
    half = lags // 2
    whole = lambda *shape: pl.BlockSpec(shape, lambda n: (0,) * len(shape))
    return pl.pallas_call(
        correlate_kernel,
        grid=(CH // GROUP,),
        in_specs=[
            pl.BlockSpec(memory_space=pltpu.SMEM),
            whole(CH, depth),
            whole(CH, depth),
            whole(CH, depth),
            whole(*table.shape),
        ],
        out_specs=pl.BlockSpec((2, GROUP, CH, lags), lambda n: (0, n, 0, 0)),
        out_shape=jax.ShapeDtypeStruct((2, CH, CH, lags), jnp.bfloat16),
        scratch_shapes=[
            pltpu.VMEM((4 * CH, depth), jnp.bfloat16),
            pltpu.VMEM((CH, depth), jnp.float32),
            pltpu.VMEM((BLOCK * half, depth), jnp.bfloat16),
            pltpu.VMEM((BLOCK * half, depth), jnp.bfloat16),
        ],
        compiler_params=pltpu.CompilerParams(vmem_limit_bytes=32 * 1024 * 1024),
        name="correlate",
    )(order, own, first, second, table)


def bring_kernel(*refs):
    for source, target in zip(refs[: len(refs) // 2], refs[len(refs) // 2 :]):
        target[...] = source[...]


def bring(*tables):
    vmem = pl.BlockSpec(memory_space=pltpu.VMEM)
    return pl.pallas_call(
        bring_kernel,
        in_specs=[vmem] * len(tables),
        out_specs=[vmem] * len(tables),
        out_shape=[jax.ShapeDtypeStruct(table.shape, table.dtype) for table in tables],
        name="bring",
    )(*tables)


def swap(tile, mask):
    count = lax.axis_size("blk")
    return lax.ppermute(tile, "blk", [(low, low ^ mask) for low in range(count)])


def exchange(tile, mask):
    count = lax.axis_size("blk")
    full = count - 1
    if count <= 16:

        def branch(m, moving):
            first = swap(moving, full)
            return first, swap(first, m ^ full) if 2 * m >= count else swap(moving, m)

        branches = [functools.partial(branch, m) for m in range(1, full)]
        return lax.switch(mask - 1, branches, tile)
    moving = tile
    for bit in range(count.bit_length() - 1):
        moving = jnp.where(mask >> bit & 1 == 1, swap(moving, 1 << bit), moving)
    return swap(tile, full), moving


def local(records, dest, slot, valid, masks):
    owners = lax.axis_size("blk")
    held, nfft = records.shape
    capacity = max(16, 2 * held // owners)
    me = lax.axis_index("blk").astype(jnp.int32).reshape(1)
    key = ((dest << SLOT_BITS) + slot << VALID_BITS) + valid
    split = owners <= 16
    outgoing = pack(me, key.reshape(1, held), records, owners, capacity, split)
    if split:
        half = owners // 2
        places = [half]
        for distance in range(1, half):
            places += [distance, half + distance]
        arrived = [swap(outgoing[distance], distance) for distance in places] + [outgoing[0]]
        places.append(0)
    else:
        places = None
        arrived = [lax.all_to_all(outgoing[0], "blk", split_axis=0, concat_axis=0, tiled=True)]
    forward, lag = bring(
        jnp.asarray(forward_table(nfft, F)),
        jnp.asarray(turn_table(nfft, F, LAGS, 1.0 / math.sqrt(W * F))),
    )
    tile = whiten(me, arrived, forward, owners, capacity, places)
    full = owners - 1
    first, second = exchange(tile, masks[0] + masks[1] - full)
    order = (masks[:1] != full).astype(jnp.int32)
    return correlate(order, tile, first, second, lag, LAGS)


def solution(mesh):
    return jax.shard_map(
        local,
        mesh=mesh,
        in_specs=(
            P(("groups", "blk"), None),
            P(("groups", "blk"), None),
            P(("groups", "blk"), None),
            P(("groups", "blk"), None),
            P(),
        ),
        out_specs=P(None, ("groups", "blk"), None, None),
        check_vma=False,
    )
```

```python
import functools
import math

import jax
import jax.numpy as jnp
import numpy as np
from jax import lax
from jax.experimental import pallas as pl
from jax.experimental.pallas import tpu as pltpu
from jax.sharding import PartitionSpec as P

CH = 128
F = 256
LAGS = 128
W = 2
SLOT_BITS = 8
VALID_BITS = 12
LOW_BITS = 4


def forward_table(nfft, bins):
    sample = np.arange(nfft, dtype=np.int64)[:, None]
    freq = np.arange(1, bins + 1, dtype=np.int64)[None, :]
    angle = (sample * freq % nfft).astype(np.float64) * (2.0 * math.pi / nfft)
    return np.concatenate([np.cos(angle), -np.sin(angle)], axis=1).astype(np.float32).astype(jnp.bfloat16)


def turn_table(nfft, bins, lags, scale):
    freq = np.arange(1, bins + 1, dtype=np.int64)[None, :]
    shift = np.arange(lags // 2 + 16, dtype=np.int64)[:, None]
    angle = (freq * shift % nfft).astype(np.float64) * (2.0 * math.pi / nfft)
    table = np.concatenate([np.cos(angle), np.sin(angle)], axis=1)
    table[: lags // 2] *= scale
    return table.astype(np.float32).astype(jnp.bfloat16)


def iota(shape, dim):
    return lax.broadcasted_iota(jnp.int32, shape, dim)


def pack_kernel(owners, capacity, me_ref, key_ref, records_ref, *out_refs):
    held, nfft = records_ref.shape
    rows = owners * capacity
    width = 512
    key = key_ref[...]
    part = key >> (SLOT_BITS + VALID_BITS)
    if len(out_refs) > 1:
        part = part ^ me_ref[0]
    match = (iota((owners, held), 0) == part).astype(jnp.float32)
    before = (iota((held, held), 0) < iota((held, held), 1)).astype(jnp.float32)
    earlier = jnp.dot(
        match.astype(jnp.bfloat16), before.astype(jnp.bfloat16), preferred_element_type=jnp.float32
    )
    rank = jnp.sum(earlier * match, axis=0, keepdims=True).astype(jnp.int32)
    position = part * capacity + rank
    order = (iota((rows, held), 0) == position).astype(jnp.float32).astype(jnp.bfloat16)
    slot = (key >> VALID_BITS) & ((1 << SLOT_BITS) - 1)
    high = (key & ((1 << VALID_BITS) - 1)) >> LOW_BITS
    low = key & ((1 << LOW_BITS) - 1)
    row = iota((16, held), 0)
    labels = jnp.where(row == 0, slot, jnp.where(row == 1, high, jnp.where(row == 2, low, 0)))
    moved = lax.dot_general(
        labels.astype(jnp.float32).astype(jnp.bfloat16),
        order,
        (((1,), (1,)), ((), ())),
        preferred_element_type=jnp.float32,
    ).astype(jnp.bfloat16)

    def put(d, at, value):
        if len(out_refs) > 1:
            out_refs[d][at : at + value.shape[0], :] = value
        else:
            out_refs[0][d, at : at + value.shape[0], :] = value

    for d in range(owners):
        at = d * capacity // 128 * 128
        put(d, nfft // 128 * capacity, moved[:, at : at + 128])
    for begin in range(0, nfft, width):
        ordered = jnp.dot(
            order, records_ref[:, begin : begin + width], preferred_element_type=jnp.float32
        ).astype(jnp.bfloat16)
        for lane in range(0, width, 128):
            at = (begin + lane) // 128 * capacity
            for d in range(owners):
                put(d, at, ordered[d * capacity : (d + 1) * capacity, lane : lane + 128])


def pack(me, key, records, owners, capacity, split):
    held, nfft = records.shape
    vmem = pl.BlockSpec(memory_space=pltpu.VMEM)
    shape = (nfft // 128 * capacity + 16, 128)
    if split:
        outs = [jax.ShapeDtypeStruct(shape, jnp.bfloat16)] * owners
    else:
        outs = [jax.ShapeDtypeStruct((owners,) + shape, jnp.bfloat16)]
    return pl.pallas_call(
        functools.partial(pack_kernel, owners, capacity),
        in_specs=[pl.BlockSpec(memory_space=pltpu.SMEM), vmem, vmem],
        out_specs=[vmem] * len(outs),
        out_shape=outs,
        compiler_params=pltpu.CompilerParams(vmem_limit_bytes=48 * 1024 * 1024),
        name="pack",
    )(me, key, records)


def whiten_kernel(owners, capacity, places, me_ref, *refs):
    *arrived_refs, table_hbm, out_ref, table_ref, trace_ref, spectrum_ref, sem = refs
    split = len(arrived_refs) > 1
    nfft = trace_ref.shape[1]
    rows = owners * capacity
    slots = CH * W
    bins = table_ref.shape[1] // 2
    shift = capacity.bit_length() - 1
    head = nfft // 128 * capacity
    width = 256
    load = pltpu.make_async_copy(table_hbm, table_ref, sem)
    load.start()

    def take(at, count):
        if split:
            return jnp.concatenate([ref[at : at + count, :] for ref in arrived_refs], axis=0)
        return arrived_refs[0][:, at : at + count, :].reshape(owners * count, 128)

    labels = take(head, 16).astype(jnp.float32).reshape(owners, 16, 128)
    which = iota((owners, 16, 128), 1)
    parts = jnp.concatenate(
        [jnp.sum(jnp.where(which == k, labels, 0.0), axis=1) for k in range(3)], axis=0
    )
    if split:
        part = iota((1, rows), 1) >> shift
        place = functools.reduce(
            lambda total, p: total + jnp.where(part == p, places[p], 0),
            range(owners),
            jnp.zeros((1, rows), jnp.int32),
        )
    else:
        place = me_ref[0]
    base = (place * capacity) & 127
    pick = iota((128, rows), 0) == base + (iota((128, rows), 1) & (capacity - 1))
    picked = jnp.dot(
        parts.astype(jnp.bfloat16),
        pick.astype(jnp.float32).astype(jnp.bfloat16),
        preferred_element_type=jnp.float32,
    )
    source = iota((owners, rows), 0) == iota((owners, rows), 1) >> shift
    rowed = [
        jnp.sum(
            jnp.where(source, picked[k * owners : (k + 1) * owners], 0.0), axis=0, keepdims=True
        )
        for k in range(3)
    ]
    slot_row = rowed[0].astype(jnp.int32)
    place = (slot_row & (W - 1)) * CH + (slot_row >> (W.bit_length() - 1))
    valid_row = rowed[1] * float(1 << LOW_BITS) + rowed[2]
    scatter = (iota((slots, rows), 0) == place).astype(jnp.float32).astype(jnp.bfloat16)
    valid_col = jnp.transpose(jnp.broadcast_to(valid_row, (128, rows))).astype(jnp.int32)
    power = jnp.zeros((slots, 128), jnp.float32)
    for begin in range(0, nfft, width):
        lanes = range(begin, begin + width, 128)
        inside = jnp.concatenate(
            [
                (iota((rows, 128), 1) + lane < valid_col).astype(jnp.float32).astype(jnp.bfloat16)
                for lane in lanes
            ],
            axis=1,
        )
        arrived = jnp.concatenate([take(lane // 128 * capacity, capacity) for lane in lanes], axis=1)
        summed = jnp.dot(scatter, arrived * inside, preferred_element_type=jnp.float32)
        coverage = jnp.dot(scatter, inside, preferred_element_type=jnp.float32)
        trace = summed / jnp.maximum(coverage, 1.0)
        trace_ref[:, begin : begin + width] = trace
        square = trace * trace
        for lane in range(0, width, 128):
            power = power + square[:, lane : lane + 128]
    meansq = jnp.sum(power, axis=1, keepdims=True) * (1.0 / nfft)
    gain = lax.rsqrt(meansq + 1e-06)
    load.wait()
    width = 512
    for begin in range(0, nfft, width):
        normed = (trace_ref[:, begin : begin + width] * gain).astype(jnp.bfloat16)
        part = jnp.dot(
            normed, table_ref[begin : begin + width, :], preferred_element_type=jnp.float32
        )
        if begin == 0:
            spectrum_ref[...] = part
        else:
            spectrum_ref[...] += part
    real_part = spectrum_ref[:, :bins]
    imag_part = spectrum_ref[:, bins:]
    amplitude = lax.rsqrt(jnp.maximum(real_part * real_part + imag_part * imag_part, nfft / 4.0))
    real_part = (real_part * amplitude).astype(jnp.bfloat16)
    imag_part = (imag_part * amplitude).astype(jnp.bfloat16)
    for w in range(W):
        at = w * 2 * bins
        out_ref[:, at : at + bins] = real_part[w * CH : (w + 1) * CH]
        out_ref[:, at + bins : at + 2 * bins] = imag_part[w * CH : (w + 1) * CH]


def whiten(me, arrived, table, owners, capacity, places):
    nfft, width = table.shape
    vmem = pl.BlockSpec(memory_space=pltpu.VMEM)
    return pl.pallas_call(
        functools.partial(whiten_kernel, owners, capacity, places),
        in_specs=[pl.BlockSpec(memory_space=pltpu.SMEM)]
        + [vmem] * len(arrived)
        + [pl.BlockSpec(memory_space=pltpu.HBM)],
        out_specs=vmem,
        out_shape=jax.ShapeDtypeStruct((CH, W * width), jnp.bfloat16),
        scratch_shapes=[
            pltpu.VMEM(table.shape, jnp.bfloat16),
            pltpu.VMEM((CH * W, nfft), jnp.float32),
            pltpu.VMEM((CH * W, width), jnp.float32),
            pltpu.SemaphoreType.DMA(()),
        ],
        compiler_params=pltpu.CompilerParams(vmem_limit_bytes=50 * 1024 * 1024),
        name="whiten",
    )(me, *arrived, table)


GROUP = 16
BLOCK = 4


def correlate_kernel(
    order_ref, own_ref, first_ref, second_ref, table_ref, out_hbm,
    back_ref, wide_ref, turned_a, turned_b, out_ref, sems,
):
    bins = table_ref.shape[1] // 2
    half = out_ref.shape[4] // 2
    blocks = GROUP // BLOCK
    turned = (turned_a, turned_b)

    def turn(start, block):
        cos = table_ref[:half, :bins]
        sin = table_ref[:half, bins:]
        for k in range(BLOCK):
            row = jnp.minimum(start + block * BLOCK + k, CH - 1)
            u = wide_ref[pl.ds(row, 1), :]
            rows = slice(k * half, (k + 1) * half)
            for w in range(W):
                at = w * 2 * bins
                ur = jnp.broadcast_to(u[:, at : at + bins], (half, bins)).astype(jnp.bfloat16)
                ui = jnp.broadcast_to(u[:, at + bins : at + 2 * bins], (half, bins)).astype(
                    jnp.bfloat16
                )
                turned[block % 2][rows, at : at + bins] = ur * cos - ui * sin
                turned[block % 2][rows, at + bins : at + 2 * bins] = ur * sin + ui * cos

    wide_ref[...] = own_ref[...].astype(jnp.float32)
    corner = table_ref[half : half + 16, :].astype(jnp.float32)
    cos, sin = corner[:1, :bins], corner[:1, bins:]
    for place, ref in ((order_ref[0], first_ref), (1 - order_ref[0], second_ref)):
        early = pl.ds(pl.multiple_of(place * 2 * CH, 2 * CH), CH)
        late = pl.ds(pl.multiple_of(place * 2 * CH + CH, CH), CH)
        back_ref[late, :] = ref[...]
        for w in range(W):
            at = w * 2 * bins
            vr = ref[:, at : at + bins].astype(jnp.float32)
            vi = ref[:, at + bins : at + 2 * bins].astype(jnp.float32)
            back_ref[early, at : at + bins] = (vr * cos - vi * sin).astype(jnp.bfloat16)
            back_ref[early, at + bins : at + 2 * bins] = (vr * sin + vi * cos).astype(jnp.bfloat16)
    turn(0, 0)

    def write(step, slot):
        start = pl.multiple_of(step * GROUP, GROUP)
        return pltpu.make_async_copy(
            out_ref.at[slot], out_hbm.at[:, pl.ds(start, GROUP)], sems.at[slot]
        )

    @pl.loop(0, CH // GROUP)
    def _(step):
        slot = step % 2

        @pl.when(step >= 2)
        def _():
            write(step - 2, slot).wait()

        for block in range(blocks):
            turn(step * GROUP, block + 1)
            lagged = lax.dot_general(
                back_ref[...],
                turned[block % 2][...],
                (((1,), (1,)), ((), ())),
                preferred_element_type=jnp.float32,
            ).astype(jnp.bfloat16)
            for k in range(BLOCK):
                lanes = slice(k * half, (k + 1) * half)
                for r in range(2):
                    top = r * 2 * CH
                    out_ref[slot, r, block * BLOCK + k] = jnp.concatenate(
                        [lagged[top : top + CH, lanes], lagged[top + CH : top + 2 * CH, lanes]],
                        axis=1,
                    )
        write(step, slot).start()

    for step in range(CH // GROUP - 2, CH // GROUP):
        write(step, step % 2).wait()


def correlate(order, own, first, second, table, lags):
    depth = own.shape[1]
    half = lags // 2
    vmem = pl.BlockSpec(memory_space=pltpu.VMEM)
    return pl.pallas_call(
        correlate_kernel,
        in_specs=[pl.BlockSpec(memory_space=pltpu.SMEM)] + [vmem] * 4,
        out_specs=pl.BlockSpec(memory_space=pltpu.HBM),
        out_shape=jax.ShapeDtypeStruct((2, CH, CH, lags), jnp.bfloat16),
        scratch_shapes=[
            pltpu.VMEM((4 * CH, depth), jnp.bfloat16),
            pltpu.VMEM((CH, depth), jnp.float32),
            pltpu.VMEM((BLOCK * half, depth), jnp.bfloat16),
            pltpu.VMEM((BLOCK * half, depth), jnp.bfloat16),
            pltpu.VMEM((2, 2, GROUP, CH, lags), jnp.bfloat16),
            pltpu.SemaphoreType.DMA((2,)),
        ],
        compiler_params=pltpu.CompilerParams(vmem_limit_bytes=32 * 1024 * 1024),
        name="correlate",
    )(order, own, first, second, table)


def bring_kernel(source_ref, target_ref):
    target_ref[...] = source_ref[...]


def bring(table):
    vmem = pl.BlockSpec(memory_space=pltpu.VMEM)
    return pl.pallas_call(
        bring_kernel,
        in_specs=[vmem],
        out_specs=vmem,
        out_shape=jax.ShapeDtypeStruct(table.shape, table.dtype),
        name="bring",
    )(table)


def swap(tile, mask):
    count = lax.axis_size("blk")
    return lax.ppermute(tile, "blk", [(low, low ^ mask) for low in range(count)])


def exchange(tile, mask):
    count = lax.axis_size("blk")
    full = count - 1
    if count <= 16:

        def branch(m, moving):
            first = swap(moving, full)
            return first, swap(first, m ^ full) if 2 * m >= count else swap(moving, m)

        branches = [functools.partial(branch, m) for m in range(1, full)]
        return lax.switch(mask - 1, branches, tile)
    moving = tile
    for bit in range(count.bit_length() - 1):
        moving = jnp.where(mask >> bit & 1 == 1, swap(moving, 1 << bit), moving)
    return swap(tile, full), moving


def local(records, dest, slot, valid, masks):
    owners = lax.axis_size("blk")
    held, nfft = records.shape
    capacity = max(16, 2 * held // owners)
    me = lax.axis_index("blk").astype(jnp.int32).reshape(1)
    key = ((dest << SLOT_BITS) + slot << VALID_BITS) + valid
    split = owners <= 16
    outgoing = pack(me, key.reshape(1, held), records, owners, capacity, split)
    if split:
        half = owners // 2
        places = [half]
        for distance in range(1, half):
            places += [distance, half + distance]
        arrived = [swap(outgoing[distance], distance) for distance in places] + [outgoing[0]]
        places.append(0)
    else:
        places = None
        arrived = [lax.all_to_all(outgoing[0], "blk", split_axis=0, concat_axis=0, tiled=True)]
    lag = bring(jnp.asarray(turn_table(nfft, F, LAGS, 1.0 / math.sqrt(W * F))))
    tile = whiten(me, arrived, jnp.asarray(forward_table(nfft, F)), owners, capacity, places)
    full = owners - 1
    first, second = exchange(tile, masks[0] + masks[1] - full)
    order = (masks[:1] != full).astype(jnp.int32)
    return correlate(order, tile, first, second, lag, LAGS)


def solution(mesh):
    return jax.shard_map(
        local,
        mesh=mesh,
        in_specs=(
            P(("groups", "blk"), None),
            P(("groups", "blk"), None),
            P(("groups", "blk"), None),
            P(("groups", "blk"), None),
            P(),
        ),
        out_specs=P(None, ("groups", "blk"), None, None),
        check_vma=False,
    )
```

```python
import functools
import math

import jax
import jax.numpy as jnp
import numpy as np
from jax import lax
from jax.experimental import pallas as pl
from jax.experimental.pallas import tpu as pltpu
from jax.sharding import PartitionSpec as P

CH = 128
F = 256
LAGS = 128
W = 2
SLOT_BITS = 8
VALID_BITS = 12
LOW_BITS = 4


def forward_table(nfft, bins):
    sample = np.arange(nfft, dtype=np.int64)[:, None]
    freq = np.arange(1, bins + 1, dtype=np.int64)[None, :]
    angle = (sample * freq % nfft).astype(np.float64) * (2.0 * math.pi / nfft)
    return np.concatenate([np.cos(angle), -np.sin(angle)], axis=1).astype(np.float32).astype(jnp.bfloat16)


def lag_tables(nfft, bins, lags, scale):
    half = lags // 2
    count = lags + 1
    place = np.arange(count)
    middle = ((count - 1 - 2 * place) / 2.0) ** 2 * math.cos(2.0 * math.pi * bins / nfft)
    aside = (place[1:] * (count - place[1:])) / 2.0
    _, basis = np.linalg.eigh(np.diag(middle) + np.diag(aside, 1) + np.diag(aside, -1))
    basis = basis[:, ::-1][:, :half]
    even, odd = basis[:, 0::2], basis[:, 1::2]
    even = even * np.sign(even[half])
    odd = odd * np.sign(odd[half + 1])
    freq = np.arange(1, bins + 1, dtype=np.int64)[None, :]
    angle = (freq * (place[:, None] - half) % nfft) * (2.0 * math.pi / nfft)
    rows = [even.T @ np.cos(angle), odd.T @ -np.sin(angle)]
    rest = np.cos(angle) - np.sin(angle) - even @ rows[0] - odd @ rows[1]
    assert np.abs(rest).max() < 1e-7
    rows = np.concatenate(rows + [-rows[1]])
    basis = np.concatenate([even, odd], axis=1)[:lags].T * scale
    blank = np.zeros_like(basis)
    pairs = np.block([[basis, blank], [blank, basis]])

    def narrow(table):
        return (np.round(table * 2.0**28) / 2.0**28).astype(np.float32).astype(jnp.bfloat16)

    return narrow(rows), narrow(pairs)


def iota(shape, dim):
    return lax.broadcasted_iota(jnp.int32, shape, dim)


def pack_kernel(owners, capacity, me_ref, key_ref, records_ref, *out_refs):
    held, nfft = records_ref.shape
    rows = owners * capacity
    width = 512
    key = key_ref[...]
    part = key >> (SLOT_BITS + VALID_BITS)
    if len(out_refs) > 1:
        part = part ^ me_ref[0]
    match = (iota((owners, held), 0) == part).astype(jnp.float32)
    before = (iota((held, held), 0) < iota((held, held), 1)).astype(jnp.float32)
    earlier = jnp.dot(
        match.astype(jnp.bfloat16), before.astype(jnp.bfloat16), preferred_element_type=jnp.float32
    )
    rank = jnp.sum(earlier * match, axis=0, keepdims=True).astype(jnp.int32)
    position = part * capacity + rank
    order = (iota((rows, held), 0) == position).astype(jnp.float32).astype(jnp.bfloat16)
    slot = (key >> VALID_BITS) & ((1 << SLOT_BITS) - 1)
    high = (key & ((1 << VALID_BITS) - 1)) >> LOW_BITS
    low = key & ((1 << LOW_BITS) - 1)
    row = iota((16, held), 0)
    labels = jnp.where(row == 0, slot, jnp.where(row == 1, high, jnp.where(row == 2, low, 0)))
    moved = lax.dot_general(
        labels.astype(jnp.float32).astype(jnp.bfloat16),
        order,
        (((1,), (1,)), ((), ())),
        preferred_element_type=jnp.float32,
    ).astype(jnp.bfloat16)

    def put(d, at, value):
        if len(out_refs) > 1:
            out_refs[d][at : at + value.shape[0], :] = value
        else:
            out_refs[0][d, at : at + value.shape[0], :] = value

    for d in range(owners):
        at = d * capacity // 128 * 128
        put(d, nfft // 128 * capacity, moved[:, at : at + 128])
    for begin in range(0, nfft, width):
        ordered = jnp.dot(
            order, records_ref[:, begin : begin + width], preferred_element_type=jnp.float32
        ).astype(jnp.bfloat16)
        for lane in range(0, width, 128):
            at = (begin + lane) // 128 * capacity
            for d in range(owners):
                put(d, at, ordered[d * capacity : (d + 1) * capacity, lane : lane + 128])


def pack(me, key, records, owners, capacity, split):
    held, nfft = records.shape
    vmem = pl.BlockSpec(memory_space=pltpu.VMEM)
    shape = (nfft // 128 * capacity + 16, 128)
    if split:
        outs = [jax.ShapeDtypeStruct(shape, jnp.bfloat16)] * owners
    else:
        outs = [jax.ShapeDtypeStruct((owners,) + shape, jnp.bfloat16)]
    return pl.pallas_call(
        functools.partial(pack_kernel, owners, capacity),
        in_specs=[pl.BlockSpec(memory_space=pltpu.SMEM), vmem, vmem],
        out_specs=[vmem] * len(outs),
        out_shape=outs,
        compiler_params=pltpu.CompilerParams(vmem_limit_bytes=48 * 1024 * 1024),
        name="pack",
    )(me, key, records)


def whiten_kernel(owners, capacity, places, me_ref, *refs):
    *arrived_refs, table_hbm, out_ref, table_ref, trace_ref, spectrum_ref, sems = refs
    split = len(arrived_refs) > 1
    nfft = trace_ref.shape[1]
    rows = owners * capacity
    slots = CH * W
    bins = table_ref.shape[1] // 2
    shift = capacity.bit_length() - 1
    head = nfft // 128 * capacity
    width = 256
    depth = 512
    loads = [
        pltpu.make_async_copy(
            table_hbm.at[pl.ds(at, depth)], table_ref.at[pl.ds(at, depth)], sems.at[at // depth]
        )
        for at in range(0, nfft, depth)
    ]
    for copy in loads:
        copy.start()

    def take(at, count):
        if split:
            return jnp.concatenate([ref[at : at + count, :] for ref in arrived_refs], axis=0)
        return arrived_refs[0][:, at : at + count, :].reshape(owners * count, 128)

    labels = take(head, 16).astype(jnp.float32).reshape(owners, 16, 128)
    which = iota((owners, 16, 128), 1)
    parts = jnp.concatenate(
        [jnp.sum(jnp.where(which == k, labels, 0.0), axis=1) for k in range(3)], axis=0
    )
    if split:
        part = iota((1, rows), 1) >> shift
        place = functools.reduce(
            lambda total, p: total + jnp.where(part == p, places[p], 0),
            range(owners),
            jnp.zeros((1, rows), jnp.int32),
        )
    else:
        place = me_ref[0]
    base = (place * capacity) & 127
    pick = iota((128, rows), 0) == base + (iota((128, rows), 1) & (capacity - 1))
    picked = jnp.dot(
        parts.astype(jnp.bfloat16),
        pick.astype(jnp.float32).astype(jnp.bfloat16),
        preferred_element_type=jnp.float32,
    )
    source = iota((owners, rows), 0) == iota((owners, rows), 1) >> shift
    rowed = [
        jnp.sum(
            jnp.where(source, picked[k * owners : (k + 1) * owners], 0.0), axis=0, keepdims=True
        )
        for k in range(3)
    ]
    slot_row = rowed[0].astype(jnp.int32)
    place = (slot_row & (W - 1)) * CH + (slot_row >> (W.bit_length() - 1))
    valid_row = rowed[1] * float(1 << LOW_BITS) + rowed[2]
    scatter = (iota((slots, rows), 0) == place).astype(jnp.float32).astype(jnp.bfloat16)
    valid_col = jnp.transpose(jnp.broadcast_to(valid_row, (128, rows))).astype(jnp.int32)
    power = jnp.zeros((slots, 128), jnp.float32)
    for begin in range(0, nfft, width):
        lanes = range(begin, begin + width, 128)
        inside = jnp.concatenate(
            [
                (iota((rows, 128), 1) + lane < valid_col).astype(jnp.float32).astype(jnp.bfloat16)
                for lane in lanes
            ],
            axis=1,
        )
        arrived = jnp.concatenate([take(lane // 128 * capacity, capacity) for lane in lanes], axis=1)
        summed = jnp.dot(scatter, arrived * inside, preferred_element_type=jnp.float32)
        coverage = jnp.dot(scatter, inside, preferred_element_type=jnp.float32)
        trace = summed / jnp.maximum(coverage, 1.0)
        trace_ref[:, begin : begin + width] = trace
        square = trace * trace
        for lane in range(0, width, 128):
            power = power + square[:, lane : lane + 128]
    meansq = jnp.sum(power, axis=1, keepdims=True) * (1.0 / nfft)
    gain = lax.rsqrt(meansq + 1e-06)
    for begin in range(0, nfft, depth):
        loads[begin // depth].wait()
        normed = (trace_ref[:, begin : begin + depth] * gain).astype(jnp.bfloat16)
        part = jnp.dot(
            normed, table_ref[begin : begin + depth, :], preferred_element_type=jnp.float32
        )
        if begin == 0:
            spectrum_ref[...] = part
        else:
            spectrum_ref[...] += part
    real_part = spectrum_ref[:, :bins]
    imag_part = spectrum_ref[:, bins:]
    amplitude = lax.rsqrt(jnp.maximum(real_part * real_part + imag_part * imag_part, nfft / 4.0))
    real_part = (real_part * amplitude).astype(jnp.bfloat16)
    imag_part = (imag_part * amplitude).astype(jnp.bfloat16)
    for w in range(W):
        at = w * 2 * bins
        out_ref[:, at : at + bins] = real_part[w * CH : (w + 1) * CH]
        out_ref[:, at + bins : at + 2 * bins] = imag_part[w * CH : (w + 1) * CH]


def whiten(me, arrived, table, owners, capacity, places):
    nfft, width = table.shape
    vmem = pl.BlockSpec(memory_space=pltpu.VMEM)
    return pl.pallas_call(
        functools.partial(whiten_kernel, owners, capacity, places),
        in_specs=[pl.BlockSpec(memory_space=pltpu.SMEM)]
        + [vmem] * len(arrived)
        + [pl.BlockSpec(memory_space=pltpu.HBM)],
        out_specs=vmem,
        out_shape=jax.ShapeDtypeStruct((CH, W * width), jnp.bfloat16),
        scratch_shapes=[
            pltpu.VMEM(table.shape, jnp.bfloat16),
            pltpu.VMEM((CH * W, nfft), jnp.float32),
            pltpu.VMEM((CH * W, width), jnp.float32),
            pltpu.SemaphoreType.DMA((nfft // 512,)),
        ],
        compiler_params=pltpu.CompilerParams(vmem_limit_bytes=50 * 1024 * 1024),
        name="whiten",
    )(me, *arrived, table)


GROUP = 16
BLOCK = 4


def correlate_kernel(
    order_ref, own_ref, first_ref, second_ref, rows_ref, pairs_ref, out_hbm,
    both_ref, wide_ref, turned_a, turned_b, out_ref, sems,
):
    bins = rows_ref.shape[1]
    terms = rows_ref.shape[0] // 3
    lags = out_ref.shape[4]
    blocks = GROUP // BLOCK
    turned = (turned_a, turned_b)

    def turn(start, block):
        even = rows_ref[:terms, :]
        odd = rows_ref[terms : 2 * terms, :]
        minus = rows_ref[2 * terms :, :]
        for k in range(BLOCK):
            row = jnp.minimum(start + block * BLOCK + k, CH - 1)
            u = wide_ref[pl.ds(row, 1), :]
            top = slice(2 * k * terms, (2 * k + 1) * terms)
            low = slice((2 * k + 1) * terms, (2 * k + 2) * terms)
            for w in range(W):
                at = w * 2 * bins
                real, imag = slice(at, at + bins), slice(at + bins, at + 2 * bins)
                ur = jnp.broadcast_to(u[:, real], (terms, bins)).astype(jnp.bfloat16)
                ui = jnp.broadcast_to(u[:, imag], (terms, bins)).astype(jnp.bfloat16)
                turned[block % 2][top, real] = ur * even
                turned[block % 2][top, imag] = ui * even
                turned[block % 2][low, real] = ui * odd
                turned[block % 2][low, imag] = ur * minus

    wide_ref[...] = own_ref[...].astype(jnp.float32)
    at = pl.multiple_of(order_ref[0] * CH, CH)
    both_ref[pl.ds(at, CH), :] = first_ref[...]
    both_ref[pl.ds(CH - at, CH), :] = second_ref[...]
    turn(0, 0)

    def write(step, slot):
        start = pl.multiple_of(step * GROUP, GROUP)
        return pltpu.make_async_copy(
            out_ref.at[slot], out_hbm.at[:, pl.ds(start, GROUP)], sems.at[slot]
        )

    @pl.loop(0, CH // GROUP)
    def _(step):
        slot = step % 2

        @pl.when(step >= 2)
        def _():
            write(step - 2, slot).wait()

        for block in range(blocks):
            turn(step * GROUP, block + 1)
            found = lax.dot_general(
                both_ref[...],
                turned[block % 2][...],
                (((1,), (1,)), ((), ())),
                preferred_element_type=jnp.float32,
            ).astype(jnp.bfloat16)
            for k in range(0, BLOCK, 2):
                lagged = jnp.dot(
                    found[:, 2 * k * terms : 2 * (k + 2) * terms],
                    pairs_ref[...],
                    preferred_element_type=jnp.float32,
                ).astype(jnp.bfloat16)
                for h in range(2):
                    for r in range(2):
                        out_ref[slot, r, block * BLOCK + k + h] = lagged[
                            r * CH : (r + 1) * CH, h * lags : (h + 1) * lags
                        ]
        write(step, slot).start()

    for step in range(CH // GROUP - 2, CH // GROUP):
        write(step, step % 2).wait()


def correlate(order, own, first, second, nfft, lags):
    depth = own.shape[1]
    bins = depth // (2 * W)
    rows, pairs = lag_tables(nfft, bins, lags, 1.0 / math.sqrt(W * bins))
    terms = rows.shape[0] // 3
    vmem = pl.BlockSpec(memory_space=pltpu.VMEM)
    return pl.pallas_call(
        correlate_kernel,
        in_specs=[pl.BlockSpec(memory_space=pltpu.SMEM)] + [vmem] * 5,
        out_specs=pl.BlockSpec(memory_space=pltpu.HBM),
        out_shape=jax.ShapeDtypeStruct((2, CH, CH, lags), jnp.bfloat16),
        scratch_shapes=[
            pltpu.VMEM((2 * CH, depth), jnp.bfloat16),
            pltpu.VMEM((CH, depth), jnp.float32),
            pltpu.VMEM((BLOCK * 2 * terms, depth), jnp.bfloat16),
            pltpu.VMEM((BLOCK * 2 * terms, depth), jnp.bfloat16),
            pltpu.VMEM((2, 2, GROUP, CH, lags), jnp.bfloat16),
            pltpu.SemaphoreType.DMA((2,)),
        ],
        compiler_params=pltpu.CompilerParams(vmem_limit_bytes=60 * 1024 * 1024),
        name="correlate",
    )(order, own, first, second, jnp.asarray(rows), jnp.asarray(pairs))


def swap(tile, mask):
    count = lax.axis_size("blk")
    return lax.ppermute(tile, "blk", [(low, low ^ mask) for low in range(count)])


def exchange(tile, mask):
    count = lax.axis_size("blk")
    full = count - 1
    if count <= 16:

        def branch(m, moving):
            first = swap(moving, full)
            return first, swap(first, m ^ full) if 2 * m >= count else swap(moving, m)

        branches = [functools.partial(branch, m) for m in range(1, full)]
        return lax.switch(mask - 1, branches, tile)
    moving = tile
    for bit in range(count.bit_length() - 1):
        moving = jnp.where(mask >> bit & 1 == 1, swap(moving, 1 << bit), moving)
    return swap(tile, full), moving


def local(records, dest, slot, valid, masks):
    owners = lax.axis_size("blk")
    held, nfft = records.shape
    capacity = max(16, 2 * held // owners)
    me = lax.axis_index("blk").astype(jnp.int32).reshape(1)
    key = ((dest << SLOT_BITS) + slot << VALID_BITS) + valid
    split = owners <= 16
    outgoing = pack(me, key.reshape(1, held), records, owners, capacity, split)
    if split:
        half = owners // 2
        places = [half]
        for distance in range(1, half):
            places += [distance, half + distance]
        arrived = [swap(outgoing[distance], distance) for distance in places] + [outgoing[0]]
        places.append(0)
    else:
        places = None
        arrived = [lax.all_to_all(outgoing[0], "blk", split_axis=0, concat_axis=0, tiled=True)]
    tile = whiten(me, arrived, jnp.asarray(forward_table(nfft, F)), owners, capacity, places)
    full = owners - 1
    first, second = exchange(tile, masks[0] + masks[1] - full)
    order = (masks[:1] != full).astype(jnp.int32)
    return correlate(order, tile, first, second, nfft, LAGS)


def solution(mesh):
    return jax.shard_map(
        local,
        mesh=mesh,
        in_specs=(
            P(("groups", "blk"), None),
            P(("groups", "blk"), None),
            P(("groups", "blk"), None),
            P(("groups", "blk"), None),
            P(),
        ),
        out_specs=P(None, ("groups", "blk"), None, None),
        check_vma=False,
    )
```

```python
import functools
import math

import jax
import jax.numpy as jnp
import numpy as np
from jax import lax
from jax.experimental import pallas as pl
from jax.experimental.pallas import tpu as pltpu
from jax.sharding import PartitionSpec as P

CH = 128
F = 256
LAGS = 128
W = 2
SLOT_BITS = 8
VALID_BITS = 12
LOW_BITS = 4


def forward_table(nfft, bins):
    sample = np.arange(nfft, dtype=np.int64)[:, None]
    freq = np.arange(1, bins + 1, dtype=np.int64)[None, :]
    angle = (sample * freq % nfft).astype(np.float64) * (2.0 * math.pi / nfft)
    return np.concatenate([np.cos(angle), -np.sin(angle)], axis=1).astype(np.float32).astype(jnp.bfloat16)


def lag_tables(nfft, bins, lags, scale):
    half = lags // 2
    count = lags + 1
    place = np.arange(count)
    middle = ((count - 1 - 2 * place) / 2.0) ** 2 * math.cos(2.0 * math.pi * bins / nfft)
    aside = (place[1:] * (count - place[1:])) / 2.0
    _, basis = np.linalg.eigh(np.diag(middle) + np.diag(aside, 1) + np.diag(aside, -1))
    basis = basis[:, ::-1][:, :half]
    even, odd = basis[:, 0::2], basis[:, 1::2]
    even = even * np.sign(even[half])
    odd = odd * np.sign(odd[half + 1])
    freq = np.arange(1, bins + 1, dtype=np.int64)[None, :]
    angle = (freq * (place[:, None] - half) % nfft) * (2.0 * math.pi / nfft)
    rows = [even.T @ np.cos(angle), odd.T @ -np.sin(angle)]
    rest = np.cos(angle) - np.sin(angle) - even @ rows[0] - odd @ rows[1]
    assert np.abs(rest).max() < 1e-7
    rows = np.concatenate(rows + [-rows[1]])
    basis = np.concatenate([even, odd], axis=1)[:lags].T * scale
    blank = np.zeros_like(basis)
    spread = np.concatenate(
        [np.concatenate([basis if k == n else blank for n in range(4)], axis=1) for k in range(4)]
    )

    def narrow(table):
        return (np.round(table * 2.0**28) / 2.0**28).astype(np.float32).astype(jnp.bfloat16)

    return narrow(rows), narrow(spread)


def iota(shape, dim):
    return lax.broadcasted_iota(jnp.int32, shape, dim)


def pack_kernel(owners, capacity, me_ref, key_ref, records_ref, *out_refs):
    held, nfft = records_ref.shape
    rows = owners * capacity
    width = 512
    key = key_ref[...]
    part = key >> (SLOT_BITS + VALID_BITS)
    if len(out_refs) > 1:
        part = part ^ me_ref[0]
    match = (iota((owners, held), 0) == part).astype(jnp.float32)
    before = (iota((held, held), 0) < iota((held, held), 1)).astype(jnp.float32)
    earlier = jnp.dot(
        match.astype(jnp.bfloat16), before.astype(jnp.bfloat16), preferred_element_type=jnp.float32
    )
    rank = jnp.sum(earlier * match, axis=0, keepdims=True).astype(jnp.int32)
    position = part * capacity + rank
    order = (iota((rows, held), 0) == position).astype(jnp.float32).astype(jnp.bfloat16)
    slot = (key >> VALID_BITS) & ((1 << SLOT_BITS) - 1)
    high = (key & ((1 << VALID_BITS) - 1)) >> LOW_BITS
    low = key & ((1 << LOW_BITS) - 1)
    row = iota((16, held), 0)
    labels = jnp.where(row == 0, slot, jnp.where(row == 1, high, jnp.where(row == 2, low, 0)))
    moved = lax.dot_general(
        labels.astype(jnp.float32).astype(jnp.bfloat16),
        order,
        (((1,), (1,)), ((), ())),
        preferred_element_type=jnp.float32,
    ).astype(jnp.bfloat16)

    def put(d, at, value):
        if len(out_refs) > 1:
            out_refs[d][at : at + value.shape[0], :] = value
        else:
            out_refs[0][d, at : at + value.shape[0], :] = value

    for d in range(owners):
        at = d * capacity // 128 * 128
        put(d, nfft // 128 * capacity, moved[:, at : at + 128])
    for begin in range(0, nfft, width):
        ordered = jnp.dot(
            order, records_ref[:, begin : begin + width], preferred_element_type=jnp.float32
        ).astype(jnp.bfloat16)
        for lane in range(0, width, 128):
            at = (begin + lane) // 128 * capacity
            for d in range(owners):
                put(d, at, ordered[d * capacity : (d + 1) * capacity, lane : lane + 128])


def pack(me, key, records, owners, capacity, split):
    held, nfft = records.shape
    vmem = pl.BlockSpec(memory_space=pltpu.VMEM)
    shape = (nfft // 128 * capacity + 16, 128)
    if split:
        outs = [jax.ShapeDtypeStruct(shape, jnp.bfloat16)] * owners
    else:
        outs = [jax.ShapeDtypeStruct((owners,) + shape, jnp.bfloat16)]
    return pl.pallas_call(
        functools.partial(pack_kernel, owners, capacity),
        in_specs=[pl.BlockSpec(memory_space=pltpu.SMEM), vmem, vmem],
        out_specs=[vmem] * len(outs),
        out_shape=outs,
        compiler_params=pltpu.CompilerParams(vmem_limit_bytes=48 * 1024 * 1024),
        name="pack",
    )(me, key, records)


def whiten_kernel(owners, capacity, places, me_ref, *refs):
    *arrived_refs, table_hbm, out_ref, table_ref, trace_ref, spectrum_ref, sems = refs
    split = len(arrived_refs) > 1
    nfft = trace_ref.shape[1]
    rows = owners * capacity
    slots = CH * W
    bins = table_ref.shape[1] // 2
    shift = capacity.bit_length() - 1
    head = nfft // 128 * capacity
    width = 256
    depth = 512
    loads = [
        pltpu.make_async_copy(
            table_hbm.at[pl.ds(at, depth)], table_ref.at[pl.ds(at, depth)], sems.at[at // depth]
        )
        for at in range(0, nfft, depth)
    ]
    for copy in loads:
        copy.start()

    def take(at, count):
        if split:
            return jnp.concatenate([ref[at : at + count, :] for ref in arrived_refs], axis=0)
        return arrived_refs[0][:, at : at + count, :].reshape(owners * count, 128)

    labels = take(head, 16).astype(jnp.float32).reshape(owners, 16, 128)
    which = iota((owners, 16, 128), 1)
    parts = jnp.concatenate(
        [jnp.sum(jnp.where(which == k, labels, 0.0), axis=1) for k in range(3)], axis=0
    )
    if split:
        part = iota((1, rows), 1) >> shift
        place = functools.reduce(
            lambda total, p: total + jnp.where(part == p, places[p], 0),
            range(owners),
            jnp.zeros((1, rows), jnp.int32),
        )
    else:
        place = me_ref[0]
    base = (place * capacity) & 127
    pick = iota((128, rows), 0) == base + (iota((128, rows), 1) & (capacity - 1))
    picked = jnp.dot(
        parts.astype(jnp.bfloat16),
        pick.astype(jnp.float32).astype(jnp.bfloat16),
        preferred_element_type=jnp.float32,
    )
    source = iota((owners, rows), 0) == iota((owners, rows), 1) >> shift
    rowed = [
        jnp.sum(
            jnp.where(source, picked[k * owners : (k + 1) * owners], 0.0), axis=0, keepdims=True
        )
        for k in range(3)
    ]
    slot_row = rowed[0].astype(jnp.int32)
    place = (slot_row & (W - 1)) * CH + (slot_row >> (W.bit_length() - 1))
    valid_row = rowed[1] * float(1 << LOW_BITS) + rowed[2]
    scatter = (iota((slots, rows), 0) == place).astype(jnp.float32).astype(jnp.bfloat16)
    valid_col = jnp.transpose(jnp.broadcast_to(valid_row, (128, rows))).astype(jnp.int32)
    power = jnp.zeros((slots, 128), jnp.float32)
    for begin in range(0, nfft, width):
        lanes = range(begin, begin + width, 128)
        inside = jnp.concatenate(
            [
                (iota((rows, 128), 1) + lane < valid_col).astype(jnp.float32).astype(jnp.bfloat16)
                for lane in lanes
            ],
            axis=1,
        )
        arrived = jnp.concatenate([take(lane // 128 * capacity, capacity) for lane in lanes], axis=1)
        summed = jnp.dot(scatter, arrived * inside, preferred_element_type=jnp.float32)
        coverage = jnp.dot(scatter, inside, preferred_element_type=jnp.float32)
        trace = summed / jnp.maximum(coverage, 1.0)
        trace_ref[:, begin : begin + width] = trace
        square = trace * trace
        for lane in range(0, width, 128):
            power = power + square[:, lane : lane + 128]
    meansq = jnp.sum(power, axis=1, keepdims=True) * (1.0 / nfft)
    gain = lax.rsqrt(meansq + 1e-06)
    for begin in range(0, nfft, depth):
        loads[begin // depth].wait()
        normed = (trace_ref[:, begin : begin + depth] * gain).astype(jnp.bfloat16)
        part = jnp.dot(
            normed, table_ref[begin : begin + depth, :], preferred_element_type=jnp.float32
        )
        if begin == 0:
            spectrum_ref[...] = part
        else:
            spectrum_ref[...] += part
    real_part = spectrum_ref[:, :bins]
    imag_part = spectrum_ref[:, bins:]
    amplitude = lax.rsqrt(jnp.maximum(real_part * real_part + imag_part * imag_part, nfft / 4.0))
    real_part = (real_part * amplitude).astype(jnp.bfloat16)
    imag_part = (imag_part * amplitude).astype(jnp.bfloat16)
    for w in range(W):
        at = w * 2 * bins
        out_ref[:, at : at + bins] = real_part[w * CH : (w + 1) * CH]
        out_ref[:, at + bins : at + 2 * bins] = imag_part[w * CH : (w + 1) * CH]


def whiten(me, arrived, table, owners, capacity, places):
    nfft, width = table.shape
    vmem = pl.BlockSpec(memory_space=pltpu.VMEM)
    return pl.pallas_call(
        functools.partial(whiten_kernel, owners, capacity, places),
        in_specs=[pl.BlockSpec(memory_space=pltpu.SMEM)]
        + [vmem] * len(arrived)
        + [pl.BlockSpec(memory_space=pltpu.HBM)],
        out_specs=vmem,
        out_shape=jax.ShapeDtypeStruct((CH, W * width), jnp.bfloat16),
        scratch_shapes=[
            pltpu.VMEM(table.shape, jnp.bfloat16),
            pltpu.VMEM((CH * W, nfft), jnp.float32),
            pltpu.VMEM((CH * W, width), jnp.float32),
            pltpu.SemaphoreType.DMA((nfft // 512,)),
        ],
        compiler_params=pltpu.CompilerParams(vmem_limit_bytes=50 * 1024 * 1024),
        name="whiten",
    )(me, *arrived, table)


BLOCK = 8


def correlate_kernel(
    order_ref, own_ref, first_ref, second_ref, rows_ref, spread_ref, out_hbm,
    both_ref, wide_ref, turned_a, turned_b, found_a, found_b, out_a, out_b, sems,
):
    bins = rows_ref.shape[1]
    terms = rows_ref.shape[0] // 3
    lags = out_a.shape[3]
    blocks = CH // BLOCK
    turned, found, out = (turned_a, turned_b), (found_a, found_b), (out_a, out_b)

    def turn(block, slot):
        even = rows_ref[:terms, :]
        odd = rows_ref[terms : 2 * terms, :]
        minus = rows_ref[2 * terms :, :]
        for k in range(BLOCK):
            row = jnp.minimum(block * BLOCK + k, CH - 1)
            u = wide_ref[pl.ds(row, 1), :]
            top = slice(2 * k * terms, (2 * k + 1) * terms)
            low = slice((2 * k + 1) * terms, (2 * k + 2) * terms)
            for w in range(W):
                at = w * 2 * bins
                real, imag = slice(at, at + bins), slice(at + bins, at + 2 * bins)
                ur = jnp.broadcast_to(u[:, real], (terms, bins)).astype(jnp.bfloat16)
                ui = jnp.broadcast_to(u[:, imag], (terms, bins)).astype(jnp.bfloat16)
                turned[slot][top, real] = ur * even
                turned[slot][top, imag] = ui * even
                turned[slot][low, real] = ui * odd
                turned[slot][low, imag] = ur * minus

    def find(slot):
        found[slot][...] = lax.dot_general(
            both_ref[...],
            turned[slot][...],
            (((1,), (1,)), ((), ())),
            preferred_element_type=jnp.float32,
        ).astype(jnp.bfloat16)

    def spread(slot):
        for k in range(0, BLOCK, 4):
            lagged = jnp.dot(
                found[slot][:, 2 * k * terms : 2 * (k + 4) * terms],
                spread_ref[...],
                preferred_element_type=jnp.float32,
            ).astype(jnp.bfloat16)
            for n in range(4):
                for r in range(2):
                    out[slot][r, k + n] = lagged[r * CH : (r + 1) * CH, n * lags : (n + 1) * lags]

    def write(block, slot):
        start = pl.multiple_of(block * BLOCK, BLOCK)
        return pltpu.make_async_copy(
            out[slot], out_hbm.at[:, pl.ds(start, BLOCK)], sems.at[slot]
        )

    wide_ref[...] = own_ref[...].astype(jnp.float32)
    at = pl.multiple_of(order_ref[0] * CH, CH)
    both_ref[pl.ds(at, CH), :] = first_ref[...]
    both_ref[pl.ds(CH - at, CH), :] = second_ref[...]
    turn(0, 0)
    turn(1, 1)
    find(0)

    @pl.loop(0, blocks // 2)
    def _(n):
        @pl.when(n >= 1)
        def _():
            write(2 * n - 2, 0).wait()
            write(2 * n - 1, 1).wait()

        turn(2 * n + 2, 0)
        find(1)
        spread(0)
        turn(2 * n + 3, 1)
        find(0)
        spread(1)
        write(2 * n, 0).start()
        write(2 * n + 1, 1).start()

    write(blocks - 2, 0).wait()
    write(blocks - 1, 1).wait()


def correlate(order, own, first, second, nfft, lags):
    depth = own.shape[1]
    bins = depth // (2 * W)
    rows, spread = lag_tables(nfft, bins, lags, 1.0 / math.sqrt(W * bins))
    terms = rows.shape[0] // 3
    vmem = pl.BlockSpec(memory_space=pltpu.VMEM)
    return pl.pallas_call(
        correlate_kernel,
        in_specs=[pl.BlockSpec(memory_space=pltpu.SMEM)] + [vmem] * 5,
        out_specs=pl.BlockSpec(memory_space=pltpu.HBM),
        out_shape=jax.ShapeDtypeStruct((2, CH, CH, lags), jnp.bfloat16),
        scratch_shapes=[
            pltpu.VMEM((2 * CH, depth), jnp.bfloat16),
            pltpu.VMEM((CH, depth), jnp.float32),
            pltpu.VMEM((BLOCK * 2 * terms, depth), jnp.bfloat16),
            pltpu.VMEM((BLOCK * 2 * terms, depth), jnp.bfloat16),
            pltpu.VMEM((2 * CH, BLOCK * 2 * terms), jnp.bfloat16),
            pltpu.VMEM((2 * CH, BLOCK * 2 * terms), jnp.bfloat16),
            pltpu.VMEM((2, BLOCK, CH, lags), jnp.bfloat16),
            pltpu.VMEM((2, BLOCK, CH, lags), jnp.bfloat16),
            pltpu.SemaphoreType.DMA((2,)),
        ],
        compiler_params=pltpu.CompilerParams(vmem_limit_bytes=60 * 1024 * 1024),
        name="correlate",
    )(order, own, first, second, jnp.asarray(rows), jnp.asarray(spread))


def swap(tile, mask):
    count = lax.axis_size("blk")
    return lax.ppermute(tile, "blk", [(low, low ^ mask) for low in range(count)])


def exchange(tile, mask):
    count = lax.axis_size("blk")
    full = count - 1
    if count <= 16:

        def branch(m, moving):
            first = swap(moving, full)
            return first, swap(first, m ^ full) if 2 * m >= count else swap(moving, m)

        branches = [functools.partial(branch, m) for m in range(1, full)]
        return lax.switch(mask - 1, branches, tile)
    moving = tile
    for bit in range(count.bit_length() - 1):
        moving = jnp.where(mask >> bit & 1 == 1, swap(moving, 1 << bit), moving)
    return swap(tile, full), moving


def local(records, dest, slot, valid, masks):
    owners = lax.axis_size("blk")
    held, nfft = records.shape
    capacity = max(16, 2 * held // owners)
    me = lax.axis_index("blk").astype(jnp.int32).reshape(1)
    key = ((dest << SLOT_BITS) + slot << VALID_BITS) + valid
    split = owners <= 16
    outgoing = pack(me, key.reshape(1, held), records, owners, capacity, split)
    if split:
        half = owners // 2
        places = [half]
        for distance in range(1, half):
            places += [distance, half + distance]
        arrived = [swap(outgoing[distance], distance) for distance in places] + [outgoing[0]]
        places.append(0)
    else:
        places = None
        arrived = [lax.all_to_all(outgoing[0], "blk", split_axis=0, concat_axis=0, tiled=True)]
    tile = whiten(me, arrived, jnp.asarray(forward_table(nfft, F)), owners, capacity, places)
    full = owners - 1
    first, second = exchange(tile, masks[0] + masks[1] - full)
    order = (masks[:1] != full).astype(jnp.int32)
    return correlate(order, tile, first, second, nfft, LAGS)


def solution(mesh):
    return jax.shard_map(
        local,
        mesh=mesh,
        in_specs=(
            P(("groups", "blk"), None),
            P(("groups", "blk"), None),
            P(("groups", "blk"), None),
            P(("groups", "blk"), None),
            P(),
        ),
        out_specs=P(None, ("groups", "blk"), None, None),
        check_vma=False,
    )
```

```python
import functools
import math

import jax
import jax.numpy as jnp
import numpy as np
from jax import lax
from jax.experimental import pallas as pl
from jax.experimental.pallas import tpu as pltpu
from jax.sharding import PartitionSpec as P

CH = 128
F = 256
LAGS = 128
W = 2
SLOT_BITS = 8
VALID_BITS = 12
LOW_BITS = 4


def forward_table(nfft, bins):
    sample = np.arange(nfft, dtype=np.int64)[:, None]
    freq = np.arange(1, bins + 1, dtype=np.int64)[None, :]
    angle = (sample * freq % nfft).astype(np.float64) * (2.0 * math.pi / nfft)
    return np.concatenate([np.cos(angle), -np.sin(angle)], axis=1).astype(np.float32).astype(jnp.bfloat16)


def lag_tables(nfft, bins, lags, scale):
    half = lags // 2
    count = lags + 1
    place = np.arange(count)
    middle = ((count - 1 - 2 * place) / 2.0) ** 2 * math.cos(2.0 * math.pi * bins / nfft)
    aside = (place[1:] * (count - place[1:])) / 2.0
    _, basis = np.linalg.eigh(np.diag(middle) + np.diag(aside, 1) + np.diag(aside, -1))
    basis = basis[:, ::-1][:, :half]
    even, odd = basis[:, 0::2], basis[:, 1::2]
    even = even * np.sign(even[half])
    odd = odd * np.sign(odd[half + 1])
    freq = np.arange(1, bins + 1, dtype=np.int64)[None, :]
    angle = (freq * (place[:, None] - half) % nfft) * (2.0 * math.pi / nfft)
    rows = [even.T @ np.cos(angle), odd.T @ -np.sin(angle)]
    rest = np.cos(angle) - np.sin(angle) - even @ rows[0] - odd @ rows[1]
    assert np.abs(rest).max() < 1e-7
    rows = np.concatenate(rows + [-rows[1]])
    basis = np.concatenate([even, odd], axis=1)[:lags].T * scale
    blank = np.zeros_like(basis)
    spread = np.concatenate(
        [np.concatenate([basis if k == n else blank for n in range(4)], axis=1) for k in range(4)]
    )

    def narrow(table):
        return (np.round(table * 2.0**28) / 2.0**28).astype(np.float32).astype(jnp.bfloat16)

    return narrow(rows), narrow(spread)


def iota(shape, dim):
    return lax.broadcasted_iota(jnp.int32, shape, dim)


def pack_kernel(owners, capacity, me_ref, key_ref, records_ref, *out_refs):
    held, nfft = records_ref.shape
    rows = owners * capacity
    width = 512
    key = key_ref[...]
    part = key >> (SLOT_BITS + VALID_BITS)
    if len(out_refs) > 1:
        part = part ^ me_ref[0]
    match = (iota((owners, held), 0) == part).astype(jnp.float32)
    before = (iota((held, held), 0) < iota((held, held), 1)).astype(jnp.float32)
    earlier = jnp.dot(
        match.astype(jnp.bfloat16), before.astype(jnp.bfloat16), preferred_element_type=jnp.float32
    )
    rank = jnp.sum(earlier * match, axis=0, keepdims=True).astype(jnp.int32)
    position = part * capacity + rank
    order = (iota((rows, held), 0) == position).astype(jnp.float32).astype(jnp.bfloat16)
    slot = (key >> VALID_BITS) & ((1 << SLOT_BITS) - 1)
    high = (key & ((1 << VALID_BITS) - 1)) >> LOW_BITS
    low = key & ((1 << LOW_BITS) - 1)
    row = iota((16, held), 0)
    labels = jnp.where(row == 0, slot, jnp.where(row == 1, high, jnp.where(row == 2, low, 0)))
    moved = lax.dot_general(
        labels.astype(jnp.float32).astype(jnp.bfloat16),
        order,
        (((1,), (1,)), ((), ())),
        preferred_element_type=jnp.float32,
    ).astype(jnp.bfloat16)

    def put(d, at, value):
        if len(out_refs) > 1:
            out_refs[d][at : at + value.shape[0], :] = value
        else:
            out_refs[0][d, at : at + value.shape[0], :] = value

    for d in range(owners):
        at = d * capacity // 128 * 128
        put(d, nfft // 128 * capacity, moved[:, at : at + 128])
    for begin in range(0, nfft, width):
        ordered = jnp.dot(
            order, records_ref[:, begin : begin + width], preferred_element_type=jnp.float32
        ).astype(jnp.bfloat16)
        for lane in range(0, width, 128):
            at = (begin + lane) // 128 * capacity
            for d in range(owners):
                put(d, at, ordered[d * capacity : (d + 1) * capacity, lane : lane + 128])


def pack(me, key, records, owners, capacity, split):
    held, nfft = records.shape
    vmem = pl.BlockSpec(memory_space=pltpu.VMEM)
    shape = (nfft // 128 * capacity + 16, 128)
    if split:
        outs = [jax.ShapeDtypeStruct(shape, jnp.bfloat16)] * owners
    else:
        outs = [jax.ShapeDtypeStruct((owners,) + shape, jnp.bfloat16)]
    return pl.pallas_call(
        functools.partial(pack_kernel, owners, capacity),
        in_specs=[pl.BlockSpec(memory_space=pltpu.SMEM), vmem, vmem],
        out_specs=[vmem] * len(outs),
        out_shape=outs,
        compiler_params=pltpu.CompilerParams(vmem_limit_bytes=48 * 1024 * 1024),
        name="pack",
    )(me, key, records)


def whiten_kernel(owners, capacity, places, me_ref, *refs):
    *arrived_refs, table_hbm, out_ref, table_ref, trace_ref, spectrum_ref, sems = refs
    split = len(arrived_refs) > 1
    nfft = trace_ref.shape[1]
    rows = owners * capacity
    slots = CH * W
    bins = table_ref.shape[1] // 2
    shift = capacity.bit_length() - 1
    head = nfft // 128 * capacity
    width = 256
    depth = 512
    loads = [
        pltpu.make_async_copy(
            table_hbm.at[pl.ds(at, depth)], table_ref.at[pl.ds(at, depth)], sems.at[at // depth]
        )
        for at in range(0, nfft, depth)
    ]
    for copy in loads:
        copy.start()

    def take(at, count):
        if split:
            return jnp.concatenate([ref[at : at + count, :] for ref in arrived_refs], axis=0)
        return arrived_refs[0][:, at : at + count, :].reshape(owners * count, 128)

    labels = take(head, 16).astype(jnp.float32).reshape(owners, 16, 128)
    which = iota((owners, 16, 128), 1)
    parts = jnp.concatenate(
        [jnp.sum(jnp.where(which == k, labels, 0.0), axis=1) for k in range(3)], axis=0
    )
    if split:
        part = iota((1, rows), 1) >> shift
        place = functools.reduce(
            lambda total, p: total + jnp.where(part == p, places[p], 0),
            range(owners),
            jnp.zeros((1, rows), jnp.int32),
        )
    else:
        place = me_ref[0]
    base = (place * capacity) & 127
    pick = iota((128, rows), 0) == base + (iota((128, rows), 1) & (capacity - 1))
    picked = jnp.dot(
        parts.astype(jnp.bfloat16),
        pick.astype(jnp.float32).astype(jnp.bfloat16),
        preferred_element_type=jnp.float32,
    )
    source = iota((owners, rows), 0) == iota((owners, rows), 1) >> shift
    rowed = [
        jnp.sum(
            jnp.where(source, picked[k * owners : (k + 1) * owners], 0.0), axis=0, keepdims=True
        )
        for k in range(3)
    ]
    slot_row = rowed[0].astype(jnp.int32)
    place = (slot_row & (W - 1)) * CH + (slot_row >> (W.bit_length() - 1))
    valid_row = rowed[1] * float(1 << LOW_BITS) + rowed[2]
    scatter = (iota((slots, rows), 0) == place).astype(jnp.float32).astype(jnp.bfloat16)
    valid_col = jnp.transpose(jnp.broadcast_to(valid_row, (128, rows))).astype(jnp.int32)
    power = jnp.zeros((slots, 128), jnp.float32)
    for begin in range(0, nfft, width):
        lanes = range(begin, begin + width, 128)
        inside = jnp.concatenate(
            [
                (iota((rows, 128), 1) + lane < valid_col).astype(jnp.float32).astype(jnp.bfloat16)
                for lane in lanes
            ],
            axis=1,
        )
        arrived = jnp.concatenate([take(lane // 128 * capacity, capacity) for lane in lanes], axis=1)
        summed = jnp.dot(scatter, arrived * inside, preferred_element_type=jnp.float32)
        coverage = jnp.dot(scatter, inside, preferred_element_type=jnp.float32)
        trace = summed / jnp.maximum(coverage, 1.0)
        trace_ref[:, begin : begin + width] = trace
        square = trace * trace
        for lane in range(0, width, 128):
            power = power + square[:, lane : lane + 128]
    meansq = jnp.sum(power, axis=1, keepdims=True) * (1.0 / nfft)
    gain = lax.rsqrt(meansq + 1e-06)
    for begin in range(0, nfft, depth):
        loads[begin // depth].wait()
        normed = (trace_ref[:, begin : begin + depth] * gain).astype(jnp.bfloat16)
        part = jnp.dot(
            normed, table_ref[begin : begin + depth, :], preferred_element_type=jnp.float32
        )
        if begin == 0:
            spectrum_ref[...] = part
        else:
            spectrum_ref[...] += part
    real_part = spectrum_ref[:, :bins]
    imag_part = spectrum_ref[:, bins:]
    amplitude = lax.rsqrt(jnp.maximum(real_part * real_part + imag_part * imag_part, nfft / 4.0))
    real_part = (real_part * amplitude).astype(jnp.bfloat16)
    imag_part = (imag_part * amplitude).astype(jnp.bfloat16)
    for w in range(W):
        at = w * 2 * bins
        out_ref[:, at : at + bins] = real_part[w * CH : (w + 1) * CH]
        out_ref[:, at + bins : at + 2 * bins] = imag_part[w * CH : (w + 1) * CH]


def whiten(me, arrived, table, owners, capacity, places):
    nfft, width = table.shape
    vmem = pl.BlockSpec(memory_space=pltpu.VMEM)
    return pl.pallas_call(
        functools.partial(whiten_kernel, owners, capacity, places),
        in_specs=[pl.BlockSpec(memory_space=pltpu.SMEM)]
        + [vmem] * len(arrived)
        + [pl.BlockSpec(memory_space=pltpu.HBM)],
        out_specs=vmem,
        out_shape=jax.ShapeDtypeStruct((CH, W * width), jnp.bfloat16),
        scratch_shapes=[
            pltpu.VMEM(table.shape, jnp.bfloat16),
            pltpu.VMEM((CH * W, nfft), jnp.float32),
            pltpu.VMEM((CH * W, width), jnp.float32),
            pltpu.SemaphoreType.DMA((nfft // 512,)),
        ],
        compiler_params=pltpu.CompilerParams(vmem_limit_bytes=50 * 1024 * 1024),
        name="whiten",
    )(me, *arrived, table)


BLOCK = 8


def correlate_kernel(
    order_ref, own_ref, first_ref, second_ref, rows_ref, spread_ref, out_hbm,
    both_ref, wide_ref, turned_a, turned_b, found_a, found_b, out_ref, sems,
):
    bins = rows_ref.shape[1]
    terms = rows_ref.shape[0] // 3
    lags = out_ref.shape[4]
    blocks = CH // BLOCK
    turned, found = (turned_a, turned_b), (found_a, found_b)

    def turn(block, slot):
        even = rows_ref[:terms, :]
        odd = rows_ref[terms : 2 * terms, :]
        minus = rows_ref[2 * terms :, :]
        for k in range(BLOCK):
            row = jnp.minimum(block * BLOCK + k, CH - 1)
            u = wide_ref[pl.ds(row, 1), :]
            top = slice(2 * k * terms, (2 * k + 1) * terms)
            low = slice((2 * k + 1) * terms, (2 * k + 2) * terms)
            for w in range(W):
                at = w * 2 * bins
                real, imag = slice(at, at + bins), slice(at + bins, at + 2 * bins)
                ur = jnp.broadcast_to(u[:, real], (terms, bins)).astype(jnp.bfloat16)
                ui = jnp.broadcast_to(u[:, imag], (terms, bins)).astype(jnp.bfloat16)
                turned[slot][top, real] = ur * even
                turned[slot][top, imag] = ui * even
                turned[slot][low, real] = ui * odd
                turned[slot][low, imag] = ur * minus

    def find(slot):
        found[slot][...] = lax.dot_general(
            both_ref[...],
            turned[slot][...],
            (((1,), (1,)), ((), ())),
            preferred_element_type=jnp.float32,
        ).astype(jnp.bfloat16)

    def spread(slot, place):
        for k in range(0, BLOCK, 4):
            lagged = jnp.dot(
                found[slot][:, 2 * k * terms : 2 * (k + 4) * terms],
                spread_ref[...],
                preferred_element_type=jnp.float32,
            ).astype(jnp.bfloat16)
            for n in range(4):
                for r in range(2):
                    out_ref[place, r, k + n] = lagged[
                        r * CH : (r + 1) * CH, n * lags : (n + 1) * lags
                    ]

    def write(block):
        start = pl.multiple_of(block * BLOCK, BLOCK)
        return pltpu.make_async_copy(
            out_ref.at[block % 4], out_hbm.at[:, pl.ds(start, BLOCK)], sems.at[block % 4]
        )

    wide_ref[...] = own_ref[...].astype(jnp.float32)
    at = pl.multiple_of(order_ref[0] * CH, CH)
    both_ref[pl.ds(at, CH), :] = first_ref[...]
    both_ref[pl.ds(CH - at, CH), :] = second_ref[...]
    turn(0, 0)
    turn(1, 1)
    find(0)

    @pl.loop(0, blocks // 2)
    def _(n):
        @pl.when(n >= 2)
        def _():
            write(2 * n - 4).wait()
            write(2 * n - 3).wait()

        place = n % 2 * 2
        turn(2 * n + 2, 0)
        find(1)
        spread(0, place)
        turn(2 * n + 3, 1)
        find(0)
        spread(1, place + 1)
        write(2 * n).start()
        write(2 * n + 1).start()

    for block in range(blocks - 4, blocks):
        write(block).wait()


def correlate(order, own, first, second, nfft, lags):
    depth = own.shape[1]
    bins = depth // (2 * W)
    rows, spread = lag_tables(nfft, bins, lags, 1.0 / math.sqrt(W * bins))
    terms = rows.shape[0] // 3
    vmem = pl.BlockSpec(memory_space=pltpu.VMEM)
    return pl.pallas_call(
        correlate_kernel,
        in_specs=[pl.BlockSpec(memory_space=pltpu.SMEM)] + [vmem] * 5,
        out_specs=pl.BlockSpec(memory_space=pltpu.HBM),
        out_shape=jax.ShapeDtypeStruct((2, CH, CH, lags), jnp.bfloat16),
        scratch_shapes=[
            pltpu.VMEM((2 * CH, depth), jnp.bfloat16),
            pltpu.VMEM((CH, depth), jnp.float32),
            pltpu.VMEM((BLOCK * 2 * terms, depth), jnp.bfloat16),
            pltpu.VMEM((BLOCK * 2 * terms, depth), jnp.bfloat16),
            pltpu.VMEM((2 * CH, BLOCK * 2 * terms), jnp.bfloat16),
            pltpu.VMEM((2 * CH, BLOCK * 2 * terms), jnp.bfloat16),
            pltpu.VMEM((4, 2, BLOCK, CH, lags), jnp.bfloat16),
            pltpu.SemaphoreType.DMA((4,)),
        ],
        compiler_params=pltpu.CompilerParams(vmem_limit_bytes=60 * 1024 * 1024),
        name="correlate",
    )(order, own, first, second, jnp.asarray(rows), jnp.asarray(spread))


def swap(tile, mask):
    count = lax.axis_size("blk")
    return lax.ppermute(tile, "blk", [(low, low ^ mask) for low in range(count)])


def exchange(tile, mask):
    count = lax.axis_size("blk")
    full = count - 1
    if count <= 16:

        def branch(m, moving):
            first = swap(moving, full)
            return first, swap(first, m ^ full) if 2 * m >= count else swap(moving, m)

        branches = [functools.partial(branch, m) for m in range(1, full)]
        return lax.switch(mask - 1, branches, tile)
    moving = tile
    for bit in range(count.bit_length() - 1):
        moving = jnp.where(mask >> bit & 1 == 1, swap(moving, 1 << bit), moving)
    return swap(tile, full), moving


def local(records, dest, slot, valid, masks):
    owners = lax.axis_size("blk")
    held, nfft = records.shape
    capacity = max(16, 2 * held // owners)
    me = lax.axis_index("blk").astype(jnp.int32).reshape(1)
    key = ((dest << SLOT_BITS) + slot << VALID_BITS) + valid
    split = owners <= 16
    outgoing = pack(me, key.reshape(1, held), records, owners, capacity, split)
    if split:
        half = owners // 2
        places = [half]
        for distance in range(1, half):
            places += [distance, half + distance]
        arrived = [swap(outgoing[distance], distance) for distance in places] + [outgoing[0]]
        places.append(0)
    else:
        places = None
        arrived = [lax.all_to_all(outgoing[0], "blk", split_axis=0, concat_axis=0, tiled=True)]
    tile = whiten(me, arrived, jnp.asarray(forward_table(nfft, F)), owners, capacity, places)
    full = owners - 1
    first, second = exchange(tile, masks[0] + masks[1] - full)
    order = (masks[:1] != full).astype(jnp.int32)
    return correlate(order, tile, first, second, nfft, LAGS)


def solution(mesh):
    return jax.shard_map(
        local,
        mesh=mesh,
        in_specs=(
            P(("groups", "blk"), None),
            P(("groups", "blk"), None),
            P(("groups", "blk"), None),
            P(("groups", "blk"), None),
            P(),
        ),
        out_specs=P(None, ("groups", "blk"), None, None),
        check_vma=False,
    )
```

```python
import functools
import math

import jax
import jax.numpy as jnp
import numpy as np
from jax import lax
from jax.experimental import pallas as pl
from jax.experimental.pallas import tpu as pltpu
from jax.sharding import PartitionSpec as P

CH = 128
F = 256
LAGS = 128
W = 2
SLOT_BITS = 8
VALID_BITS = 12
LOW_BITS = 4


def forward_table(nfft, bins):
    sample = np.arange(nfft, dtype=np.int64)[:, None]
    freq = np.arange(1, bins + 1, dtype=np.int64)[None, :]
    angle = (sample * freq % nfft).astype(np.float64) * (2.0 * math.pi / nfft)
    return np.concatenate([np.cos(angle), -np.sin(angle)], axis=1).astype(np.float32).astype(jnp.bfloat16)


def lag_tables(nfft, bins, lags, scale):
    half = lags // 2
    count = lags + 1
    place = np.arange(count)
    middle = ((count - 1 - 2 * place) / 2.0) ** 2 * math.cos(2.0 * math.pi * bins / nfft)
    aside = (place[1:] * (count - place[1:])) / 2.0
    _, basis = np.linalg.eigh(np.diag(middle) + np.diag(aside, 1) + np.diag(aside, -1))
    basis = basis[:, ::-1][:, :half]
    even, odd = basis[:, 0::2], basis[:, 1::2]
    even = even * np.sign(even[half])
    odd = odd * np.sign(odd[half + 1])
    freq = np.arange(1, bins + 1, dtype=np.int64)[None, :]
    angle = (freq * (place[:, None] - half) % nfft) * (2.0 * math.pi / nfft)
    rows = [even.T @ np.cos(angle), odd.T @ -np.sin(angle)]
    rest = np.cos(angle) - np.sin(angle) - even @ rows[0] - odd @ rows[1]
    assert np.abs(rest).max() < 1e-7
    rows = np.concatenate(rows + [-rows[1]])
    basis = np.concatenate([even, odd], axis=1)[:lags].T * scale
    blank = np.zeros_like(basis)
    spread = np.concatenate(
        [np.concatenate([basis if k == n else blank for n in range(4)], axis=1) for k in range(4)]
    )

    def narrow(table):
        return (np.round(table * 2.0**28) / 2.0**28).astype(np.float32).astype(jnp.bfloat16)

    return narrow(rows), narrow(spread)


def iota(shape, dim):
    return lax.broadcasted_iota(jnp.int32, shape, dim)


LABELS = 8


def full_plan(capacity, chunks):
    return (capacity,) * chunks


def short_plan(capacity, chunks):
    def rows(c):
        return capacity if 16 * c < 11 * chunks else capacity * 3 // 4 if 16 * c < 13 * chunks else capacity // 2

    return tuple(rows(c) for c in range(chunks))


def pack_kernel(owners, capacity, plans, me_ref, key_ref, records_ref, *out_refs):
    held, nfft = records_ref.shape
    rows = owners * capacity
    width = 512
    key = key_ref[...]
    part = key >> (SLOT_BITS + VALID_BITS)
    if len(out_refs) > 1:
        part = part ^ me_ref[0]
    valid = key & ((1 << VALID_BITS) - 1)
    first = valid * held + (held - 1 - iota((1, held), 1))

    def column(row):
        wide = jnp.transpose(jnp.broadcast_to(row.astype(jnp.float32), (128, held)))
        return jnp.concatenate([wide] * (held // 128), axis=1)

    same = column(part) == part.astype(jnp.float32)
    before = jnp.where(same & (column(first) > first.astype(jnp.float32)), 1.0, 0.0)
    rank = jnp.sum(before, axis=0, keepdims=True).astype(jnp.int32)
    over = jnp.zeros((1, held), jnp.int32)
    for plan in sorted(set(plans)):
        member = functools.reduce(
            jnp.logical_or, [part == d for d in range(owners) if plans[d] == plan]
        )
        for size in sorted(set(plan)):
            if size < capacity:
                reach = 128 * sum(count > size for count in plan)
                over += jnp.where(member & (rank >= size) & (valid > reach), 1, 0)
    over = jnp.max(jnp.minimum(over, 1).astype(jnp.float32), axis=1, keepdims=True)
    position = part * capacity + rank
    order = (iota((rows, held), 0) == position).astype(jnp.float32).astype(jnp.bfloat16)
    slot = (key >> VALID_BITS) & ((1 << SLOT_BITS) - 1)
    row = iota((16, held), 0)
    labels = jnp.where(
        row == 0,
        slot,
        jnp.where(
            row == 1,
            valid >> LOW_BITS,
            jnp.where(row == 2, valid & ((1 << LOW_BITS) - 1), 0),
        ),
    )
    moved = lax.dot_general(
        labels.astype(jnp.float32).astype(jnp.bfloat16),
        order,
        (((1,), (1,)), ((), ())),
        preferred_element_type=jnp.float32,
    )
    moved = jnp.where(iota((16, rows), 0) == 3, over, moved).astype(jnp.bfloat16)

    def put(d, at, value):
        if len(out_refs) > 1:
            out_refs[d][at : at + value.shape[0], :] = value
        else:
            out_refs[0][d, at : at + value.shape[0], :] = value

    for d in range(owners):
        at = d * capacity // 128 * 128
        put(d, sum(plans[d]), moved[:LABELS, at : at + 128])
    for begin in range(0, nfft, width):
        ordered = jnp.dot(
            order, records_ref[:, begin : begin + width], preferred_element_type=jnp.float32
        ).astype(jnp.bfloat16)
        for lane in range(0, width, 128):
            c = (begin + lane) // 128
            for d in range(owners):
                top = d * capacity
                put(d, sum(plans[d][:c]), ordered[top : top + plans[d][c], lane : lane + 128])


def pack(me, key, records, capacity, plans, split):
    held, nfft = records.shape
    owners = len(plans)
    vmem = pl.BlockSpec(memory_space=pltpu.VMEM)
    shapes = [(sum(plan) + LABELS, 128) for plan in plans]
    if not split:
        shapes = [(owners,) + shapes[0]]
    return pl.pallas_call(
        functools.partial(pack_kernel, owners, capacity, plans),
        in_specs=[pl.BlockSpec(memory_space=pltpu.SMEM), vmem, vmem],
        out_specs=[vmem] * len(shapes),
        out_shape=[jax.ShapeDtypeStruct(shape, jnp.bfloat16) for shape in shapes],
        compiler_params=pltpu.CompilerParams(vmem_limit_bytes=48 * 1024 * 1024),
        name="pack",
    )(me, key, records)


def whiten_kernel(capacity, plans, places, me_ref, mask_ref, *refs):
    *arrived_refs, table_hbm, out_ref, branch_ref, table_ref, trace_ref, spectrum_ref, sems = refs
    owners = len(plans)
    split = len(arrived_refs) > 1
    nfft = trace_ref.shape[1]
    rows = owners * capacity
    slots = CH * W
    bins = table_ref.shape[1] // 2
    shift = capacity.bit_length() - 1
    width = 256
    depth = 512
    loads = [
        pltpu.make_async_copy(
            table_hbm.at[pl.ds(at, depth)], table_ref.at[pl.ds(at, depth)], sems.at[at // depth]
        )
        for at in range(0, nfft, depth)
    ]
    for copy in loads:
        copy.start()

    def take(c):
        if not split:
            at, count = sum(plans[0][:c]), plans[0][c] if c < len(plans[0]) else LABELS
            return arrived_refs[0][:, at : at + count, :].reshape(owners * count, 128)
        pieces = []
        for ref, plan in zip(arrived_refs, plans):
            at, count = sum(plan[:c]), plan[c] if c < len(plan) else LABELS
            pieces.append(ref[at : at + count, :])
            if c < len(plan) and count < capacity:
                pieces.append(jnp.zeros((capacity - count, 128), jnp.bfloat16))
        return jnp.concatenate(pieces, axis=0)

    labels = take(len(plans[0])).astype(jnp.float32).reshape(owners, LABELS, 128)
    which = iota((owners, LABELS, 128), 1)
    over = jnp.max(jnp.where(which == 3, labels, 0.0))
    branch_ref[0] = jnp.where(over > 0.0, owners - 2, mask_ref[0] - 1)
    parts = jnp.concatenate(
        [jnp.sum(jnp.where(which == k, labels, 0.0), axis=1) for k in range(3)], axis=0
    )
    if split:
        part = iota((1, rows), 1) >> shift
        place = functools.reduce(
            lambda total, p: total + jnp.where(part == p, places[p], 0),
            range(owners),
            jnp.zeros((1, rows), jnp.int32),
        )
    else:
        place = me_ref[0]
    base = (place * capacity) & 127
    pick = iota((128, rows), 0) == base + (iota((128, rows), 1) & (capacity - 1))
    picked = jnp.dot(
        parts.astype(jnp.bfloat16),
        pick.astype(jnp.float32).astype(jnp.bfloat16),
        preferred_element_type=jnp.float32,
    )
    source = iota((owners, rows), 0) == iota((owners, rows), 1) >> shift
    rowed = [
        jnp.sum(
            jnp.where(source, picked[k * owners : (k + 1) * owners], 0.0), axis=0, keepdims=True
        )
        for k in range(3)
    ]
    slot_row = rowed[0].astype(jnp.int32)
    place = (slot_row & (W - 1)) * CH + (slot_row >> (W.bit_length() - 1))
    valid_row = rowed[1] * float(1 << LOW_BITS) + rowed[2]
    scatter = (iota((slots, rows), 0) == place).astype(jnp.float32).astype(jnp.bfloat16)
    valid_col = jnp.transpose(jnp.broadcast_to(valid_row, (128, rows))).astype(jnp.int32)
    power = jnp.zeros((slots, 128), jnp.float32)
    for begin in range(0, nfft, width):
        lanes = range(begin, begin + width, 128)
        inside = jnp.concatenate(
            [
                (iota((rows, 128), 1) + lane < valid_col).astype(jnp.float32).astype(jnp.bfloat16)
                for lane in lanes
            ],
            axis=1,
        )
        arrived = jnp.concatenate([take(lane // 128) for lane in lanes], axis=1)
        summed = jnp.dot(scatter, arrived * inside, preferred_element_type=jnp.float32)
        coverage = jnp.dot(scatter, inside, preferred_element_type=jnp.float32)
        trace = summed / jnp.maximum(coverage, 1.0)
        trace_ref[:, begin : begin + width] = trace
        square = trace * trace
        for lane in range(0, width, 128):
            power = power + square[:, lane : lane + 128]
    meansq = jnp.sum(power, axis=1, keepdims=True) * (1.0 / nfft)
    gain = lax.rsqrt(meansq + 1e-06)
    for begin in range(0, nfft, depth):
        loads[begin // depth].wait()
        normed = (trace_ref[:, begin : begin + depth] * gain).astype(jnp.bfloat16)
        part = jnp.dot(
            normed, table_ref[begin : begin + depth, :], preferred_element_type=jnp.float32
        )
        if begin == 0:
            spectrum_ref[...] = part
        else:
            spectrum_ref[...] += part
    real_part = spectrum_ref[:, :bins]
    imag_part = spectrum_ref[:, bins:]
    amplitude = lax.rsqrt(jnp.maximum(real_part * real_part + imag_part * imag_part, nfft / 4.0))
    real_part = (real_part * amplitude).astype(jnp.bfloat16)
    imag_part = (imag_part * amplitude).astype(jnp.bfloat16)
    for w in range(W):
        at = w * 2 * bins
        out_ref[:, at : at + bins] = real_part[w * CH : (w + 1) * CH]
        out_ref[:, at + bins : at + 2 * bins] = imag_part[w * CH : (w + 1) * CH]


def whiten(me, mask, arrived, table, capacity, plans, places):
    nfft, width = table.shape
    vmem = pl.BlockSpec(memory_space=pltpu.VMEM)
    smem = pl.BlockSpec(memory_space=pltpu.SMEM)
    return pl.pallas_call(
        functools.partial(whiten_kernel, capacity, plans, places),
        in_specs=[smem, smem]
        + [vmem] * len(arrived)
        + [pl.BlockSpec(memory_space=pltpu.HBM)],
        out_specs=[vmem, smem],
        out_shape=[
            jax.ShapeDtypeStruct((CH, W * width), jnp.bfloat16),
            jax.ShapeDtypeStruct((1,), jnp.int32),
        ],
        scratch_shapes=[
            pltpu.VMEM(table.shape, jnp.bfloat16),
            pltpu.VMEM((CH * W, nfft), jnp.float32),
            pltpu.VMEM((CH * W, width), jnp.float32),
            pltpu.SemaphoreType.DMA((nfft // 512,)),
        ],
        compiler_params=pltpu.CompilerParams(vmem_limit_bytes=50 * 1024 * 1024),
        name="whiten",
    )(me, mask, *arrived, table)


BLOCK = 8


def correlate_kernel(
    order_ref, own_ref, first_ref, second_ref, rows_ref, spread_ref, out_hbm,
    both_ref, wide_ref, turned_a, turned_b, found_a, found_b, out_ref, sems,
):
    bins = rows_ref.shape[1]
    terms = rows_ref.shape[0] // 3
    lags = out_ref.shape[4]
    blocks = CH // BLOCK
    turned, found = (turned_a, turned_b), (found_a, found_b)

    def turn(block, slot):
        even = rows_ref[:terms, :]
        odd = rows_ref[terms : 2 * terms, :]
        minus = rows_ref[2 * terms :, :]
        for k in range(BLOCK):
            row = jnp.minimum(block * BLOCK + k, CH - 1)
            u = wide_ref[pl.ds(row, 1), :]
            top = slice(2 * k * terms, (2 * k + 1) * terms)
            low = slice((2 * k + 1) * terms, (2 * k + 2) * terms)
            for w in range(W):
                at = w * 2 * bins
                real, imag = slice(at, at + bins), slice(at + bins, at + 2 * bins)
                ur = jnp.broadcast_to(u[:, real], (terms, bins)).astype(jnp.bfloat16)
                ui = jnp.broadcast_to(u[:, imag], (terms, bins)).astype(jnp.bfloat16)
                turned[slot][top, real] = ur * even
                turned[slot][top, imag] = ui * even
                turned[slot][low, real] = ui * odd
                turned[slot][low, imag] = ur * minus

    def find(slot):
        found[slot][...] = lax.dot_general(
            both_ref[...],
            turned[slot][...],
            (((1,), (1,)), ((), ())),
            preferred_element_type=jnp.float32,
        ).astype(jnp.bfloat16)

    def spread(slot, place):
        for k in range(0, BLOCK, 4):
            lagged = jnp.dot(
                found[slot][:, 2 * k * terms : 2 * (k + 4) * terms],
                spread_ref[...],
                preferred_element_type=jnp.float32,
            ).astype(jnp.bfloat16)
            for n in range(4):
                for r in range(2):
                    out_ref[place, r, k + n] = lagged[
                        r * CH : (r + 1) * CH, n * lags : (n + 1) * lags
                    ]

    def write(block):
        start = pl.multiple_of(block * BLOCK, BLOCK)
        return pltpu.make_async_copy(
            out_ref.at[block % 4], out_hbm.at[:, pl.ds(start, BLOCK)], sems.at[block % 4]
        )

    wide_ref[...] = own_ref[...].astype(jnp.float32)
    at = pl.multiple_of(order_ref[0] * CH, CH)
    both_ref[pl.ds(at, CH), :] = first_ref[...]
    both_ref[pl.ds(CH - at, CH), :] = second_ref[...]
    turn(0, 0)
    turn(1, 1)
    find(0)

    @pl.loop(0, blocks // 2)
    def _(n):
        @pl.when(n >= 2)
        def _():
            write(2 * n - 4).wait()
            write(2 * n - 3).wait()

        place = n % 2 * 2
        turn(2 * n + 2, 0)
        find(1)
        spread(0, place)
        turn(2 * n + 3, 1)
        find(0)
        spread(1, place + 1)
        write(2 * n).start()
        write(2 * n + 1).start()

    for block in range(blocks - 4, blocks):
        write(block).wait()


def correlate(order, own, first, second, nfft, lags):
    depth = own.shape[1]
    bins = depth // (2 * W)
    rows, spread = lag_tables(nfft, bins, lags, 1.0 / math.sqrt(W * bins))
    terms = rows.shape[0] // 3
    vmem = pl.BlockSpec(memory_space=pltpu.VMEM)
    return pl.pallas_call(
        correlate_kernel,
        in_specs=[pl.BlockSpec(memory_space=pltpu.SMEM)] + [vmem] * 5,
        out_specs=pl.BlockSpec(memory_space=pltpu.HBM),
        out_shape=jax.ShapeDtypeStruct((2, CH, CH, lags), jnp.bfloat16),
        scratch_shapes=[
            pltpu.VMEM((2 * CH, depth), jnp.bfloat16),
            pltpu.VMEM((CH, depth), jnp.float32),
            pltpu.VMEM((BLOCK * 2 * terms, depth), jnp.bfloat16),
            pltpu.VMEM((BLOCK * 2 * terms, depth), jnp.bfloat16),
            pltpu.VMEM((2 * CH, BLOCK * 2 * terms), jnp.bfloat16),
            pltpu.VMEM((2 * CH, BLOCK * 2 * terms), jnp.bfloat16),
            pltpu.VMEM((4, 2, BLOCK, CH, lags), jnp.bfloat16),
            pltpu.SemaphoreType.DMA((4,)),
        ],
        compiler_params=pltpu.CompilerParams(vmem_limit_bytes=60 * 1024 * 1024),
        name="correlate",
    )(order, own, first, second, jnp.asarray(rows), jnp.asarray(spread))


def swap(tile, mask):
    count = lax.axis_size("blk")
    return lax.ppermute(tile, "blk", [(low, low ^ mask) for low in range(count)])


def exchange(mask, moving):
    count = lax.axis_size("blk")
    full = count - 1
    first = swap(moving, full)
    return moving, first, swap(first, mask ^ full) if 2 * mask >= count else swap(moving, mask)


def deliver(me, mask, key, records, plan):
    owners = lax.axis_size("blk")
    held, nfft = records.shape
    capacity = max(16, 2 * held // owners)
    whole = full_plan(capacity, nfft // 128)
    table = jnp.asarray(forward_table(nfft, F))
    if owners > 16:
        plans = (whole,) * owners
        (outgoing,) = pack(me, key, records, capacity, plans, False)
        arrived = [lax.all_to_all(outgoing, "blk", split_axis=0, concat_axis=0, tiled=True)]
        return whiten(me, mask, arrived, table, capacity, plans, None)
    half = owners // 2
    plans = (whole,) * half + (plan(capacity, nfft // 128),) * half
    outgoing = pack(me, key, records, capacity, plans, True)
    places = [half]
    for distance in range(1, half):
        places += [distance, half + distance]
    arrived = [swap(outgoing[distance], distance) for distance in places] + [outgoing[0]]
    places.append(0)
    ordered = tuple(plans[distance] for distance in places)
    return whiten(me, mask, arrived, table, capacity, ordered, places)


def local(records, dest, slot, valid, masks):
    owners = lax.axis_size("blk")
    held, nfft = records.shape
    full = owners - 1
    me = lax.axis_index("blk").astype(jnp.int32).reshape(1)
    mask = (masks[0] + masks[1] - full).reshape(1)
    key = (((dest << SLOT_BITS) + slot << VALID_BITS) + valid).reshape(1, held)
    if owners <= 16:
        tile, branch = deliver(me, mask, key, records, short_plan)
        known = [functools.partial(exchange, m) for m in range(1, full)]

        def again(tile):
            tile, branch = deliver(me, mask, key, records, full_plan)
            return lax.switch(branch[0], known, tile)

        own, first, second = lax.switch(branch[0], known + [again], tile)
    else:
        own, _ = deliver(me, mask, key, records, full_plan)
        second = own
        for bit in range(owners.bit_length() - 1):
            second = jnp.where(mask >> bit & 1 == 1, swap(second, 1 << bit), second)
        first = swap(own, full)
    order = (masks[:1] != full).astype(jnp.int32)
    return correlate(order, own, first, second, nfft, LAGS)


def solution(mesh):
    return jax.shard_map(
        local,
        mesh=mesh,
        in_specs=(
            P(("groups", "blk"), None),
            P(("groups", "blk"), None),
            P(("groups", "blk"), None),
            P(("groups", "blk"), None),
            P(),
        ),
        out_specs=P(None, ("groups", "blk"), None, None),
        check_vma=False,
    )
```

```python
import functools
import math

import jax
import jax.numpy as jnp
import numpy as np
from jax import lax
from jax.experimental import pallas as pl
from jax.experimental.pallas import tpu as pltpu
from jax.sharding import PartitionSpec as P

CH = 128
F = 256
LAGS = 128
W = 2
SLOT_BITS = 8
VALID_BITS = 12
LOW_BITS = 4


def forward_table(nfft, bins):
    sample = np.arange(nfft, dtype=np.int64)[:, None]
    freq = np.arange(1, bins + 1, dtype=np.int64)[None, :]
    angle = (sample * freq % nfft).astype(np.float64) * (2.0 * math.pi / nfft)
    return np.concatenate([np.cos(angle), -np.sin(angle)], axis=1).astype(np.float32).astype(jnp.bfloat16)


def lag_tables(nfft, bins, lags, scale):
    half = lags // 2
    count = lags + 1
    place = np.arange(count)
    middle = ((count - 1 - 2 * place) / 2.0) ** 2 * math.cos(2.0 * math.pi * bins / nfft)
    aside = (place[1:] * (count - place[1:])) / 2.0
    _, basis = np.linalg.eigh(np.diag(middle) + np.diag(aside, 1) + np.diag(aside, -1))
    basis = basis[:, ::-1][:, :half]
    even, odd = basis[:, 0::2], basis[:, 1::2]
    even = even * np.sign(even[half])
    odd = odd * np.sign(odd[half + 1])
    freq = np.arange(1, bins + 1, dtype=np.int64)[None, :]
    angle = (freq * (place[:, None] - half) % nfft) * (2.0 * math.pi / nfft)
    rows = [even.T @ np.cos(angle), odd.T @ -np.sin(angle)]
    rest = np.cos(angle) - np.sin(angle) - even @ rows[0] - odd @ rows[1]
    assert np.abs(rest).max() < 1e-7
    rows = np.concatenate(rows + [-rows[1]])
    basis = np.concatenate([even, odd], axis=1)[:lags].T * scale
    blank = np.zeros_like(basis)
    spread = np.concatenate(
        [np.concatenate([basis if k == n else blank for n in range(4)], axis=1) for k in range(4)]
    )

    def narrow(table):
        return (np.round(table * 2.0**28) / 2.0**28).astype(np.float32).astype(jnp.bfloat16)

    return narrow(rows), narrow(spread)


def iota(shape, dim):
    return lax.broadcasted_iota(jnp.int32, shape, dim)


LABELS = 8


def full_plan(capacity, chunks):
    return (capacity,) * chunks


def short_plan(capacity, chunks):
    def rows(c):
        return capacity if 16 * c < 11 * chunks else capacity * 3 // 4 if 16 * c < 13 * chunks else capacity // 2

    return tuple(rows(c) for c in range(chunks))


def pack_kernel(owners, capacity, plans, me_ref, key_ref, records_ref, *out_refs):
    held, nfft = records_ref.shape
    rows = owners * capacity
    width = 512
    key = key_ref[...]
    part = key >> (SLOT_BITS + VALID_BITS)
    if len(out_refs) > 1:
        part = part ^ me_ref[0]
    valid = key & ((1 << VALID_BITS) - 1)
    first = valid * held + (held - 1 - iota((1, held), 1))

    def column(row):
        wide = jnp.transpose(jnp.broadcast_to(row.astype(jnp.float32), (128, held)))
        return jnp.concatenate([wide] * (held // 128), axis=1)

    same = column(part) == part.astype(jnp.float32)
    before = jnp.where(same & (column(first) > first.astype(jnp.float32)), 1.0, 0.0)
    rank = jnp.sum(before, axis=0, keepdims=True).astype(jnp.int32)
    over = jnp.zeros((1, held), jnp.int32)
    for plan in sorted(set(plans)):
        member = functools.reduce(
            jnp.logical_or, [part == d for d in range(owners) if plans[d] == plan]
        )
        for size in sorted(set(plan)):
            if size < capacity:
                reach = 128 * sum(count > size for count in plan)
                over += jnp.where(member & (rank >= size) & (valid > reach), 1, 0)
    over = jnp.max(jnp.minimum(over, 1).astype(jnp.float32), axis=1, keepdims=True)
    position = part * capacity + rank
    order = (iota((rows, held), 0) == position).astype(jnp.float32).astype(jnp.bfloat16)
    slot = (key >> VALID_BITS) & ((1 << SLOT_BITS) - 1)
    row = iota((16, held), 0)
    labels = jnp.where(
        row == 0,
        slot,
        jnp.where(
            row == 1,
            valid >> LOW_BITS,
            jnp.where(row == 2, valid & ((1 << LOW_BITS) - 1), 0),
        ),
    )
    moved = lax.dot_general(
        labels.astype(jnp.float32).astype(jnp.bfloat16),
        order,
        (((1,), (1,)), ((), ())),
        preferred_element_type=jnp.float32,
    )
    moved = jnp.where(iota((16, rows), 0) == 3, over, moved).astype(jnp.bfloat16)

    def put(d, at, value):
        if len(out_refs) > 1:
            out_refs[d][at : at + value.shape[0], :] = value
        else:
            out_refs[0][d, at : at + value.shape[0], :] = value

    for d in range(owners):
        at = d * capacity // 128 * 128
        put(d, sum(plans[d]), moved[:LABELS, at : at + 128])
    for begin in range(0, nfft, width):
        ordered = jnp.dot(
            order, records_ref[:, begin : begin + width], preferred_element_type=jnp.float32
        ).astype(jnp.bfloat16)
        for lane in range(0, width, 128):
            c = (begin + lane) // 128
            for d in range(owners):
                top = d * capacity
                put(d, sum(plans[d][:c]), ordered[top : top + plans[d][c], lane : lane + 128])


def pack(me, key, records, capacity, plans, split):
    held, nfft = records.shape
    owners = len(plans)
    vmem = pl.BlockSpec(memory_space=pltpu.VMEM)
    shapes = [(sum(plan) + LABELS, 128) for plan in plans]
    if not split:
        shapes = [(owners,) + shapes[0]]
    return pl.pallas_call(
        functools.partial(pack_kernel, owners, capacity, plans),
        in_specs=[pl.BlockSpec(memory_space=pltpu.SMEM), vmem, vmem],
        out_specs=[vmem] * len(shapes),
        out_shape=[jax.ShapeDtypeStruct(shape, jnp.bfloat16) for shape in shapes],
        compiler_params=pltpu.CompilerParams(vmem_limit_bytes=48 * 1024 * 1024),
        name="pack",
    )(me, key, records)


def whiten_kernel(capacity, plans, places, me_ref, mask_ref, *refs):
    *arrived_refs, table_hbm, out_ref, branch_ref, table_ref, trace_ref, spectrum_ref, sems = refs
    owners = len(plans)
    split = len(arrived_refs) > 1
    nfft = trace_ref.shape[1]
    rows = owners * capacity
    slots = CH * W
    bins = table_ref.shape[1] // 2
    shift = capacity.bit_length() - 1
    width = 256
    depth = 512
    loads = [
        pltpu.make_async_copy(
            table_hbm.at[pl.ds(at, depth)], table_ref.at[pl.ds(at, depth)], sems.at[at // depth]
        )
        for at in range(0, nfft, depth)
    ]
    for copy in loads:
        copy.start()

    def take(c):
        if not split:
            at, count = sum(plans[0][:c]), plans[0][c] if c < len(plans[0]) else LABELS
            return arrived_refs[0][:, at : at + count, :].reshape(owners * count, 128)
        pieces = []
        for ref, plan in zip(arrived_refs, plans):
            at, count = sum(plan[:c]), plan[c] if c < len(plan) else LABELS
            pieces.append(ref[at : at + count, :])
            if c < len(plan) and count < capacity:
                pieces.append(jnp.zeros((capacity - count, 128), jnp.bfloat16))
        return jnp.concatenate(pieces, axis=0)

    labels = take(len(plans[0])).astype(jnp.float32).reshape(owners, LABELS, 128)
    which = iota((owners, LABELS, 128), 1)
    over = jnp.max(jnp.where(which == 3, labels, 0.0))
    branch_ref[0] = jnp.where(over > 0.0, owners - 2, mask_ref[0] - 1)
    parts = jnp.concatenate(
        [jnp.sum(jnp.where(which == k, labels, 0.0), axis=1) for k in range(3)], axis=0
    )
    if split:
        part = iota((1, rows), 1) >> shift
        place = functools.reduce(
            lambda total, p: total + jnp.where(part == p, places[p], 0),
            range(owners),
            jnp.zeros((1, rows), jnp.int32),
        )
    else:
        place = me_ref[0]
    base = (place * capacity) & 127
    pick = iota((128, rows), 0) == base + (iota((128, rows), 1) & (capacity - 1))
    picked = jnp.dot(
        parts.astype(jnp.bfloat16),
        pick.astype(jnp.float32).astype(jnp.bfloat16),
        preferred_element_type=jnp.float32,
    )
    source = iota((owners, rows), 0) == iota((owners, rows), 1) >> shift
    rowed = [
        jnp.sum(
            jnp.where(source, picked[k * owners : (k + 1) * owners], 0.0), axis=0, keepdims=True
        )
        for k in range(3)
    ]
    slot_row = rowed[0].astype(jnp.int32)
    place = (slot_row & (W - 1)) * CH + (slot_row >> (W.bit_length() - 1))
    valid_row = rowed[1] * float(1 << LOW_BITS) + rowed[2]
    scatter = (iota((slots, rows), 0) == place).astype(jnp.float32).astype(jnp.bfloat16)
    valid_col = jnp.transpose(jnp.broadcast_to(valid_row, (128, rows))).astype(jnp.int32)
    power = jnp.zeros((slots, 128), jnp.float32)
    for begin in range(0, nfft, width):
        lanes = range(begin, begin + width, 128)
        inside = jnp.concatenate(
            [
                (iota((rows, 128), 1) + lane < valid_col).astype(jnp.float32).astype(jnp.bfloat16)
                for lane in lanes
            ],
            axis=1,
        )
        arrived = jnp.concatenate([take(lane // 128) for lane in lanes], axis=1)
        summed = jnp.dot(scatter, arrived * inside, preferred_element_type=jnp.float32)
        coverage = jnp.dot(scatter, inside, preferred_element_type=jnp.float32)
        trace = summed / jnp.maximum(coverage, 1.0)
        trace_ref[:, begin : begin + width] = trace
        square = trace * trace
        for lane in range(0, width, 128):
            power = power + square[:, lane : lane + 128]
    meansq = jnp.sum(power, axis=1, keepdims=True) * (1.0 / nfft)
    gain = lax.rsqrt(meansq + 1e-06)
    for begin in range(0, nfft, depth):
        loads[begin // depth].wait()
        normed = (trace_ref[:, begin : begin + depth] * gain).astype(jnp.bfloat16)
        part = jnp.dot(
            normed, table_ref[begin : begin + depth, :], preferred_element_type=jnp.float32
        )
        if begin == 0:
            spectrum_ref[...] = part
        else:
            spectrum_ref[...] += part
    real_part = spectrum_ref[:, :bins]
    imag_part = spectrum_ref[:, bins:]
    amplitude = lax.rsqrt(jnp.maximum(real_part * real_part + imag_part * imag_part, nfft / 4.0))
    real_part = (real_part * amplitude).astype(jnp.bfloat16)
    imag_part = (imag_part * amplitude).astype(jnp.bfloat16)
    for w in range(W):
        at = w * 2 * bins
        out_ref[:, at : at + bins] = real_part[w * CH : (w + 1) * CH]
        out_ref[:, at + bins : at + 2 * bins] = imag_part[w * CH : (w + 1) * CH]


def whiten(me, mask, arrived, table, capacity, plans, places):
    nfft, width = table.shape
    vmem = pl.BlockSpec(memory_space=pltpu.VMEM)
    smem = pl.BlockSpec(memory_space=pltpu.SMEM)
    return pl.pallas_call(
        functools.partial(whiten_kernel, capacity, plans, places),
        in_specs=[smem, smem]
        + [vmem] * len(arrived)
        + [pl.BlockSpec(memory_space=pltpu.HBM)],
        out_specs=[vmem, smem],
        out_shape=[
            jax.ShapeDtypeStruct((CH, W * width), jnp.bfloat16),
            jax.ShapeDtypeStruct((1,), jnp.int32),
        ],
        scratch_shapes=[
            pltpu.VMEM(table.shape, jnp.bfloat16),
            pltpu.VMEM((CH * W, nfft), jnp.float32),
            pltpu.VMEM((CH * W, width), jnp.float32),
            pltpu.SemaphoreType.DMA((nfft // 512,)),
        ],
        compiler_params=pltpu.CompilerParams(vmem_limit_bytes=50 * 1024 * 1024),
        name="whiten",
    )(me, mask, *arrived, table)


BLOCK = 8


def correlate_kernel(
    order_ref, own_ref, first_ref, second_ref, rows_ref, spread_ref, out_hbm,
    both_ref, wide_ref, turned_a, turned_b, found_a, found_b, out_ref, sems,
):
    bins = rows_ref.shape[1]
    terms = rows_ref.shape[0] // 3
    lags = out_ref.shape[4]
    blocks = CH // BLOCK
    turned, found = (turned_a, turned_b), (found_a, found_b)

    def turn(block, slot):
        even = rows_ref[:terms, :]
        odd = rows_ref[terms : 2 * terms, :]
        minus = rows_ref[2 * terms :, :]
        for k in range(BLOCK):
            row = jnp.minimum(block * BLOCK + k, CH - 1)
            u = wide_ref[pl.ds(row, 1), :]
            top = slice(2 * k * terms, (2 * k + 1) * terms)
            low = slice((2 * k + 1) * terms, (2 * k + 2) * terms)
            for w in range(W):
                at = w * 2 * bins
                real, imag = slice(at, at + bins), slice(at + bins, at + 2 * bins)
                ur = jnp.broadcast_to(u[:, real], (terms, bins)).astype(jnp.bfloat16)
                ui = jnp.broadcast_to(u[:, imag], (terms, bins)).astype(jnp.bfloat16)
                turned[slot][top, real] = ur * even
                turned[slot][top, imag] = ui * even
                turned[slot][low, real] = ui * odd
                turned[slot][low, imag] = ur * minus

    def find(slot):
        found[slot][...] = lax.dot_general(
            both_ref[...],
            turned[slot][...],
            (((1,), (1,)), ((), ())),
            preferred_element_type=jnp.float32,
        ).astype(jnp.bfloat16)

    def spread(slot, place):
        for k in range(0, BLOCK, 4):
            lagged = jnp.dot(
                found[slot][:, 2 * k * terms : 2 * (k + 4) * terms],
                spread_ref[...],
                preferred_element_type=jnp.float32,
            ).astype(jnp.bfloat16)
            for n in range(4):
                for r in range(2):
                    out_ref[place, r, k + n] = lagged[
                        r * CH : (r + 1) * CH, n * lags : (n + 1) * lags
                    ]

    def write(block):
        start = pl.multiple_of(block * BLOCK, BLOCK)
        return pltpu.make_async_copy(
            out_ref.at[block % 4], out_hbm.at[:, pl.ds(start, BLOCK)], sems.at[block % 4]
        )

    wide_ref[...] = own_ref[...].astype(jnp.float32)
    at = pl.multiple_of(order_ref[0] * CH, CH)
    both_ref[pl.ds(at, CH), :] = first_ref[...]
    both_ref[pl.ds(CH - at, CH), :] = second_ref[...]
    turn(0, 0)
    turn(1, 1)
    find(0)

    @pl.loop(0, blocks // 2)
    def _(n):
        @pl.when(n >= 2)
        def _():
            write(2 * n - 4).wait()
            write(2 * n - 3).wait()

        place = n % 2 * 2
        turn(2 * n + 2, 0)
        find(1)
        spread(0, place)
        turn(2 * n + 3, 1)
        find(0)
        spread(1, place + 1)
        write(2 * n).start()
        write(2 * n + 1).start()

    for block in range(blocks - 4, blocks):
        write(block).wait()


def correlate(order, own, first, second, nfft, lags):
    depth = own.shape[1]
    bins = depth // (2 * W)
    rows, spread = lag_tables(nfft, bins, lags, 1.0 / math.sqrt(W * bins))
    terms = rows.shape[0] // 3
    vmem = pl.BlockSpec(memory_space=pltpu.VMEM)
    return pl.pallas_call(
        correlate_kernel,
        in_specs=[pl.BlockSpec(memory_space=pltpu.SMEM)] + [vmem] * 5,
        out_specs=pl.BlockSpec(memory_space=pltpu.HBM),
        out_shape=jax.ShapeDtypeStruct((2, CH, CH, lags), jnp.bfloat16),
        scratch_shapes=[
            pltpu.VMEM((2 * CH, depth), jnp.bfloat16),
            pltpu.VMEM((CH, depth), jnp.float32),
            pltpu.VMEM((BLOCK * 2 * terms, depth), jnp.bfloat16),
            pltpu.VMEM((BLOCK * 2 * terms, depth), jnp.bfloat16),
            pltpu.VMEM((2 * CH, BLOCK * 2 * terms), jnp.bfloat16),
            pltpu.VMEM((2 * CH, BLOCK * 2 * terms), jnp.bfloat16),
            pltpu.VMEM((4, 2, BLOCK, CH, lags), jnp.bfloat16),
            pltpu.SemaphoreType.DMA((4,)),
        ],
        compiler_params=pltpu.CompilerParams(vmem_limit_bytes=60 * 1024 * 1024),
        name="correlate",
    )(order, own, first, second, jnp.asarray(rows), jnp.asarray(spread))


def swap(tile, mask):
    count = lax.axis_size("blk")
    return lax.ppermute(tile, "blk", [(low, low ^ mask) for low in range(count)])


def exchange(mask, moving):
    count = lax.axis_size("blk")
    full = count - 1
    first = swap(moving, full)
    return moving, first, swap(first, mask ^ full) if 2 * mask >= count else swap(moving, mask)


def deliver(me, mask, key, records, plan):
    owners = lax.axis_size("blk")
    held, nfft = records.shape
    capacity = max(16, 2 * held // owners)
    whole = full_plan(capacity, nfft // 128)
    table = jnp.asarray(forward_table(nfft, F))
    if owners > 16:
        plans = (whole,) * owners
        (outgoing,) = pack(me, key, records, capacity, plans, False)
        arrived = [lax.all_to_all(outgoing, "blk", split_axis=0, concat_axis=0, tiled=True)]
        return whiten(me, mask, arrived, table, capacity, plans, None)
    half = owners // 2
    plans = (whole,) + (plan(capacity, nfft // 128),) * (owners - 1)
    outgoing = pack(me, key, records, capacity, plans, True)
    places = [half]
    for distance in range(1, half):
        places += [distance, half + distance]
    arrived = [swap(outgoing[distance], distance) for distance in places] + [outgoing[0]]
    places.append(0)
    ordered = tuple(plans[distance] for distance in places)
    return whiten(me, mask, arrived, table, capacity, ordered, places)


def local(records, dest, slot, valid, masks):
    owners = lax.axis_size("blk")
    held, nfft = records.shape
    full = owners - 1
    me = lax.axis_index("blk").astype(jnp.int32).reshape(1)
    mask = (masks[0] + masks[1] - full).reshape(1)
    key = (((dest << SLOT_BITS) + slot << VALID_BITS) + valid).reshape(1, held)
    if owners <= 16:
        tile, branch = deliver(me, mask, key, records, short_plan)
        known = [functools.partial(exchange, m) for m in range(1, full)]

        def again(tile):
            tile, branch = deliver(me, mask, key, records, full_plan)
            return lax.switch(branch[0], known, tile)

        own, first, second = lax.switch(branch[0], known + [again], tile)
    else:
        own, _ = deliver(me, mask, key, records, full_plan)
        second = own
        for bit in range(owners.bit_length() - 1):
            second = jnp.where(mask >> bit & 1 == 1, swap(second, 1 << bit), second)
        first = swap(own, full)
    order = (masks[:1] != full).astype(jnp.int32)
    return correlate(order, own, first, second, nfft, LAGS)


def solution(mesh):
    return jax.shard_map(
        local,
        mesh=mesh,
        in_specs=(
            P(("groups", "blk"), None),
            P(("groups", "blk"), None),
            P(("groups", "blk"), None),
            P(("groups", "blk"), None),
            P(),
        ),
        out_specs=P(None, ("groups", "blk"), None, None),
        check_vma=False,
    )
```

```python
import functools
import math

import jax
import jax.numpy as jnp
import numpy as np
from jax import lax
from jax.experimental import pallas as pl
from jax.experimental.pallas import tpu as pltpu
from jax.sharding import PartitionSpec as P

CH = 128
F = 256
LAGS = 128
W = 2
SLOT_BITS = 8
VALID_BITS = 12
LOW_BITS = 4


def bin_order(bins):
    return np.concatenate([np.arange(2, bins + 1, 2), np.arange(1, bins + 1, 2)])


def forward_table(nfft, bins):
    sample = np.arange(nfft // 2, dtype=np.int64)[:, None]
    angle = (sample * bin_order(bins)[None, :] % nfft) * (2.0 * math.pi / nfft)
    cos, sin = np.cos(angle), np.sin(angle)
    half = bins // 2
    table = [cos[:, :half], -sin[:, :half], cos[:, half:], -sin[:, half:]]
    return np.concatenate(table, axis=1).astype(np.float32).astype(jnp.bfloat16)


def lag_tables(nfft, bins, lags, scale):
    half = lags // 2
    count = lags + 1
    place = np.arange(count)
    middle = ((count - 1 - 2 * place) / 2.0) ** 2 * math.cos(2.0 * math.pi * bins / nfft)
    aside = (place[1:] * (count - place[1:])) / 2.0
    _, basis = np.linalg.eigh(np.diag(middle) + np.diag(aside, 1) + np.diag(aside, -1))
    basis = basis[:, ::-1][:, :half]
    even, odd = basis[:, 0::2], basis[:, 1::2]
    even = even * np.sign(even[half])
    odd = odd * np.sign(odd[half + 1])
    freq = bin_order(bins)[None, :]
    angle = (freq * (place[:, None] - half) % nfft) * (2.0 * math.pi / nfft)
    rows = [even.T @ np.cos(angle), odd.T @ -np.sin(angle)]
    rest = np.cos(angle) - np.sin(angle) - even @ rows[0] - odd @ rows[1]
    assert np.abs(rest).max() < 1e-7
    rows = np.concatenate(rows + [-rows[1]])
    basis = np.concatenate([even, odd], axis=1)[:lags].T * scale
    blank = np.zeros_like(basis)
    spread = np.concatenate(
        [np.concatenate([basis if k == n else blank for n in range(4)], axis=1) for k in range(4)]
    )

    def narrow(table):
        return (np.round(table * 2.0**28) / 2.0**28).astype(np.float32).astype(jnp.bfloat16)

    return narrow(rows), narrow(spread)


def iota(shape, dim):
    return lax.broadcasted_iota(jnp.int32, shape, dim)


LABELS = 8


def full_plan(capacity, chunks):
    return (capacity,) * chunks


def short_plan(capacity, chunks):
    def rows(c):
        return capacity if 16 * c < 11 * chunks else capacity * 3 // 4 if 16 * c < 13 * chunks else capacity // 2

    return tuple(rows(c) for c in range(chunks))


def pack_kernel(owners, capacity, plans, me_ref, key_ref, records_ref, *out_refs):
    held, nfft = records_ref.shape
    rows = owners * capacity
    width = 512
    key = key_ref[...]
    part = key >> (SLOT_BITS + VALID_BITS)
    if len(out_refs) > 1:
        part = part ^ me_ref[0]
    valid = key & ((1 << VALID_BITS) - 1)
    first = valid * held + (held - 1 - iota((1, held), 1))

    def column(row):
        wide = jnp.transpose(jnp.broadcast_to(row.astype(jnp.float32), (128, held)))
        return jnp.concatenate([wide] * (held // 128), axis=1)

    same = column(part) == part.astype(jnp.float32)
    before = jnp.where(same & (column(first) > first.astype(jnp.float32)), 1.0, 0.0)
    rank = jnp.sum(before, axis=0, keepdims=True).astype(jnp.int32)
    over = jnp.zeros((1, held), jnp.int32)
    for plan in sorted(set(plans)):
        member = functools.reduce(
            jnp.logical_or, [part == d for d in range(owners) if plans[d] == plan]
        )
        for size in sorted(set(plan)):
            if size < capacity:
                reach = 128 * sum(count > size for count in plan)
                over += jnp.where(member & (rank >= size) & (valid > reach), 1, 0)
    over = jnp.max(jnp.minimum(over, 1).astype(jnp.float32), axis=1, keepdims=True)
    position = part * capacity + rank
    order = (iota((rows, held), 0) == position).astype(jnp.float32).astype(jnp.bfloat16)
    slot = (key >> VALID_BITS) & ((1 << SLOT_BITS) - 1)
    row = iota((16, held), 0)
    labels = jnp.where(
        row == 0,
        slot,
        jnp.where(
            row == 1,
            valid >> LOW_BITS,
            jnp.where(row == 2, valid & ((1 << LOW_BITS) - 1), 0),
        ),
    )
    moved = lax.dot_general(
        labels.astype(jnp.float32).astype(jnp.bfloat16),
        order,
        (((1,), (1,)), ((), ())),
        preferred_element_type=jnp.float32,
    )
    moved = jnp.where(iota((16, rows), 0) == 3, over, moved).astype(jnp.bfloat16)

    def put(d, at, value):
        if len(out_refs) > 1:
            out_refs[d][at : at + value.shape[0], :] = value
        else:
            out_refs[0][d, at : at + value.shape[0], :] = value

    for d in range(owners):
        at = d * capacity // 128 * 128
        put(d, sum(plans[d]), moved[:LABELS, at : at + 128])
    for begin in range(0, nfft, width):
        ordered = jnp.dot(
            order, records_ref[:, begin : begin + width], preferred_element_type=jnp.float32
        ).astype(jnp.bfloat16)
        for lane in range(0, width, 128):
            c = (begin + lane) // 128
            for d in range(owners):
                top = d * capacity
                put(d, sum(plans[d][:c]), ordered[top : top + plans[d][c], lane : lane + 128])


def pack(me, key, records, capacity, plans, split):
    held, nfft = records.shape
    owners = len(plans)
    vmem = pl.BlockSpec(memory_space=pltpu.VMEM)
    shapes = [(sum(plan) + LABELS, 128) for plan in plans]
    if not split:
        shapes = [(owners,) + shapes[0]]
    return pl.pallas_call(
        functools.partial(pack_kernel, owners, capacity, plans),
        in_specs=[pl.BlockSpec(memory_space=pltpu.SMEM), vmem, vmem],
        out_specs=[vmem] * len(shapes),
        out_shape=[jax.ShapeDtypeStruct(shape, jnp.bfloat16) for shape in shapes],
        compiler_params=pltpu.CompilerParams(vmem_limit_bytes=48 * 1024 * 1024),
        name="pack",
    )(me, key, records)


def whiten_kernel(capacity, plans, places, me_ref, mask_ref, *refs):
    *arrived_refs, table_hbm, low_ref, high_ref, branch_ref, table_ref, trace_ref, spectrum_ref, sems = refs
    owners = len(plans)
    split = len(arrived_refs) > 1
    nfft = trace_ref.shape[1]
    rows = owners * capacity
    slots = CH * W
    bins = table_ref.shape[1] // 2
    shift = capacity.bit_length() - 1
    width = 256
    depth = 512
    loads = [
        pltpu.make_async_copy(
            table_hbm.at[pl.ds(at, depth)], table_ref.at[pl.ds(at, depth)], sems.at[at // depth]
        )
        for at in range(0, nfft // 2, depth)
    ]
    for copy in loads:
        copy.start()

    def take(c):
        if not split:
            at, count = sum(plans[0][:c]), plans[0][c] if c < len(plans[0]) else LABELS
            return arrived_refs[0][:, at : at + count, :].reshape(owners * count, 128)
        pieces = []
        for ref, plan in zip(arrived_refs, plans):
            at, count = sum(plan[:c]), plan[c] if c < len(plan) else LABELS
            pieces.append(ref[at : at + count, :])
            if c < len(plan) and count < capacity:
                pieces.append(jnp.zeros((capacity - count, 128), jnp.bfloat16))
        return jnp.concatenate(pieces, axis=0)

    labels = take(len(plans[0])).astype(jnp.float32).reshape(owners, LABELS, 128)
    which = iota((owners, LABELS, 128), 1)
    over = jnp.max(jnp.where(which == 3, labels, 0.0))
    branch_ref[0] = jnp.where(over > 0.0, owners - 2, mask_ref[0] - 1)
    parts = jnp.concatenate(
        [jnp.sum(jnp.where(which == k, labels, 0.0), axis=1) for k in range(3)], axis=0
    )
    if split:
        part = iota((1, rows), 1) >> shift
        place = functools.reduce(
            lambda total, p: total + jnp.where(part == p, places[p], 0),
            range(owners),
            jnp.zeros((1, rows), jnp.int32),
        )
    else:
        place = me_ref[0]
    base = (place * capacity) & 127
    pick = iota((128, rows), 0) == base + (iota((128, rows), 1) & (capacity - 1))
    picked = jnp.dot(
        parts.astype(jnp.bfloat16),
        pick.astype(jnp.float32).astype(jnp.bfloat16),
        preferred_element_type=jnp.float32,
    )
    source = iota((owners, rows), 0) == iota((owners, rows), 1) >> shift
    rowed = [
        jnp.sum(
            jnp.where(source, picked[k * owners : (k + 1) * owners], 0.0), axis=0, keepdims=True
        )
        for k in range(3)
    ]
    slot_row = rowed[0].astype(jnp.int32)
    place = (slot_row & (W - 1)) * CH + (slot_row >> (W.bit_length() - 1))
    valid_row = rowed[1] * float(1 << LOW_BITS) + rowed[2]
    scatter = (iota((slots, rows), 0) == place).astype(jnp.float32).astype(jnp.bfloat16)
    valid_col = jnp.transpose(jnp.broadcast_to(valid_row, (128, rows))).astype(jnp.int32)
    power = jnp.zeros((slots, 128), jnp.float32)
    for begin in range(0, nfft, width):
        lanes = range(begin, begin + width, 128)
        inside = jnp.concatenate(
            [
                (iota((rows, 128), 1) + lane < valid_col).astype(jnp.float32).astype(jnp.bfloat16)
                for lane in lanes
            ],
            axis=1,
        )
        arrived = jnp.concatenate([take(lane // 128) for lane in lanes], axis=1)
        summed = jnp.dot(scatter, arrived * inside, preferred_element_type=jnp.float32)
        coverage = jnp.dot(scatter, inside, preferred_element_type=jnp.float32)
        trace = summed / jnp.maximum(coverage, 1.0)
        trace_ref[:, begin : begin + width] = trace
        square = trace * trace
        for lane in range(0, width, 128):
            power = power + square[:, lane : lane + 128]
    meansq = jnp.sum(power, axis=1, keepdims=True) * (1.0 / nfft)
    gain = lax.rsqrt(meansq + 1e-06)
    for begin in range(0, nfft // 2, depth):
        loads[begin // depth].wait()
        near = trace_ref[:, begin : begin + depth] * gain
        far = trace_ref[:, begin + nfft // 2 : begin + nfft // 2 + depth] * gain
        for at, folded in ((0, near + far), (bins, near - far)):
            part = jnp.dot(
                folded.astype(jnp.bfloat16),
                table_ref[begin : begin + depth, at : at + bins],
                preferred_element_type=jnp.float32,
            )
            if begin == 0:
                spectrum_ref[:, at : at + bins] = part
            else:
                spectrum_ref[:, at : at + bins] += part
    half = bins // 2
    for at in (0, bins):
        real_part = spectrum_ref[:, at : at + half]
        imag_part = spectrum_ref[:, at + half : at + bins]
        amplitude = lax.rsqrt(
            jnp.maximum(real_part * real_part + imag_part * imag_part, nfft / 4.0)
        )
        for part, offset in ((real_part, 0), (imag_part, bins)):
            white = (part * amplitude).astype(jnp.bfloat16)
            for w in range(W):
                lane = w * 2 * bins + offset + at // 2
                top = w * CH
                low_ref[:, lane : lane + half] = white[top : top + CH // 2]
                high_ref[:, lane : lane + half] = white[top + CH // 2 : top + CH]


def whiten(me, mask, arrived, table, capacity, plans, places):
    nfft, width = 2 * table.shape[0], table.shape[1]
    vmem = pl.BlockSpec(memory_space=pltpu.VMEM)
    smem = pl.BlockSpec(memory_space=pltpu.SMEM)
    return pl.pallas_call(
        functools.partial(whiten_kernel, capacity, plans, places),
        in_specs=[smem, smem]
        + [vmem] * len(arrived)
        + [pl.BlockSpec(memory_space=pltpu.HBM)],
        out_specs=[vmem, vmem, smem],
        out_shape=[
            jax.ShapeDtypeStruct((CH // 2, W * width), jnp.bfloat16),
            jax.ShapeDtypeStruct((CH // 2, W * width), jnp.bfloat16),
            jax.ShapeDtypeStruct((1,), jnp.int32),
        ],
        scratch_shapes=[
            pltpu.VMEM(table.shape, jnp.bfloat16),
            pltpu.VMEM((CH * W, nfft), jnp.float32),
            pltpu.VMEM((CH * W, width), jnp.float32),
            pltpu.SemaphoreType.DMA((nfft // 1024,)),
        ],
        compiler_params=pltpu.CompilerParams(vmem_limit_bytes=50 * 1024 * 1024),
        name="whiten",
    )(me, mask, *arrived, table)


BLOCK = 8


def correlate_kernel(
    order_ref, own_low, own_high, first_low, first_high, second_low, second_high,
    rows_ref, spread_ref, out_hbm,
    both_ref, wide_ref, turned_a, turned_b, found_a, found_b, out_ref, sems,
):
    bins = rows_ref.shape[1]
    terms = rows_ref.shape[0] // 3
    lags = out_ref.shape[4]
    blocks = CH // BLOCK
    turned, found = (turned_a, turned_b), (found_a, found_b)

    def turn(block, slot):
        even = rows_ref[:terms, :]
        odd = rows_ref[terms : 2 * terms, :]
        minus = rows_ref[2 * terms :, :]
        for k in range(BLOCK):
            row = jnp.minimum(block * BLOCK + k, CH - 1)
            u = wide_ref[pl.ds(row, 1), :]
            top = slice(2 * k * terms, (2 * k + 1) * terms)
            low = slice((2 * k + 1) * terms, (2 * k + 2) * terms)
            for w in range(W):
                at = w * 2 * bins
                real, imag = slice(at, at + bins), slice(at + bins, at + 2 * bins)
                ur = jnp.broadcast_to(u[:, real], (terms, bins)).astype(jnp.bfloat16)
                ui = jnp.broadcast_to(u[:, imag], (terms, bins)).astype(jnp.bfloat16)
                turned[slot][top, real] = ur * even
                turned[slot][top, imag] = ui * even
                turned[slot][low, real] = ui * odd
                turned[slot][low, imag] = ur * minus

    def find(slot):
        found[slot][...] = lax.dot_general(
            both_ref[...],
            turned[slot][...],
            (((1,), (1,)), ((), ())),
            preferred_element_type=jnp.float32,
        ).astype(jnp.bfloat16)

    def spread(slot, place):
        for k in range(0, BLOCK, 4):
            lagged = jnp.dot(
                found[slot][:, 2 * k * terms : 2 * (k + 4) * terms],
                spread_ref[...],
                preferred_element_type=jnp.float32,
            ).astype(jnp.bfloat16)
            for n in range(4):
                for r in range(2):
                    out_ref[place, r, k + n] = lagged[
                        r * CH : (r + 1) * CH, n * lags : (n + 1) * lags
                    ]

    def write(block):
        start = pl.multiple_of(block * BLOCK, BLOCK)
        return pltpu.make_async_copy(
            out_ref.at[block % 4], out_hbm.at[:, pl.ds(start, BLOCK)], sems.at[block % 4]
        )

    half = CH // 2
    wide_ref[:half, :] = own_low[...].astype(jnp.float32)
    wide_ref[half:, :] = own_high[...].astype(jnp.float32)
    at = pl.multiple_of(order_ref[0] * CH, CH)
    both_ref[pl.ds(at, half), :] = first_low[...]
    both_ref[pl.ds(at + half, half), :] = first_high[...]
    both_ref[pl.ds(CH - at, half), :] = second_low[...]
    both_ref[pl.ds(CH - at + half, half), :] = second_high[...]
    turn(0, 0)
    turn(1, 1)
    find(0)

    @pl.loop(0, blocks // 2)
    def _(n):
        @pl.when(n >= 2)
        def _():
            write(2 * n - 4).wait()
            write(2 * n - 3).wait()

        place = n % 2 * 2
        turn(2 * n + 2, 0)
        find(1)
        spread(0, place)
        turn(2 * n + 3, 1)
        find(0)
        spread(1, place + 1)
        write(2 * n).start()
        write(2 * n + 1).start()

    for block in range(blocks - 4, blocks):
        write(block).wait()


def correlate(order, own, first, second, nfft, lags):
    depth = own[0].shape[1]
    bins = depth // (2 * W)
    rows, spread = lag_tables(nfft, bins, lags, 1.0 / math.sqrt(W * bins))
    terms = rows.shape[0] // 3
    vmem = pl.BlockSpec(memory_space=pltpu.VMEM)
    return pl.pallas_call(
        correlate_kernel,
        in_specs=[pl.BlockSpec(memory_space=pltpu.SMEM)] + [vmem] * 8,
        out_specs=pl.BlockSpec(memory_space=pltpu.HBM),
        out_shape=jax.ShapeDtypeStruct((2, CH, CH, lags), jnp.bfloat16),
        scratch_shapes=[
            pltpu.VMEM((2 * CH, depth), jnp.bfloat16),
            pltpu.VMEM((CH, depth), jnp.float32),
            pltpu.VMEM((BLOCK * 2 * terms, depth), jnp.bfloat16),
            pltpu.VMEM((BLOCK * 2 * terms, depth), jnp.bfloat16),
            pltpu.VMEM((2 * CH, BLOCK * 2 * terms), jnp.bfloat16),
            pltpu.VMEM((2 * CH, BLOCK * 2 * terms), jnp.bfloat16),
            pltpu.VMEM((4, 2, BLOCK, CH, lags), jnp.bfloat16),
            pltpu.SemaphoreType.DMA((4,)),
        ],
        compiler_params=pltpu.CompilerParams(vmem_limit_bytes=60 * 1024 * 1024),
        name="correlate",
    )(order, *own, *first, *second, jnp.asarray(rows), jnp.asarray(spread))


def swap(block, mask):
    count = lax.axis_size("blk")
    return lax.ppermute(block, "blk", [(low, low ^ mask) for low in range(count)])


def swap_halves(tile, mask):
    return tuple(swap(half, mask) for half in tile)


def exchange(mask, moving):
    count = lax.axis_size("blk")
    full = count - 1
    first = swap_halves(moving, full)
    if 2 * mask >= count:
        return moving, first, swap_halves(first, mask ^ full)
    return moving, first, swap_halves(moving, mask)


def deliver(me, mask, key, records, plan):
    owners = lax.axis_size("blk")
    held, nfft = records.shape
    capacity = max(16, 2 * held // owners)
    whole = full_plan(capacity, nfft // 128)
    table = jnp.asarray(forward_table(nfft, F))
    if owners > 16:
        plans = (whole,) * owners
        (outgoing,) = pack(me, key, records, capacity, plans, False)
        arrived = [lax.all_to_all(outgoing, "blk", split_axis=0, concat_axis=0, tiled=True)]
        *tile, branch = whiten(me, mask, arrived, table, capacity, plans, None)
        return tuple(tile), branch
    half = owners // 2
    plans = (whole,) + (plan(capacity, nfft // 128),) * (owners - 1)
    outgoing = pack(me, key, records, capacity, plans, True)
    places = [half]
    for distance in range(1, half):
        places += [distance, half + distance]
    arrived = [swap(outgoing[distance], distance) for distance in places] + [outgoing[0]]
    places.append(0)
    ordered = tuple(plans[distance] for distance in places)
    *tile, branch = whiten(me, mask, arrived, table, capacity, ordered, places)
    return tuple(tile), branch


def local(records, dest, slot, valid, masks):
    owners = lax.axis_size("blk")
    held, nfft = records.shape
    full = owners - 1
    me = lax.axis_index("blk").astype(jnp.int32).reshape(1)
    mask = (masks[0] + masks[1] - full).reshape(1)
    key = (((dest << SLOT_BITS) + slot << VALID_BITS) + valid).reshape(1, held)
    if owners <= 16:
        tile, branch = deliver(me, mask, key, records, short_plan)
        known = [functools.partial(exchange, m) for m in range(1, full)]

        def again(tile):
            tile, branch = deliver(me, mask, key, records, full_plan)
            return lax.switch(branch[0], known, tile)

        own, first, second = lax.switch(branch[0], known + [again], tile)
    else:
        own, _ = deliver(me, mask, key, records, full_plan)
        second = own
        for bit in range(owners.bit_length() - 1):
            moved = swap_halves(second, 1 << bit)
            flip = mask >> bit & 1 == 1
            second = tuple(jnp.where(flip, new, old) for new, old in zip(moved, second))
        first = swap_halves(own, full)
    order = (masks[:1] != full).astype(jnp.int32)
    return correlate(order, own, first, second, nfft, LAGS)


def solution(mesh):
    return jax.shard_map(
        local,
        mesh=mesh,
        in_specs=(
            P(("groups", "blk"), None),
            P(("groups", "blk"), None),
            P(("groups", "blk"), None),
            P(("groups", "blk"), None),
            P(),
        ),
        out_specs=P(None, ("groups", "blk"), None, None),
        check_vma=False,
    )
```

```python
import functools
import math

import jax
import jax.numpy as jnp
import numpy as np
from jax import lax
from jax.experimental import pallas as pl
from jax.experimental.pallas import tpu as pltpu
from jax.sharding import PartitionSpec as P

CH = 128
F = 256
LAGS = 128
W = 2
SLOT_BITS = 8
VALID_BITS = 12
LOW_BITS = 4


def bin_order(bins):
    return np.concatenate([np.arange(2, bins + 1, 2), np.arange(1, bins + 1, 2)])


def forward_table(nfft, bins):
    sample = np.arange(nfft // 2, dtype=np.int64)[:, None]
    angle = (sample * bin_order(bins)[None, :] % nfft) * (2.0 * math.pi / nfft)
    cos, sin = np.cos(angle), np.sin(angle)
    half = bins // 2
    table = [cos[:, :half], -sin[:, :half], cos[:, half:], -sin[:, half:]]
    return np.concatenate(table, axis=1).astype(np.float32).astype(jnp.bfloat16)


def lag_tables(nfft, bins, lags, scale):
    half = lags // 2
    count = lags + 1
    place = np.arange(count)
    middle = ((count - 1 - 2 * place) / 2.0) ** 2 * math.cos(2.0 * math.pi * bins / nfft)
    aside = (place[1:] * (count - place[1:])) / 2.0
    _, basis = np.linalg.eigh(np.diag(middle) + np.diag(aside, 1) + np.diag(aside, -1))
    basis = basis[:, ::-1][:, :half]
    even, odd = basis[:, 0::2], basis[:, 1::2]
    even = even * np.sign(even[half])
    odd = odd * np.sign(odd[half + 1])
    freq = bin_order(bins)[None, :]
    angle = (freq * (place[:, None] - half) % nfft) * (2.0 * math.pi / nfft)
    rows = [even.T @ np.cos(angle), odd.T @ -np.sin(angle)]
    rest = np.cos(angle) - np.sin(angle) - even @ rows[0] - odd @ rows[1]
    assert np.abs(rest).max() < 1e-7
    rows = np.concatenate(rows + [-rows[1]])
    basis = np.concatenate([even, odd], axis=1)[:lags].T * scale
    blank = np.zeros_like(basis)
    spread = np.block([[basis, blank], [blank, basis]])

    def narrow(table):
        return (np.round(table * 2.0**28) / 2.0**28).astype(np.float32).astype(jnp.bfloat16)

    return narrow(rows), narrow(spread)


def iota(shape, dim):
    return lax.broadcasted_iota(jnp.int32, shape, dim)


LABELS = 8


def full_plan(capacity, chunks):
    return (capacity,) * chunks


def short_plan(capacity, chunks):
    eighths = (8, 8, 8, 8, 8, 8, 8, 8, 8, 7, 7, 6, 6, 5, 4, 3)
    return tuple(capacity * eighths[c * len(eighths) // chunks] // 8 for c in range(chunks))


def pack_kernel(owners, capacity, plans, me_ref, key_ref, records_ref, *out_refs):
    held, nfft = records_ref.shape
    rows = owners * capacity
    width = 512
    key = key_ref[...]
    part = key >> (SLOT_BITS + VALID_BITS)
    if len(out_refs) > 1:
        part = part ^ me_ref[0]
    valid = key & ((1 << VALID_BITS) - 1)
    first = valid * held + (held - 1 - iota((1, held), 1))

    def column(row):
        wide = jnp.transpose(jnp.broadcast_to(row.astype(jnp.float32), (128, held)))
        return jnp.concatenate([wide] * (held // 128), axis=1)

    same = column(part) == part.astype(jnp.float32)
    before = jnp.where(same & (column(first) > first.astype(jnp.float32)), 1.0, 0.0)
    rank = jnp.sum(before, axis=0, keepdims=True).astype(jnp.int32)
    over = jnp.zeros((1, held), jnp.int32)
    for plan in sorted(set(plans)):
        member = functools.reduce(
            jnp.logical_or, [part == d for d in range(owners) if plans[d] == plan]
        )
        for size in sorted(set(plan)):
            if size < capacity:
                reach = 128 * sum(count > size for count in plan)
                over += jnp.where(member & (rank >= size) & (valid > reach), 1, 0)
    over = jnp.max(jnp.minimum(over, 1).astype(jnp.float32), axis=1, keepdims=True)
    position = part * capacity + rank
    order = (iota((rows, held), 0) == position).astype(jnp.float32).astype(jnp.bfloat16)
    slot = (key >> VALID_BITS) & ((1 << SLOT_BITS) - 1)
    row = iota((16, held), 0)
    labels = jnp.where(
        row == 0,
        slot,
        jnp.where(
            row == 1,
            valid >> LOW_BITS,
            jnp.where(row == 2, valid & ((1 << LOW_BITS) - 1), 0),
        ),
    )
    moved = lax.dot_general(
        labels.astype(jnp.float32).astype(jnp.bfloat16),
        order,
        (((1,), (1,)), ((), ())),
        preferred_element_type=jnp.float32,
    )
    moved = jnp.where(iota((16, rows), 0) == 3, over, moved).astype(jnp.bfloat16)

    def put(d, at, value):
        if len(out_refs) > 1:
            out_refs[d][at : at + value.shape[0], :] = value
        else:
            out_refs[0][d, at : at + value.shape[0], :] = value

    for d in range(owners):
        at = d * capacity // 128 * 128
        put(d, sum(plans[d]), moved[:LABELS, at : at + 128])
    for begin in range(0, nfft, width):
        ordered = jnp.dot(
            order, records_ref[:, begin : begin + width], preferred_element_type=jnp.float32
        ).astype(jnp.bfloat16)
        for lane in range(0, width, 128):
            c = (begin + lane) // 128
            for d in range(owners):
                top = d * capacity
                put(d, sum(plans[d][:c]), ordered[top : top + plans[d][c], lane : lane + 128])


def pack(me, key, records, capacity, plans, split):
    held, nfft = records.shape
    owners = len(plans)
    vmem = pl.BlockSpec(memory_space=pltpu.VMEM)
    shapes = [(sum(plan) + LABELS, 128) for plan in plans]
    if not split:
        shapes = [(owners,) + shapes[0]]
    return pl.pallas_call(
        functools.partial(pack_kernel, owners, capacity, plans),
        in_specs=[pl.BlockSpec(memory_space=pltpu.SMEM), vmem, vmem],
        out_specs=[vmem] * len(shapes),
        out_shape=[jax.ShapeDtypeStruct(shape, jnp.bfloat16) for shape in shapes],
        compiler_params=pltpu.CompilerParams(vmem_limit_bytes=48 * 1024 * 1024),
        name="pack",
    )(me, key, records)


def whiten_kernel(capacity, plans, places, me_ref, mask_ref, *refs):
    *arrived_refs, table_hbm, low_ref, high_ref, branch_ref, table_ref, trace_ref, spectrum_ref, sems = refs
    owners = len(plans)
    split = len(arrived_refs) > 1
    nfft = trace_ref.shape[1]
    rows = owners * capacity
    slots = CH * W
    bins = table_ref.shape[1] // 2
    shift = capacity.bit_length() - 1
    width = 256
    depth = 512
    loads = [
        pltpu.make_async_copy(
            table_hbm.at[pl.ds(at, depth)], table_ref.at[pl.ds(at, depth)], sems.at[at // depth]
        )
        for at in range(0, nfft // 2, depth)
    ]
    for copy in loads:
        copy.start()

    def take(c):
        if not split:
            at, count = sum(plans[0][:c]), plans[0][c] if c < len(plans[0]) else LABELS
            return arrived_refs[0][:, at : at + count, :].reshape(owners * count, 128)
        pieces = []
        for ref, plan in zip(arrived_refs, plans):
            at, count = sum(plan[:c]), plan[c] if c < len(plan) else LABELS
            pieces.append(ref[at : at + count, :])
            if c < len(plan) and count < capacity:
                pieces.append(jnp.zeros((capacity - count, 128), jnp.bfloat16))
        return jnp.concatenate(pieces, axis=0)

    labels = take(len(plans[0])).astype(jnp.float32).reshape(owners, LABELS, 128)
    which = iota((owners, LABELS, 128), 1)
    over = jnp.max(jnp.where(which == 3, labels, 0.0))
    branch_ref[0] = jnp.where(over > 0.0, owners - 2, mask_ref[0] - 1)
    parts = jnp.concatenate(
        [jnp.sum(jnp.where(which == k, labels, 0.0), axis=1) for k in range(3)], axis=0
    )
    if split:
        part = iota((1, rows), 1) >> shift
        place = functools.reduce(
            lambda total, p: total + jnp.where(part == p, places[p], 0),
            range(owners),
            jnp.zeros((1, rows), jnp.int32),
        )
    else:
        place = me_ref[0]
    base = (place * capacity) & 127
    pick = iota((128, rows), 0) == base + (iota((128, rows), 1) & (capacity - 1))
    picked = jnp.dot(
        parts.astype(jnp.bfloat16),
        pick.astype(jnp.float32).astype(jnp.bfloat16),
        preferred_element_type=jnp.float32,
    )
    source = iota((owners, rows), 0) == iota((owners, rows), 1) >> shift
    rowed = [
        jnp.sum(
            jnp.where(source, picked[k * owners : (k + 1) * owners], 0.0), axis=0, keepdims=True
        )
        for k in range(3)
    ]
    slot_row = rowed[0].astype(jnp.int32)
    place = (slot_row & (W - 1)) * CH + (slot_row >> (W.bit_length() - 1))
    valid_row = rowed[1] * float(1 << LOW_BITS) + rowed[2]
    scatter = (iota((slots, rows), 0) == place).astype(jnp.float32).astype(jnp.bfloat16)
    valid_col = jnp.transpose(jnp.broadcast_to(valid_row, (128, rows))).astype(jnp.int32)
    power = jnp.zeros((slots, 128), jnp.float32)
    for begin in range(0, nfft, width):
        lanes = range(begin, begin + width, 128)
        inside = jnp.concatenate(
            [
                (iota((rows, 128), 1) + lane < valid_col).astype(jnp.float32).astype(jnp.bfloat16)
                for lane in lanes
            ],
            axis=1,
        )
        arrived = jnp.concatenate([take(lane // 128) for lane in lanes], axis=1)
        summed = jnp.dot(scatter, arrived * inside, preferred_element_type=jnp.float32)
        coverage = jnp.dot(scatter, inside, preferred_element_type=jnp.float32)
        trace = summed / jnp.maximum(coverage, 1.0)
        trace_ref[:, begin : begin + width] = trace
        square = trace * trace
        for lane in range(0, width, 128):
            power = power + square[:, lane : lane + 128]
    meansq = jnp.sum(power, axis=1, keepdims=True) * (1.0 / nfft)
    gain = lax.rsqrt(meansq + 1e-06)
    for begin in range(0, nfft // 2, depth):
        loads[begin // depth].wait()
        near = trace_ref[:, begin : begin + depth] * gain
        far = trace_ref[:, begin + nfft // 2 : begin + nfft // 2 + depth] * gain
        for at, folded in ((0, near + far), (bins, near - far)):
            part = jnp.dot(
                folded.astype(jnp.bfloat16),
                table_ref[begin : begin + depth, at : at + bins],
                preferred_element_type=jnp.float32,
            )
            if begin == 0:
                spectrum_ref[:, at : at + bins] = part
            else:
                spectrum_ref[:, at : at + bins] += part
    half = bins // 2
    for at in (0, bins):
        real_part = spectrum_ref[:, at : at + half]
        imag_part = spectrum_ref[:, at + half : at + bins]
        amplitude = lax.rsqrt(
            jnp.maximum(real_part * real_part + imag_part * imag_part, nfft / 4.0)
        )
        for part, offset in ((real_part, 0), (imag_part, bins)):
            white = (part * amplitude).astype(jnp.bfloat16)
            for w in range(W):
                lane = w * 2 * bins + offset + at // 2
                top = w * CH
                low_ref[:, lane : lane + half] = white[top : top + CH // 2]
                high_ref[:, lane : lane + half] = white[top + CH // 2 : top + CH]


def whiten(me, mask, arrived, table, capacity, plans, places):
    nfft, width = 2 * table.shape[0], table.shape[1]
    vmem = pl.BlockSpec(memory_space=pltpu.VMEM)
    smem = pl.BlockSpec(memory_space=pltpu.SMEM)
    return pl.pallas_call(
        functools.partial(whiten_kernel, capacity, plans, places),
        in_specs=[smem, smem]
        + [vmem] * len(arrived)
        + [pl.BlockSpec(memory_space=pltpu.HBM)],
        out_specs=[vmem, vmem, smem],
        out_shape=[
            jax.ShapeDtypeStruct((CH // 2, W * width), jnp.bfloat16),
            jax.ShapeDtypeStruct((CH // 2, W * width), jnp.bfloat16),
            jax.ShapeDtypeStruct((1,), jnp.int32),
        ],
        scratch_shapes=[
            pltpu.VMEM(table.shape, jnp.bfloat16),
            pltpu.VMEM((CH * W, nfft), jnp.float32),
            pltpu.VMEM((CH * W, width), jnp.float32),
            pltpu.SemaphoreType.DMA((nfft // 1024,)),
        ],
        compiler_params=pltpu.CompilerParams(vmem_limit_bytes=50 * 1024 * 1024),
        name="whiten",
    )(me, mask, *arrived, table)


BLOCK = 8


def correlate_kernel(
    order_ref, own_low, own_high, first_low, first_high, second_low, second_high,
    rows_ref, spread_ref, out_hbm,
    both_ref, wide_ref, turned_a, turned_b, found_a, found_b, out_ref, sems,
):
    bins = rows_ref.shape[1]
    terms = rows_ref.shape[0] // 3
    lags = out_ref.shape[4]
    blocks = CH // BLOCK
    turned, found = (turned_a, turned_b), (found_a, found_b)

    def turn(block, slot):
        even = rows_ref[:terms, :]
        odd = rows_ref[terms : 2 * terms, :]
        minus = rows_ref[2 * terms :, :]
        for k in range(BLOCK):
            row = jnp.minimum(block * BLOCK + k, CH - 1)
            u = wide_ref[pl.ds(row, 1), :]
            top = slice(2 * k * terms, (2 * k + 1) * terms)
            low = slice((2 * k + 1) * terms, (2 * k + 2) * terms)
            for w in range(W):
                at = w * 2 * bins
                real, imag = slice(at, at + bins), slice(at + bins, at + 2 * bins)
                ur = jnp.broadcast_to(u[:, real], (terms, bins)).astype(jnp.bfloat16)
                ui = jnp.broadcast_to(u[:, imag], (terms, bins)).astype(jnp.bfloat16)
                turned[slot][top, real] = ur * even
                turned[slot][top, imag] = ui * even
                turned[slot][low, real] = ui * odd
                turned[slot][low, imag] = ur * minus

    def find(slot):
        found[slot][...] = lax.dot_general(
            both_ref[...],
            turned[slot][...],
            (((1,), (1,)), ((), ())),
            preferred_element_type=jnp.float32,
        ).astype(jnp.bfloat16)

    def spread(slot, place):
        for k in range(0, BLOCK, 2):
            for r in range(2):
                lagged = jnp.dot(
                    found[slot][r * CH : (r + 1) * CH, 2 * k * terms : 2 * (k + 2) * terms],
                    spread_ref[...],
                    preferred_element_type=jnp.float32,
                ).astype(jnp.bfloat16)
                for n in range(2):
                    out_ref[place, r, k + n] = lagged[:, n * lags : (n + 1) * lags]

    def write(block):
        start = pl.multiple_of(block * BLOCK, BLOCK)
        return pltpu.make_async_copy(
            out_ref.at[block % 4], out_hbm.at[:, pl.ds(start, BLOCK)], sems.at[block % 4]
        )

    half = CH // 2
    wide_ref[:half, :] = own_low[...].astype(jnp.float32)
    wide_ref[half:, :] = own_high[...].astype(jnp.float32)
    at = pl.multiple_of(order_ref[0] * CH, CH)
    both_ref[pl.ds(at, half), :] = first_low[...]
    both_ref[pl.ds(at + half, half), :] = first_high[...]
    both_ref[pl.ds(CH - at, half), :] = second_low[...]
    both_ref[pl.ds(CH - at + half, half), :] = second_high[...]
    turn(0, 0)
    turn(1, 1)
    find(0)

    @pl.loop(0, blocks // 2)
    def _(n):
        @pl.when(n >= 2)
        def _():
            write(2 * n - 4).wait()
            write(2 * n - 3).wait()

        place = n % 2 * 2
        turn(2 * n + 2, 0)
        find(1)
        spread(0, place)
        turn(2 * n + 3, 1)
        find(0)
        spread(1, place + 1)
        write(2 * n).start()
        write(2 * n + 1).start()

    for block in range(blocks - 4, blocks):
        write(block).wait()


def correlate(order, own, first, second, nfft, lags):
    depth = own[0].shape[1]
    bins = depth // (2 * W)
    rows, spread = lag_tables(nfft, bins, lags, 1.0 / math.sqrt(W * bins))
    terms = rows.shape[0] // 3
    vmem = pl.BlockSpec(memory_space=pltpu.VMEM)
    return pl.pallas_call(
        correlate_kernel,
        in_specs=[pl.BlockSpec(memory_space=pltpu.SMEM)] + [vmem] * 8,
        out_specs=pl.BlockSpec(memory_space=pltpu.HBM),
        out_shape=jax.ShapeDtypeStruct((2, CH, CH, lags), jnp.bfloat16),
        scratch_shapes=[
            pltpu.VMEM((2 * CH, depth), jnp.bfloat16),
            pltpu.VMEM((CH, depth), jnp.float32),
            pltpu.VMEM((BLOCK * 2 * terms, depth), jnp.bfloat16),
            pltpu.VMEM((BLOCK * 2 * terms, depth), jnp.bfloat16),
            pltpu.VMEM((2 * CH, BLOCK * 2 * terms), jnp.bfloat16),
            pltpu.VMEM((2 * CH, BLOCK * 2 * terms), jnp.bfloat16),
            pltpu.VMEM((4, 2, BLOCK, CH, lags), jnp.bfloat16),
            pltpu.SemaphoreType.DMA((4,)),
        ],
        compiler_params=pltpu.CompilerParams(vmem_limit_bytes=60 * 1024 * 1024),
        name="correlate",
    )(order, *own, *first, *second, jnp.asarray(rows), jnp.asarray(spread))


def swap(block, mask):
    count = lax.axis_size("blk")
    return lax.ppermute(block, "blk", [(low, low ^ mask) for low in range(count)])


def swap_halves(tile, mask):
    return tuple(swap(half, mask) for half in tile)


def exchange(mask, moving):
    count = lax.axis_size("blk")
    full = count - 1
    first = swap_halves(moving, full)
    if 2 * mask >= count:
        return moving, first, swap_halves(first, mask ^ full)
    return moving, first, swap_halves(moving, mask)


def deliver(me, mask, key, records, plan):
    owners = lax.axis_size("blk")
    held, nfft = records.shape
    capacity = max(16, 2 * held // owners)
    whole = full_plan(capacity, nfft // 128)
    table = jnp.asarray(forward_table(nfft, F))
    if owners > 16:
        plans = (whole,) * owners
        (outgoing,) = pack(me, key, records, capacity, plans, False)
        arrived = [lax.all_to_all(outgoing, "blk", split_axis=0, concat_axis=0, tiled=True)]
        *tile, branch = whiten(me, mask, arrived, table, capacity, plans, None)
        return tuple(tile), branch
    half = owners // 2
    plans = (whole,) + (plan(capacity, nfft // 128),) * (owners - 1)
    outgoing = pack(me, key, records, capacity, plans, True)
    places = [half]
    for distance in range(1, half):
        places += [distance, half + distance]
    arrived = [swap(outgoing[distance], distance) for distance in places] + [outgoing[0]]
    places.append(0)
    ordered = tuple(plans[distance] for distance in places)
    *tile, branch = whiten(me, mask, arrived, table, capacity, ordered, places)
    return tuple(tile), branch


def local(records, dest, slot, valid, masks):
    owners = lax.axis_size("blk")
    held, nfft = records.shape
    full = owners - 1
    me = lax.axis_index("blk").astype(jnp.int32).reshape(1)
    mask = (masks[0] + masks[1] - full).reshape(1)
    key = (((dest << SLOT_BITS) + slot << VALID_BITS) + valid).reshape(1, held)
    if owners <= 16:
        tile, branch = deliver(me, mask, key, records, short_plan)
        known = [functools.partial(exchange, m) for m in range(1, full)]

        def again(tile):
            tile, branch = deliver(me, mask, key, records, full_plan)
            return lax.switch(branch[0], known, tile)

        own, first, second = lax.switch(branch[0], known + [again], tile)
    else:
        own, _ = deliver(me, mask, key, records, full_plan)
        second = own
        for bit in range(owners.bit_length() - 1):
            moved = swap_halves(second, 1 << bit)
            flip = mask >> bit & 1 == 1
            second = tuple(jnp.where(flip, new, old) for new, old in zip(moved, second))
        first = swap_halves(own, full)
    order = (masks[:1] != full).astype(jnp.int32)
    return correlate(order, own, first, second, nfft, LAGS)


def solution(mesh):
    return jax.shard_map(
        local,
        mesh=mesh,
        in_specs=(
            P(("groups", "blk"), None),
            P(("groups", "blk"), None),
            P(("groups", "blk"), None),
            P(("groups", "blk"), None),
            P(),
        ),
        out_specs=P(None, ("groups", "blk"), None, None),
        check_vma=False,
    )
```

```python
import functools
import math

import jax
import jax.numpy as jnp
import numpy as np
from jax import lax
from jax.experimental import pallas as pl
from jax.experimental.pallas import tpu as pltpu
from jax.sharding import PartitionSpec as P

CH = 128
F = 256
LAGS = 128
W = 2
SLOT_BITS = 8
VALID_BITS = 12
LOW_BITS = 4


def bin_order(bins):
    return np.concatenate([np.arange(2, bins + 1, 2), np.arange(1, bins + 1, 2)])


def forward_table(nfft, bins):
    sample = np.arange(nfft // 2, dtype=np.int64)[:, None]
    angle = (sample * bin_order(bins)[None, :] % nfft) * (2.0 * math.pi / nfft)
    cos, sin = np.cos(angle), np.sin(angle)
    half = bins // 2
    table = [cos[:, :half], -sin[:, :half], cos[:, half:], -sin[:, half:]]
    return np.concatenate(table, axis=1).astype(np.float32).astype(jnp.bfloat16)


def lag_tables(nfft, bins, lags, scale):
    half = lags // 2
    count = lags + 1
    place = np.arange(count)
    middle = ((count - 1 - 2 * place) / 2.0) ** 2 * math.cos(2.0 * math.pi * bins / nfft)
    aside = (place[1:] * (count - place[1:])) / 2.0
    _, basis = np.linalg.eigh(np.diag(middle) + np.diag(aside, 1) + np.diag(aside, -1))
    basis = basis[:, ::-1][:, :half]
    even, odd = basis[:, 0::2], basis[:, 1::2]
    even = even * np.sign(even[half])
    odd = odd * np.sign(odd[half + 1])
    freq = bin_order(bins)[None, :]
    angle = (freq * (place[:, None] - half) % nfft) * (2.0 * math.pi / nfft)
    rows = [even.T @ np.cos(angle), odd.T @ -np.sin(angle)]
    rest = np.cos(angle) - np.sin(angle) - even @ rows[0] - odd @ rows[1]
    assert np.abs(rest).max() < 1e-7
    rows = np.concatenate(rows + [-rows[1]])
    basis = np.concatenate([even, odd], axis=1)[:lags].T * scale
    blank = np.zeros_like(basis)
    spread = np.concatenate(
        [np.concatenate([basis if k == n else blank for n in range(4)], axis=1) for k in range(4)]
    )

    def narrow(table):
        return (np.round(table * 2.0**28) / 2.0**28).astype(np.float32).astype(jnp.bfloat16)

    return narrow(rows), narrow(spread)


def iota(shape, dim):
    return lax.broadcasted_iota(jnp.int32, shape, dim)


LABELS = 8


def full_plan(capacity, chunks):
    return (capacity,) * chunks


def short_plan(capacity, chunks):
    eighths = (8, 8, 8, 8, 8, 8, 8, 8, 8, 7, 7, 6, 6, 5, 4, 3)
    return tuple(capacity * eighths[c * len(eighths) // chunks] // 8 for c in range(chunks))


def pack_kernel(owners, capacity, plans, me_ref, key_ref, records_ref, *out_refs):
    held, nfft = records_ref.shape
    rows = owners * capacity
    width = 512
    key = key_ref[...]
    part = key >> (SLOT_BITS + VALID_BITS)
    if len(out_refs) > 1:
        part = part ^ me_ref[0]
    valid = key & ((1 << VALID_BITS) - 1)
    first = valid * held + (held - 1 - iota((1, held), 1))

    def column(row):
        wide = jnp.transpose(jnp.broadcast_to(row.astype(jnp.float32), (128, held)))
        return jnp.concatenate([wide] * (held // 128), axis=1)

    same = column(part) == part.astype(jnp.float32)
    before = jnp.where(same & (column(first) > first.astype(jnp.float32)), 1.0, 0.0)
    rank = jnp.sum(before, axis=0, keepdims=True).astype(jnp.int32)
    over = jnp.zeros((1, held), jnp.int32)
    for plan in sorted(set(plans)):
        member = functools.reduce(
            jnp.logical_or, [part == d for d in range(owners) if plans[d] == plan]
        )
        for size in sorted(set(plan)):
            if size < capacity:
                reach = 128 * sum(count > size for count in plan)
                over += jnp.where(member & (rank >= size) & (valid > reach), 1, 0)
    over = jnp.max(jnp.minimum(over, 1).astype(jnp.float32), axis=1, keepdims=True)
    position = part * capacity + rank
    order = (iota((rows, held), 0) == position).astype(jnp.float32).astype(jnp.bfloat16)
    slot = (key >> VALID_BITS) & ((1 << SLOT_BITS) - 1)
    row = iota((16, held), 0)
    labels = jnp.where(
        row == 0,
        slot,
        jnp.where(
            row == 1,
            valid >> LOW_BITS,
            jnp.where(row == 2, valid & ((1 << LOW_BITS) - 1), 0),
        ),
    )
    moved = lax.dot_general(
        labels.astype(jnp.float32).astype(jnp.bfloat16),
        order,
        (((1,), (1,)), ((), ())),
        preferred_element_type=jnp.float32,
    )
    moved = jnp.where(iota((16, rows), 0) == 3, over, moved).astype(jnp.bfloat16)

    def put(d, at, value):
        if len(out_refs) > 1:
            out_refs[d][at : at + value.shape[0], :] = value
        else:
            out_refs[0][d, at : at + value.shape[0], :] = value

    for d in range(owners):
        at = d * capacity // 128 * 128
        put(d, sum(plans[d]), moved[:LABELS, at : at + 128])
    for begin in range(0, nfft, width):
        ordered = jnp.dot(
            order, records_ref[:, begin : begin + width], preferred_element_type=jnp.float32
        ).astype(jnp.bfloat16)
        for lane in range(0, width, 128):
            c = (begin + lane) // 128
            for d in range(owners):
                top = d * capacity
                put(d, sum(plans[d][:c]), ordered[top : top + plans[d][c], lane : lane + 128])


def pack(me, key, records, capacity, plans, split):
    held, nfft = records.shape
    owners = len(plans)
    vmem = pl.BlockSpec(memory_space=pltpu.VMEM)
    shapes = [(sum(plan) + LABELS, 128) for plan in plans]
    if not split:
        shapes = [(owners,) + shapes[0]]
    return pl.pallas_call(
        functools.partial(pack_kernel, owners, capacity, plans),
        in_specs=[pl.BlockSpec(memory_space=pltpu.SMEM), vmem, vmem],
        out_specs=[vmem] * len(shapes),
        out_shape=[jax.ShapeDtypeStruct(shape, jnp.bfloat16) for shape in shapes],
        compiler_params=pltpu.CompilerParams(vmem_limit_bytes=48 * 1024 * 1024),
        name="pack",
    )(me, key, records)


def whiten_kernel(capacity, plans, places, me_ref, mask_ref, *refs):
    *arrived_refs, table_hbm, low_ref, high_ref, branch_ref, table_ref, trace_ref, spectrum_ref, sems = refs
    owners = len(plans)
    split = len(arrived_refs) > 1
    nfft = trace_ref.shape[1]
    rows = owners * capacity
    slots = CH * W
    bins = table_ref.shape[1] // 2
    shift = capacity.bit_length() - 1
    width = 256
    depth = 512
    loads = [
        pltpu.make_async_copy(
            table_hbm.at[pl.ds(at, depth)], table_ref.at[pl.ds(at, depth)], sems.at[at // depth]
        )
        for at in range(0, nfft // 2, depth)
    ]
    for copy in loads:
        copy.start()

    def take(c):
        if not split:
            at, count = sum(plans[0][:c]), plans[0][c] if c < len(plans[0]) else LABELS
            return arrived_refs[0][:, at : at + count, :].reshape(owners * count, 128)
        pieces = []
        for ref, plan in zip(arrived_refs, plans):
            at, count = sum(plan[:c]), plan[c] if c < len(plan) else LABELS
            pieces.append(ref[at : at + count, :])
            if c < len(plan) and count < capacity:
                pieces.append(jnp.zeros((capacity - count, 128), jnp.bfloat16))
        return jnp.concatenate(pieces, axis=0)

    labels = take(len(plans[0])).astype(jnp.float32).reshape(owners, LABELS, 128)
    which = iota((owners, LABELS, 128), 1)
    over = jnp.max(jnp.where(which == 3, labels, 0.0))
    branch_ref[0] = jnp.where(over > 0.0, owners - 2, mask_ref[0] - 1)
    parts = jnp.concatenate(
        [jnp.sum(jnp.where(which == k, labels, 0.0), axis=1) for k in range(3)], axis=0
    )
    if split:
        part = iota((1, rows), 1) >> shift
        place = functools.reduce(
            lambda total, p: total + jnp.where(part == p, places[p], 0),
            range(owners),
            jnp.zeros((1, rows), jnp.int32),
        )
    else:
        place = me_ref[0]
    base = (place * capacity) & 127
    pick = iota((128, rows), 0) == base + (iota((128, rows), 1) & (capacity - 1))
    picked = jnp.dot(
        parts.astype(jnp.bfloat16),
        pick.astype(jnp.float32).astype(jnp.bfloat16),
        preferred_element_type=jnp.float32,
    )
    source = iota((owners, rows), 0) == iota((owners, rows), 1) >> shift
    rowed = [
        jnp.sum(
            jnp.where(source, picked[k * owners : (k + 1) * owners], 0.0), axis=0, keepdims=True
        )
        for k in range(3)
    ]
    slot_row = rowed[0].astype(jnp.int32)
    place = (slot_row & (W - 1)) * CH + (slot_row >> (W.bit_length() - 1))
    valid_row = rowed[1] * float(1 << LOW_BITS) + rowed[2]
    scatter = (iota((slots, rows), 0) == place).astype(jnp.float32).astype(jnp.bfloat16)
    valid_col = jnp.transpose(jnp.broadcast_to(valid_row, (128, rows))).astype(jnp.int32)
    power = jnp.zeros((slots, 128), jnp.float32)
    for begin in range(0, nfft, width):
        lanes = range(begin, begin + width, 128)
        inside = jnp.concatenate(
            [
                (iota((rows, 128), 1) + lane < valid_col).astype(jnp.float32).astype(jnp.bfloat16)
                for lane in lanes
            ],
            axis=1,
        )
        arrived = jnp.concatenate([take(lane // 128) for lane in lanes], axis=1)
        summed = jnp.dot(scatter, arrived * inside, preferred_element_type=jnp.float32)
        coverage = jnp.dot(scatter, inside, preferred_element_type=jnp.float32)
        trace = summed / jnp.maximum(coverage, 1.0)
        trace_ref[:, begin : begin + width] = trace
        square = trace * trace
        for lane in range(0, width, 128):
            power = power + square[:, lane : lane + 128]
    meansq = jnp.sum(power, axis=1, keepdims=True) * (1.0 / nfft)
    gain = lax.rsqrt(meansq + 1e-06)
    for begin in range(0, nfft // 2, depth):
        loads[begin // depth].wait()
        near = trace_ref[:, begin : begin + depth] * gain
        far = trace_ref[:, begin + nfft // 2 : begin + nfft // 2 + depth] * gain
        for at, folded in ((0, near + far), (bins, near - far)):
            part = jnp.dot(
                folded.astype(jnp.bfloat16),
                table_ref[begin : begin + depth, at : at + bins],
                preferred_element_type=jnp.float32,
            )
            if begin == 0:
                spectrum_ref[:, at : at + bins] = part
            else:
                spectrum_ref[:, at : at + bins] += part
    half = bins // 2
    for at in (0, bins):
        real_part = spectrum_ref[:, at : at + half]
        imag_part = spectrum_ref[:, at + half : at + bins]
        amplitude = lax.rsqrt(
            jnp.maximum(real_part * real_part + imag_part * imag_part, nfft / 4.0)
        )
        for part, offset in ((real_part, 0), (imag_part, bins)):
            white = (part * amplitude).astype(jnp.bfloat16)
            for w in range(W):
                lane = w * 2 * bins + offset + at // 2
                top = w * CH
                low_ref[:, lane : lane + half] = white[top : top + CH // 2]
                high_ref[:, lane : lane + half] = white[top + CH // 2 : top + CH]


def whiten(me, mask, arrived, table, capacity, plans, places):
    nfft, width = 2 * table.shape[0], table.shape[1]
    vmem = pl.BlockSpec(memory_space=pltpu.VMEM)
    smem = pl.BlockSpec(memory_space=pltpu.SMEM)
    return pl.pallas_call(
        functools.partial(whiten_kernel, capacity, plans, places),
        in_specs=[smem, smem]
        + [vmem] * len(arrived)
        + [pl.BlockSpec(memory_space=pltpu.HBM)],
        out_specs=[vmem, vmem, smem],
        out_shape=[
            jax.ShapeDtypeStruct((CH // 2, W * width), jnp.bfloat16),
            jax.ShapeDtypeStruct((CH // 2, W * width), jnp.bfloat16),
            jax.ShapeDtypeStruct((1,), jnp.int32),
        ],
        scratch_shapes=[
            pltpu.VMEM(table.shape, jnp.bfloat16),
            pltpu.VMEM((CH * W, nfft), jnp.float32),
            pltpu.VMEM((CH * W, width), jnp.float32),
            pltpu.SemaphoreType.DMA((nfft // 1024,)),
        ],
        compiler_params=pltpu.CompilerParams(vmem_limit_bytes=50 * 1024 * 1024),
        name="whiten",
    )(me, mask, *arrived, table)


BLOCK = 16


def correlate_kernel(
    order_ref, own_low, own_high, first_low, first_high, second_low, second_high,
    rows_ref, spread_ref, out_hbm,
    both_ref, wide_ref, turned_a, turned_b, found_a, found_b, out_ref, sems,
):
    bins = rows_ref.shape[1]
    terms = rows_ref.shape[0] // 3
    lags = out_ref.shape[4]
    blocks = CH // BLOCK
    turned, found = (turned_a, turned_b), (found_a, found_b)

    def turn(block, slot):
        even = rows_ref[:terms, :]
        odd = rows_ref[terms : 2 * terms, :]
        minus = rows_ref[2 * terms :, :]
        for k in range(BLOCK):
            row = jnp.minimum(block * BLOCK + k, CH - 1)
            u = wide_ref[pl.ds(row, 1), :]
            top = slice(2 * k * terms, (2 * k + 1) * terms)
            low = slice((2 * k + 1) * terms, (2 * k + 2) * terms)
            for w in range(W):
                at = w * 2 * bins
                real, imag = slice(at, at + bins), slice(at + bins, at + 2 * bins)
                ur = jnp.broadcast_to(u[:, real], (terms, bins)).astype(jnp.bfloat16)
                ui = jnp.broadcast_to(u[:, imag], (terms, bins)).astype(jnp.bfloat16)
                turned[slot][top, real] = ur * even
                turned[slot][top, imag] = ui * even
                turned[slot][low, real] = ui * odd
                turned[slot][low, imag] = ur * minus

    def find(slot):
        sums = jnp.dot(turned[slot][...], both_ref[...], preferred_element_type=jnp.float32)
        found[slot][...] = jnp.transpose(sums.astype(jnp.bfloat16))

    def spread(slot, place):
        wide = 8 * terms
        stacked = jnp.concatenate(
            [found[slot][:, k : k + wide] for k in range(0, 2 * BLOCK * terms, wide)], axis=0
        )
        lagged = jnp.dot(stacked, spread_ref[...], preferred_element_type=jnp.float32).astype(
            jnp.bfloat16
        )
        for k in range(BLOCK):
            for r in range(2):
                top = (k // 4 * 2 + r) * CH
                lane = k % 4 * lags
                out_ref[place, r, k] = lagged[top : top + CH, lane : lane + lags]

    def write(block):
        start = pl.multiple_of(block * BLOCK, BLOCK)
        return pltpu.make_async_copy(
            out_ref.at[block % 4], out_hbm.at[:, pl.ds(start, BLOCK)], sems.at[block % 4]
        )

    half = CH // 2
    wide_ref[:half, :] = own_low[...].astype(jnp.float32)
    wide_ref[half:, :] = own_high[...].astype(jnp.float32)
    at = pl.multiple_of(order_ref[0] * CH, CH)
    both_ref[:, pl.ds(at, CH)] = jnp.transpose(
        jnp.concatenate([first_low[...], first_high[...]], axis=0)
    )
    both_ref[:, pl.ds(CH - at, CH)] = jnp.transpose(
        jnp.concatenate([second_low[...], second_high[...]], axis=0)
    )
    turn(0, 0)
    turn(1, 1)
    find(0)

    @pl.loop(0, blocks // 2)
    def _(n):
        @pl.when(n >= 2)
        def _():
            write(2 * n - 4).wait()
            write(2 * n - 3).wait()

        place = n % 2 * 2
        turn(2 * n + 2, 0)
        find(1)
        spread(0, place)
        turn(2 * n + 3, 1)
        find(0)
        spread(1, place + 1)
        write(2 * n).start()
        write(2 * n + 1).start()

    for block in range(blocks - 4, blocks):
        write(block).wait()


def correlate(order, own, first, second, nfft, lags):
    depth = own[0].shape[1]
    bins = depth // (2 * W)
    rows, spread = lag_tables(nfft, bins, lags, 1.0 / math.sqrt(W * bins))
    terms = rows.shape[0] // 3
    vmem = pl.BlockSpec(memory_space=pltpu.VMEM)
    return pl.pallas_call(
        correlate_kernel,
        in_specs=[pl.BlockSpec(memory_space=pltpu.SMEM)] + [vmem] * 8,
        out_specs=pl.BlockSpec(memory_space=pltpu.HBM),
        out_shape=jax.ShapeDtypeStruct((2, CH, CH, lags), jnp.bfloat16),
        scratch_shapes=[
            pltpu.VMEM((depth, 2 * CH), jnp.bfloat16),
            pltpu.VMEM((CH, depth), jnp.float32),
            pltpu.VMEM((BLOCK * 2 * terms, depth), jnp.bfloat16),
            pltpu.VMEM((BLOCK * 2 * terms, depth), jnp.bfloat16),
            pltpu.VMEM((2 * CH, BLOCK * 2 * terms), jnp.bfloat16),
            pltpu.VMEM((2 * CH, BLOCK * 2 * terms), jnp.bfloat16),
            pltpu.VMEM((4, 2, BLOCK, CH, lags), jnp.bfloat16),
            pltpu.SemaphoreType.DMA((4,)),
        ],
        compiler_params=pltpu.CompilerParams(vmem_limit_bytes=60 * 1024 * 1024),
        name="correlate",
    )(order, *own, *first, *second, jnp.asarray(rows), jnp.asarray(spread))


def swap(block, mask):
    count = lax.axis_size("blk")
    return lax.ppermute(block, "blk", [(low, low ^ mask) for low in range(count)])


def swap_halves(tile, mask):
    return tuple(swap(half, mask) for half in tile)


def exchange(mask, moving):
    count = lax.axis_size("blk")
    full = count - 1
    first = swap_halves(moving, full)
    if 2 * mask >= count:
        return moving, first, swap_halves(first, mask ^ full)
    return moving, first, swap_halves(moving, mask)


def deliver(me, mask, key, records, plan):
    owners = lax.axis_size("blk")
    held, nfft = records.shape
    capacity = max(16, 2 * held // owners)
    whole = full_plan(capacity, nfft // 128)
    table = jnp.asarray(forward_table(nfft, F))
    if owners > 16:
        plans = (whole,) * owners
        (outgoing,) = pack(me, key, records, capacity, plans, False)
        arrived = [lax.all_to_all(outgoing, "blk", split_axis=0, concat_axis=0, tiled=True)]
        *tile, branch = whiten(me, mask, arrived, table, capacity, plans, None)
        return tuple(tile), branch
    half = owners // 2
    plans = (whole,) + (plan(capacity, nfft // 128),) * (owners - 1)
    outgoing = pack(me, key, records, capacity, plans, True)
    places = [half]
    for distance in range(1, half):
        places += [distance, half + distance]
    arrived = [swap(outgoing[distance], distance) for distance in places] + [outgoing[0]]
    places.append(0)
    ordered = tuple(plans[distance] for distance in places)
    *tile, branch = whiten(me, mask, arrived, table, capacity, ordered, places)
    return tuple(tile), branch


def local(records, dest, slot, valid, masks):
    owners = lax.axis_size("blk")
    held, nfft = records.shape
    full = owners - 1
    me = lax.axis_index("blk").astype(jnp.int32).reshape(1)
    mask = (masks[0] + masks[1] - full).reshape(1)
    key = (((dest << SLOT_BITS) + slot << VALID_BITS) + valid).reshape(1, held)
    if owners <= 16:
        tile, branch = deliver(me, mask, key, records, short_plan)
        known = [functools.partial(exchange, m) for m in range(1, full)]

        def again(tile):
            tile, branch = deliver(me, mask, key, records, full_plan)
            return lax.switch(branch[0], known, tile)

        own, first, second = lax.switch(branch[0], known + [again], tile)
    else:
        own, _ = deliver(me, mask, key, records, full_plan)
        second = own
        for bit in range(owners.bit_length() - 1):
            moved = swap_halves(second, 1 << bit)
            flip = mask >> bit & 1 == 1
            second = tuple(jnp.where(flip, new, old) for new, old in zip(moved, second))
        first = swap_halves(own, full)
    order = (masks[:1] != full).astype(jnp.int32)
    return correlate(order, own, first, second, nfft, LAGS)


def solution(mesh):
    return jax.shard_map(
        local,
        mesh=mesh,
        in_specs=(
            P(("groups", "blk"), None),
            P(("groups", "blk"), None),
            P(("groups", "blk"), None),
            P(("groups", "blk"), None),
            P(),
        ),
        out_specs=P(None, ("groups", "blk"), None, None),
        check_vma=False,
    )
```

```python
import functools
import math

import jax
import jax.numpy as jnp
import numpy as np
from jax import lax
from jax.experimental import pallas as pl
from jax.experimental.pallas import tpu as pltpu
from jax.sharding import PartitionSpec as P

CH = 128
F = 256
LAGS = 128
W = 2
SLOT_BITS = 8
VALID_BITS = 12
LOW_BITS = 4


def bin_order(bins):
    return np.concatenate([np.arange(2, bins + 1, 2), np.arange(1, bins + 1, 2)])


def forward_table(nfft, bins):
    sample = np.arange(nfft // 2, dtype=np.int64)[:, None]
    angle = (sample * bin_order(bins)[None, :] % nfft) * (2.0 * math.pi / nfft)
    cos, sin = np.cos(angle), np.sin(angle)
    half = bins // 2
    table = [cos[:, :half], -sin[:, :half], cos[:, half:], -sin[:, half:]]
    return np.concatenate(table, axis=1).astype(np.float32).astype(jnp.bfloat16)


def lag_tables(nfft, bins, lags, scale):
    half = lags // 2
    count = lags + 1
    place = np.arange(count)
    middle = ((count - 1 - 2 * place) / 2.0) ** 2 * math.cos(2.0 * math.pi * bins / nfft)
    aside = (place[1:] * (count - place[1:])) / 2.0
    _, basis = np.linalg.eigh(np.diag(middle) + np.diag(aside, 1) + np.diag(aside, -1))
    basis = basis[:, ::-1][:, :half]
    even, odd = basis[:, 0::2], basis[:, 1::2]
    even = even * np.sign(even[half])
    odd = odd * np.sign(odd[half + 1])
    freq = bin_order(bins)[None, :]
    angle = (freq * (place[:, None] - half) % nfft) * (2.0 * math.pi / nfft)
    rows = [even.T @ np.cos(angle), odd.T @ -np.sin(angle)]
    rest = np.cos(angle) - np.sin(angle) - even @ rows[0] - odd @ rows[1]
    assert np.abs(rest).max() < 1e-7
    rows = np.concatenate(rows + [-rows[1]])
    basis = np.concatenate([even, odd], axis=1)[:lags].T * scale
    blank = np.zeros_like(basis)
    spread = np.concatenate(
        [np.concatenate([basis if k == n else blank for n in range(4)], axis=1) for k in range(4)]
    )

    def narrow(table):
        return (np.round(table * 2.0**28) / 2.0**28).astype(np.float32).astype(jnp.bfloat16)

    return narrow(rows), narrow(spread)


def iota(shape, dim):
    return lax.broadcasted_iota(jnp.int32, shape, dim)


LABELS = 8


def full_plan(capacity, chunks):
    return (capacity,) * chunks


def short_plan(capacity, chunks):
    eighths = (8, 8, 8, 8, 8, 8, 8, 8, 8, 7, 7, 6, 6, 5, 4, 3)
    return tuple(capacity * eighths[c * len(eighths) // chunks] // 8 for c in range(chunks))


def pack_kernel(owners, capacity, plans, me_ref, key_ref, records_ref, *out_refs):
    held, nfft = records_ref.shape
    rows = owners * capacity
    width = 512
    key = key_ref[...]
    part = key >> (SLOT_BITS + VALID_BITS)
    if len(out_refs) > 1:
        part = part ^ me_ref[0]
    valid = key & ((1 << VALID_BITS) - 1)
    first = valid * held + (held - 1 - iota((1, held), 1))

    def column(row):
        wide = jnp.transpose(jnp.broadcast_to(row.astype(jnp.float32), (128, held)))
        return jnp.concatenate([wide] * (held // 128), axis=1)

    same = column(part) == part.astype(jnp.float32)
    before = jnp.where(same & (column(first) > first.astype(jnp.float32)), 1.0, 0.0)
    rank = jnp.sum(before, axis=0, keepdims=True).astype(jnp.int32)
    over = jnp.zeros((1, held), jnp.int32)
    for plan in sorted(set(plans)):
        member = functools.reduce(
            jnp.logical_or, [part == d for d in range(owners) if plans[d] == plan]
        )
        for size in sorted(set(plan)):
            if size < capacity:
                reach = 128 * sum(count > size for count in plan)
                over += jnp.where(member & (rank >= size) & (valid > reach), 1, 0)
    over = jnp.max(jnp.minimum(over, 1).astype(jnp.float32), axis=1, keepdims=True)
    position = part * capacity + rank
    order = (iota((rows, held), 0) == position).astype(jnp.float32).astype(jnp.bfloat16)
    slot = (key >> VALID_BITS) & ((1 << SLOT_BITS) - 1)
    row = iota((16, held), 0)
    labels = jnp.where(
        row == 0,
        slot,
        jnp.where(
            row == 1,
            valid >> LOW_BITS,
            jnp.where(row == 2, valid & ((1 << LOW_BITS) - 1), 0),
        ),
    )
    moved = lax.dot_general(
        labels.astype(jnp.float32).astype(jnp.bfloat16),
        order,
        (((1,), (1,)), ((), ())),
        preferred_element_type=jnp.float32,
    )
    moved = jnp.where(iota((16, rows), 0) == 3, over, moved).astype(jnp.bfloat16)

    def put(d, at, value):
        if len(out_refs) > 1:
            out_refs[d][at : at + value.shape[0], :] = value
        else:
            out_refs[0][d, at : at + value.shape[0], :] = value

    for d in range(owners):
        at = d * capacity // 128 * 128
        put(d, sum(plans[d]), moved[:LABELS, at : at + 128])
    for begin in range(0, nfft, width):
        ordered = jnp.dot(
            order, records_ref[:, begin : begin + width], preferred_element_type=jnp.float32
        ).astype(jnp.bfloat16)
        for lane in range(0, width, 128):
            c = (begin + lane) // 128
            for d in range(owners):
                top = d * capacity
                put(d, sum(plans[d][:c]), ordered[top : top + plans[d][c], lane : lane + 128])


def pack(me, key, records, capacity, plans, split):
    held, nfft = records.shape
    owners = len(plans)
    vmem = pl.BlockSpec(memory_space=pltpu.VMEM)
    shapes = [(sum(plan) + LABELS, 128) for plan in plans]
    if not split:
        shapes = [(owners,) + shapes[0]]
    return pl.pallas_call(
        functools.partial(pack_kernel, owners, capacity, plans),
        in_specs=[pl.BlockSpec(memory_space=pltpu.SMEM), vmem, vmem],
        out_specs=[vmem] * len(shapes),
        out_shape=[jax.ShapeDtypeStruct(shape, jnp.bfloat16) for shape in shapes],
        compiler_params=pltpu.CompilerParams(vmem_limit_bytes=48 * 1024 * 1024),
        name="pack",
    )(me, key, records)


def whiten_kernel(capacity, plans, places, me_ref, mask_ref, *refs):
    *arrived_refs, table_hbm, low_ref, high_ref, branch_ref, table_ref, trace_ref, spectrum_ref, sems = refs
    owners = len(plans)
    split = len(arrived_refs) > 1
    nfft = trace_ref.shape[1]
    rows = owners * capacity
    slots = CH * W
    bins = table_ref.shape[1] // 2
    shift = capacity.bit_length() - 1
    width = 256
    depth = 512
    loads = [
        pltpu.make_async_copy(
            table_hbm.at[pl.ds(at, depth)], table_ref.at[pl.ds(at, depth)], sems.at[at // depth]
        )
        for at in range(0, nfft // 2, depth)
    ]
    for copy in loads:
        copy.start()

    def take(c):
        if not split:
            at, count = sum(plans[0][:c]), plans[0][c] if c < len(plans[0]) else LABELS
            return arrived_refs[0][:, at : at + count, :].reshape(owners * count, 128)
        pieces = []
        for ref, plan in zip(arrived_refs, plans):
            at, count = sum(plan[:c]), plan[c] if c < len(plan) else LABELS
            pieces.append(ref[at : at + count, :])
            if c < len(plan) and count < capacity:
                pieces.append(jnp.zeros((capacity - count, 128), jnp.bfloat16))
        return jnp.concatenate(pieces, axis=0)

    labels = take(len(plans[0])).astype(jnp.float32).reshape(owners, LABELS, 128)
    which = iota((owners, LABELS, 128), 1)
    over = jnp.max(jnp.where(which == 3, labels, 0.0))
    branch_ref[0] = jnp.where(over > 0.0, owners - 2, mask_ref[0] - 1)
    parts = jnp.concatenate(
        [jnp.sum(jnp.where(which == k, labels, 0.0), axis=1) for k in range(3)], axis=0
    )
    if split:
        part = iota((1, rows), 1) >> shift
        place = functools.reduce(
            lambda total, p: total + jnp.where(part == p, places[p], 0),
            range(owners),
            jnp.zeros((1, rows), jnp.int32),
        )
    else:
        place = me_ref[0]
    base = (place * capacity) & 127
    pick = iota((128, rows), 0) == base + (iota((128, rows), 1) & (capacity - 1))
    picked = jnp.dot(
        parts.astype(jnp.bfloat16),
        pick.astype(jnp.float32).astype(jnp.bfloat16),
        preferred_element_type=jnp.float32,
    )
    source = iota((owners, rows), 0) == iota((owners, rows), 1) >> shift
    rowed = [
        jnp.sum(
            jnp.where(source, picked[k * owners : (k + 1) * owners], 0.0), axis=0, keepdims=True
        )
        for k in range(3)
    ]
    slot_row = rowed[0].astype(jnp.int32)
    place = (slot_row & (W - 1)) * CH + (slot_row >> (W.bit_length() - 1))
    valid_row = rowed[1] * float(1 << LOW_BITS) + rowed[2]
    scatter = (iota((slots, rows), 0) == place).astype(jnp.float32).astype(jnp.bfloat16)
    valid_col = jnp.transpose(jnp.broadcast_to(valid_row, (128, rows))).astype(jnp.int32)
    power = jnp.zeros((slots, 128), jnp.float32)
    for begin in range(0, nfft, width):
        lanes = range(begin, begin + width, 128)
        inside = jnp.concatenate(
            [
                (iota((rows, 128), 1) + lane < valid_col).astype(jnp.float32).astype(jnp.bfloat16)
                for lane in lanes
            ],
            axis=1,
        )
        arrived = jnp.concatenate([take(lane // 128) for lane in lanes], axis=1)
        summed = jnp.dot(scatter, arrived * inside, preferred_element_type=jnp.float32)
        coverage = jnp.dot(scatter, inside, preferred_element_type=jnp.float32)
        trace = summed / jnp.maximum(coverage, 1.0)
        trace_ref[:, begin : begin + width] = trace
        square = trace * trace
        for lane in range(0, width, 128):
            power = power + square[:, lane : lane + 128]
    meansq = jnp.sum(power, axis=1, keepdims=True) * (1.0 / nfft)
    gain = lax.rsqrt(meansq + 1e-06)
    for begin in range(0, nfft // 2, depth):
        loads[begin // depth].wait()
        near = trace_ref[:, begin : begin + depth] * gain
        far = trace_ref[:, begin + nfft // 2 : begin + nfft // 2 + depth] * gain
        for at, folded in ((0, near + far), (bins, near - far)):
            part = jnp.dot(
                folded.astype(jnp.bfloat16),
                table_ref[begin : begin + depth, at : at + bins],
                preferred_element_type=jnp.float32,
            )
            if begin == 0:
                spectrum_ref[:, at : at + bins] = part
            else:
                spectrum_ref[:, at : at + bins] += part
    half = bins // 2
    for at in (0, bins):
        real_part = spectrum_ref[:, at : at + half]
        imag_part = spectrum_ref[:, at + half : at + bins]
        amplitude = lax.rsqrt(
            jnp.maximum(real_part * real_part + imag_part * imag_part, nfft / 4.0)
        )
        for part, offset in ((real_part, 0), (imag_part, bins)):
            white = (part * amplitude).astype(jnp.bfloat16)
            for w in range(W):
                lane = w * 2 * bins + offset + at // 2
                top = w * CH
                low_ref[:, lane : lane + half] = white[top : top + CH // 2]
                high_ref[:, lane : lane + half] = white[top + CH // 2 : top + CH]


def whiten(me, mask, arrived, table, capacity, plans, places):
    nfft, width = 2 * table.shape[0], table.shape[1]
    vmem = pl.BlockSpec(memory_space=pltpu.VMEM)
    smem = pl.BlockSpec(memory_space=pltpu.SMEM)
    return pl.pallas_call(
        functools.partial(whiten_kernel, capacity, plans, places),
        in_specs=[smem, smem]
        + [vmem] * len(arrived)
        + [pl.BlockSpec(memory_space=pltpu.HBM)],
        out_specs=[vmem, vmem, smem],
        out_shape=[
            jax.ShapeDtypeStruct((CH // 2, W * width), jnp.bfloat16),
            jax.ShapeDtypeStruct((CH // 2, W * width), jnp.bfloat16),
            jax.ShapeDtypeStruct((1,), jnp.int32),
        ],
        scratch_shapes=[
            pltpu.VMEM(table.shape, jnp.bfloat16),
            pltpu.VMEM((CH * W, nfft), jnp.float32),
            pltpu.VMEM((CH * W, width), jnp.float32),
            pltpu.SemaphoreType.DMA((nfft // 1024,)),
        ],
        compiler_params=pltpu.CompilerParams(vmem_limit_bytes=50 * 1024 * 1024),
        name="whiten",
    )(me, mask, *arrived, table)


BLOCK = 16


def correlate_kernel(
    order_ref, own_low, own_high, first_low, first_high, second_low, second_high,
    rows_ref, spread_ref, out_hbm,
    both_ref, wide_ref, turned_a, turned_b, found_a, found_b, out_ref, sems,
):
    bins = rows_ref.shape[1]
    terms = rows_ref.shape[0] // 3
    lags = out_ref.shape[4]
    blocks = CH // BLOCK
    turned, found = (turned_a, turned_b), (found_a, found_b)

    def turn(block, slot):
        even = rows_ref[:terms, :]
        odd = rows_ref[terms : 2 * terms, :]
        minus = rows_ref[2 * terms :, :]
        for k in range(BLOCK):
            u = wide_ref[pl.ds(block * BLOCK + k, 1), :]
            top = slice(2 * k * terms, (2 * k + 1) * terms)
            low = slice((2 * k + 1) * terms, (2 * k + 2) * terms)
            for w in range(W):
                at = w * 2 * bins
                real, imag = slice(at, at + bins), slice(at + bins, at + 2 * bins)
                ur = jnp.broadcast_to(u[:, real], (terms, bins)).astype(jnp.bfloat16)
                ui = jnp.broadcast_to(u[:, imag], (terms, bins)).astype(jnp.bfloat16)
                turned[slot][top, real] = ur * even
                turned[slot][top, imag] = ui * even
                turned[slot][low, real] = ui * odd
                turned[slot][low, imag] = ur * minus

    def find(slot):
        sums = jnp.dot(turned[slot][...], both_ref[...], preferred_element_type=jnp.float32)
        found[slot][...] = jnp.transpose(sums.astype(jnp.bfloat16))

    def spread(slot, place):
        wide = 8 * terms
        stacked = jnp.concatenate(
            [found[slot][:, k : k + wide] for k in range(0, 2 * BLOCK * terms, wide)], axis=0
        )
        lagged = jnp.dot(stacked, spread_ref[...], preferred_element_type=jnp.float32).astype(
            jnp.bfloat16
        )
        for k in range(BLOCK):
            for r in range(2):
                top = (k // 4 * 2 + r) * CH
                lane = k % 4 * lags
                out_ref[place, r, k] = lagged[top : top + CH, lane : lane + lags]

    def write(block):
        start = pl.multiple_of(block * BLOCK, BLOCK)
        return pltpu.make_async_copy(
            out_ref.at[block % 4], out_hbm.at[:, pl.ds(start, BLOCK)], sems.at[block % 4]
        )

    half = CH // 2
    wide_ref[:half, :] = own_low[...].astype(jnp.float32)
    wide_ref[half:, :] = own_high[...].astype(jnp.float32)
    at = pl.multiple_of(order_ref[0] * CH, CH)
    both_ref[:, pl.ds(at, CH)] = jnp.transpose(
        jnp.concatenate([first_low[...], first_high[...]], axis=0)
    )
    both_ref[:, pl.ds(CH - at, CH)] = jnp.transpose(
        jnp.concatenate([second_low[...], second_high[...]], axis=0)
    )
    turn(0, 0)
    turn(1, 1)
    find(0)

    @pl.loop(0, blocks // 2 - 1)
    def _(n):
        @pl.when(n >= 2)
        def _():
            write(2 * n - 4).wait()
            write(2 * n - 3).wait()

        place = n % 2 * 2
        turn(2 * n + 2, 0)
        find(1)
        spread(0, place)
        turn(2 * n + 3, 1)
        find(0)
        spread(1, place + 1)
        write(2 * n).start()
        write(2 * n + 1).start()

    place = (blocks - 2) % 4
    write(blocks - 6).wait()
    write(blocks - 5).wait()
    find(1)
    spread(0, place)
    write(blocks - 2).start()
    spread(1, place + 1)
    write(blocks - 1).start()
    for block in range(blocks - 4, blocks):
        write(block).wait()


def correlate(order, own, first, second, nfft, lags):
    depth = own[0].shape[1]
    bins = depth // (2 * W)
    rows, spread = lag_tables(nfft, bins, lags, 1.0 / math.sqrt(W * bins))
    terms = rows.shape[0] // 3
    vmem = pl.BlockSpec(memory_space=pltpu.VMEM)
    return pl.pallas_call(
        correlate_kernel,
        in_specs=[pl.BlockSpec(memory_space=pltpu.SMEM)] + [vmem] * 8,
        out_specs=pl.BlockSpec(memory_space=pltpu.HBM),
        out_shape=jax.ShapeDtypeStruct((2, CH, CH, lags), jnp.bfloat16),
        scratch_shapes=[
            pltpu.VMEM((depth, 2 * CH), jnp.bfloat16),
            pltpu.VMEM((CH, depth), jnp.float32),
            pltpu.VMEM((BLOCK * 2 * terms, depth), jnp.bfloat16),
            pltpu.VMEM((BLOCK * 2 * terms, depth), jnp.bfloat16),
            pltpu.VMEM((2 * CH, BLOCK * 2 * terms), jnp.bfloat16),
            pltpu.VMEM((2 * CH, BLOCK * 2 * terms), jnp.bfloat16),
            pltpu.VMEM((4, 2, BLOCK, CH, lags), jnp.bfloat16),
            pltpu.SemaphoreType.DMA((4,)),
        ],
        compiler_params=pltpu.CompilerParams(vmem_limit_bytes=60 * 1024 * 1024),
        name="correlate",
    )(order, *own, *first, *second, jnp.asarray(rows), jnp.asarray(spread))


def swap(block, mask):
    count = lax.axis_size("blk")
    return lax.ppermute(block, "blk", [(low, low ^ mask) for low in range(count)])


def swap_halves(tile, mask):
    return tuple(swap(half, mask) for half in tile)


def exchange(mask, moving):
    count = lax.axis_size("blk")
    full = count - 1
    first = swap_halves(moving, full)
    if 2 * mask >= count:
        return moving, first, swap_halves(first, mask ^ full)
    return moving, first, swap_halves(moving, mask)


def deliver(me, mask, key, records, plan):
    owners = lax.axis_size("blk")
    held, nfft = records.shape
    capacity = max(16, 2 * held // owners)
    whole = full_plan(capacity, nfft // 128)
    table = jnp.asarray(forward_table(nfft, F))
    if owners > 16:
        plans = (whole,) * owners
        (outgoing,) = pack(me, key, records, capacity, plans, False)
        arrived = [lax.all_to_all(outgoing, "blk", split_axis=0, concat_axis=0, tiled=True)]
        *tile, branch = whiten(me, mask, arrived, table, capacity, plans, None)
        return tuple(tile), branch
    half = owners // 2
    plans = (whole,) + (plan(capacity, nfft // 128),) * (owners - 1)
    outgoing = pack(me, key, records, capacity, plans, True)
    places = [half]
    for distance in range(1, half):
        places += [distance, half + distance]
    arrived = [swap(outgoing[distance], distance) for distance in places] + [outgoing[0]]
    places.append(0)
    ordered = tuple(plans[distance] for distance in places)
    *tile, branch = whiten(me, mask, arrived, table, capacity, ordered, places)
    return tuple(tile), branch


def local(records, dest, slot, valid, masks):
    owners = lax.axis_size("blk")
    held, nfft = records.shape
    full = owners - 1
    me = lax.axis_index("blk").astype(jnp.int32).reshape(1)
    mask = (masks[0] + masks[1] - full).reshape(1)
    key = (((dest << SLOT_BITS) + slot << VALID_BITS) + valid).reshape(1, held)
    if owners <= 16:
        tile, branch = deliver(me, mask, key, records, short_plan)
        known = [functools.partial(exchange, m) for m in range(1, full)]

        def again(tile):
            tile, branch = deliver(me, mask, key, records, full_plan)
            return lax.switch(branch[0], known, tile)

        own, first, second = lax.switch(branch[0], known + [again], tile)
    else:
        own, _ = deliver(me, mask, key, records, full_plan)
        second = own
        for bit in range(owners.bit_length() - 1):
            moved = swap_halves(second, 1 << bit)
            flip = mask >> bit & 1 == 1
            second = tuple(jnp.where(flip, new, old) for new, old in zip(moved, second))
        first = swap_halves(own, full)
    order = (masks[:1] != full).astype(jnp.int32)
    return correlate(order, own, first, second, nfft, LAGS)


def solution(mesh):
    return jax.shard_map(
        local,
        mesh=mesh,
        in_specs=(
            P(("groups", "blk"), None),
            P(("groups", "blk"), None),
            P(("groups", "blk"), None),
            P(("groups", "blk"), None),
            P(),
        ),
        out_specs=P(None, ("groups", "blk"), None, None),
        check_vma=False,
    )
```

```python
import functools
import math

import jax
import jax.numpy as jnp
import numpy as np
from jax import lax
from jax.experimental import pallas as pl
from jax.experimental.pallas import tpu as pltpu
from jax.sharding import PartitionSpec as P

CH = 128
F = 256
LAGS = 128
W = 2
SLOT_BITS = 8
VALID_BITS = 12
LOW_BITS = 4


def bin_order(bins):
    return np.concatenate([np.arange(2, bins + 1, 2), np.arange(1, bins + 1, 2)])


def forward_table(nfft, bins):
    sample = np.arange(nfft // 2, dtype=np.int64)[:, None]
    angle = (sample * bin_order(bins)[None, :] % nfft) * (2.0 * math.pi / nfft)
    cos, sin = np.cos(angle), np.sin(angle)
    half = bins // 2
    table = [cos[:, :half], -sin[:, :half], cos[:, half:], -sin[:, half:]]
    return np.concatenate(table, axis=1).astype(np.float32).astype(jnp.bfloat16)


def lag_tables(nfft, bins, lags, scale):
    half = lags // 2
    count = lags + 1
    place = np.arange(count)
    middle = ((count - 1 - 2 * place) / 2.0) ** 2 * math.cos(2.0 * math.pi * bins / nfft)
    aside = (place[1:] * (count - place[1:])) / 2.0
    _, basis = np.linalg.eigh(np.diag(middle) + np.diag(aside, 1) + np.diag(aside, -1))
    basis = basis[:, ::-1][:, :half]
    even, odd = basis[:, 0::2], basis[:, 1::2]
    even = even * np.sign(even[half])
    odd = odd * np.sign(odd[half + 1])
    freq = bin_order(bins)[None, :]
    angle = (freq * (place[:, None] - half) % nfft) * (2.0 * math.pi / nfft)
    rows = [even.T @ np.cos(angle), odd.T @ -np.sin(angle)]
    rest = np.cos(angle) - np.sin(angle) - even @ rows[0] - odd @ rows[1]
    assert np.abs(rest).max() < 1e-7
    rows = np.concatenate(rows + [-rows[1]])
    basis = np.concatenate([even, odd], axis=1)[:lags].T * scale
    blank = np.zeros_like(basis)
    spread = np.concatenate(
        [np.concatenate([basis if k == n else blank for n in range(4)], axis=1) for k in range(4)]
    )

    def narrow(table):
        return (np.round(table * 2.0**28) / 2.0**28).astype(np.float32).astype(jnp.bfloat16)

    return narrow(rows), narrow(spread)


def iota(shape, dim):
    return lax.broadcasted_iota(jnp.int32, shape, dim)


LABELS = 8


def full_plan(capacity, chunks):
    return (capacity,) * chunks


def short_plan(capacity, chunks):
    eighths = (8, 8, 8, 8, 8, 8, 8, 8, 8, 7, 7, 6, 6, 5, 4, 3)
    return tuple(capacity * eighths[c * len(eighths) // chunks] // 8 for c in range(chunks))


def pack_kernel(owners, capacity, plans, me_ref, key_ref, records_ref, *out_refs):
    held, nfft = records_ref.shape
    rows = owners * capacity
    width = 512
    key = key_ref[...]
    part = key >> (SLOT_BITS + VALID_BITS)
    if len(out_refs) > 1:
        part = part ^ me_ref[0]
    valid = key & ((1 << VALID_BITS) - 1)
    first = valid * held + (held - 1 - iota((1, held), 1))

    def column(row):
        wide = jnp.transpose(jnp.broadcast_to(row.astype(jnp.float32), (128, held)))
        return jnp.concatenate([wide] * (held // 128), axis=1)

    same = column(part) == part.astype(jnp.float32)
    before = jnp.where(same & (column(first) > first.astype(jnp.float32)), 1.0, 0.0)
    rank = jnp.sum(before, axis=0, keepdims=True).astype(jnp.int32)
    over = jnp.zeros((1, held), jnp.int32)
    for plan in sorted(set(plans)):
        member = functools.reduce(
            jnp.logical_or, [part == d for d in range(owners) if plans[d] == plan]
        )
        for size in sorted(set(plan)):
            if size < capacity:
                reach = 128 * sum(count > size for count in plan)
                over += jnp.where(member & (rank >= size) & (valid > reach), 1, 0)
    over = jnp.max(jnp.minimum(over, 1).astype(jnp.float32), axis=1, keepdims=True)
    position = part * capacity + rank
    order = (iota((rows, held), 0) == position).astype(jnp.float32).astype(jnp.bfloat16)
    slot = (key >> VALID_BITS) & ((1 << SLOT_BITS) - 1)
    row = iota((16, held), 0)
    labels = jnp.where(
        row == 0,
        slot,
        jnp.where(
            row == 1,
            valid >> LOW_BITS,
            jnp.where(row == 2, valid & ((1 << LOW_BITS) - 1), 0),
        ),
    )
    moved = lax.dot_general(
        labels.astype(jnp.float32).astype(jnp.bfloat16),
        order,
        (((1,), (1,)), ((), ())),
        preferred_element_type=jnp.float32,
    )
    moved = jnp.where(iota((16, rows), 0) == 3, over, moved).astype(jnp.bfloat16)

    def put(d, at, value):
        if len(out_refs) > 1:
            out_refs[d][at : at + value.shape[0], :] = value
        else:
            out_refs[0][d, at : at + value.shape[0], :] = value

    for d in range(owners):
        at = d * capacity // 128 * 128
        put(d, sum(plans[d]), moved[:LABELS, at : at + 128])
    for begin in range(0, nfft, width):
        ordered = jnp.dot(
            order, records_ref[:, begin : begin + width], preferred_element_type=jnp.float32
        ).astype(jnp.bfloat16)
        for lane in range(0, width, 128):
            c = (begin + lane) // 128
            for d in range(owners):
                top = d * capacity
                put(d, sum(plans[d][:c]), ordered[top : top + plans[d][c], lane : lane + 128])


def pack(me, key, records, capacity, plans, split):
    held, nfft = records.shape
    owners = len(plans)
    vmem = pl.BlockSpec(memory_space=pltpu.VMEM)
    shapes = [(sum(plan) + LABELS, 128) for plan in plans]
    if not split:
        shapes = [(owners,) + shapes[0]]
    return pl.pallas_call(
        functools.partial(pack_kernel, owners, capacity, plans),
        in_specs=[pl.BlockSpec(memory_space=pltpu.SMEM), vmem, vmem],
        out_specs=[vmem] * len(shapes),
        out_shape=[jax.ShapeDtypeStruct(shape, jnp.bfloat16) for shape in shapes],
        compiler_params=pltpu.CompilerParams(vmem_limit_bytes=48 * 1024 * 1024),
        name="pack",
    )(me, key, records)


def whiten_kernel(capacity, plans, places, me_ref, mask_ref, *refs):
    *arrived_refs, table_hbm, low_ref, high_ref, branch_ref, table_ref, trace_ref, spectrum_ref, sems = refs
    owners = len(plans)
    split = len(arrived_refs) > 1
    nfft = trace_ref.shape[1]
    rows = owners * capacity
    slots = CH * W
    bins = table_ref.shape[1] // 2
    shift = capacity.bit_length() - 1
    width = 256
    depth = 512
    loads = [
        pltpu.make_async_copy(
            table_hbm.at[pl.ds(at, depth)], table_ref.at[pl.ds(at, depth)], sems.at[at // depth]
        )
        for at in range(0, nfft // 2, depth)
    ]
    for copy in loads:
        copy.start()

    def take(c):
        if not split:
            at, count = sum(plans[0][:c]), plans[0][c] if c < len(plans[0]) else LABELS
            return arrived_refs[0][:, at : at + count, :].reshape(owners * count, 128)
        pieces = []
        for ref, plan in zip(arrived_refs, plans):
            at, count = sum(plan[:c]), plan[c] if c < len(plan) else LABELS
            pieces.append(ref[at : at + count, :])
            if c < len(plan) and count < capacity:
                pieces.append(jnp.zeros((capacity - count, 128), jnp.bfloat16))
        return jnp.concatenate(pieces, axis=0)

    labels = take(len(plans[0])).astype(jnp.float32).reshape(owners, LABELS, 128)
    which = iota((owners, LABELS, 128), 1)
    over = jnp.max(jnp.where(which == 3, labels, 0.0))
    branch_ref[0] = jnp.where(over > 0.0, owners - 2, mask_ref[0] - 1)
    parts = jnp.concatenate(
        [jnp.sum(jnp.where(which == k, labels, 0.0), axis=1) for k in range(3)], axis=0
    )
    if split:
        part = iota((1, rows), 1) >> shift
        place = functools.reduce(
            lambda total, p: total + jnp.where(part == p, places[p], 0),
            range(owners),
            jnp.zeros((1, rows), jnp.int32),
        )
    else:
        place = me_ref[0]
    base = (place * capacity) & 127
    pick = iota((128, rows), 0) == base + (iota((128, rows), 1) & (capacity - 1))
    picked = jnp.dot(
        parts.astype(jnp.bfloat16),
        pick.astype(jnp.float32).astype(jnp.bfloat16),
        preferred_element_type=jnp.float32,
    )
    source = iota((owners, rows), 0) == iota((owners, rows), 1) >> shift
    rowed = [
        jnp.sum(
            jnp.where(source, picked[k * owners : (k + 1) * owners], 0.0), axis=0, keepdims=True
        )
        for k in range(3)
    ]
    slot_row = rowed[0].astype(jnp.int32)
    place = (slot_row & (W - 1)) * CH + (slot_row >> (W.bit_length() - 1))
    valid_row = rowed[1] * float(1 << LOW_BITS) + rowed[2]
    scatter = (iota((slots, rows), 0) == place).astype(jnp.float32).astype(jnp.bfloat16)
    valid_col = jnp.transpose(jnp.broadcast_to(valid_row, (128, rows))).astype(jnp.int32)
    power = jnp.zeros((slots, 128), jnp.float32)
    for begin in range(0, nfft, width):
        lanes = range(begin, begin + width, 128)
        inside = jnp.concatenate(
            [
                (iota((rows, 128), 1) + lane < valid_col).astype(jnp.float32).astype(jnp.bfloat16)
                for lane in lanes
            ],
            axis=1,
        )
        arrived = jnp.concatenate([take(lane // 128) for lane in lanes], axis=1)
        summed = jnp.dot(scatter, arrived * inside, preferred_element_type=jnp.float32)
        coverage = jnp.dot(scatter, inside, preferred_element_type=jnp.float32)
        count = jnp.maximum(coverage, 1.0)
        share = pl.reciprocal(count, approx=True)
        trace = summed * (share * (2.0 - count * share))
        trace_ref[:, begin : begin + width] = trace
        square = trace * trace
        for lane in range(0, width, 128):
            power = power + square[:, lane : lane + 128]
    meansq = jnp.sum(power, axis=1, keepdims=True) * (1.0 / nfft)
    gain = lax.rsqrt(meansq + 1e-06)
    for begin in range(0, nfft // 2, depth):
        loads[begin // depth].wait()
        near = trace_ref[:, begin : begin + depth] * gain
        far = trace_ref[:, begin + nfft // 2 : begin + nfft // 2 + depth] * gain
        for at, folded in ((0, near + far), (bins, near - far)):
            part = jnp.dot(
                folded.astype(jnp.bfloat16),
                table_ref[begin : begin + depth, at : at + bins],
                preferred_element_type=jnp.float32,
            )
            if begin == 0:
                spectrum_ref[:, at : at + bins] = part
            else:
                spectrum_ref[:, at : at + bins] += part
    half = bins // 2
    for at in (0, bins):
        real_part = spectrum_ref[:, at : at + half]
        imag_part = spectrum_ref[:, at + half : at + bins]
        amplitude = lax.rsqrt(
            jnp.maximum(real_part * real_part + imag_part * imag_part, nfft / 4.0)
        )
        for part, offset in ((real_part, 0), (imag_part, bins)):
            white = (part * amplitude).astype(jnp.bfloat16)
            for w in range(W):
                lane = w * 2 * bins + offset + at // 2
                top = w * CH
                low_ref[:, lane : lane + half] = white[top : top + CH // 2]
                high_ref[:, lane : lane + half] = white[top + CH // 2 : top + CH]


def whiten(me, mask, arrived, table, capacity, plans, places):
    nfft, width = 2 * table.shape[0], table.shape[1]
    vmem = pl.BlockSpec(memory_space=pltpu.VMEM)
    smem = pl.BlockSpec(memory_space=pltpu.SMEM)
    return pl.pallas_call(
        functools.partial(whiten_kernel, capacity, plans, places),
        in_specs=[smem, smem]
        + [vmem] * len(arrived)
        + [pl.BlockSpec(memory_space=pltpu.HBM)],
        out_specs=[vmem, vmem, smem],
        out_shape=[
            jax.ShapeDtypeStruct((CH // 2, W * width), jnp.bfloat16),
            jax.ShapeDtypeStruct((CH // 2, W * width), jnp.bfloat16),
            jax.ShapeDtypeStruct((1,), jnp.int32),
        ],
        scratch_shapes=[
            pltpu.VMEM(table.shape, jnp.bfloat16),
            pltpu.VMEM((CH * W, nfft), jnp.float32),
            pltpu.VMEM((CH * W, width), jnp.float32),
            pltpu.SemaphoreType.DMA((nfft // 1024,)),
        ],
        compiler_params=pltpu.CompilerParams(vmem_limit_bytes=50 * 1024 * 1024),
        name="whiten",
    )(me, mask, *arrived, table)


BLOCK = 8


def correlate_kernel(
    order_ref, own_low, own_high, rows_ref, spread_ref, *refs
):
    *partners, out_hbm, both_ref, wide_ref, near_ref, turned_a, turned_b, found_a, found_b, out_ref, sems, loaded = refs
    bins = rows_ref.shape[1]
    terms = rows_ref.shape[0] // 3
    lags = out_ref.shape[4]
    blocks = CH // BLOCK
    turned, found = (turned_a, turned_b), (found_a, found_b)

    def turn(block, slot):
        even = rows_ref[:terms, :]
        odd = rows_ref[terms : 2 * terms, :]
        minus = rows_ref[2 * terms :, :]
        for k in range(BLOCK):
            u = wide_ref[pl.ds(block * BLOCK + k, 1), :]
            top = slice(2 * k * terms, (2 * k + 1) * terms)
            low = slice((2 * k + 1) * terms, (2 * k + 2) * terms)
            for w in range(W):
                at = w * 2 * bins
                real, imag = slice(at, at + bins), slice(at + bins, at + 2 * bins)
                ur = jnp.broadcast_to(u[:, real], (terms, bins)).astype(jnp.bfloat16)
                ui = jnp.broadcast_to(u[:, imag], (terms, bins)).astype(jnp.bfloat16)
                turned[slot][top, real] = ur * even
                turned[slot][top, imag] = ui * even
                turned[slot][low, real] = ui * odd
                turned[slot][low, imag] = ur * minus

    def find(slot):
        sums = jnp.dot(turned[slot][...], both_ref[...], preferred_element_type=jnp.float32)
        found[slot][...] = jnp.transpose(sums.astype(jnp.bfloat16))

    def spread(slot, place):
        wide = 8 * terms
        stacked = jnp.concatenate(
            [found[slot][:, k : k + wide] for k in range(0, 2 * BLOCK * terms, wide)], axis=0
        )
        lagged = jnp.dot(stacked, spread_ref[...], preferred_element_type=jnp.float32).astype(
            jnp.bfloat16
        )
        for k in range(BLOCK):
            for r in range(2):
                top = (k // 4 * 2 + r) * CH
                lane = k % 4 * lags
                out_ref[place, r, k] = lagged[top : top + CH, lane : lane + lags]

    def write(block):
        start = pl.multiple_of(block * BLOCK, BLOCK)
        return pltpu.make_async_copy(
            out_ref.at[block % 4], out_hbm.at[:, pl.ds(start, BLOCK)], sems.at[block % 4]
        )

    half = CH // 2
    loads = [
        pltpu.make_async_copy(source, near_ref.at[pl.ds(k * half, half)], loaded.at[k])
        for k, source in enumerate(partners)
    ]
    for copy in loads:
        copy.start()
    wide_ref[:half, :] = own_low[...].astype(jnp.float32)
    wide_ref[half:, :] = own_high[...].astype(jnp.float32)
    turn(0, 0)
    turn(1, 1)
    for copy in loads:
        copy.wait()
    at = pl.multiple_of(order_ref[0] * CH, CH)
    both_ref[:, pl.ds(at, CH)] = jnp.transpose(near_ref[:CH, :])
    both_ref[:, pl.ds(CH - at, CH)] = jnp.transpose(near_ref[CH:, :])
    find(0)

    @pl.loop(0, blocks // 2 - 1)
    def _(n):
        @pl.when(n >= 2)
        def _():
            write(2 * n - 4).wait()
            write(2 * n - 3).wait()

        place = n % 2 * 2
        turn(2 * n + 2, 0)
        find(1)
        spread(0, place)
        turn(2 * n + 3, 1)
        find(0)
        spread(1, place + 1)
        write(2 * n).start()
        write(2 * n + 1).start()

    place = (blocks - 2) % 4
    write(blocks - 6).wait()
    write(blocks - 5).wait()
    find(1)
    spread(0, place)
    write(blocks - 2).start()
    spread(1, place + 1)
    write(blocks - 1).start()
    for block in range(blocks - 4, blocks):
        write(block).wait()


def correlate(order, own, first, second, nfft, lags):
    depth = own[0].shape[1]
    bins = depth // (2 * W)
    rows, spread = lag_tables(nfft, bins, lags, 1.0 / math.sqrt(W * bins))
    terms = rows.shape[0] // 3
    vmem = pl.BlockSpec(memory_space=pltpu.VMEM)
    return pl.pallas_call(
        correlate_kernel,
        in_specs=[pl.BlockSpec(memory_space=pltpu.SMEM)]
        + [vmem] * 4
        + [pl.BlockSpec(memory_space=pltpu.HBM)] * 4,
        out_specs=pl.BlockSpec(memory_space=pltpu.HBM),
        out_shape=jax.ShapeDtypeStruct((2, CH, CH, lags), jnp.bfloat16),
        scratch_shapes=[
            pltpu.VMEM((depth, 2 * CH), jnp.bfloat16),
            pltpu.VMEM((CH, depth), jnp.float32),
            pltpu.VMEM((2 * CH, depth), jnp.bfloat16),
            pltpu.VMEM((BLOCK * 2 * terms, depth), jnp.bfloat16),
            pltpu.VMEM((BLOCK * 2 * terms, depth), jnp.bfloat16),
            pltpu.VMEM((2 * CH, BLOCK * 2 * terms), jnp.bfloat16),
            pltpu.VMEM((2 * CH, BLOCK * 2 * terms), jnp.bfloat16),
            pltpu.VMEM((4, 2, BLOCK, CH, lags), jnp.bfloat16),
            pltpu.SemaphoreType.DMA((4,)),
            pltpu.SemaphoreType.DMA((4,)),
        ],
        compiler_params=pltpu.CompilerParams(vmem_limit_bytes=60 * 1024 * 1024),
        name="correlate",
    )(order, *own, jnp.asarray(rows), jnp.asarray(spread), *first, *second)


def swap(block, mask):
    count = lax.axis_size("blk")
    return lax.ppermute(block, "blk", [(low, low ^ mask) for low in range(count)])


def swap_halves(tile, mask):
    return tuple(swap(half, mask) for half in tile)


def exchange(mask, moving):
    count = lax.axis_size("blk")
    full = count - 1
    first = swap_halves(moving, full)
    if 2 * mask >= count:
        return moving, first, swap_halves(first, mask ^ full)
    return moving, first, swap_halves(moving, mask)


def deliver(me, mask, key, records, plan):
    owners = lax.axis_size("blk")
    held, nfft = records.shape
    capacity = max(16, 2 * held // owners)
    whole = full_plan(capacity, nfft // 128)
    table = jnp.asarray(forward_table(nfft, F))
    if owners > 16:
        plans = (whole,) * owners
        (outgoing,) = pack(me, key, records, capacity, plans, False)
        arrived = [lax.all_to_all(outgoing, "blk", split_axis=0, concat_axis=0, tiled=True)]
        *tile, branch = whiten(me, mask, arrived, table, capacity, plans, None)
        return tuple(tile), branch
    half = owners // 2
    plans = (whole,) + (plan(capacity, nfft // 128),) * (owners - 1)
    outgoing = pack(me, key, records, capacity, plans, True)
    places = [half]
    for distance in range(1, half):
        places += [distance, half + distance]
    arrived = [swap(outgoing[distance], distance) for distance in places] + [outgoing[0]]
    places.append(0)
    ordered = tuple(plans[distance] for distance in places)
    *tile, branch = whiten(me, mask, arrived, table, capacity, ordered, places)
    return tuple(tile), branch


def local(records, dest, slot, valid, masks):
    owners = lax.axis_size("blk")
    held, nfft = records.shape
    full = owners - 1
    me = lax.axis_index("blk").astype(jnp.int32).reshape(1)
    mask = (masks[0] + masks[1] - full).reshape(1)
    key = (((dest << SLOT_BITS) + slot << VALID_BITS) + valid).reshape(1, held)
    if owners <= 16:
        tile, branch = deliver(me, mask, key, records, short_plan)
        known = [functools.partial(exchange, m) for m in range(1, full)]

        def again(tile):
            tile, branch = deliver(me, mask, key, records, full_plan)
            return lax.switch(branch[0], known, tile)

        own, first, second = lax.switch(branch[0], known + [again], tile)
    else:
        own, _ = deliver(me, mask, key, records, full_plan)
        second = own
        for bit in range(owners.bit_length() - 1):
            moved = swap_halves(second, 1 << bit)
            flip = mask >> bit & 1 == 1
            second = tuple(jnp.where(flip, new, old) for new, old in zip(moved, second))
        first = swap_halves(own, full)
    order = (masks[:1] != full).astype(jnp.int32)
    return correlate(order, own, first, second, nfft, LAGS)


def solution(mesh):
    return jax.shard_map(
        local,
        mesh=mesh,
        in_specs=(
            P(("groups", "blk"), None),
            P(("groups", "blk"), None),
            P(("groups", "blk"), None),
            P(("groups", "blk"), None),
            P(),
        ),
        out_specs=P(None, ("groups", "blk"), None, None),
        check_vma=False,
    )
```

```python
import functools
import math

import jax
import jax.numpy as jnp
import numpy as np
from jax import lax
from jax.experimental import pallas as pl
from jax.experimental.pallas import tpu as pltpu
from jax.sharding import PartitionSpec as P

CH = 128
F = 256
LAGS = 128
W = 2
LOW_BITS = 4


def bin_order(bins):
    return np.concatenate([np.arange(2, bins + 1, 2), np.arange(1, bins + 1, 2)])


def forward_table(nfft, bins):
    sample = np.arange(nfft // 2, dtype=np.int64)[:, None]
    angle = (sample * bin_order(bins)[None, :] % nfft) * (2.0 * math.pi / nfft)
    cos, sin = np.cos(angle), np.sin(angle)
    half = bins // 2
    table = [cos[:, :half], -sin[:, :half], cos[:, half:], -sin[:, half:]]
    return np.concatenate(table, axis=1).astype(np.float32).astype(jnp.bfloat16)


def lag_tables(nfft, bins, lags, scale):
    half = lags // 2
    count = lags + 1
    place = np.arange(count)
    middle = ((count - 1 - 2 * place) / 2.0) ** 2 * math.cos(2.0 * math.pi * bins / nfft)
    aside = (place[1:] * (count - place[1:])) / 2.0
    _, basis = np.linalg.eigh(np.diag(middle) + np.diag(aside, 1) + np.diag(aside, -1))
    basis = basis[:, ::-1][:, :half]
    even, odd = basis[:, 0::2], basis[:, 1::2]
    even = even * np.sign(even[half])
    odd = odd * np.sign(odd[half + 1])
    freq = bin_order(bins)[None, :]
    angle = (freq * (place[:, None] - half) % nfft) * (2.0 * math.pi / nfft)
    rows = [even.T @ np.cos(angle), odd.T @ -np.sin(angle)]
    rest = np.cos(angle) - np.sin(angle) - even @ rows[0] - odd @ rows[1]
    assert np.abs(rest).max() < 1e-7
    rows = np.concatenate(rows + [-rows[1]])
    basis = np.concatenate([even, odd], axis=1)[:lags].T * scale
    blank = np.zeros_like(basis)
    spread = np.concatenate(
        [np.concatenate([basis if k == n else blank for n in range(4)], axis=1) for k in range(4)]
    )

    def narrow(table):
        return (np.round(table * 2.0**28) / 2.0**28).astype(np.float32).astype(jnp.bfloat16)

    return narrow(rows), narrow(spread)


def iota(shape, dim):
    return lax.broadcasted_iota(jnp.int32, shape, dim)


LABELS = 8


def full_plan(capacity, chunks):
    return (capacity,) * chunks


def short_plan(capacity, chunks):
    eighths = (8, 8, 8, 8, 8, 8, 8, 8, 8, 7, 7, 6, 6, 5, 4, 3)
    return tuple(capacity * eighths[c * len(eighths) // chunks] // 8 for c in range(chunks))


def pack_kernel(
    owners, capacity, plans, me_ref, dest_hbm, slot_hbm, valid_hbm, records_hbm, *refs
):
    *out_refs, dest_ref, slot_ref, valid_ref, records_ref, sems = refs
    held, nfft = records_ref.shape
    rows = owners * capacity
    width = 512
    small = [
        pltpu.make_async_copy(source, target, sems.at[k])
        for k, (source, target) in enumerate(
            [(dest_hbm, dest_ref), (slot_hbm, slot_ref), (valid_hbm, valid_ref)]
        )
    ]
    large = [
        pltpu.make_async_copy(
            records_hbm.at[:, pl.ds(begin, width)],
            records_ref.at[:, pl.ds(begin, width)],
            sems.at[3 + begin // width],
        )
        for begin in range(0, nfft, width)
    ]
    for copy in small + large:
        copy.start()
    for copy in small:
        copy.wait()
    part = dest_ref[...]
    if len(out_refs) > 1:
        part = part ^ me_ref[0]
    valid = valid_ref[...]
    first = valid * held + (held - 1 - iota((1, held), 1))

    def column(row):
        wide = jnp.transpose(jnp.broadcast_to(row.astype(jnp.float32), (128, held)))
        return jnp.concatenate([wide] * (held // 128), axis=1)

    same = column(part) == part.astype(jnp.float32)
    before = jnp.where(same & (column(first) > first.astype(jnp.float32)), 1.0, 0.0)
    rank = jnp.sum(before, axis=0, keepdims=True).astype(jnp.int32)
    over = jnp.zeros((1, held), jnp.int32)
    for plan in sorted(set(plans)):
        member = functools.reduce(
            jnp.logical_or, [part == d for d in range(owners) if plans[d] == plan]
        )
        for size in sorted(set(plan)):
            if size < capacity:
                reach = 128 * sum(count > size for count in plan)
                over += jnp.where(member & (rank >= size) & (valid > reach), 1, 0)
    over = jnp.max(jnp.minimum(over, 1).astype(jnp.float32), axis=1, keepdims=True)
    position = part * capacity + rank
    order = (iota((rows, held), 0) == position).astype(jnp.float32).astype(jnp.bfloat16)
    row = iota((16, held), 0)
    labels = jnp.where(
        row == 0,
        slot_ref[...],
        jnp.where(
            row == 1,
            valid >> LOW_BITS,
            jnp.where(row == 2, valid & ((1 << LOW_BITS) - 1), 0),
        ),
    )
    moved = lax.dot_general(
        labels.astype(jnp.float32).astype(jnp.bfloat16),
        order,
        (((1,), (1,)), ((), ())),
        preferred_element_type=jnp.float32,
    )
    moved = jnp.where(iota((16, rows), 0) == 3, over, moved).astype(jnp.bfloat16)

    def put(d, at, value):
        if len(out_refs) > 1:
            out_refs[d][at : at + value.shape[0], :] = value
        else:
            out_refs[0][d, at : at + value.shape[0], :] = value

    for d in range(owners):
        at = d * capacity // 128 * 128
        put(d, sum(plans[d]), moved[:LABELS, at : at + 128])
    for begin in range(0, nfft, width):
        large[begin // width].wait()
        ordered = jnp.dot(
            order, records_ref[:, begin : begin + width], preferred_element_type=jnp.float32
        ).astype(jnp.bfloat16)
        for lane in range(0, width, 128):
            c = (begin + lane) // 128
            for d in range(owners):
                top = d * capacity
                put(d, sum(plans[d][:c]), ordered[top : top + plans[d][c], lane : lane + 128])


def pack(me, labels, records, capacity, plans, split):
    held, nfft = records.shape
    owners = len(plans)
    hbm = pl.BlockSpec(memory_space=pltpu.HBM)
    vmem = pl.BlockSpec(memory_space=pltpu.VMEM)
    shapes = [(sum(plan) + LABELS, 128) for plan in plans]
    if not split:
        shapes = [(owners,) + shapes[0]]
    return pl.pallas_call(
        functools.partial(pack_kernel, owners, capacity, plans),
        in_specs=[pl.BlockSpec(memory_space=pltpu.SMEM)] + [hbm] * 4,
        out_specs=[vmem] * len(shapes),
        out_shape=[jax.ShapeDtypeStruct(shape, jnp.bfloat16) for shape in shapes],
        scratch_shapes=[pltpu.VMEM((1, held), jnp.int32)] * 3
        + [pltpu.VMEM((held, nfft), jnp.bfloat16), pltpu.SemaphoreType.DMA((3 + nfft // 512,))],
        compiler_params=pltpu.CompilerParams(vmem_limit_bytes=48 * 1024 * 1024),
        name="pack",
    )(me, *labels, records)


def whiten_kernel(capacity, plans, places, me_ref, mask_ref, *refs):
    *arrived_refs, table_hbm, low_ref, high_ref, branch_ref, table_ref, trace_ref, spectrum_ref, sems = refs
    owners = len(plans)
    split = len(arrived_refs) > 1
    nfft = trace_ref.shape[1]
    rows = owners * capacity
    slots = CH * W
    bins = table_ref.shape[1] // 2
    shift = capacity.bit_length() - 1
    width = 256
    depth = 512
    loads = [
        pltpu.make_async_copy(
            table_hbm.at[pl.ds(at, depth)], table_ref.at[pl.ds(at, depth)], sems.at[at // depth]
        )
        for at in range(0, nfft // 2, depth)
    ]
    for copy in loads:
        copy.start()

    def take(c):
        if not split:
            at, count = sum(plans[0][:c]), plans[0][c] if c < len(plans[0]) else LABELS
            return arrived_refs[0][:, at : at + count, :].reshape(owners * count, 128)
        pieces = []
        for ref, plan in zip(arrived_refs, plans):
            at, count = sum(plan[:c]), plan[c] if c < len(plan) else LABELS
            pieces.append(ref[at : at + count, :])
            if c < len(plan) and count < capacity:
                pieces.append(jnp.zeros((capacity - count, 128), jnp.bfloat16))
        return jnp.concatenate(pieces, axis=0)

    labels = take(len(plans[0])).astype(jnp.float32).reshape(owners, LABELS, 128)
    which = iota((owners, LABELS, 128), 1)
    over = jnp.max(jnp.where(which == 3, labels, 0.0))
    branch_ref[0] = jnp.where(over > 0.0, owners - 2, mask_ref[0] - 1)
    parts = jnp.concatenate(
        [jnp.sum(jnp.where(which == k, labels, 0.0), axis=1) for k in range(3)], axis=0
    )
    if split:
        part = iota((1, rows), 1) >> shift
        place = functools.reduce(
            lambda total, p: total + jnp.where(part == p, places[p], 0),
            range(owners),
            jnp.zeros((1, rows), jnp.int32),
        )
    else:
        place = me_ref[0]
    base = (place * capacity) & 127
    pick = iota((128, rows), 0) == base + (iota((128, rows), 1) & (capacity - 1))
    picked = jnp.dot(
        parts.astype(jnp.bfloat16),
        pick.astype(jnp.float32).astype(jnp.bfloat16),
        preferred_element_type=jnp.float32,
    )
    source = iota((owners, rows), 0) == iota((owners, rows), 1) >> shift
    rowed = [
        jnp.sum(
            jnp.where(source, picked[k * owners : (k + 1) * owners], 0.0), axis=0, keepdims=True
        )
        for k in range(3)
    ]
    slot_row = rowed[0].astype(jnp.int32)
    place = (slot_row & (W - 1)) * CH + (slot_row >> (W.bit_length() - 1))
    valid_row = rowed[1] * float(1 << LOW_BITS) + rowed[2]
    scatter = (iota((slots, rows), 0) == place).astype(jnp.float32).astype(jnp.bfloat16)
    valid_col = jnp.transpose(jnp.broadcast_to(valid_row, (128, rows))).astype(jnp.int32)
    power = jnp.zeros((slots, 128), jnp.float32)
    for begin in range(0, nfft, width):
        lanes = range(begin, begin + width, 128)
        inside = jnp.concatenate(
            [
                (iota((rows, 128), 1) + lane < valid_col).astype(jnp.float32).astype(jnp.bfloat16)
                for lane in lanes
            ],
            axis=1,
        )
        arrived = jnp.concatenate([take(lane // 128) for lane in lanes], axis=1)
        summed = jnp.dot(scatter, arrived * inside, preferred_element_type=jnp.float32)
        coverage = jnp.dot(scatter, inside, preferred_element_type=jnp.float32)
        trace = summed / jnp.maximum(coverage, 1.0)
        trace_ref[:, begin : begin + width] = trace
        square = trace * trace
        for lane in range(0, width, 128):
            power = power + square[:, lane : lane + 128]
    meansq = jnp.sum(power, axis=1, keepdims=True) * (1.0 / nfft)
    gain = lax.rsqrt(meansq + 1e-06)
    for begin in range(0, nfft // 2, depth):
        loads[begin // depth].wait()
        near = trace_ref[:, begin : begin + depth] * gain
        far = trace_ref[:, begin + nfft // 2 : begin + nfft // 2 + depth] * gain
        for at, folded in ((0, near + far), (bins, near - far)):
            part = jnp.dot(
                folded.astype(jnp.bfloat16),
                table_ref[begin : begin + depth, at : at + bins],
                preferred_element_type=jnp.float32,
            )
            if begin == 0:
                spectrum_ref[:, at : at + bins] = part
            else:
                spectrum_ref[:, at : at + bins] += part
    half = bins // 2
    for at in (0, bins):
        real_part = spectrum_ref[:, at : at + half]
        imag_part = spectrum_ref[:, at + half : at + bins]
        amplitude = lax.rsqrt(
            jnp.maximum(real_part * real_part + imag_part * imag_part, nfft / 4.0)
        )
        for part, offset in ((real_part, 0), (imag_part, bins)):
            white = (part * amplitude).astype(jnp.bfloat16)
            for w in range(W):
                lane = w * 2 * bins + offset + at // 2
                top = w * CH
                low_ref[:, lane : lane + half] = white[top : top + CH // 2]
                high_ref[:, lane : lane + half] = white[top + CH // 2 : top + CH]


def whiten(me, mask, arrived, table, capacity, plans, places):
    nfft, width = 2 * table.shape[0], table.shape[1]
    vmem = pl.BlockSpec(memory_space=pltpu.VMEM)
    smem = pl.BlockSpec(memory_space=pltpu.SMEM)
    return pl.pallas_call(
        functools.partial(whiten_kernel, capacity, plans, places),
        in_specs=[smem, smem]
        + [vmem] * len(arrived)
        + [pl.BlockSpec(memory_space=pltpu.HBM)],
        out_specs=[vmem, vmem, smem],
        out_shape=[
            jax.ShapeDtypeStruct((CH // 2, W * width), jnp.bfloat16),
            jax.ShapeDtypeStruct((CH // 2, W * width), jnp.bfloat16),
            jax.ShapeDtypeStruct((1,), jnp.int32),
        ],
        scratch_shapes=[
            pltpu.VMEM(table.shape, jnp.bfloat16),
            pltpu.VMEM((CH * W, nfft), jnp.float32),
            pltpu.VMEM((CH * W, width), jnp.float32),
            pltpu.SemaphoreType.DMA((nfft // 1024,)),
        ],
        compiler_params=pltpu.CompilerParams(vmem_limit_bytes=50 * 1024 * 1024),
        name="whiten",
    )(me, mask, *arrived, table)


BLOCK = 32
PIECE = 16


def correlate_kernel(
    order_ref, own_low, own_high, rows_ref, spread_ref, *refs
):
    *partners, out_hbm, both_ref, wide_ref, near_ref, turned_a, turned_b, found_a, found_b, out_ref, sems, loaded = refs
    bins = rows_ref.shape[1]
    terms = rows_ref.shape[0] // 3
    lags = out_ref.shape[4]
    blocks = CH // BLOCK
    turned, found = (turned_a, turned_b), (found_a, found_b)

    def turn(block, slot):
        even = rows_ref[:terms, :]
        odd = rows_ref[terms : 2 * terms, :]
        minus = rows_ref[2 * terms :, :]
        for k in range(BLOCK):
            u = wide_ref[pl.ds(block * BLOCK + k, 1), :]
            top = slice(2 * k * terms, (2 * k + 1) * terms)
            low = slice((2 * k + 1) * terms, (2 * k + 2) * terms)
            for w in range(W):
                at = w * 2 * bins
                real, imag = slice(at, at + bins), slice(at + bins, at + 2 * bins)
                ur = jnp.broadcast_to(u[:, real], (terms, bins)).astype(jnp.bfloat16)
                ui = jnp.broadcast_to(u[:, imag], (terms, bins)).astype(jnp.bfloat16)
                turned[slot][top, real] = ur * even
                turned[slot][top, imag] = ui * even
                turned[slot][low, real] = ui * odd
                turned[slot][low, imag] = ur * minus

    def find(slot):
        sums = jnp.dot(turned[slot][...], both_ref[...], preferred_element_type=jnp.float32)
        found[slot][...] = jnp.transpose(sums.astype(jnp.bfloat16))

    def spread(slot, block):
        wide = 8 * terms
        for piece in range(BLOCK // PIECE):
            start = 2 * piece * PIECE * terms
            stacked = jnp.concatenate(
                [
                    found[slot][:, k : k + wide]
                    for k in range(start, start + 2 * PIECE * terms, wide)
                ],
                axis=0,
            )
            lagged = jnp.dot(
                stacked, spread_ref[...], preferred_element_type=jnp.float32
            ).astype(jnp.bfloat16)
            unit = block * (BLOCK // PIECE) + piece
            for k in range(PIECE):
                for r in range(2):
                    top = (k // 4 * 2 + r) * CH
                    lane = k % 4 * lags
                    out_ref[unit, r, k] = lagged[top : top + CH, lane : lane + lags]
            write(unit).start()

    def write(unit):
        return pltpu.make_async_copy(
            out_ref.at[unit], out_hbm.at[:, pl.ds(unit * PIECE, PIECE)], sems.at[unit]
        )

    half = CH // 2
    loads = [
        pltpu.make_async_copy(source, near_ref.at[pl.ds(k * half, half)], loaded.at[k])
        for k, source in enumerate(partners)
    ]
    for copy in loads:
        copy.start()
    wide_ref[:half, :] = own_low[...].astype(jnp.float32)
    wide_ref[half:, :] = own_high[...].astype(jnp.float32)
    turn(0, 0)
    for copy in loads:
        copy.wait()
    at = pl.multiple_of(order_ref[0] * CH, CH)
    both_ref[:, pl.ds(at, CH)] = jnp.transpose(near_ref[:CH, :])
    both_ref[:, pl.ds(CH - at, CH)] = jnp.transpose(near_ref[CH:, :])
    turn(1, 1)
    find(0)
    for block in range(1, blocks):
        if block + 1 < blocks:
            turn(block + 1, (block + 1) % 2)
        find(block % 2)
        spread((block - 1) % 2, block - 1)
    spread((blocks - 1) % 2, blocks - 1)
    for unit in range(CH // PIECE):
        write(unit).wait()


def correlate(order, own, first, second, nfft, lags):
    depth = own[0].shape[1]
    bins = depth // (2 * W)
    rows, spread = lag_tables(nfft, bins, lags, 1.0 / math.sqrt(W * bins))
    terms = rows.shape[0] // 3
    vmem = pl.BlockSpec(memory_space=pltpu.VMEM)
    return pl.pallas_call(
        correlate_kernel,
        in_specs=[pl.BlockSpec(memory_space=pltpu.SMEM)]
        + [vmem] * 4
        + [pl.BlockSpec(memory_space=pltpu.HBM)] * 4,
        out_specs=pl.BlockSpec(memory_space=pltpu.HBM),
        out_shape=jax.ShapeDtypeStruct((2, CH, CH, lags), jnp.bfloat16),
        scratch_shapes=[
            pltpu.VMEM((depth, 2 * CH), jnp.bfloat16),
            pltpu.VMEM((CH, depth), jnp.float32),
            pltpu.VMEM((2 * CH, depth), jnp.bfloat16),
            pltpu.VMEM((BLOCK * 2 * terms, depth), jnp.bfloat16),
            pltpu.VMEM((BLOCK * 2 * terms, depth), jnp.bfloat16),
            pltpu.VMEM((2 * CH, BLOCK * 2 * terms), jnp.bfloat16),
            pltpu.VMEM((2 * CH, BLOCK * 2 * terms), jnp.bfloat16),
            pltpu.VMEM((CH // PIECE, 2, PIECE, CH, lags), jnp.bfloat16),
            pltpu.SemaphoreType.DMA((CH // PIECE,)),
            pltpu.SemaphoreType.DMA((4,)),
        ],
        compiler_params=pltpu.CompilerParams(vmem_limit_bytes=60 * 1024 * 1024),
        name="correlate",
    )(order, *own, jnp.asarray(rows), jnp.asarray(spread), *first, *second)


def swap(block, mask):
    count = lax.axis_size("blk")
    return lax.ppermute(block, "blk", [(low, low ^ mask) for low in range(count)])


def swap_halves(tile, mask):
    return tuple(swap(half, mask) for half in tile)


def exchange(mask, moving):
    count = lax.axis_size("blk")
    full = count - 1
    first = swap_halves(moving, full)
    if 2 * mask >= count:
        return moving, first, swap_halves(first, mask ^ full)
    return moving, first, swap_halves(moving, mask)


def deliver(me, mask, labels, records, plan):
    owners = lax.axis_size("blk")
    held, nfft = records.shape
    capacity = max(16, 2 * held // owners)
    whole = full_plan(capacity, nfft // 128)
    table = jnp.asarray(forward_table(nfft, F))
    if owners > 16:
        plans = (whole,) * owners
        (outgoing,) = pack(me, labels, records, capacity, plans, False)
        arrived = [lax.all_to_all(outgoing, "blk", split_axis=0, concat_axis=0, tiled=True)]
        *tile, branch = whiten(me, mask, arrived, table, capacity, plans, None)
        return tuple(tile), branch
    half = owners // 2
    plans = (whole,) + (plan(capacity, nfft // 128),) * (owners - 1)
    outgoing = pack(me, labels, records, capacity, plans, True)
    places = [half]
    for distance in range(1, half):
        places += [distance, half + distance]
    arrived = [swap(outgoing[distance], distance) for distance in places] + [outgoing[0]]
    places.append(0)
    ordered = tuple(plans[distance] for distance in places)
    *tile, branch = whiten(me, mask, arrived, table, capacity, ordered, places)
    return tuple(tile), branch


def local(records, dest, slot, valid, masks):
    owners = lax.axis_size("blk")
    held, nfft = records.shape
    full = owners - 1
    me = lax.axis_index("blk").astype(jnp.int32).reshape(1)
    mask = (masks[0] + masks[1] - full).reshape(1)
    labels = [label.reshape(1, held) for label in (dest, slot, valid)]
    if owners <= 16:
        tile, branch = deliver(me, mask, labels, records, short_plan)
        known = [functools.partial(exchange, m) for m in range(1, full)]

        def again(tile):
            tile, branch = deliver(me, mask, labels, records, full_plan)
            return lax.switch(branch[0], known, tile)

        own, first, second = lax.switch(branch[0], known + [again], tile)
    else:
        own, _ = deliver(me, mask, labels, records, full_plan)
        second = own
        for bit in range(owners.bit_length() - 1):
            moved = swap_halves(second, 1 << bit)
            flip = mask >> bit & 1 == 1
            second = tuple(jnp.where(flip, new, old) for new, old in zip(moved, second))
        first = swap_halves(own, full)
    order = (masks[:1] != full).astype(jnp.int32)
    return correlate(order, own, first, second, nfft, LAGS)


def solution(mesh):
    return jax.shard_map(
        local,
        mesh=mesh,
        in_specs=(
            P(("groups", "blk"), None),
            P(("groups", "blk"), None),
            P(("groups", "blk"), None),
            P(("groups", "blk"), None),
            P(),
        ),
        out_specs=P(None, ("groups", "blk"), None, None),
        check_vma=False,
    )
```

```python
import functools
import math

import jax
import jax.numpy as jnp
import numpy as np
from jax import lax
from jax.experimental import pallas as pl
from jax.experimental.pallas import tpu as pltpu
from jax.sharding import PartitionSpec as P

CH = 128
F = 256
LAGS = 128
W = 2
LOW_BITS = 4


def bin_order(bins):
    return np.concatenate([np.arange(2, bins + 1, 2), np.arange(1, bins + 1, 2)])


def forward_table(nfft, bins):
    sample = np.arange(nfft // 2, dtype=np.int64)[:, None]
    angle = (sample * bin_order(bins)[None, :] % nfft) * (2.0 * math.pi / nfft)
    cos, sin = np.cos(angle), np.sin(angle)
    half = bins // 2
    table = [cos[:, :half], -sin[:, :half], cos[:, half:], -sin[:, half:]]
    return np.concatenate(table, axis=1).astype(np.float32).astype(jnp.bfloat16)


def lag_tables(nfft, bins, lags, scale):
    half = lags // 2
    count = lags + 1
    place = np.arange(count)
    middle = ((count - 1 - 2 * place) / 2.0) ** 2 * math.cos(2.0 * math.pi * bins / nfft)
    aside = (place[1:] * (count - place[1:])) / 2.0
    _, basis = np.linalg.eigh(np.diag(middle) + np.diag(aside, 1) + np.diag(aside, -1))
    basis = basis[:, ::-1][:, :half]
    even, odd = basis[:, 0::2], basis[:, 1::2]
    even = even * np.sign(even[half])
    odd = odd * np.sign(odd[half + 1])
    freq = bin_order(bins)[None, :]
    angle = (freq * (place[:, None] - half) % nfft) * (2.0 * math.pi / nfft)
    rows = [even.T @ np.cos(angle), odd.T @ -np.sin(angle)]
    rest = np.cos(angle) - np.sin(angle) - even @ rows[0] - odd @ rows[1]
    assert np.abs(rest).max() < 1e-7
    rows = np.concatenate(rows + [-rows[1]])
    basis = np.concatenate([even, odd], axis=1)[:lags].T * scale
    blank = np.zeros_like(basis)
    spread = np.concatenate(
        [np.concatenate([basis if k == n else blank for n in range(4)], axis=1) for k in range(4)]
    )

    def narrow(table):
        return (np.round(table * 2.0**28) / 2.0**28).astype(np.float32).astype(jnp.bfloat16)

    return narrow(rows), narrow(spread)


def iota(shape, dim):
    return lax.broadcasted_iota(jnp.int32, shape, dim)


LABELS = 8


def full_plan(capacity, chunks):
    return (capacity,) * chunks


def short_plan(capacity, chunks):
    eighths = (8, 8, 8, 8, 8, 8, 8, 8, 8, 7, 7, 6, 6, 5, 4, 3)
    return tuple(capacity * eighths[c * len(eighths) // chunks] // 8 for c in range(chunks))


def pack_kernel(
    owners, capacity, plans, me_ref, dest_hbm, slot_hbm, valid_hbm, records_hbm, *refs
):
    *out_refs, dest_ref, slot_ref, valid_ref, records_ref, sems = refs
    held, nfft = records_ref.shape
    rows = owners * capacity
    width = 512
    small = [
        pltpu.make_async_copy(source, target, sems.at[k])
        for k, (source, target) in enumerate(
            [(dest_hbm, dest_ref), (slot_hbm, slot_ref), (valid_hbm, valid_ref)]
        )
    ]
    large = [
        pltpu.make_async_copy(
            records_hbm.at[:, pl.ds(begin, width)],
            records_ref.at[:, pl.ds(begin, width)],
            sems.at[3 + begin // width],
        )
        for begin in range(0, nfft, width)
    ]
    for copy in small + large:
        copy.start()
    for copy in small:
        copy.wait()
    part = dest_ref[...]
    if len(out_refs) > 1:
        part = part ^ me_ref[0]
    valid = valid_ref[...]
    first = valid * held + (held - 1 - iota((1, held), 1))

    def column(row):
        wide = jnp.transpose(jnp.broadcast_to(row.astype(jnp.float32), (128, held)))
        return jnp.concatenate([wide] * (held // 128), axis=1)

    same = column(part) == part.astype(jnp.float32)
    before = jnp.where(same & (column(first) > first.astype(jnp.float32)), 1.0, 0.0)
    rank = jnp.sum(before, axis=0, keepdims=True).astype(jnp.int32)
    over = jnp.zeros((1, held), jnp.int32)
    for plan in sorted(set(plans)):
        member = functools.reduce(
            jnp.logical_or, [part == d for d in range(owners) if plans[d] == plan]
        )
        for size in sorted(set(plan)):
            if size < capacity:
                reach = 128 * sum(count > size for count in plan)
                over += jnp.where(member & (rank >= size) & (valid > reach), 1, 0)
    over = jnp.max(jnp.minimum(over, 1).astype(jnp.float32), axis=1, keepdims=True)
    position = part * capacity + rank
    order = (iota((rows, held), 0) == position).astype(jnp.float32).astype(jnp.bfloat16)
    row = iota((16, held), 0)
    labels = jnp.where(
        row == 0,
        slot_ref[...],
        jnp.where(
            row == 1,
            valid >> LOW_BITS,
            jnp.where(row == 2, valid & ((1 << LOW_BITS) - 1), 0),
        ),
    )
    moved = lax.dot_general(
        labels.astype(jnp.float32).astype(jnp.bfloat16),
        order,
        (((1,), (1,)), ((), ())),
        preferred_element_type=jnp.float32,
    )
    moved = jnp.where(iota((16, rows), 0) == 3, over, moved).astype(jnp.bfloat16)

    def put(d, at, value):
        if len(out_refs) > 1:
            out_refs[d][at : at + value.shape[0], :] = value
        else:
            out_refs[0][d, at : at + value.shape[0], :] = value

    for d in range(owners):
        at = d * capacity // 128 * 128
        put(d, sum(plans[d]), moved[:LABELS, at : at + 128])
    for begin in range(0, nfft, width):
        large[begin // width].wait()
        ordered = jnp.dot(
            order, records_ref[:, begin : begin + width], preferred_element_type=jnp.float32
        ).astype(jnp.bfloat16)
        for lane in range(0, width, 128):
            c = (begin + lane) // 128
            for d in range(owners):
                top = d * capacity
                put(d, sum(plans[d][:c]), ordered[top : top + plans[d][c], lane : lane + 128])


def pack(me, labels, records, capacity, plans, split):
    held, nfft = records.shape
    owners = len(plans)
    hbm = pl.BlockSpec(memory_space=pltpu.HBM)
    vmem = pl.BlockSpec(memory_space=pltpu.VMEM)
    shapes = [(sum(plan) + LABELS, 128) for plan in plans]
    if not split:
        shapes = [(owners,) + shapes[0]]
    return pl.pallas_call(
        functools.partial(pack_kernel, owners, capacity, plans),
        in_specs=[pl.BlockSpec(memory_space=pltpu.SMEM)] + [hbm] * 4,
        out_specs=[vmem] * len(shapes),
        out_shape=[jax.ShapeDtypeStruct(shape, jnp.bfloat16) for shape in shapes],
        scratch_shapes=[pltpu.VMEM((1, held), jnp.int32)] * 3
        + [pltpu.VMEM((held, nfft), jnp.bfloat16), pltpu.SemaphoreType.DMA((3 + nfft // 512,))],
        compiler_params=pltpu.CompilerParams(vmem_limit_bytes=48 * 1024 * 1024),
        name="pack",
    )(me, *labels, records)


def whiten_kernel(capacity, plans, places, me_ref, mask_ref, *refs):
    *arrived_refs, table_hbm, low_ref, high_ref, branch_ref, table_ref, trace_ref, spectrum_ref, sems = refs
    owners = len(plans)
    split = len(arrived_refs) > 1
    nfft = trace_ref.shape[1]
    rows = owners * capacity
    slots = CH * W
    bins = table_ref.shape[1] // 2
    shift = capacity.bit_length() - 1
    width = 256
    depth = 512
    loads = [
        pltpu.make_async_copy(
            table_hbm.at[pl.ds(at, depth)], table_ref.at[pl.ds(at, depth)], sems.at[at // depth]
        )
        for at in range(0, nfft // 2, depth)
    ]
    for copy in loads:
        copy.start()

    def take(c):
        if not split:
            at, count = sum(plans[0][:c]), plans[0][c] if c < len(plans[0]) else LABELS
            return arrived_refs[0][:, at : at + count, :].reshape(owners * count, 128)
        pieces = []
        for ref, plan in zip(arrived_refs, plans):
            at, count = sum(plan[:c]), plan[c] if c < len(plan) else LABELS
            pieces.append(ref[at : at + count, :])
            if c < len(plan) and count < capacity:
                pieces.append(jnp.zeros((capacity - count, 128), jnp.bfloat16))
        return jnp.concatenate(pieces, axis=0)

    labels = take(len(plans[0])).astype(jnp.float32).reshape(owners, LABELS, 128)
    which = iota((owners, LABELS, 128), 1)
    over = jnp.max(jnp.where(which == 3, labels, 0.0))
    branch_ref[0] = jnp.where(over > 0.0, owners - 2, mask_ref[0] - 1)
    parts = jnp.concatenate(
        [jnp.sum(jnp.where(which == k, labels, 0.0), axis=1) for k in range(3)], axis=0
    )
    if split:
        part = iota((1, rows), 1) >> shift
        place = functools.reduce(
            lambda total, p: total + jnp.where(part == p, places[p], 0),
            range(owners),
            jnp.zeros((1, rows), jnp.int32),
        )
    else:
        place = me_ref[0]
    base = (place * capacity) & 127
    pick = iota((128, rows), 0) == base + (iota((128, rows), 1) & (capacity - 1))
    picked = jnp.dot(
        parts.astype(jnp.bfloat16),
        pick.astype(jnp.float32).astype(jnp.bfloat16),
        preferred_element_type=jnp.float32,
    )
    source = iota((owners, rows), 0) == iota((owners, rows), 1) >> shift
    rowed = [
        jnp.sum(
            jnp.where(source, picked[k * owners : (k + 1) * owners], 0.0), axis=0, keepdims=True
        )
        for k in range(3)
    ]
    slot_row = rowed[0].astype(jnp.int32)
    place = (slot_row & (W - 1)) * CH + (slot_row >> (W.bit_length() - 1))
    valid_row = rowed[1] * float(1 << LOW_BITS) + rowed[2]
    scatter = (iota((slots, rows), 0) == place).astype(jnp.float32).astype(jnp.bfloat16)
    valid_col = jnp.transpose(jnp.broadcast_to(valid_row, (128, rows))).astype(jnp.int32)
    power = jnp.zeros((slots, 128), jnp.float32)
    for begin in range(0, nfft, width):
        lanes = range(begin, begin + width, 128)
        inside = jnp.concatenate(
            [
                (iota((rows, 128), 1) + lane < valid_col).astype(jnp.float32).astype(jnp.bfloat16)
                for lane in lanes
            ],
            axis=1,
        )
        arrived = jnp.concatenate([take(lane // 128) for lane in lanes], axis=1)
        summed = jnp.dot(scatter, arrived * inside, preferred_element_type=jnp.float32)
        coverage = jnp.dot(scatter, inside, preferred_element_type=jnp.float32)
        trace = summed / jnp.maximum(coverage, 1.0)
        trace_ref[:, begin : begin + width] = trace
        square = trace * trace
        for lane in range(0, width, 128):
            power = power + square[:, lane : lane + 128]
    meansq = jnp.sum(power, axis=1, keepdims=True) * (1.0 / nfft)
    gain = lax.rsqrt(meansq + 1e-06)
    for begin in range(0, nfft // 2, depth):
        loads[begin // depth].wait()
        near = trace_ref[:, begin : begin + depth] * gain
        far = trace_ref[:, begin + nfft // 2 : begin + nfft // 2 + depth] * gain
        for at, folded in ((0, near + far), (bins, near - far)):
            part = jnp.dot(
                folded.astype(jnp.bfloat16),
                table_ref[begin : begin + depth, at : at + bins],
                preferred_element_type=jnp.float32,
            )
            if begin == 0:
                spectrum_ref[:, at : at + bins] = part
            else:
                spectrum_ref[:, at : at + bins] += part
    half = bins // 2
    for at in (0, bins):
        real_part = spectrum_ref[:, at : at + half]
        imag_part = spectrum_ref[:, at + half : at + bins]
        amplitude = lax.rsqrt(
            jnp.maximum(real_part * real_part + imag_part * imag_part, nfft / 4.0)
        )
        for part, offset in ((real_part, 0), (imag_part, bins)):
            white = (part * amplitude).astype(jnp.bfloat16)
            for w in range(W):
                lane = w * 2 * bins + offset + at // 2
                top = w * CH
                low_ref[:, lane : lane + half] = white[top : top + CH // 2]
                high_ref[:, lane : lane + half] = white[top + CH // 2 : top + CH]


def whiten(me, mask, arrived, table, capacity, plans, places):
    nfft, width = 2 * table.shape[0], table.shape[1]
    vmem = pl.BlockSpec(memory_space=pltpu.VMEM)
    smem = pl.BlockSpec(memory_space=pltpu.SMEM)
    return pl.pallas_call(
        functools.partial(whiten_kernel, capacity, plans, places),
        in_specs=[smem, smem]
        + [vmem] * len(arrived)
        + [pl.BlockSpec(memory_space=pltpu.HBM)],
        out_specs=[vmem, vmem, smem],
        out_shape=[
            jax.ShapeDtypeStruct((CH // 2, W * width), jnp.bfloat16),
            jax.ShapeDtypeStruct((CH // 2, W * width), jnp.bfloat16),
            jax.ShapeDtypeStruct((1,), jnp.int32),
        ],
        scratch_shapes=[
            pltpu.VMEM(table.shape, jnp.bfloat16),
            pltpu.VMEM((CH * W, nfft), jnp.float32),
            pltpu.VMEM((CH * W, width), jnp.float32),
            pltpu.SemaphoreType.DMA((nfft // 1024,)),
        ],
        compiler_params=pltpu.CompilerParams(vmem_limit_bytes=50 * 1024 * 1024),
        name="whiten",
    )(me, mask, *arrived, table)


BLOCK = 64
PIECE = 16


def correlate_kernel(
    order_ref, own_low, own_high, rows_ref, spread_ref, *refs
):
    *partners, out_hbm, both_ref, wide_ref, near_ref, turned_a, turned_b, found_a, found_b, out_ref, sems, loaded = refs
    bins = rows_ref.shape[1]
    terms = rows_ref.shape[0] // 3
    lags = out_ref.shape[4]
    blocks = CH // BLOCK
    turned, found = (turned_a, turned_b), (found_a, found_b)

    def turn(block, slot):
        even = rows_ref[:terms, :]
        odd = rows_ref[terms : 2 * terms, :]
        minus = rows_ref[2 * terms :, :]
        for k in range(BLOCK):
            u = wide_ref[pl.ds(block * BLOCK + k, 1), :]
            top = slice(2 * k * terms, (2 * k + 1) * terms)
            low = slice((2 * k + 1) * terms, (2 * k + 2) * terms)
            for w in range(W):
                at = w * 2 * bins
                real, imag = slice(at, at + bins), slice(at + bins, at + 2 * bins)
                ur = jnp.broadcast_to(u[:, real], (terms, bins)).astype(jnp.bfloat16)
                ui = jnp.broadcast_to(u[:, imag], (terms, bins)).astype(jnp.bfloat16)
                turned[slot][top, real] = ur * even
                turned[slot][top, imag] = ui * even
                turned[slot][low, real] = ui * odd
                turned[slot][low, imag] = ur * minus

    def find(slot):
        sums = jnp.dot(turned[slot][...], both_ref[...], preferred_element_type=jnp.float32)
        found[slot][...] = jnp.transpose(sums.astype(jnp.bfloat16))

    def spread(slot, block):
        wide = 8 * terms
        for piece in range(BLOCK // PIECE):
            start = 2 * piece * PIECE * terms
            stacked = jnp.concatenate(
                [
                    found[slot][:, k : k + wide]
                    for k in range(start, start + 2 * PIECE * terms, wide)
                ],
                axis=0,
            )
            lagged = jnp.dot(
                stacked, spread_ref[...], preferred_element_type=jnp.float32
            ).astype(jnp.bfloat16)
            unit = block * (BLOCK // PIECE) + piece
            for k in range(PIECE):
                for r in range(2):
                    top = (k // 4 * 2 + r) * CH
                    lane = k % 4 * lags
                    out_ref[unit, r, k] = lagged[top : top + CH, lane : lane + lags]
            write(unit).start()

    def write(unit):
        return pltpu.make_async_copy(
            out_ref.at[unit], out_hbm.at[:, pl.ds(unit * PIECE, PIECE)], sems.at[unit]
        )

    half = CH // 2
    loads = [
        pltpu.make_async_copy(source, near_ref.at[pl.ds(k * half, half)], loaded.at[k])
        for k, source in enumerate(partners)
    ]
    for copy in loads:
        copy.start()
    wide_ref[:half, :] = own_low[...].astype(jnp.float32)
    wide_ref[half:, :] = own_high[...].astype(jnp.float32)
    turn(0, 0)
    for copy in loads:
        copy.wait()
    at = pl.multiple_of(order_ref[0] * CH, CH)
    both_ref[:, pl.ds(at, CH)] = jnp.transpose(near_ref[:CH, :])
    both_ref[:, pl.ds(CH - at, CH)] = jnp.transpose(near_ref[CH:, :])
    turn(1, 1)
    find(0)
    for block in range(1, blocks):
        if block + 1 < blocks:
            turn(block + 1, (block + 1) % 2)
        find(block % 2)
        spread((block - 1) % 2, block - 1)
    spread((blocks - 1) % 2, blocks - 1)
    for unit in range(CH // PIECE):
        write(unit).wait()


def correlate(order, own, first, second, nfft, lags):
    depth = own[0].shape[1]
    bins = depth // (2 * W)
    rows, spread = lag_tables(nfft, bins, lags, 1.0 / math.sqrt(W * bins))
    terms = rows.shape[0] // 3
    vmem = pl.BlockSpec(memory_space=pltpu.VMEM)
    return pl.pallas_call(
        correlate_kernel,
        in_specs=[pl.BlockSpec(memory_space=pltpu.SMEM)]
        + [vmem] * 4
        + [pl.BlockSpec(memory_space=pltpu.HBM)] * 4,
        out_specs=pl.BlockSpec(memory_space=pltpu.HBM),
        out_shape=jax.ShapeDtypeStruct((2, CH, CH, lags), jnp.bfloat16),
        scratch_shapes=[
            pltpu.VMEM((depth, 2 * CH), jnp.bfloat16),
            pltpu.VMEM((CH, depth), jnp.float32),
            pltpu.VMEM((2 * CH, depth), jnp.bfloat16),
            pltpu.VMEM((BLOCK * 2 * terms, depth), jnp.bfloat16),
            pltpu.VMEM((BLOCK * 2 * terms, depth), jnp.bfloat16),
            pltpu.VMEM((2 * CH, BLOCK * 2 * terms), jnp.bfloat16),
            pltpu.VMEM((2 * CH, BLOCK * 2 * terms), jnp.bfloat16),
            pltpu.VMEM((CH // PIECE, 2, PIECE, CH, lags), jnp.bfloat16),
            pltpu.SemaphoreType.DMA((CH // PIECE,)),
            pltpu.SemaphoreType.DMA((4,)),
        ],
        compiler_params=pltpu.CompilerParams(vmem_limit_bytes=60 * 1024 * 1024),
        name="correlate",
    )(order, *own, jnp.asarray(rows), jnp.asarray(spread), *first, *second)


def swap(block, mask):
    count = lax.axis_size("blk")
    return lax.ppermute(block, "blk", [(low, low ^ mask) for low in range(count)])


def swap_halves(tile, mask):
    return tuple(swap(half, mask) for half in tile)


def exchange(mask, moving):
    count = lax.axis_size("blk")
    full = count - 1
    first = swap_halves(moving, full)
    if 2 * mask >= count:
        return moving, swap_halves(first, mask ^ full), first
    return moving, swap_halves(moving, mask), first


def deliver(me, mask, labels, records, plan):
    owners = lax.axis_size("blk")
    held, nfft = records.shape
    capacity = max(16, 2 * held // owners)
    whole = full_plan(capacity, nfft // 128)
    table = jnp.asarray(forward_table(nfft, F))
    if owners > 16:
        plans = (whole,) * owners
        (outgoing,) = pack(me, labels, records, capacity, plans, False)
        arrived = [lax.all_to_all(outgoing, "blk", split_axis=0, concat_axis=0, tiled=True)]
        *tile, branch = whiten(me, mask, arrived, table, capacity, plans, None)
        return tuple(tile), branch
    half = owners // 2
    plans = (whole,) + (plan(capacity, nfft // 128),) * (owners - 1)
    outgoing = pack(me, labels, records, capacity, plans, True)
    places = [half]
    for distance in range(1, half):
        places += [distance, half + distance]
    arrived = [swap(outgoing[distance], distance) for distance in places] + [outgoing[0]]
    places.append(0)
    ordered = tuple(plans[distance] for distance in places)
    *tile, branch = whiten(me, mask, arrived, table, capacity, ordered, places)
    return tuple(tile), branch


def local(records, dest, slot, valid, masks):
    owners = lax.axis_size("blk")
    held, nfft = records.shape
    full = owners - 1
    me = lax.axis_index("blk").astype(jnp.int32).reshape(1)
    mask = (masks[0] + masks[1] - full).reshape(1)
    labels = [label.reshape(1, held) for label in (dest, slot, valid)]
    if owners <= 16:
        tile, branch = deliver(me, mask, labels, records, short_plan)
        known = [functools.partial(exchange, m) for m in range(1, full)]

        def again(tile):
            tile, branch = deliver(me, mask, labels, records, full_plan)
            return lax.switch(branch[0], known, tile)

        own, second, first = lax.switch(branch[0], known + [again], tile)
    else:
        own, _ = deliver(me, mask, labels, records, full_plan)
        second = own
        for bit in range(owners.bit_length() - 1):
            moved = swap_halves(second, 1 << bit)
            flip = mask >> bit & 1 == 1
            second = tuple(jnp.where(flip, new, old) for new, old in zip(moved, second))
        first = swap_halves(own, full)
    order = (masks[:1] != full).astype(jnp.int32)
    return correlate(order, own, first, second, nfft, LAGS)


def solution(mesh):
    return jax.shard_map(
        local,
        mesh=mesh,
        in_specs=(
            P(("groups", "blk"), None),
            P(("groups", "blk"), None),
            P(("groups", "blk"), None),
            P(("groups", "blk"), None),
            P(),
        ),
        out_specs=P(None, ("groups", "blk"), None, None),
        check_vma=False,
    )
```

```python
import functools
import math

import jax
import jax.numpy as jnp
import numpy as np
from jax import lax
from jax.experimental import pallas as pl
from jax.experimental.pallas import tpu as pltpu
from jax.sharding import PartitionSpec as P

CH = 128
F = 256
LAGS = 128
W = 2
LOW_BITS = 4


def bin_order(bins):
    return np.concatenate([np.arange(2, bins + 1, 2), np.arange(1, bins + 1, 2)])


def forward_table(nfft, bins):
    sample = np.arange(nfft // 2, dtype=np.int64)[:, None]
    angle = (sample * bin_order(bins)[None, :] % nfft) * (2.0 * math.pi / nfft)
    cos, sin = np.cos(angle), np.sin(angle)
    half = bins // 2
    table = [cos[:, :half], -sin[:, :half], cos[:, half:], -sin[:, half:]]
    return np.concatenate(table, axis=1).astype(np.float32).astype(jnp.bfloat16)


def lag_tables(nfft, bins, lags, scale):
    half = lags // 2
    count = lags + 1
    place = np.arange(count)
    middle = ((count - 1 - 2 * place) / 2.0) ** 2 * math.cos(2.0 * math.pi * bins / nfft)
    aside = (place[1:] * (count - place[1:])) / 2.0
    _, basis = np.linalg.eigh(np.diag(middle) + np.diag(aside, 1) + np.diag(aside, -1))
    basis = basis[:, ::-1][:, :half]
    even, odd = basis[:, 0::2], basis[:, 1::2]
    even = even * np.sign(even[half])
    odd = odd * np.sign(odd[half + 1])
    freq = bin_order(bins)[None, :]
    angle = (freq * (place[:, None] - half) % nfft) * (2.0 * math.pi / nfft)
    rows = [even.T @ np.cos(angle), odd.T @ -np.sin(angle)]
    rest = np.cos(angle) - np.sin(angle) - even @ rows[0] - odd @ rows[1]
    assert np.abs(rest).max() < 1e-7
    rows = np.concatenate(rows + [-rows[1]])
    basis = np.concatenate([even, odd], axis=1)[:lags].T * scale
    blank = np.zeros_like(basis)
    spread = np.concatenate(
        [np.concatenate([basis if k == n else blank for n in range(4)], axis=1) for k in range(4)]
    )

    def narrow(table):
        return (np.round(table * 2.0**28) / 2.0**28).astype(np.float32).astype(jnp.bfloat16)

    return narrow(rows), narrow(spread)


def iota(shape, dim):
    return lax.broadcasted_iota(jnp.int32, shape, dim)


LABELS = 8


def full_plan(capacity, chunks):
    return (capacity,) * chunks


def short_plan(capacity, chunks):
    eighths = (8, 8, 8, 8, 8, 8, 8, 8, 8, 7, 7, 6, 6, 5, 4, 3)
    return tuple(capacity * eighths[c * len(eighths) // chunks] // 8 for c in range(chunks))


def pack_kernel(
    owners, capacity, plans, me_ref, dest_hbm, slot_hbm, valid_hbm, records_hbm, *refs
):
    *out_refs, dest_ref, slot_ref, valid_ref, records_ref, sems = refs
    held, nfft = records_ref.shape
    rows = owners * capacity
    width = 512
    small = [
        pltpu.make_async_copy(source, target, sems.at[k])
        for k, (source, target) in enumerate(
            [(dest_hbm, dest_ref), (slot_hbm, slot_ref), (valid_hbm, valid_ref)]
        )
    ]
    large = [
        pltpu.make_async_copy(
            records_hbm.at[:, pl.ds(begin, width)],
            records_ref.at[:, pl.ds(begin, width)],
            sems.at[3 + begin // width],
        )
        for begin in range(0, nfft, width)
    ]
    for copy in small + large:
        copy.start()
    for copy in small:
        copy.wait()
    part = dest_ref[...]
    if len(out_refs) > 1:
        part = part ^ me_ref[0]
    valid = valid_ref[...]
    first = valid * held + (held - 1 - iota((1, held), 1))

    def column(row):
        wide = jnp.transpose(jnp.broadcast_to(row.astype(jnp.float32), (128, held)))
        return jnp.concatenate([wide] * (held // 128), axis=1)

    same = column(part) == part.astype(jnp.float32)
    before = jnp.where(same & (column(first) > first.astype(jnp.float32)), 1.0, 0.0)
    rank = jnp.sum(before, axis=0, keepdims=True).astype(jnp.int32)
    over = jnp.zeros((1, held), jnp.int32)
    for plan in sorted(set(plans)):
        member = functools.reduce(
            jnp.logical_or, [part == d for d in range(owners) if plans[d] == plan]
        )
        for size in sorted(set(plan)):
            if size < capacity:
                reach = 128 * sum(count > size for count in plan)
                over += jnp.where(member & (rank >= size) & (valid > reach), 1, 0)
    over = jnp.max(jnp.minimum(over, 1).astype(jnp.float32), axis=1, keepdims=True)
    position = part * capacity + rank
    order = (iota((rows, held), 0) == position).astype(jnp.float32).astype(jnp.bfloat16)
    row = iota((16, held), 0)
    labels = jnp.where(
        row == 0,
        slot_ref[...],
        jnp.where(
            row == 1,
            valid >> LOW_BITS,
            jnp.where(row == 2, valid & ((1 << LOW_BITS) - 1), 0),
        ),
    )
    moved = lax.dot_general(
        labels.astype(jnp.float32).astype(jnp.bfloat16),
        order,
        (((1,), (1,)), ((), ())),
        preferred_element_type=jnp.float32,
    )
    moved = jnp.where(iota((16, rows), 0) == 3, over, moved).astype(jnp.bfloat16)

    def put(d, at, value):
        if len(out_refs) > 1:
            out_refs[d][at : at + value.shape[0], :] = value
        else:
            out_refs[0][d, at : at + value.shape[0], :] = value

    for d in range(owners):
        at = d * capacity // 128 * 128
        put(d, sum(plans[d]), moved[:LABELS, at : at + 128])
    for begin in range(0, nfft, width):
        large[begin // width].wait()
        ordered = jnp.dot(
            order, records_ref[:, begin : begin + width], preferred_element_type=jnp.float32
        ).astype(jnp.bfloat16)
        for lane in range(0, width, 128):
            c = (begin + lane) // 128
            for d in range(owners):
                top = d * capacity
                put(d, sum(plans[d][:c]), ordered[top : top + plans[d][c], lane : lane + 128])


def pack(me, labels, records, capacity, plans, split):
    held, nfft = records.shape
    owners = len(plans)
    hbm = pl.BlockSpec(memory_space=pltpu.HBM)
    vmem = pl.BlockSpec(memory_space=pltpu.VMEM)
    shapes = [(sum(plan) + LABELS, 128) for plan in plans]
    if not split:
        shapes = [(owners,) + shapes[0]]
    return pl.pallas_call(
        functools.partial(pack_kernel, owners, capacity, plans),
        in_specs=[pl.BlockSpec(memory_space=pltpu.SMEM)] + [hbm] * 4,
        out_specs=[vmem] * len(shapes),
        out_shape=[jax.ShapeDtypeStruct(shape, jnp.bfloat16) for shape in shapes],
        scratch_shapes=[pltpu.VMEM((1, held), jnp.int32)] * 3
        + [pltpu.VMEM((held, nfft), jnp.bfloat16), pltpu.SemaphoreType.DMA((3 + nfft // 512,))],
        compiler_params=pltpu.CompilerParams(vmem_limit_bytes=48 * 1024 * 1024),
        name="pack",
    )(me, *labels, records)


def whiten_kernel(capacity, plans, places, me_ref, mask_ref, *refs):
    *arrived_refs, table_hbm, low_ref, high_ref, branch_ref, table_ref, trace_ref, spectrum_ref, sems = refs
    owners = len(plans)
    split = len(arrived_refs) > 1
    nfft = trace_ref.shape[1]
    rows = owners * capacity
    slots = CH * W
    bins = table_ref.shape[1] // 2
    shift = capacity.bit_length() - 1
    width = 512
    depth = 512
    loads = [
        pltpu.make_async_copy(
            table_hbm.at[pl.ds(at, depth)], table_ref.at[pl.ds(at, depth)], sems.at[at // depth]
        )
        for at in range(0, nfft // 2, depth)
    ]
    for copy in loads:
        copy.start()

    def take(c):
        if not split:
            at, count = sum(plans[0][:c]), plans[0][c] if c < len(plans[0]) else LABELS
            return arrived_refs[0][:, at : at + count, :].reshape(owners * count, 128)
        pieces = []
        for ref, plan in zip(arrived_refs, plans):
            at, count = sum(plan[:c]), plan[c] if c < len(plan) else LABELS
            pieces.append(ref[at : at + count, :])
            if c < len(plan) and count < capacity:
                pieces.append(jnp.zeros((capacity - count, 128), jnp.bfloat16))
        return jnp.concatenate(pieces, axis=0)

    labels = take(len(plans[0])).astype(jnp.float32).reshape(owners, LABELS, 128)
    which = iota((owners, LABELS, 128), 1)
    over = jnp.max(jnp.where(which == 3, labels, 0.0))
    branch_ref[0] = jnp.where(over > 0.0, owners - 2, mask_ref[0] - 1)
    parts = jnp.concatenate(
        [jnp.sum(jnp.where(which == k, labels, 0.0), axis=1) for k in range(3)], axis=0
    )
    if split:
        part = iota((1, rows), 1) >> shift
        place = functools.reduce(
            lambda total, p: total + jnp.where(part == p, places[p], 0),
            range(owners),
            jnp.zeros((1, rows), jnp.int32),
        )
    else:
        place = me_ref[0]
    base = (place * capacity) & 127
    pick = iota((128, rows), 0) == base + (iota((128, rows), 1) & (capacity - 1))
    picked = jnp.dot(
        parts.astype(jnp.bfloat16),
        pick.astype(jnp.float32).astype(jnp.bfloat16),
        preferred_element_type=jnp.float32,
    )
    source = iota((owners, rows), 0) == iota((owners, rows), 1) >> shift
    rowed = [
        jnp.sum(
            jnp.where(source, picked[k * owners : (k + 1) * owners], 0.0), axis=0, keepdims=True
        )
        for k in range(3)
    ]
    slot_row = rowed[0].astype(jnp.int32)
    place = (slot_row & (W - 1)) * CH + (slot_row >> (W.bit_length() - 1))
    valid_row = rowed[1] * float(1 << LOW_BITS) + rowed[2]
    scatter = (iota((slots, rows), 0) == place).astype(jnp.float32).astype(jnp.bfloat16)
    valid_col = jnp.transpose(jnp.broadcast_to(valid_row, (128, rows))).astype(jnp.int32)
    power = jnp.zeros((slots, 128), jnp.float32)
    for begin in range(0, nfft, width):
        lanes = range(begin, begin + width, 128)
        inside = jnp.concatenate(
            [
                (iota((rows, 128), 1) + lane < valid_col).astype(jnp.float32).astype(jnp.bfloat16)
                for lane in lanes
            ],
            axis=1,
        )
        arrived = jnp.concatenate([take(lane // 128) for lane in lanes], axis=1)
        summed = jnp.dot(scatter, arrived * inside, preferred_element_type=jnp.float32)
        coverage = jnp.dot(scatter, inside, preferred_element_type=jnp.float32)
        trace = summed / jnp.maximum(coverage, 1.0)
        trace_ref[:, begin : begin + width] = trace
        square = trace * trace
        for lane in range(0, width, 128):
            power = power + square[:, lane : lane + 128]
    meansq = jnp.sum(power, axis=1, keepdims=True) * (1.0 / nfft)
    gain = lax.rsqrt(meansq + 1e-06)
    for begin in range(0, nfft // 2, depth):
        loads[begin // depth].wait()
        near = trace_ref[:, begin : begin + depth] * gain
        far = trace_ref[:, begin + nfft // 2 : begin + nfft // 2 + depth] * gain
        for at, folded in ((0, near + far), (bins, near - far)):
            part = jnp.dot(
                folded.astype(jnp.bfloat16),
                table_ref[begin : begin + depth, at : at + bins],
                preferred_element_type=jnp.float32,
            )
            if begin == 0:
                spectrum_ref[:, at : at + bins] = part
            else:
                spectrum_ref[:, at : at + bins] += part
    half = bins // 2
    for at in (0, bins):
        real_part = spectrum_ref[:, at : at + half]
        imag_part = spectrum_ref[:, at + half : at + bins]
        amplitude = lax.rsqrt(
            jnp.maximum(real_part * real_part + imag_part * imag_part, nfft / 4.0)
        )
        for part, offset in ((real_part, 0), (imag_part, bins)):
            white = (part * amplitude).astype(jnp.bfloat16)
            for w in range(W):
                lane = w * 2 * bins + offset + at // 2
                top = w * CH
                low_ref[:, lane : lane + half] = white[top : top + CH // 2]
                high_ref[:, lane : lane + half] = white[top + CH // 2 : top + CH]


def whiten(me, mask, arrived, table, capacity, plans, places):
    nfft, width = 2 * table.shape[0], table.shape[1]
    vmem = pl.BlockSpec(memory_space=pltpu.VMEM)
    smem = pl.BlockSpec(memory_space=pltpu.SMEM)
    return pl.pallas_call(
        functools.partial(whiten_kernel, capacity, plans, places),
        in_specs=[smem, smem]
        + [vmem] * len(arrived)
        + [pl.BlockSpec(memory_space=pltpu.HBM)],
        out_specs=[vmem, vmem, smem],
        out_shape=[
            jax.ShapeDtypeStruct((CH // 2, W * width), jnp.bfloat16),
            jax.ShapeDtypeStruct((CH // 2, W * width), jnp.bfloat16),
            jax.ShapeDtypeStruct((1,), jnp.int32),
        ],
        scratch_shapes=[
            pltpu.VMEM(table.shape, jnp.bfloat16),
            pltpu.VMEM((CH * W, nfft), jnp.float32),
            pltpu.VMEM((CH * W, width), jnp.float32),
            pltpu.SemaphoreType.DMA((nfft // 1024,)),
        ],
        compiler_params=pltpu.CompilerParams(vmem_limit_bytes=50 * 1024 * 1024),
        name="whiten",
    )(me, mask, *arrived, table)


BLOCK = 32
PIECE = 16


def correlate_kernel(
    order_ref, own_low, own_high, rows_ref, spread_ref, *refs
):
    *partners, out_hbm, both_ref, wide_ref, near_ref, turned_a, turned_b, found_a, found_b, out_ref, sems, loaded = refs
    bins = rows_ref.shape[1]
    terms = rows_ref.shape[0] // 3
    lags = out_ref.shape[4]
    blocks = CH // BLOCK
    turned, found = (turned_a, turned_b), (found_a, found_b)

    def turn(block, slot):
        even = rows_ref[:terms, :]
        odd = rows_ref[terms : 2 * terms, :]
        minus = rows_ref[2 * terms :, :]
        for k in range(BLOCK):
            u = wide_ref[pl.ds(block * BLOCK + k, 1), :]
            top = slice(2 * k * terms, (2 * k + 1) * terms)
            low = slice((2 * k + 1) * terms, (2 * k + 2) * terms)
            for w in range(W):
                at = w * 2 * bins
                real, imag = slice(at, at + bins), slice(at + bins, at + 2 * bins)
                ur = jnp.broadcast_to(u[:, real], (terms, bins)).astype(jnp.bfloat16)
                ui = jnp.broadcast_to(u[:, imag], (terms, bins)).astype(jnp.bfloat16)
                turned[slot][top, real] = ur * even
                turned[slot][top, imag] = ui * even
                turned[slot][low, real] = ui * odd
                turned[slot][low, imag] = ur * minus

    def find(slot):
        sums = jnp.dot(turned[slot][...], both_ref[...], preferred_element_type=jnp.float32)
        found[slot][...] = jnp.transpose(sums.astype(jnp.bfloat16))

    def spread(slot, block):
        wide = 8 * terms
        for piece in range(BLOCK // PIECE):
            start = 2 * piece * PIECE * terms
            stacked = jnp.concatenate(
                [
                    found[slot][:, k : k + wide]
                    for k in range(start, start + 2 * PIECE * terms, wide)
                ],
                axis=0,
            )
            lagged = jnp.dot(
                stacked, spread_ref[...], preferred_element_type=jnp.float32
            ).astype(jnp.bfloat16)
            unit = block * (BLOCK // PIECE) + piece
            for k in range(PIECE):
                for r in range(2):
                    top = (k // 4 * 2 + r) * CH
                    lane = k % 4 * lags
                    out_ref[unit, r, k] = lagged[top : top + CH, lane : lane + lags]
            write(unit).start()

    def write(unit):
        return pltpu.make_async_copy(
            out_ref.at[unit], out_hbm.at[:, pl.ds(unit * PIECE, PIECE)], sems.at[unit]
        )

    half = CH // 2
    loads = [
        pltpu.make_async_copy(source, near_ref.at[pl.ds(k * half, half)], loaded.at[k])
        for k, source in enumerate(partners)
    ]
    for copy in loads:
        copy.start()
    wide_ref[:half, :] = own_low[...].astype(jnp.float32)
    wide_ref[half:, :] = own_high[...].astype(jnp.float32)
    turn(0, 0)
    for copy in loads:
        copy.wait()
    at = pl.multiple_of(order_ref[0] * CH, CH)
    both_ref[:, pl.ds(at, CH)] = jnp.transpose(near_ref[:CH, :])
    both_ref[:, pl.ds(CH - at, CH)] = jnp.transpose(near_ref[CH:, :])
    turn(1, 1)
    find(0)
    for block in range(1, blocks):
        if block + 1 < blocks:
            turn(block + 1, (block + 1) % 2)
        find(block % 2)
        spread((block - 1) % 2, block - 1)
    spread((blocks - 1) % 2, blocks - 1)
    for unit in range(CH // PIECE):
        write(unit).wait()


def correlate(order, own, first, second, nfft, lags):
    depth = own[0].shape[1]
    bins = depth // (2 * W)
    rows, spread = lag_tables(nfft, bins, lags, 1.0 / math.sqrt(W * bins))
    terms = rows.shape[0] // 3
    vmem = pl.BlockSpec(memory_space=pltpu.VMEM)
    return pl.pallas_call(
        correlate_kernel,
        in_specs=[pl.BlockSpec(memory_space=pltpu.SMEM)]
        + [vmem] * 4
        + [pl.BlockSpec(memory_space=pltpu.HBM)] * 4,
        out_specs=pl.BlockSpec(memory_space=pltpu.HBM),
        out_shape=jax.ShapeDtypeStruct((2, CH, CH, lags), jnp.bfloat16),
        scratch_shapes=[
            pltpu.VMEM((depth, 2 * CH), jnp.bfloat16),
            pltpu.VMEM((CH, depth), jnp.float32),
            pltpu.VMEM((2 * CH, depth), jnp.bfloat16),
            pltpu.VMEM((BLOCK * 2 * terms, depth), jnp.bfloat16),
            pltpu.VMEM((BLOCK * 2 * terms, depth), jnp.bfloat16),
            pltpu.VMEM((2 * CH, BLOCK * 2 * terms), jnp.bfloat16),
            pltpu.VMEM((2 * CH, BLOCK * 2 * terms), jnp.bfloat16),
            pltpu.VMEM((CH // PIECE, 2, PIECE, CH, lags), jnp.bfloat16),
            pltpu.SemaphoreType.DMA((CH // PIECE,)),
            pltpu.SemaphoreType.DMA((4,)),
        ],
        compiler_params=pltpu.CompilerParams(vmem_limit_bytes=60 * 1024 * 1024),
        name="correlate",
    )(order, *own, jnp.asarray(rows), jnp.asarray(spread), *first, *second)


def swap(block, mask):
    count = lax.axis_size("blk")
    return lax.ppermute(block, "blk", [(low, low ^ mask) for low in range(count)])


def swap_halves(tile, mask):
    return tuple(swap(half, mask) for half in tile)


def exchange(mask, moving):
    count = lax.axis_size("blk")
    full = count - 1
    first = swap_halves(moving, full)
    if 2 * mask >= count:
        return moving, swap_halves(first, mask ^ full), first
    return moving, swap_halves(moving, mask), first


def deliver(me, mask, labels, records, plan):
    owners = lax.axis_size("blk")
    held, nfft = records.shape
    capacity = max(16, 2 * held // owners)
    whole = full_plan(capacity, nfft // 128)
    table = jnp.asarray(forward_table(nfft, F))
    if owners > 16:
        plans = (whole,) * owners
        (outgoing,) = pack(me, labels, records, capacity, plans, False)
        arrived = [lax.all_to_all(outgoing, "blk", split_axis=0, concat_axis=0, tiled=True)]
        *tile, branch = whiten(me, mask, arrived, table, capacity, plans, None)
        return tuple(tile), branch
    half = owners // 2
    plans = (whole,) + (plan(capacity, nfft // 128),) * (owners - 1)
    outgoing = pack(me, labels, records, capacity, plans, True)
    places = [half]
    for distance in range(1, half):
        places += [distance, half + distance]
    arrived = [swap(outgoing[distance], distance) for distance in places] + [outgoing[0]]
    places.append(0)
    ordered = tuple(plans[distance] for distance in places)
    *tile, branch = whiten(me, mask, arrived, table, capacity, ordered, places)
    return tuple(tile), branch


def local(records, dest, slot, valid, masks):
    owners = lax.axis_size("blk")
    held, nfft = records.shape
    full = owners - 1
    me = lax.axis_index("blk").astype(jnp.int32).reshape(1)
    mask = (masks[0] + masks[1] - full).reshape(1)
    labels = [label.reshape(1, held) for label in (dest, slot, valid)]
    if owners <= 16:
        tile, branch = deliver(me, mask, labels, records, short_plan)
        known = [functools.partial(exchange, m) for m in range(1, full)]

        def again(tile):
            tile, branch = deliver(me, mask, labels, records, full_plan)
            return lax.switch(branch[0], known, tile)

        own, second, first = lax.switch(branch[0], known + [again], tile)
    else:
        own, _ = deliver(me, mask, labels, records, full_plan)
        second = own
        for bit in range(owners.bit_length() - 1):
            moved = swap_halves(second, 1 << bit)
            flip = mask >> bit & 1 == 1
            second = tuple(jnp.where(flip, new, old) for new, old in zip(moved, second))
        first = swap_halves(own, full)
    order = (masks[:1] != full).astype(jnp.int32)
    return correlate(order, own, first, second, nfft, LAGS)


def solution(mesh):
    return jax.shard_map(
        local,
        mesh=mesh,
        in_specs=(
            P(("groups", "blk"), None),
            P(("groups", "blk"), None),
            P(("groups", "blk"), None),
            P(("groups", "blk"), None),
            P(),
        ),
        out_specs=P(None, ("groups", "blk"), None, None),
        check_vma=False,
    )
```

```python
import functools
import math

import jax
import jax.numpy as jnp
import numpy as np
from jax import lax
from jax.experimental import pallas as pl
from jax.experimental.pallas import tpu as pltpu
from jax.sharding import PartitionSpec as P

CH = 128
F = 256
LAGS = 128
W = 2
LOW_BITS = 4


def bin_order(bins):
    return np.concatenate([np.arange(2, bins + 1, 2), np.arange(1, bins + 1, 2)])


def forward_table(nfft, bins):
    sample = np.arange(nfft // 2, dtype=np.int64)[:, None]
    angle = (sample * bin_order(bins)[None, :] % nfft) * (2.0 * math.pi / nfft)
    cos, sin = np.cos(angle), np.sin(angle)
    half = bins // 2
    table = [cos[:, :half], -sin[:, :half], cos[:, half:], -sin[:, half:]]
    return np.concatenate(table, axis=1).astype(np.float32).astype(jnp.bfloat16)


def lag_tables(nfft, bins, lags, scale):
    half = lags // 2
    count = lags + 1
    place = np.arange(count)
    middle = ((count - 1 - 2 * place) / 2.0) ** 2 * math.cos(2.0 * math.pi * bins / nfft)
    aside = (place[1:] * (count - place[1:])) / 2.0
    _, basis = np.linalg.eigh(np.diag(middle) + np.diag(aside, 1) + np.diag(aside, -1))
    basis = basis[:, ::-1][:, :half]
    even, odd = basis[:, 0::2], basis[:, 1::2]
    even = even * np.sign(even[half])
    odd = odd * np.sign(odd[half + 1])
    freq = bin_order(bins)[None, :]
    angle = (freq * (place[:, None] - half) % nfft) * (2.0 * math.pi / nfft)
    rows = [even.T @ np.cos(angle), odd.T @ -np.sin(angle)]
    rest = np.cos(angle) - np.sin(angle) - even @ rows[0] - odd @ rows[1]
    assert np.abs(rest).max() < 1e-7
    rows = np.concatenate(rows + [-rows[1]])
    basis = np.concatenate([even, odd], axis=1)[:lags].T * scale
    blank = np.zeros_like(basis)
    spread = np.concatenate(
        [np.concatenate([basis if k == n else blank for n in range(4)], axis=1) for k in range(4)]
    )

    def narrow(table):
        return (np.round(table * 2.0**28) / 2.0**28).astype(np.float32).astype(jnp.bfloat16)

    return narrow(rows), narrow(spread)


def iota(shape, dim):
    return lax.broadcasted_iota(jnp.int32, shape, dim)


LABELS = 8


def full_plan(capacity, chunks):
    return (capacity,) * chunks


def short_plan(capacity, chunks):
    eighths = (8, 8, 8, 8, 8, 8, 8, 8, 8, 7, 7, 6, 6, 5, 4, 3)
    return tuple(capacity * eighths[c * len(eighths) // chunks] // 8 for c in range(chunks))


def pack_kernel(
    owners, capacity, plans, me_ref, dest_hbm, slot_hbm, valid_hbm, records_hbm, *refs
):
    *out_refs, dest_ref, slot_ref, valid_ref, records_ref, sems = refs
    held, nfft = records_ref.shape
    rows = owners * capacity
    width = 512
    small = [
        pltpu.make_async_copy(source, target, sems.at[k])
        for k, (source, target) in enumerate(
            [(dest_hbm, dest_ref), (slot_hbm, slot_ref), (valid_hbm, valid_ref)]
        )
    ]
    large = [
        pltpu.make_async_copy(
            records_hbm.at[:, pl.ds(begin, width)],
            records_ref.at[:, pl.ds(begin, width)],
            sems.at[3 + begin // width],
        )
        for begin in range(0, nfft, width)
    ]
    for copy in small + large:
        copy.start()
    for copy in small:
        copy.wait()
    part = dest_ref[...]
    if len(out_refs) > 1:
        part = part ^ me_ref[0]
    valid = valid_ref[...]
    first = valid * held + (held - 1 - iota((1, held), 1))

    def column(row):
        wide = jnp.transpose(jnp.broadcast_to(row.astype(jnp.float32), (128, held)))
        return jnp.concatenate([wide] * (held // 128), axis=1)

    same = column(part) == part.astype(jnp.float32)
    before = jnp.where(same & (column(first) > first.astype(jnp.float32)), 1.0, 0.0)
    rank = jnp.sum(before, axis=0, keepdims=True).astype(jnp.int32)
    over = jnp.zeros((1, held), jnp.int32)
    for plan in sorted(set(plans)):
        member = functools.reduce(
            jnp.logical_or, [part == d for d in range(owners) if plans[d] == plan]
        )
        for size in sorted(set(plan)):
            if size < capacity:
                reach = 128 * sum(count > size for count in plan)
                over += jnp.where(member & (rank >= size) & (valid > reach), 1, 0)
    over = jnp.max(jnp.minimum(over, 1).astype(jnp.float32), axis=1, keepdims=True)
    position = part * capacity + rank
    order = (iota((rows, held), 0) == position).astype(jnp.float32).astype(jnp.bfloat16)
    row = iota((16, held), 0)
    labels = jnp.where(
        row == 0,
        slot_ref[...],
        jnp.where(
            row == 1,
            valid >> LOW_BITS,
            jnp.where(row == 2, valid & ((1 << LOW_BITS) - 1), 0),
        ),
    )
    moved = lax.dot_general(
        labels.astype(jnp.float32).astype(jnp.bfloat16),
        order,
        (((1,), (1,)), ((), ())),
        preferred_element_type=jnp.float32,
    )
    moved = jnp.where(iota((16, rows), 0) == 3, over, moved).astype(jnp.bfloat16)

    def put(d, at, value):
        if len(out_refs) > 1:
            out_refs[d][at : at + value.shape[0], :] = value
        else:
            out_refs[0][d, at : at + value.shape[0], :] = value

    for d in range(owners):
        at = d * capacity // 128 * 128
        put(d, sum(plans[d]), moved[:LABELS, at : at + 128])
    for begin in range(0, nfft, width):
        large[begin // width].wait()
        ordered = jnp.dot(
            order, records_ref[:, begin : begin + width], preferred_element_type=jnp.float32
        ).astype(jnp.bfloat16)
        for lane in range(0, width, 128):
            c = (begin + lane) // 128
            for d in range(owners):
                top = d * capacity
                put(d, sum(plans[d][:c]), ordered[top : top + plans[d][c], lane : lane + 128])


def pack(me, labels, records, capacity, plans, split):
    held, nfft = records.shape
    owners = len(plans)
    hbm = pl.BlockSpec(memory_space=pltpu.HBM)
    vmem = pl.BlockSpec(memory_space=pltpu.VMEM)
    shapes = [(sum(plan) + LABELS, 128) for plan in plans]
    if not split:
        shapes = [(owners,) + shapes[0]]
    return pl.pallas_call(
        functools.partial(pack_kernel, owners, capacity, plans),
        in_specs=[pl.BlockSpec(memory_space=pltpu.SMEM)] + [hbm] * 4,
        out_specs=[vmem] * len(shapes),
        out_shape=[jax.ShapeDtypeStruct(shape, jnp.bfloat16) for shape in shapes],
        scratch_shapes=[pltpu.VMEM((1, held), jnp.int32)] * 3
        + [pltpu.VMEM((held, nfft), jnp.bfloat16), pltpu.SemaphoreType.DMA((3 + nfft // 512,))],
        compiler_params=pltpu.CompilerParams(vmem_limit_bytes=48 * 1024 * 1024),
        name="pack",
    )(me, *labels, records)


def whiten_kernel(capacity, plans, places, me_ref, mask_ref, *refs):
    *arrived_refs, table_hbm, low_ref, high_ref, branch_ref, table_ref, trace_ref, spectrum_ref, sems = refs
    owners = len(plans)
    split = len(arrived_refs) > 1
    nfft = trace_ref.shape[1]
    rows = owners * capacity
    slots = CH * W
    bins = table_ref.shape[1] // 2
    shift = capacity.bit_length() - 1
    width = 256
    depth = 512
    loads = [
        pltpu.make_async_copy(
            table_hbm.at[pl.ds(at, depth)], table_ref.at[pl.ds(at, depth)], sems.at[at // depth]
        )
        for at in range(0, nfft // 2, depth)
    ]
    for copy in loads:
        copy.start()

    def take(c):
        if not split:
            at, count = sum(plans[0][:c]), plans[0][c] if c < len(plans[0]) else LABELS
            return arrived_refs[0][:, at : at + count, :].reshape(owners * count, 128)
        pieces = []
        for ref, plan in zip(arrived_refs, plans):
            at, count = sum(plan[:c]), plan[c] if c < len(plan) else LABELS
            pieces.append(ref[at : at + count, :])
            if c < len(plan) and count < capacity:
                pieces.append(jnp.zeros((capacity - count, 128), jnp.bfloat16))
        return jnp.concatenate(pieces, axis=0)

    labels = take(len(plans[0])).astype(jnp.float32).reshape(owners, LABELS, 128)
    which = iota((owners, LABELS, 128), 1)
    over = jnp.max(jnp.where(which == 3, labels, 0.0))
    branch_ref[0] = jnp.where(over > 0.0, owners - 2, mask_ref[0] - 1)
    parts = jnp.concatenate(
        [jnp.sum(jnp.where(which == k, labels, 0.0), axis=1) for k in range(3)], axis=0
    )
    if split:
        part = iota((1, rows), 1) >> shift
        place = functools.reduce(
            lambda total, p: total + jnp.where(part == p, places[p], 0),
            range(owners),
            jnp.zeros((1, rows), jnp.int32),
        )
    else:
        place = me_ref[0]
    base = (place * capacity) & 127
    pick = iota((128, rows), 0) == base + (iota((128, rows), 1) & (capacity - 1))
    picked = jnp.dot(
        parts.astype(jnp.bfloat16),
        pick.astype(jnp.float32).astype(jnp.bfloat16),
        preferred_element_type=jnp.float32,
    )
    source = iota((owners, rows), 0) == iota((owners, rows), 1) >> shift
    rowed = [
        jnp.sum(
            jnp.where(source, picked[k * owners : (k + 1) * owners], 0.0), axis=0, keepdims=True
        )
        for k in range(3)
    ]
    slot_row = rowed[0].astype(jnp.int32)
    place = (slot_row & (W - 1)) * CH + (slot_row >> (W.bit_length() - 1))
    valid_row = rowed[1] * float(1 << LOW_BITS) + rowed[2]
    scatter = (iota((slots, rows), 0) == place).astype(jnp.float32).astype(jnp.bfloat16)
    valid_col = jnp.transpose(jnp.broadcast_to(valid_row, (128, rows))).astype(jnp.int32)
    power = jnp.zeros((slots, 128), jnp.float32)
    for begin in range(0, nfft, width):
        lanes = range(begin, begin + width, 128)
        inside = jnp.concatenate(
            [
                (iota((rows, 128), 1) + lane < valid_col).astype(jnp.float32).astype(jnp.bfloat16)
                for lane in lanes
            ],
            axis=1,
        )
        arrived = jnp.concatenate([take(lane // 128) for lane in lanes], axis=1)
        summed = jnp.dot(scatter, arrived * inside, preferred_element_type=jnp.float32)
        coverage = jnp.dot(scatter, inside, preferred_element_type=jnp.float32)
        trace = summed / jnp.maximum(coverage, 1.0)
        trace_ref[:, begin : begin + width] = trace
        square = trace * trace
        for lane in range(0, width, 128):
            power = power + square[:, lane : lane + 128]
    meansq = jnp.sum(power, axis=1, keepdims=True) * (1.0 / nfft)
    gain = lax.rsqrt(meansq + 1e-06)
    for begin in range(0, nfft // 2, depth):
        loads[begin // depth].wait()
        near = trace_ref[:, begin : begin + depth] * gain
        far = trace_ref[:, begin + nfft // 2 : begin + nfft // 2 + depth] * gain
        for at, folded in ((0, near + far), (bins, near - far)):
            part = jnp.dot(
                folded.astype(jnp.bfloat16),
                table_ref[begin : begin + depth, at : at + bins],
                preferred_element_type=jnp.float32,
            )
            if begin == 0:
                spectrum_ref[:, at : at + bins] = part
            else:
                spectrum_ref[:, at : at + bins] += part
    half = bins // 2
    for at in (0, bins):
        real_part = spectrum_ref[:, at : at + half]
        imag_part = spectrum_ref[:, at + half : at + bins]
        amplitude = lax.rsqrt(
            jnp.maximum(real_part * real_part + imag_part * imag_part, nfft / 4.0)
        )
        for part, offset in ((real_part, 0), (imag_part, bins)):
            white = (part * amplitude).astype(jnp.bfloat16)
            for w in range(W):
                lane = w * 2 * bins + offset + at // 2
                top = w * CH
                low_ref[:, lane : lane + half] = white[top : top + CH // 2]
                high_ref[:, lane : lane + half] = white[top + CH // 2 : top + CH]


def whiten(me, mask, arrived, table, capacity, plans, places):
    nfft, width = 2 * table.shape[0], table.shape[1]
    vmem = pl.BlockSpec(memory_space=pltpu.VMEM)
    smem = pl.BlockSpec(memory_space=pltpu.SMEM)
    return pl.pallas_call(
        functools.partial(whiten_kernel, capacity, plans, places),
        in_specs=[smem, smem]
        + [vmem] * len(arrived)
        + [pl.BlockSpec(memory_space=pltpu.HBM)],
        out_specs=[vmem, vmem, smem],
        out_shape=[
            jax.ShapeDtypeStruct((CH // 2, W * width), jnp.bfloat16),
            jax.ShapeDtypeStruct((CH // 2, W * width), jnp.bfloat16),
            jax.ShapeDtypeStruct((1,), jnp.int32),
        ],
        scratch_shapes=[
            pltpu.VMEM(table.shape, jnp.bfloat16),
            pltpu.VMEM((CH * W, nfft), jnp.float32),
            pltpu.VMEM((CH * W, width), jnp.float32),
            pltpu.SemaphoreType.DMA((nfft // 1024,)),
        ],
        compiler_params=pltpu.CompilerParams(vmem_limit_bytes=50 * 1024 * 1024),
        name="whiten",
    )(me, mask, *arrived, table)


BLOCK = 32
PIECE = 32


def correlate_kernel(
    order_ref, own_low, own_high, rows_ref, spread_ref, *refs
):
    *partners, out_hbm, both_ref, wide_ref, near_ref, turned_a, turned_b, found_a, found_b, out_ref, sems, loaded = refs
    bins = rows_ref.shape[1]
    terms = rows_ref.shape[0] // 3
    lags = out_ref.shape[4]
    blocks = CH // BLOCK
    turned, found = (turned_a, turned_b), (found_a, found_b)

    def turn(block, slot):
        even = rows_ref[:terms, :]
        odd = rows_ref[terms : 2 * terms, :]
        minus = rows_ref[2 * terms :, :]
        for k in range(BLOCK):
            u = wide_ref[pl.ds(block * BLOCK + k, 1), :]
            top = slice(2 * k * terms, (2 * k + 1) * terms)
            low = slice((2 * k + 1) * terms, (2 * k + 2) * terms)
            for w in range(W):
                at = w * 2 * bins
                real, imag = slice(at, at + bins), slice(at + bins, at + 2 * bins)
                ur = jnp.broadcast_to(u[:, real], (terms, bins)).astype(jnp.bfloat16)
                ui = jnp.broadcast_to(u[:, imag], (terms, bins)).astype(jnp.bfloat16)
                turned[slot][top, real] = ur * even
                turned[slot][top, imag] = ui * even
                turned[slot][low, real] = ui * odd
                turned[slot][low, imag] = ur * minus

    def find(slot):
        sums = jnp.dot(turned[slot][...], both_ref[...], preferred_element_type=jnp.float32)
        found[slot][...] = jnp.transpose(sums.astype(jnp.bfloat16))

    def spread(slot, block):
        wide = 8 * terms
        for piece in range(BLOCK // PIECE):
            start = 2 * piece * PIECE * terms
            stacked = jnp.concatenate(
                [
                    found[slot][:, k : k + wide]
                    for k in range(start, start + 2 * PIECE * terms, wide)
                ],
                axis=0,
            )
            lagged = jnp.dot(
                stacked, spread_ref[...], preferred_element_type=jnp.float32
            ).astype(jnp.bfloat16)
            unit = block * (BLOCK // PIECE) + piece
            for k in range(PIECE):
                for r in range(2):
                    top = (k // 4 * 2 + r) * CH
                    lane = k % 4 * lags
                    out_ref[unit, r, k] = lagged[top : top + CH, lane : lane + lags]
            write(unit).start()

    def write(unit):
        return pltpu.make_async_copy(
            out_ref.at[unit], out_hbm.at[:, pl.ds(unit * PIECE, PIECE)], sems.at[unit]
        )

    half = CH // 2
    loads = [
        pltpu.make_async_copy(source, near_ref.at[pl.ds(k * half, half)], loaded.at[k])
        for k, source in enumerate(partners)
    ]
    for copy in loads:
        copy.start()
    wide_ref[:half, :] = own_low[...].astype(jnp.float32)
    wide_ref[half:, :] = own_high[...].astype(jnp.float32)
    turn(0, 0)
    for copy in loads:
        copy.wait()
    at = pl.multiple_of(order_ref[0] * CH, CH)
    both_ref[:, pl.ds(at, CH)] = jnp.transpose(near_ref[:CH, :])
    both_ref[:, pl.ds(CH - at, CH)] = jnp.transpose(near_ref[CH:, :])
    turn(1, 1)
    find(0)
    for block in range(1, blocks):
        if block + 1 < blocks:
            turn(block + 1, (block + 1) % 2)
        find(block % 2)
        spread((block - 1) % 2, block - 1)
    spread((blocks - 1) % 2, blocks - 1)
    for unit in range(CH // PIECE):
        write(unit).wait()


def correlate(order, own, first, second, nfft, lags):
    depth = own[0].shape[1]
    bins = depth // (2 * W)
    rows, spread = lag_tables(nfft, bins, lags, 1.0 / math.sqrt(W * bins))
    terms = rows.shape[0] // 3
    vmem = pl.BlockSpec(memory_space=pltpu.VMEM)
    return pl.pallas_call(
        correlate_kernel,
        in_specs=[pl.BlockSpec(memory_space=pltpu.SMEM)]
        + [vmem] * 4
        + [pl.BlockSpec(memory_space=pltpu.HBM)] * 4,
        out_specs=pl.BlockSpec(memory_space=pltpu.HBM),
        out_shape=jax.ShapeDtypeStruct((2, CH, CH, lags), jnp.bfloat16),
        scratch_shapes=[
            pltpu.VMEM((depth, 2 * CH), jnp.bfloat16),
            pltpu.VMEM((CH, depth), jnp.float32),
            pltpu.VMEM((2 * CH, depth), jnp.bfloat16),
            pltpu.VMEM((BLOCK * 2 * terms, depth), jnp.bfloat16),
            pltpu.VMEM((BLOCK * 2 * terms, depth), jnp.bfloat16),
            pltpu.VMEM((2 * CH, BLOCK * 2 * terms), jnp.bfloat16),
            pltpu.VMEM((2 * CH, BLOCK * 2 * terms), jnp.bfloat16),
            pltpu.VMEM((CH // PIECE, 2, PIECE, CH, lags), jnp.bfloat16),
            pltpu.SemaphoreType.DMA((CH // PIECE,)),
            pltpu.SemaphoreType.DMA((4,)),
        ],
        compiler_params=pltpu.CompilerParams(vmem_limit_bytes=60 * 1024 * 1024),
        name="correlate",
    )(order, *own, jnp.asarray(rows), jnp.asarray(spread), *first, *second)


def swap(block, mask):
    count = lax.axis_size("blk")
    return lax.ppermute(block, "blk", [(low, low ^ mask) for low in range(count)])


def swap_halves(tile, mask):
    return tuple(swap(half, mask) for half in tile)


def exchange(mask, moving):
    count = lax.axis_size("blk")
    full = count - 1
    first = swap_halves(moving, full)
    if 2 * mask >= count:
        return moving, swap_halves(first, mask ^ full), first
    return moving, swap_halves(moving, mask), first


def deliver(me, mask, labels, records, plan):
    owners = lax.axis_size("blk")
    held, nfft = records.shape
    capacity = max(16, 2 * held // owners)
    whole = full_plan(capacity, nfft // 128)
    table = jnp.asarray(forward_table(nfft, F))
    if owners > 16:
        plans = (whole,) * owners
        (outgoing,) = pack(me, labels, records, capacity, plans, False)
        arrived = [lax.all_to_all(outgoing, "blk", split_axis=0, concat_axis=0, tiled=True)]
        *tile, branch = whiten(me, mask, arrived, table, capacity, plans, None)
        return tuple(tile), branch
    half = owners // 2
    plans = (whole,) + (plan(capacity, nfft // 128),) * (owners - 1)
    outgoing = pack(me, labels, records, capacity, plans, True)
    places = [half]
    for distance in range(1, half):
        places += [distance, half + distance]
    arrived = [swap(outgoing[distance], distance) for distance in places] + [outgoing[0]]
    places.append(0)
    ordered = tuple(plans[distance] for distance in places)
    *tile, branch = whiten(me, mask, arrived, table, capacity, ordered, places)
    return tuple(tile), branch


def local(records, dest, slot, valid, masks):
    owners = lax.axis_size("blk")
    held, nfft = records.shape
    full = owners - 1
    me = lax.axis_index("blk").astype(jnp.int32).reshape(1)
    mask = (masks[0] + masks[1] - full).reshape(1)
    labels = [label.reshape(1, held) for label in (dest, slot, valid)]
    if owners <= 16:
        tile, branch = deliver(me, mask, labels, records, short_plan)
        known = [functools.partial(exchange, m) for m in range(1, full)]

        def again(tile):
            tile, branch = deliver(me, mask, labels, records, full_plan)
            return lax.switch(branch[0], known, tile)

        own, second, first = lax.switch(branch[0], known + [again], tile)
    else:
        own, _ = deliver(me, mask, labels, records, full_plan)
        second = own
        for bit in range(owners.bit_length() - 1):
            moved = swap_halves(second, 1 << bit)
            flip = mask >> bit & 1 == 1
            second = tuple(jnp.where(flip, new, old) for new, old in zip(moved, second))
        first = swap_halves(own, full)
    order = (masks[:1] != full).astype(jnp.int32)
    return correlate(order, own, first, second, nfft, LAGS)


def solution(mesh):
    return jax.shard_map(
        local,
        mesh=mesh,
        in_specs=(
            P(("groups", "blk"), None),
            P(("groups", "blk"), None),
            P(("groups", "blk"), None),
            P(("groups", "blk"), None),
            P(),
        ),
        out_specs=P(None, ("groups", "blk"), None, None),
        check_vma=False,
    )
```

```python
import functools
import math

import jax
import jax.numpy as jnp
import numpy as np
from jax import lax
from jax.experimental import pallas as pl
from jax.experimental.pallas import tpu as pltpu
from jax.sharding import PartitionSpec as P

CH = 128
F = 256
LAGS = 128
W = 2
LOW_BITS = 4


def bin_order(bins):
    return np.concatenate([np.arange(2, bins + 1, 2), np.arange(1, bins + 1, 2)])


def forward_table(nfft, bins):
    sample = np.arange(nfft // 2, dtype=np.int64)[:, None]
    angle = (sample * bin_order(bins)[None, :] % nfft) * (2.0 * math.pi / nfft)
    cos, sin = np.cos(angle), np.sin(angle)
    half = bins // 2
    table = [cos[:, :half], -sin[:, :half], cos[:, half:], -sin[:, half:]]
    return np.concatenate(table, axis=1).astype(np.float32).astype(jnp.bfloat16)


def lag_tables(nfft, bins, lags, scale):
    half = lags // 2
    count = lags + 1
    place = np.arange(count)
    middle = ((count - 1 - 2 * place) / 2.0) ** 2 * math.cos(2.0 * math.pi * bins / nfft)
    aside = (place[1:] * (count - place[1:])) / 2.0
    _, basis = np.linalg.eigh(np.diag(middle) + np.diag(aside, 1) + np.diag(aside, -1))
    basis = basis[:, ::-1][:, :half]
    even, odd = basis[:, 0::2], basis[:, 1::2]
    even = even * np.sign(even[half])
    odd = odd * np.sign(odd[half + 1])
    freq = bin_order(bins)[None, :]
    angle = (freq * (place[:, None] - half) % nfft) * (2.0 * math.pi / nfft)
    rows = [even.T @ np.cos(angle), odd.T @ -np.sin(angle)]
    rest = np.cos(angle) - np.sin(angle) - even @ rows[0] - odd @ rows[1]
    assert np.abs(rest).max() < 1e-7
    rows = np.concatenate(rows + [-rows[1]])
    basis = np.concatenate([even, odd], axis=1)[:lags].T * scale
    blank = np.zeros_like(basis)
    spread = np.concatenate(
        [np.concatenate([basis if k == n else blank for n in range(4)], axis=1) for k in range(4)]
    )

    def narrow(table):
        return (np.round(table * 2.0**28) / 2.0**28).astype(np.float32).astype(jnp.bfloat16)

    return narrow(rows), narrow(spread)


def iota(shape, dim):
    return lax.broadcasted_iota(jnp.int32, shape, dim)


LABELS = 8


def full_plan(capacity, chunks):
    return (capacity,) * chunks


def short_plan(capacity, chunks):
    eighths = (8, 8, 8, 8, 8, 8, 8, 8, 8, 7, 7, 6, 6, 5, 4, 3)
    return tuple(capacity * eighths[c * len(eighths) // chunks] // 8 for c in range(chunks))


def pack_kernel(
    owners, capacity, plans, me_ref, dest_hbm, slot_hbm, valid_hbm, records_hbm, *refs
):
    *out_refs, dest_ref, slot_ref, valid_ref, records_ref, sems = refs
    held, nfft = records_ref.shape
    rows = owners * capacity
    width = 512
    small = [
        pltpu.make_async_copy(source, target, sems.at[k])
        for k, (source, target) in enumerate(
            [(dest_hbm, dest_ref), (slot_hbm, slot_ref), (valid_hbm, valid_ref)]
        )
    ]
    large = [
        pltpu.make_async_copy(
            records_hbm.at[:, pl.ds(begin, width)],
            records_ref.at[:, pl.ds(begin, width)],
            sems.at[3 + begin // width],
        )
        for begin in range(0, nfft, width)
    ]
    for copy in small + large:
        copy.start()
    for copy in small:
        copy.wait()
    part = dest_ref[...]
    if len(out_refs) > 1:
        part = part ^ me_ref[0]
    valid = valid_ref[...]
    first = valid * held + (held - 1 - iota((1, held), 1))

    def column(row):
        wide = jnp.transpose(jnp.broadcast_to(row.astype(jnp.float32), (128, held)))
        return jnp.concatenate([wide] * (held // 128), axis=1)

    same = column(part) == part.astype(jnp.float32)
    before = jnp.where(same & (column(first) > first.astype(jnp.float32)), 1.0, 0.0)
    rank = jnp.sum(before, axis=0, keepdims=True).astype(jnp.int32)
    over = jnp.zeros((1, held), jnp.int32)
    for plan in sorted(set(plans)):
        member = functools.reduce(
            jnp.logical_or, [part == d for d in range(owners) if plans[d] == plan]
        )
        for size in sorted(set(plan)):
            if size < capacity:
                reach = 128 * sum(count > size for count in plan)
                over += jnp.where(member & (rank >= size) & (valid > reach), 1, 0)
    over = jnp.max(jnp.minimum(over, 1).astype(jnp.float32), axis=1, keepdims=True)
    position = part * capacity + rank
    order = (iota((rows, held), 0) == position).astype(jnp.float32).astype(jnp.bfloat16)
    row = iota((16, held), 0)
    labels = jnp.where(
        row == 0,
        slot_ref[...],
        jnp.where(
            row == 1,
            valid >> LOW_BITS,
            jnp.where(row == 2, valid & ((1 << LOW_BITS) - 1), 0),
        ),
    )
    moved = lax.dot_general(
        labels.astype(jnp.float32).astype(jnp.bfloat16),
        order,
        (((1,), (1,)), ((), ())),
        preferred_element_type=jnp.float32,
    )
    moved = jnp.where(iota((16, rows), 0) == 3, over, moved).astype(jnp.bfloat16)

    def put(d, at, value):
        if len(out_refs) > 1:
            out_refs[d][at : at + value.shape[0], :] = value
        else:
            out_refs[0][d, at : at + value.shape[0], :] = value

    for d in range(owners):
        at = d * capacity // 128 * 128
        put(d, sum(plans[d]), moved[:LABELS, at : at + 128])
    for begin in range(0, nfft, width):
        large[begin // width].wait()
        ordered = jnp.dot(
            order, records_ref[:, begin : begin + width], preferred_element_type=jnp.float32
        ).astype(jnp.bfloat16)
        for lane in range(0, width, 128):
            c = (begin + lane) // 128
            for d in range(owners):
                top = d * capacity
                put(d, sum(plans[d][:c]), ordered[top : top + plans[d][c], lane : lane + 128])


def pack(me, labels, records, capacity, plans, split):
    held, nfft = records.shape
    owners = len(plans)
    hbm = pl.BlockSpec(memory_space=pltpu.HBM)
    vmem = pl.BlockSpec(memory_space=pltpu.VMEM)
    shapes = [(sum(plan) + LABELS, 128) for plan in plans]
    if not split:
        shapes = [(owners,) + shapes[0]]
    return pl.pallas_call(
        functools.partial(pack_kernel, owners, capacity, plans),
        in_specs=[pl.BlockSpec(memory_space=pltpu.SMEM)] + [hbm] * 4,
        out_specs=[vmem] * len(shapes),
        out_shape=[jax.ShapeDtypeStruct(shape, jnp.bfloat16) for shape in shapes],
        scratch_shapes=[pltpu.VMEM((1, held), jnp.int32)] * 3
        + [pltpu.VMEM((held, nfft), jnp.bfloat16), pltpu.SemaphoreType.DMA((3 + nfft // 512,))],
        compiler_params=pltpu.CompilerParams(vmem_limit_bytes=48 * 1024 * 1024),
        name="pack",
    )(me, *labels, records)


def whiten_kernel(capacity, plans, places, me_ref, mask_ref, *refs):
    *arrived_refs, table_hbm, low_ref, high_ref, branch_ref, table_ref, trace_ref, spectrum_ref, sems = refs
    owners = len(plans)
    split = len(arrived_refs) > 1
    nfft = trace_ref.shape[1]
    rows = owners * capacity
    slots = CH * W
    bins = table_ref.shape[1] // 2
    shift = capacity.bit_length() - 1
    width = 256
    depth = 512
    loads = [
        pltpu.make_async_copy(
            table_hbm.at[pl.ds(at, depth)], table_ref.at[pl.ds(at, depth)], sems.at[at // depth]
        )
        for at in range(0, nfft // 2, depth)
    ]
    for copy in loads:
        copy.start()

    def take(c):
        if not split:
            at, count = sum(plans[0][:c]), plans[0][c] if c < len(plans[0]) else LABELS
            return arrived_refs[0][:, at : at + count, :].reshape(owners * count, 128)
        pieces = []
        for ref, plan in zip(arrived_refs, plans):
            at, count = sum(plan[:c]), plan[c] if c < len(plan) else LABELS
            pieces.append(ref[at : at + count, :])
            if c < len(plan) and count < capacity:
                pieces.append(jnp.zeros((capacity - count, 128), jnp.bfloat16))
        return jnp.concatenate(pieces, axis=0)

    labels = take(len(plans[0])).astype(jnp.float32).reshape(owners, LABELS, 128)
    which = iota((owners, LABELS, 128), 1)
    over = jnp.max(jnp.where(which == 3, labels, 0.0))
    branch_ref[0] = jnp.where(over > 0.0, owners - 2, mask_ref[0] - 1)
    parts = jnp.concatenate(
        [jnp.sum(jnp.where(which == k, labels, 0.0), axis=1) for k in range(3)], axis=0
    )
    if split:
        part = iota((1, rows), 1) >> shift
        place = functools.reduce(
            lambda total, p: total + jnp.where(part == p, places[p], 0),
            range(owners),
            jnp.zeros((1, rows), jnp.int32),
        )
    else:
        place = me_ref[0]
    base = (place * capacity) & 127
    pick = iota((128, rows), 0) == base + (iota((128, rows), 1) & (capacity - 1))
    picked = jnp.dot(
        parts.astype(jnp.bfloat16),
        pick.astype(jnp.float32).astype(jnp.bfloat16),
        preferred_element_type=jnp.float32,
    )
    source = iota((owners, rows), 0) == iota((owners, rows), 1) >> shift
    rowed = [
        jnp.sum(
            jnp.where(source, picked[k * owners : (k + 1) * owners], 0.0), axis=0, keepdims=True
        )
        for k in range(3)
    ]
    slot_row = rowed[0].astype(jnp.int32)
    place = (slot_row & (W - 1)) * CH + (slot_row >> (W.bit_length() - 1))
    valid_row = rowed[1] * float(1 << LOW_BITS) + rowed[2]
    scatter = (iota((slots, rows), 0) == place).astype(jnp.float32).astype(jnp.bfloat16)
    valid_col = jnp.transpose(jnp.broadcast_to(valid_row, (128, rows))).astype(jnp.int32)
    power = jnp.zeros((slots, 128), jnp.float32)
    for begin in range(0, nfft, width):
        lanes = range(begin, begin + width, 128)
        inside = jnp.concatenate(
            [
                (iota((rows, 128), 1) + lane < valid_col).astype(jnp.float32).astype(jnp.bfloat16)
                for lane in lanes
            ],
            axis=1,
        )
        arrived = jnp.concatenate([take(lane // 128) for lane in lanes], axis=1)
        summed = jnp.dot(scatter, arrived * inside, preferred_element_type=jnp.float32)
        coverage = jnp.dot(scatter, inside, preferred_element_type=jnp.float32)
        trace = summed / jnp.maximum(coverage, 1.0)
        trace_ref[:, begin : begin + width] = trace
        square = trace * trace
        for lane in range(0, width, 128):
            power = power + square[:, lane : lane + 128]
    meansq = jnp.sum(power, axis=1, keepdims=True) * (1.0 / nfft)
    gain = lax.rsqrt(meansq + 1e-06)
    for begin in range(0, nfft // 2, depth):
        loads[begin // depth].wait()
        near = trace_ref[:, begin : begin + depth] * gain
        far = trace_ref[:, begin + nfft // 2 : begin + nfft // 2 + depth] * gain
        for at, folded in ((0, near + far), (bins, near - far)):
            part = jnp.dot(
                folded.astype(jnp.bfloat16),
                table_ref[begin : begin + depth, at : at + bins],
                preferred_element_type=jnp.float32,
            )
            if begin == 0:
                spectrum_ref[:, at : at + bins] = part
            else:
                spectrum_ref[:, at : at + bins] += part
    half = bins // 2
    for at in (0, bins):
        real_part = spectrum_ref[:, at : at + half]
        imag_part = spectrum_ref[:, at + half : at + bins]
        amplitude = lax.rsqrt(
            jnp.maximum(real_part * real_part + imag_part * imag_part, nfft / 4.0)
        )
        for part, offset in ((real_part, 0), (imag_part, bins)):
            white = (part * amplitude).astype(jnp.bfloat16)
            for w in range(W):
                lane = w * 2 * bins + offset + at // 2
                top = w * CH
                low_ref[:, lane : lane + half] = white[top : top + CH // 2]
                high_ref[:, lane : lane + half] = white[top + CH // 2 : top + CH]


def whiten(me, mask, arrived, table, capacity, plans, places):
    nfft, width = 2 * table.shape[0], table.shape[1]
    vmem = pl.BlockSpec(memory_space=pltpu.VMEM)
    smem = pl.BlockSpec(memory_space=pltpu.SMEM)
    return pl.pallas_call(
        functools.partial(whiten_kernel, capacity, plans, places),
        in_specs=[smem, smem]
        + [vmem] * len(arrived)
        + [pl.BlockSpec(memory_space=pltpu.HBM)],
        out_specs=[vmem, vmem, smem],
        out_shape=[
            jax.ShapeDtypeStruct((CH // 2, W * width), jnp.bfloat16),
            jax.ShapeDtypeStruct((CH // 2, W * width), jnp.bfloat16),
            jax.ShapeDtypeStruct((1,), jnp.int32),
        ],
        scratch_shapes=[
            pltpu.VMEM(table.shape, jnp.bfloat16),
            pltpu.VMEM((CH * W, nfft), jnp.float32),
            pltpu.VMEM((CH * W, width), jnp.float32),
            pltpu.SemaphoreType.DMA((nfft // 1024,)),
        ],
        compiler_params=pltpu.CompilerParams(vmem_limit_bytes=50 * 1024 * 1024),
        name="whiten",
    )(me, mask, *arrived, table)


BLOCK = 32
PIECE = 16


def correlate_kernel(
    order_ref, own_low, own_high, rows_ref, spread_ref, *refs
):
    *partners, out_hbm, both_ref, wide_ref, near_ref, turned_a, turned_b, found_a, found_b, out_ref, sems, loaded = refs
    bins = rows_ref.shape[1]
    terms = rows_ref.shape[0] // 3
    lags = out_ref.shape[4]
    blocks = CH // BLOCK
    turned, found = (turned_a, turned_b), (found_a, found_b)

    def turn(block, slot):
        even = rows_ref[:terms, :]
        odd = rows_ref[terms : 2 * terms, :]
        minus = rows_ref[2 * terms :, :]
        for k in range(BLOCK):
            u = wide_ref[pl.ds(block * BLOCK + k, 1), :]
            top = slice(2 * k * terms, (2 * k + 1) * terms)
            low = slice((2 * k + 1) * terms, (2 * k + 2) * terms)
            for w in range(W):
                at = w * 2 * bins
                real, imag = slice(at, at + bins), slice(at + bins, at + 2 * bins)
                ur = jnp.broadcast_to(u[:, real], (terms, bins)).astype(jnp.bfloat16)
                ui = jnp.broadcast_to(u[:, imag], (terms, bins)).astype(jnp.bfloat16)
                turned[slot][top, real] = ur * even
                turned[slot][top, imag] = ui * even
                turned[slot][low, real] = ui * odd
                turned[slot][low, imag] = ur * minus

    def find(slot):
        sums = jnp.dot(turned[slot][...], both_ref[...], preferred_element_type=jnp.float32)
        found[slot][...] = jnp.transpose(sums.astype(jnp.bfloat16))

    def spread(slot, block):
        wide = 8 * terms
        for piece in range(BLOCK // PIECE):
            start = 2 * piece * PIECE * terms
            stacked = jnp.concatenate(
                [
                    found[slot][:, k : k + wide]
                    for k in range(start, start + 2 * PIECE * terms, wide)
                ],
                axis=0,
            )
            lagged = jnp.dot(
                stacked, spread_ref[...], preferred_element_type=jnp.float32
            ).astype(jnp.bfloat16)
            unit = block * (BLOCK // PIECE) + piece
            for k in range(PIECE):
                for r in range(2):
                    top = (k // 4 * 2 + r) * CH
                    lane = k % 4 * lags
                    out_ref[unit, r, k] = lagged[top : top + CH, lane : lane + lags]
            write(unit).start()

    def write(unit):
        return pltpu.make_async_copy(
            out_ref.at[unit], out_hbm.at[:, pl.ds(unit * PIECE, PIECE)], sems.at[unit]
        )

    half = CH // 2
    loads = [
        pltpu.make_async_copy(source, near_ref.at[pl.ds(k * half, half)], loaded.at[k])
        for k, source in enumerate(partners)
    ]
    for copy in loads:
        copy.start()
    wide_ref[:half, :] = own_low[...].astype(jnp.float32)
    wide_ref[half:, :] = own_high[...].astype(jnp.float32)
    turn(0, 0)
    for copy in loads:
        copy.wait()
    at = pl.multiple_of(order_ref[0] * CH, CH)
    both_ref[:, pl.ds(at, CH)] = jnp.transpose(near_ref[:CH, :])
    both_ref[:, pl.ds(CH - at, CH)] = jnp.transpose(near_ref[CH:, :])
    turn(1, 1)
    find(0)
    for block in range(1, blocks):
        if block + 1 < blocks:
            turn(block + 1, (block + 1) % 2)
        find(block % 2)
        spread((block - 1) % 2, block - 1)
    spread((blocks - 1) % 2, blocks - 1)
    for unit in range(CH // PIECE):
        write(unit).wait()


def correlate(order, own, first, second, nfft, lags):
    depth = own[0].shape[1]
    bins = depth // (2 * W)
    rows, spread = lag_tables(nfft, bins, lags, 1.0 / math.sqrt(W * bins))
    terms = rows.shape[0] // 3
    vmem = pl.BlockSpec(memory_space=pltpu.VMEM)
    return pl.pallas_call(
        correlate_kernel,
        in_specs=[pl.BlockSpec(memory_space=pltpu.SMEM)]
        + [vmem] * 4
        + [pl.BlockSpec(memory_space=pltpu.HBM)] * 4,
        out_specs=pl.BlockSpec(memory_space=pltpu.HBM),
        out_shape=jax.ShapeDtypeStruct((2, CH, CH, lags), jnp.bfloat16),
        scratch_shapes=[
            pltpu.VMEM((depth, 2 * CH), jnp.bfloat16),
            pltpu.VMEM((CH, depth), jnp.float32),
            pltpu.VMEM((2 * CH, depth), jnp.bfloat16),
            pltpu.VMEM((BLOCK * 2 * terms, depth), jnp.bfloat16),
            pltpu.VMEM((BLOCK * 2 * terms, depth), jnp.bfloat16),
            pltpu.VMEM((2 * CH, BLOCK * 2 * terms), jnp.bfloat16),
            pltpu.VMEM((2 * CH, BLOCK * 2 * terms), jnp.bfloat16),
            pltpu.VMEM((CH // PIECE, 2, PIECE, CH, lags), jnp.bfloat16),
            pltpu.SemaphoreType.DMA((CH // PIECE,)),
            pltpu.SemaphoreType.DMA((4,)),
        ],
        compiler_params=pltpu.CompilerParams(vmem_limit_bytes=60 * 1024 * 1024),
        name="correlate",
    )(order, *own, jnp.asarray(rows), jnp.asarray(spread), *first, *second)


def swap(block, mask):
    count = lax.axis_size("blk")
    return lax.ppermute(block, "blk", [(low, low ^ mask) for low in range(count)])


def swap_halves(tile, mask):
    return tuple(swap(half, mask) for half in tile)


def exchange(mask, moving):
    count = lax.axis_size("blk")
    full = count - 1
    first = swap_halves(moving, full)
    if 2 * mask >= count:
        return moving, swap_halves(first, mask ^ full), first
    return moving, swap_halves(moving, mask), first


def deliver(me, mask, labels, records, plan):
    owners = lax.axis_size("blk")
    held, nfft = records.shape
    capacity = max(16, 2 * held // owners)
    whole = full_plan(capacity, nfft // 128)
    table = jnp.asarray(forward_table(nfft, F))
    if owners > 16:
        plans = (whole,) * owners
        (outgoing,) = pack(me, labels, records, capacity, plans, False)
        arrived = [lax.all_to_all(outgoing, "blk", split_axis=0, concat_axis=0, tiled=True)]
        *tile, branch = whiten(me, mask, arrived, table, capacity, plans, None)
        return tuple(tile), branch
    half = owners // 2
    plans = (whole,) + (plan(capacity, nfft // 128),) * (owners - 1)
    outgoing = pack(me, labels, records, capacity, plans, True)
    places = [half]
    for distance in range(1, half):
        places += [distance, half + distance]
    arrived = [swap(outgoing[distance], distance) for distance in places] + [outgoing[0]]
    places.append(0)
    ordered = tuple(plans[distance] for distance in places)
    *tile, branch = whiten(me, mask, arrived, table, capacity, ordered, places)
    return tuple(tile), branch


def local(records, dest, slot, valid, masks):
    owners = lax.axis_size("blk")
    held, nfft = records.shape
    full = owners - 1
    me = lax.axis_index("blk").astype(jnp.int32).reshape(1)
    mask = (masks[0] + masks[1] - full).reshape(1)
    labels = [label.reshape(1, held) for label in (dest, slot, valid)]
    if owners <= 16:
        tile, branch = deliver(me, mask, labels, records, short_plan)
        known = [functools.partial(exchange, m) for m in range(1, full)]

        def again(tile):
            tile, branch = deliver(me, mask, labels, records, full_plan)
            return lax.switch(branch[0], known, tile)

        own, second, first = lax.switch(branch[0], known + [again], tile)
    else:
        own, _ = deliver(me, mask, labels, records, full_plan)
        second = own
        for bit in range(owners.bit_length() - 1):
            moved = swap_halves(second, 1 << bit)
            flip = mask >> bit & 1 == 1
            second = tuple(jnp.where(flip, new, old) for new, old in zip(moved, second))
        first = swap_halves(own, full)
    order = (masks[:1] != full).astype(jnp.int32)
    return correlate(order, own, first, second, nfft, LAGS)


def solution(mesh):
    return jax.shard_map(
        local,
        mesh=mesh,
        in_specs=(
            P(("groups", "blk"), None),
            P(("groups", "blk"), None),
            P(("groups", "blk"), None),
            P(("groups", "blk"), None),
            P(),
        ),
        out_specs=P(None, ("groups", "blk"), None, None),
        check_vma=False,
    )
```
